128 devices in a mesh: seq: 64 (over x, y_hi, z, core), ffn: 2 (over y_lo).
Axes of the slice: x: 4, y: 4 (y_hi: 2, y_lo: 2; y = y_hi * 2 + y_lo), z: 4, core: 2. Of those that a mesh axis runs over, the one named last changes fastest.
Arguments:
- layer_input: bfloat16 [8192, 2048], P('seq', 'ffn'), may hold values from -6 to 6
- w_qkv: bfloat16 [2048, 3, 2048], P('seq', None, 'ffn'), may hold values from -0.125 to 0.125
- w_out: bfloat16 [2048, 2048], P('seq', 'ffn'), may hold values from -0.125 to 0.125
- w_up: bfloat16 [2048, 8192], P('seq', 'ffn'), may hold values from -0.125 to 0.125
- w_down: bfloat16 [2048, 8192], P('seq', 'ffn'), may hold values from -0.0625 to 0.0625
- b_qkv: float32 [3, 2048], replicated, may hold values from -1.75 to 1.75
- b_out: float32 [2048], replicated, may hold values from -1.75 to 1.75
- b_up: float32 [8192], replicated, may hold values from -1.75 to 1.75
- b_down: float32 [2048], replicated, may hold values from -1.75 to 1.75
- norm_gains: float32 [3, 2048], replicated, may hold values from 0.5 to 1.5
- norm_shifts: float32 [3, 2048], replicated, may hold values from -1.75 to 1.75
- hidden_gain: float32 [8192], replicated, may hold values from 0.5 to 1.5
- hidden_shift: float32 [8192], replicated, may hold values from -1.75 to 1.75
- seq_ids: int32 [8192], P('seq'), may hold values from 0 to 1, as said below
- positions: int32 [8192], P('seq'), may hold values from 0 to 4095, as said below
- d_out: bfloat16 [8192, 2048], P('seq', 'ffn'), may hold values from -6 to 6
Outputs:
- layer_output: float32 [8192, 2048], P('seq', 'ffn')
- input_grad: float32 [8192, 2048], P('seq', 'ffn')
- w_qkv_grad: float32 [2048, 3, 2048], P('seq', None, 'ffn')
- w_out_grad: float32 [2048, 2048], P('seq', 'ffn')
- w_up_grad: float32 [2048, 8192], P('seq', 'ffn')
- w_down_grad: float32 [2048, 8192], P('seq', 'ffn')
- b_qkv_grad: float32 [3, 2048], replicated
- b_out_grad: float32 [2048], replicated
- b_up_grad: float32 [8192], replicated
- b_down_grad: float32 [2048], replicated
- norm_gains_grad: float32 [3, 2048], replicated
- norm_shifts_grad: float32 [3, 2048], replicated
- hidden_gain_grad: float32 [8192], replicated
- hidden_shift_grad: float32 [8192], replicated
The draws below stay inside these ranges and needn't reach their ends.
Inputs may be any that keep to these rules, and one draw needn't show every extreme that they name: `seq_ids`: each of the 2 sequences holds each of its 4096 positions exactly once. The token order is made of runs of 64 tokens, each run starting at a multiple of 64; a run belongs to one sequence and holds 64 consecutive positions starting at a multiple of 64. Some sequence has its first run at the first token and its last run at the last token. `positions`: as stated for seq_ids.
All inputs are finite; a program needn't handle non-finite values.
Results may differ from the reference program's by a relative error of at most 0.017.
Values may be sent and summed in bfloat16 or wider, within the bound.
A program may use at most 576 MiB of HBM per device.

```python
import math
import jax
import jax.numpy as jnp
from jax import lax

D = 2048
HEADS = 32
HEAD_DIM = 64
FF = 8192
PIECE = 64
TOKENS = 8192
SEQ_LEN = 4096


def swap_slots(order, first_slot, second_slot):
    first_value = order[first_slot]
    second_value = order[second_slot]
    return order.at[first_slot].set(second_value).at[second_slot].set(first_value)


def piece_order(key):
    piece_count = TOKENS // PIECE
    per_sequence = SEQ_LEN // PIECE
    order = jax.random.permutation(jax.random.fold_in(key, 71), piece_count).astype(jnp.int32)
    chosen = jax.random.randint(jax.random.fold_in(key, 72), (), 0, TOKENS // SEQ_LEN).astype(jnp.int32)
    opening = chosen * per_sequence
    closing = opening + per_sequence - 1
    order = swap_slots(order, 0, jnp.argmax(order == opening))
    order = swap_slots(order, piece_count - 1, jnp.argmax(order == closing))
    return order


def draw_seq_ids(key, part):
    order = piece_order(key)
    return jnp.repeat(order // (SEQ_LEN // PIECE), PIECE).astype(jnp.int32)


def draw_positions(key, part):
    order = piece_order(key)
    within = order % (SEQ_LEN // PIECE)
    offsets = jnp.tile(jnp.arange(PIECE, dtype=jnp.int32), TOKENS // PIECE)
    return (jnp.repeat(within * PIECE, PIECE) + offsets).astype(jnp.int32)


def steps_of(rng, dims, shards, smallest, largest):
    level = 1.0
    for axis_at, shards_of in shards:
        heights = jax.random.uniform(jax.random.fold_in(jax.random.fold_in(rng, 6), axis_at), (shards_of,), jnp.float32, smallest / len(shards), largest / len(shards))
        level = level * jnp.repeat(jnp.exp(heights), dims[axis_at] // shards_of).reshape((-1,) + (1,) * (len(dims) - 1 - axis_at))
    return level


def centred(own_key, extent, width, bound, cuts=(), kind=jnp.bfloat16):
    level = steps_of(own_key, extent, cuts, -0.22, 0.18) if cuts else 1.0
    values = jax.random.normal(own_key, extent, jnp.float32) * width * level
    return jnp.minimum(jnp.maximum(values, -bound), bound).astype(kind)


def setup_inputs(seed: int = 0) -> dict:
    key_list = jax.random.split(jax.random.key(seed), 17)
    layer_input = centred(key_list[0], (TOKENS, D), 1.0, 6.0, ((0, 64), (1, 2)))
    w_qkv = centred(key_list[1], (D, 3, D), D ** -0.5, 0.125, ((0, 64), (2, 2)))
    w_out = centred(key_list[2], (D, D), D ** -0.5, 0.125, ((0, 64), (1, 2)))
    w_up = centred(key_list[3], (D, FF), D ** -0.5, 0.125, ((0, 64), (1, 2)))
    w_down = centred(key_list[4], (D, FF), FF ** -0.5, 0.0625, ((0, 64), (1, 2)))
    b_qkv = centred(key_list[5], (3, D), 0.3, 1.75, (), jnp.float32)
    b_out = centred(key_list[6], (D,), 0.3, 1.75, (), jnp.float32)
    b_up = centred(key_list[7], (FF,), 0.3, 1.75, (), jnp.float32)
    b_down = centred(key_list[8], (D,), 0.3, 1.75, (), jnp.float32)
    norm_gains = jnp.clip(1.0 + 0.1 * jax.random.normal(key_list[9], (3, D), jnp.float32), 0.5, 1.5)
    norm_shifts = centred(key_list[10], (3, D), 0.3, 1.75, (), jnp.float32)
    hidden_gain = jnp.clip(1.0 + 0.1 * jax.random.normal(key_list[11], (FF,), jnp.float32), 0.5, 1.5)
    hidden_shift = centred(key_list[12], (FF,), 0.3, 1.75, (), jnp.float32)
    seq_ids = draw_seq_ids(jax.random.fold_in(key_list[16], 71), 0)
    positions = draw_positions(jax.random.fold_in(key_list[16], 71), 0)
    d_out = centred(key_list[15], (TOKENS, D), 1.0, 6.0, ((0, 64), (1, 2)))
    return {"layer_input": layer_input, "w_qkv": w_qkv, "w_out": w_out, "w_up": w_up, "w_down": w_down, "b_qkv": b_qkv, "b_out": b_out, "b_up": b_up, "b_down": b_down, "norm_gains": norm_gains, "norm_shifts": norm_shifts, "hidden_gain": hidden_gain, "hidden_shift": hidden_shift, "seq_ids": seq_ids, "positions": positions, "d_out": d_out}


@jax.custom_vjp
def low(v):
    return lax.optimization_barrier(v.astype(jnp.bfloat16)).astype(jnp.float32)

@jax.custom_vjp
def low_back(v):
    return v

def low_keep(v):
    return (low(v), None)

def low_pass(kept, grad):
    return (grad,)

def back_keep(v):
    return (v, None)

def back_low(kept, grad):
    return (low(grad),)
low.defvjp(low_keep, low_pass)
low_back.defvjp(back_keep, back_low)
epsilon = 1e-05
xpos_base = 512.0
far_below = -1e+30
highest = lax.Precision.HIGHEST

def layer_norm(values, gain, shift):
    center = lax.optimization_barrier(jnp.mean(values, axis=-1, keepdims=True))
    centered = values - center
    variance = lax.optimization_barrier(jnp.mean(centered * centered, axis=-1, keepdims=True))
    return centered * lax.rsqrt(variance + epsilon) * gain + shift

def xpos_tables(places):
    half_size = HEAD_DIM // 2
    indices = jnp.arange(half_size, dtype=jnp.float32)
    inverse_freq = jnp.exp(-jnp.log(10000.0) * indices / half_size)
    spots = places.astype(jnp.float32)
    angles = spots[:, None] * inverse_freq[None, :]
    ratios = (2.0 * indices + 0.4 * HEAD_DIM) / (1.4 * HEAD_DIM)
    powers = (spots - SEQ_LEN // 2) / xpos_base
    growth = jnp.exp(powers[:, None] * jnp.log(ratios)[None, :])
    return (jnp.cos(angles), jnp.sin(angles), growth)

def rotate(values, cosine, sine, factor):
    half_size = values.shape[-1] // 2
    first_half = values[..., :half_size]
    second_half = values[..., half_size:]
    cos_b = cosine[:, None, :]
    sin_b = sine[:, None, :]
    fac_b = factor[:, None, :]
    return jnp.concatenate([(first_half * cos_b - second_half * sin_b) * fac_b, (second_half * cos_b + first_half * sin_b) * fac_b], axis=-1)

def attend_one(block):
    queries, keys, values, places = block
    scores = low_back(jnp.dot(queries, keys.T, precision=highest) * (1.0 / math.sqrt(HEAD_DIM)))
    visible = places[None, :] <= places[:, None]
    scores = jnp.where(visible, scores, far_below)
    peak = lax.optimization_barrier(jnp.max(scores, axis=-1, keepdims=True))
    weights = jnp.exp(scores - peak)
    probs = weights / lax.optimization_barrier(jnp.sum(weights, axis=-1, keepdims=True))
    return jnp.dot(low(probs), values, precision=highest)

def forward(layer_input, w_qkv, w_out, w_up, w_down, b_qkv, b_out, b_up, b_down, norm_gains, norm_shifts, hidden_gain, hidden_shift, seq_ids, positions):
    total_rows = layer_input.shape[0]
    normed_in = layer_norm(layer_input, norm_gains[0], norm_shifts[0])
    qkv = low_back(jnp.einsum('td,dkh->tkh', low(normed_in), w_qkv, precision=highest) + b_qkv[None])
    cosine, sine, growth = xpos_tables(positions)

    def heads_of(rows):
        return rows.reshape(total_rows, HEADS, HEAD_DIM)
    query_rot = low(rotate(heads_of(qkv[:, 0]), cosine, sine, growth))
    key_rot = low(rotate(heads_of(qkv[:, 1]), cosine, sine, 1.0 / growth))
    value_low = low(heads_of(qkv[:, 2]))
    order = jnp.argsort(seq_ids * SEQ_LEN + positions)
    restore = jnp.argsort(order)
    seq_count = total_rows // SEQ_LEN

    def by_sequence(rows):
        grouped = rows[order].reshape(seq_count, SEQ_LEN, HEADS, HEAD_DIM)
        return grouped.transpose(0, 2, 1, 3).reshape(seq_count * HEADS, SEQ_LEN, HEAD_DIM)
    places = jnp.repeat(positions[order].reshape(seq_count, SEQ_LEN), HEADS, axis=0)
    mixed = lax.map(jax.checkpoint(attend_one), (by_sequence(query_rot), by_sequence(key_rot), by_sequence(value_low), places))
    attended = mixed.reshape(seq_count, HEADS, SEQ_LEN, HEAD_DIM).transpose(0, 2, 1, 3).reshape(total_rows, D)[restore]
    attended = low_back(attended)
    normed_attn = layer_norm(attended, norm_gains[1], norm_shifts[1])
    branch = low_back(jnp.dot(low(normed_attn), w_out.T, precision=highest) + b_out)
    mid_state = layer_input + branch
    normed_mid = layer_norm(mid_state, norm_gains[2], norm_shifts[2])
    pre_act = low_back(jnp.dot(low(normed_mid), w_up, precision=highest) + b_up)
    activated = jax.nn.gelu(pre_act, approximate=False)
    normed_hidden = layer_norm(activated, hidden_gain, hidden_shift)
    return mid_state + jnp.dot(low(normed_hidden), w_down.T, precision=highest) + b_down

def reference(layer_input, w_qkv, w_out, w_up, w_down, b_qkv, b_out, b_up, b_down, norm_gains, norm_shifts, hidden_gain, hidden_shift, seq_ids, positions, d_out):

    def layer(inputs, qkv_w, out_w, up_w, down_w, qkv_b, out_b, up_b, down_b, gains, shifts, hid_gain, hid_shift):
        return forward(inputs, qkv_w, out_w, up_w, down_w, qkv_b, out_b, up_b, down_b, gains, shifts, hid_gain, hid_shift, seq_ids, positions)
    layer_output, pullback = jax.vjp(layer, layer_input.astype(jnp.float32), w_qkv.astype(jnp.float32), w_out.astype(jnp.float32), w_up.astype(jnp.float32), w_down.astype(jnp.float32), b_qkv.astype(jnp.float32), b_out.astype(jnp.float32), b_up.astype(jnp.float32), b_down.astype(jnp.float32), norm_gains.astype(jnp.float32), norm_shifts.astype(jnp.float32), hidden_gain.astype(jnp.float32), hidden_shift.astype(jnp.float32))
    grads = pullback(d_out.astype(jnp.float32))
    return (layer_output, grads[0], grads[1], grads[2], grads[3], grads[4], grads[5], grads[6], grads[7], grads[8], grads[9], grads[10], grads[11], grads[12])
```

```python
import functools
import math

import jax
import jax.numpy as jnp
from jax import lax
from jax.experimental import pallas as pl
from jax.experimental.pallas import tpu as pltpu
from jax.sharding import Mesh
from jax.sharding import PartitionSpec as P

SEQ = ("x", "h", "z", "c")
TOK = ("x", "h")
HEAD = 64
RUN = 64
CHUNK = 512
EPS = 1e-05
MESH = pl.DeviceIdType.MESH
BF = jnp.bfloat16
F32 = jnp.float32
DMA = pltpu.SemaphoreType.DMA
ANY = pl.BlockSpec(memory_space=pl.ANY)
VMEM = pl.BlockSpec(memory_space=pltpu.VMEM)
G_OFFS = ((1, 0), (3, 0), (0, 1), (2, 0), (1, 1), (3, 1), (2, 1))
NT = (((1,), (1,)), ((), ()))
TN = (((0,), (0,)), ((), ()))
NN = (((1,), (0,)), ((), ()))


def sds(shape, dtype):
    return jax.ShapeDtypeStruct(shape, dtype)


def remote(src, dst, send, recv, device):
    return pltpu.make_async_remote_copy(
        src_ref=src,
        dst_ref=dst,
        send_sem=send,
        recv_sem=recv,
        device_id=device,
        device_id_type=MESH,
    )


def greet(devices):
    barrier = pltpu.get_barrier_semaphore()
    for device in devices:
        pl.semaphore_signal(barrier, inc=1, device_id=device, device_id_type=MESH)
    pl.semaphore_wait(barrier, len(devices))


def comm_call(kernel, name, number, out_shape, scratch, in_specs, out_specs, *args):
    return pl.pallas_call(
        kernel,
        out_shape=out_shape,
        in_specs=in_specs,
        out_specs=out_specs,
        scratch_shapes=scratch,
        name=name,
        compiler_params=pltpu.CompilerParams(
            collective_id=number, has_side_effects=True, vmem_limit_bytes=48 << 20
        ),
    )(*args)


def g_place():
    return lax.axis_index("z"), lax.axis_index("c"), lax.axis_index("f")


def gather_g_kernel(wide, x_ref, o_ref, send, recv, send2, recv2, local):
    z, c, f = g_place()
    rows = x_ref.shape[0]

    def dev(o):
        return {"z": lax.rem(z + o[0], 4), "f": lax.rem(f + o[1], 2)}

    sibling = {"c": 1 - c}
    greet([dev(o) for o in G_OFFS] + [sibling])

    def slot(zz, cc, ff):
        if wide:
            return o_ref.at[pl.ds(((zz * 2 + cc) * 2 + ff) * rows, rows)]
        half = x_ref.shape[1]
        return o_ref.at[pl.ds((zz * 2 + cc) * rows, rows), pl.ds(ff * half, half)]

    mine = slot(z, c, f)
    copies = []
    for k, o in enumerate(G_OFFS):
        copy = remote(x_ref, mine, send.at[k], recv.at[k], dev(o))
        copy.start()
        copies.append(copy)
    across = remote(x_ref, mine, send2.at[7], recv2.at[7], sibling)
    across.start()
    here = pltpu.make_async_copy(x_ref, mine, local)
    here.start()
    passed = []
    for k, o in enumerate(G_OFFS):
        copies[k].wait_recv()
        landed = slot(lax.rem(z + 4 - o[0], 4), c, lax.rem(f + 2 - o[1], 2))
        copy = remote(landed, landed, send2.at[k], recv2.at[k], sibling)
        copy.start()
        passed.append(copy)
    for copy in copies:
        copy.wait_send()
    for copy in passed:
        copy.wait()
    across.wait()
    here.wait()


def gather_g(values, number, name):
    rows, width = values.shape
    wide = width == 2048
    return comm_call(
        functools.partial(gather_g_kernel, wide),
        name,
        number,
        sds((16 * rows * width // 2048, 2048), values.dtype),
        [DMA((7,)), DMA((7,)), DMA((8,)), DMA((8,)), DMA],
        [ANY],
        ANY,
        values,
    )


def scatter_g_kernel(x_ref, o_ref, half, landed, send, recv, send2, recv2, local):
    z, c, f = g_place()
    offs = G_OFFS + ((0, 0),)

    def dev(o):
        return {"z": lax.rem(z + o[0], 4), "f": lax.rem(f + o[1], 2)}

    sibling = {"c": 1 - c}
    greet([dev(o) for o in G_OFFS] + [sibling])
    first, here = [], []
    for k, o in enumerate(offs):
        to = dev(o)
        copy = remote(
            x_ref.at[(to["z"] * 2 + 1 - c) * 2 + to["f"]], half.at[k], send.at[k], recv.at[k], sibling
        )
        copy.start()
        first.append(copy)
        copy = pltpu.make_async_copy(
            x_ref.at[(to["z"] * 2 + c) * 2 + to["f"]], half.at[8 + k], local.at[k]
        )
        copy.start()
        here.append(copy)
    second = []
    for k, o in enumerate(offs):
        first[k].wait_recv()
        here[k].wait()
        half[8 + k] = (half[8 + k].astype(F32) + half[k].astype(F32)).astype(BF)
        if k < 7:
            copy = remote(half.at[8 + k], landed.at[k], send2.at[k], recv2.at[k], dev(o))
            copy.start()
            second.append(copy)
    for copy in second:
        copy.wait_recv()

    def add(i, carry):
        rows = pl.ds(pl.multiple_of(i * 16, 16), 16)
        total = half[15, rows].astype(F32)
        for k in range(7):
            total = total + landed[k, rows].astype(F32)
        o_ref[rows] = total
        return carry

    lax.fori_loop(0, 4, add, 0)
    for copy in first:
        copy.wait_send()
    for copy in second:
        copy.wait_send()


def scatter_g(partial_rows, number, name):
    return comm_call(
        scatter_g_kernel,
        name,
        number,
        sds((64, 2048), F32),
        [
            pltpu.VMEM((16, 64, 2048), BF),
            pltpu.VMEM((7, 64, 2048), BF),
            DMA((8,)),
            DMA((8,)),
            DMA((7,)),
            DMA((7,)),
            DMA((8,)),
        ],
        [ANY],
        VMEM,
        partial_rows.astype(BF).reshape(16, 64, 2048),
    )


def stats_kernel(x_ref, o_ref, send, recv):
    z, c, f = g_place()
    me = (z * 2 + c) * 2 + f
    offs = [(a, b, d) for a in range(4) for b in range(2) for d in range(2)][1:]

    def dev(o):
        return {"z": lax.rem(z + o[0], 4), "c": lax.rem(c + o[1], 2), "f": lax.rem(f + o[2], 2)}

    greet([dev(o) for o in offs])
    copies = []
    for k, o in enumerate(offs):
        copy = remote(x_ref, o_ref.at[me], send.at[k], recv.at[k], dev(o))
        copy.start()
        copies.append(copy)
    o_ref[me] = x_ref[...]
    for copy in copies:
        copy.wait()


def stats_g(stats, number, name):
    count, tokens = stats.shape
    sent = stats.reshape(count * tokens // 128, 128)
    out = comm_call(
        stats_kernel,
        name,
        number,
        sds((16,) + sent.shape, F32),
        [DMA((15,)), DMA((15,))],
        [VMEM],
        VMEM,
        sent,
    )
    return out.reshape(16, count, tokens)


def t_place():
    return lax.axis_index("x"), lax.axis_index("h")


def gather_t_kernel(x_ref, o_ref, send, recv, local):
    x, h = t_place()
    rows = x_ref.shape[0]

    def dev(o):
        return {"x": lax.rem(x + o[0], 4), "h": lax.rem(h + o[1], 2)}

    greet([dev(o) for o in G_OFFS])
    mine = o_ref.at[pl.ds((x * 2 + h) * rows, rows)]
    copies = []
    for k, o in enumerate(G_OFFS):
        copy = remote(x_ref, mine, send.at[k], recv.at[k], dev(o))
        copy.start()
        copies.append(copy)
    here = pltpu.make_async_copy(x_ref, mine, local)
    here.start()
    for copy in copies:
        copy.wait()
    here.wait()


def gather_t(values, number, name):
    rows, width = values.shape
    return comm_call(
        gather_t_kernel,
        name,
        number,
        sds((8 * rows, width), values.dtype),
        [DMA((7,)), DMA((7,)), DMA],
        [ANY],
        ANY,
        values,
    )


def scatter_t_kernel(x_ref, o_ref, landed, send, recv, local):
    x, h = t_place()

    def dev(o):
        return {"x": lax.rem(x + o[0], 4), "h": lax.rem(h + o[1], 2)}

    greet([dev(o) for o in G_OFFS])
    copies = []
    for k, o in enumerate(G_OFFS):
        to = dev(o)
        copy = remote(
            x_ref.at[to["x"] * 2 + to["h"]], landed.at[k], send.at[k], recv.at[k], to
        )
        copy.start()
        copies.append(copy)
    here = pltpu.make_async_copy(x_ref.at[x * 2 + h], landed.at[7], local)
    here.start()
    for copy in copies:
        copy.wait()
    here.wait()

    def add(i, carry):
        rows = pl.ds(pl.multiple_of(i * 32, 32), 32)
        total = landed[7, rows].astype(F32)
        for k in range(7):
            total = total + landed[k, rows].astype(F32)
        o_ref[rows] = total
        return carry

    lax.fori_loop(0, o_ref.shape[0] // 32, add, 0)


def scatter_t(partial_rows, number, name):
    total, width = partial_rows.shape
    rows = total // 8
    return comm_call(
        scatter_t_kernel,
        name,
        number,
        sds((rows, width), F32),
        [pltpu.VMEM((8, rows, width), BF), DMA((7,)), DMA((7,)), DMA],
        [ANY],
        VMEM,
        partial_rows.astype(BF).reshape(8, rows, width),
    )


def small_kernel(r_ref, s_ref, o_ref, rbuf, packed, tbuf, s1, r1, s2, r2, s3, r3):
    z, c, f = g_place()
    x, h = t_place()
    me = (z * 2 + c) * 2 + f
    offs = [(a, b, d) for a in range(4) for b in range(2) for d in range(2)][1:]

    def dev(o):
        return {"z": lax.rem(z + o[0], 4), "c": lax.rem(c + o[1], 2), "f": lax.rem(f + o[2], 2)}

    def dev_t(o):
        return {"x": lax.rem(x + o[0], 4), "h": lax.rem(h + o[1], 2)}

    greet([dev(o) for o in offs] + [dev_t(o) for o in G_OFFS])
    copies = []
    for k, o in enumerate(offs):
        to = dev(o)
        copy = remote(
            r_ref.at[(to["z"] * 2 + to["c"]) * 2 + to["f"]], rbuf.at[k], s1.at[k], r1.at[k], to
        )
        copy.start()
        copies.append(copy)
    for copy in copies:
        copy.wait()
    total = r_ref[me]
    for k in range(15):
        total = total + rbuf[k]
    packed[0:8] = total
    packed[8:32] = s_ref[...]
    copies = []
    for k, o in enumerate(G_OFFS):
        copy = remote(packed, tbuf.at[k], s2.at[k], r2.at[k], dev_t(o))
        copy.start()
        copies.append(copy)
    for copy in copies:
        copy.wait()
    total = packed[...]
    for k in range(7):
        total = total + tbuf[k]
    o_ref[me] = total
    copies = []
    for k, o in enumerate(offs):
        copy = remote(o_ref.at[me], o_ref.at[me], s3.at[k], r3.at[k], dev(o))
        copy.start()
        copies.append(copy)
    for copy in copies:
        copy.wait()


def sum_small(r_parts, s_parts, number):
    return comm_call(
        small_kernel,
        "sum_small",
        number,
        sds((16, 32, 128), F32),
        [
            pltpu.VMEM((15, 8, 128), F32),
            pltpu.VMEM((32, 128), F32),
            pltpu.VMEM((7, 32, 128), F32),
            DMA((15,)),
            DMA((15,)),
            DMA((7,)),
            DMA((7,)),
            DMA((15,)),
            DMA((15,)),
        ],
        [VMEM, VMEM],
        VMEM,
        r_parts,
        s_parts,
    )


def both_heads(rows, zero):
    lanes = lax.broadcasted_iota(jnp.int32, rows.shape, 1)
    return jnp.where(lanes < HEAD, rows, zero), jnp.where(lanes >= HEAD, rows, zero)


def run_rows(ref, run):
    return ref[pl.ds(pl.multiple_of(run * RUN, RUN), RUN), :]


def pair_rows(ref, run_a, run_b, dtype):
    zero = jnp.zeros((), dtype)
    a = both_heads(run_rows(ref, run_a).astype(dtype), zero)
    b = both_heads(run_rows(ref, run_b).astype(dtype), zero)
    return jnp.concatenate(a + b, axis=0)


def pair_bounds(rank_a, rank_b):
    lanes = lax.broadcasted_iota(jnp.int32, (1, 256), 1)
    rank = jnp.where(lanes < 128, rank_a, rank_b)
    last = rank * RUN + lax.rem(lanes, RUN)
    return (rank // 64) * 4096, last


def seen(chunk, low, last):
    keys = chunk * CHUNK + lax.broadcasted_iota(jnp.int32, (CHUNK, 256), 0)
    return (keys >= low) & (keys <= last)


def sort_keys(rank, kv_ref, keys, values):
    def move(r, carry):
        to = pl.ds(pl.multiple_of(rank[r] * RUN, RUN), RUN)
        rows = run_rows(kv_ref, r)
        keys[to, :] = rows[:, :128]
        values[to, :] = rows[:, 128:]
        return carry

    lax.fori_loop(0, 128, move, 0)


def flip(source, target):
    def one(i, carry):
        rows = source[pl.ds(pl.multiple_of(i * CHUNK, CHUNK), CHUNK), :]
        target[i] = rows.T
        return carry

    lax.fori_loop(0, 16, one, 0)


def chunk_rows(ref, i):
    return ref[pl.ds(pl.multiple_of(i * CHUNK, CHUNK), CHUNK), :]


def lane_heads(total):
    turned = total.T
    lanes = lax.broadcasted_iota(jnp.int32, (RUN, 128), 1)
    a = jnp.where(lanes < HEAD, turned[0:64], turned[64:128])
    b = jnp.where(lanes < HEAD, turned[128:192], turned[192:256])
    return a, b


def attend_kernel(rank, srun, srank, q_ref, kv_ref, o_ref, lse_ref, keys, values, flipped):
    sort_keys(rank, kv_ref, keys, values)
    flip(values, flipped)

    def pair(p, carry):
        run_a, run_b = srun[2 * p], srun[2 * p + 1]
        rank_a, rank_b = srank[2 * p], srank[2 * p + 1]
        queries = pair_rows(q_ref, run_a, run_b, BF)
        low, last = pair_bounds(rank_a, rank_b)

        def step(i, state):
            peak, total, mixed = state
            scores = lax.dot_general(
                chunk_rows(keys, i), queries, NT, preferred_element_type=F32
            )
            scores = jnp.where(seen(i, low, last), scores, -1e30)
            new_peak = jnp.maximum(peak, jnp.max(scores, axis=0, keepdims=True))
            weights = jnp.exp(scores - new_peak)
            shrink = jnp.exp(peak - new_peak)
            total = total * shrink + jnp.sum(weights, axis=0, keepdims=True)
            mixed = mixed * shrink + lax.dot_general(
                flipped[i], weights.astype(BF), NN, preferred_element_type=F32
            )
            return new_peak, total, mixed

        start = (
            jnp.full((1, 256), -1e20, F32),
            jnp.zeros((1, 256), F32),
            jnp.zeros((128, 256), F32),
        )
        peak, total, mixed = lax.fori_loop((rank_a // 64) * 8, rank_b // 8 + 1, step, start)
        a, b = lane_heads(mixed / total)
        o_ref[pl.ds(pl.multiple_of(run_a * RUN, RUN), RUN), :] = a
        o_ref[pl.ds(pl.multiple_of(run_b * RUN, RUN), RUN), :] = b
        lse_ref[p] = peak + jnp.log(total)
        return carry

    lax.fori_loop(0, 8, pair, 0)


def attend(order, queries, kv):
    return pl.pallas_call(
        attend_kernel,
        out_shape=(sds((1024, 128), F32), sds((8, 1, 256), F32)),
        grid_spec=pltpu.PrefetchScalarGridSpec(
            num_scalar_prefetch=3,
            grid=(1,),
            in_specs=[VMEM, VMEM],
            out_specs=(VMEM, VMEM),
            scratch_shapes=[
                pltpu.VMEM((8192, 128), BF),
                pltpu.VMEM((8192, 128), BF),
                pltpu.VMEM((16, 128, CHUNK), BF),
            ],
        ),
        name="attend",
        compiler_params=pltpu.CompilerParams(vmem_limit_bytes=48 << 20),
    )(*order, queries, kv)


def attend_back_kernel(
    rank, srun, srank, q_ref, kv_ref, g_ref, a_ref, lse_ref, dq_ref, dkv_ref, keys, values, flipped, dkeys, dvalues
):
    sort_keys(rank, kv_ref, keys, values)
    flip(keys, flipped)

    def clear(i, carry):
        rows = pl.ds(pl.multiple_of(i * CHUNK, CHUNK), CHUNK)
        dkeys[rows, :] = jnp.zeros((CHUNK, 128), F32)
        dvalues[rows, :] = jnp.zeros((CHUNK, 128), F32)
        return carry

    lax.fori_loop(0, 16, clear, 0)

    def pair(p, carry):
        run_a, run_b = srun[2 * p], srun[2 * p + 1]
        rank_a, rank_b = srank[2 * p], srank[2 * p + 1]
        queries = pair_rows(q_ref, run_a, run_b, BF)
        grads = pair_rows(g_ref, run_a, run_b, BF)
        low, last = pair_bounds(rank_a, rank_b)
        product = pair_rows(g_ref, run_a, run_b, F32) * pair_rows(a_ref, run_a, run_b, F32)
        delta = lax.dot_general(
            jnp.ones((8, 128), F32),
            product,
            NT,
            preferred_element_type=F32,
            precision=lax.Precision.HIGHEST,
        )[0:1]
        log_total = lse_ref[p]

        def step(i, dq):
            rows = pl.ds(pl.multiple_of(i * CHUNK, CHUNK), CHUNK)
            scores = lax.dot_general(keys[rows, :], queries, NT, preferred_element_type=F32)
            probs = jnp.where(seen(i, low, last), jnp.exp(scores - log_total), 0.0)
            dprobs = lax.dot_general(values[rows, :], grads, NT, preferred_element_type=F32)
            dscores = (probs * (dprobs - delta)).astype(BF)
            dvalues[rows, :] += lax.dot_general(
                probs.astype(BF), grads, NN, preferred_element_type=F32
            )
            dkeys[rows, :] += lax.dot_general(dscores, queries, NN, preferred_element_type=F32)
            return dq + lax.dot_general(flipped[i], dscores, NN, preferred_element_type=F32)

        dq = lax.fori_loop(
            (rank_a // 64) * 8, rank_b // 8 + 1, step, jnp.zeros((128, 256), F32)
        )
        a, b = lane_heads(dq)
        dq_ref[pl.ds(pl.multiple_of(run_a * RUN, RUN), RUN), :] = a * 0.125
        dq_ref[pl.ds(pl.multiple_of(run_b * RUN, RUN), RUN), :] = b * 0.125
        return carry

    lax.fori_loop(0, 8, pair, 0)

    def back(r, carry):
        source = pl.ds(pl.multiple_of(rank[r] * RUN, RUN), RUN)
        to = pl.ds(pl.multiple_of(r * RUN, RUN), RUN)
        dkv_ref[to, 0:128] = dkeys[source, :].astype(BF)
        dkv_ref[to, 128:256] = dvalues[source, :].astype(BF)
        return carry

    lax.fori_loop(0, 128, back, 0)


def attend_back(order, queries, kv, grads, attended, log_total):
    return pl.pallas_call(
        attend_back_kernel,
        out_shape=(sds((1024, 128), F32), sds((8192, 256), BF)),
        grid_spec=pltpu.PrefetchScalarGridSpec(
            num_scalar_prefetch=3,
            grid=(1,),
            in_specs=[VMEM] * 5,
            out_specs=(VMEM, VMEM),
            scratch_shapes=[
                pltpu.VMEM((8192, 128), BF),
                pltpu.VMEM((8192, 128), BF),
                pltpu.VMEM((16, 128, CHUNK), BF),
                pltpu.VMEM((8192, 128), F32),
                pltpu.VMEM((8192, 128), F32),
            ],
        ),
        name="attend_back",
        compiler_params=pltpu.CompilerParams(vmem_limit_bytes=56 << 20),
    )(*order, queries, kv, grads, attended, log_total)


def lane_tables(places, seq_length):
    half = HEAD // 2
    lanes = jnp.arange(128, dtype=jnp.int32)
    indices = (lanes % half).astype(F32)
    inverse_freq = jnp.exp(-jnp.log(10000.0) * indices / half)
    spots = places.astype(F32)
    angles = spots[:, None] * inverse_freq[None, :]
    ratios = (2.0 * indices + 0.4 * HEAD) / (1.4 * HEAD)
    powers = (spots - seq_length // 2) / 512.0
    growth = jnp.exp(powers[:, None] * jnp.log(ratios)[None, :])
    sign = jnp.where(lanes % HEAD < half, -1.0, 1.0)
    return jnp.cos(angles), jnp.sin(angles) * sign[None, :], growth


def swap_halves(values):
    half = HEAD // 2
    first = (jnp.arange(128) % HEAD < half)[None, :]
    return jnp.where(first, jnp.roll(values, -half, axis=1), jnp.roll(values, half, axis=1))


def normal(values):
    center = jnp.mean(values, axis=1, keepdims=True)
    centered = values - center
    variance = jnp.mean(centered * centered, axis=1, keepdims=True)
    inv = lax.rsqrt(variance + EPS)
    return centered * inv, inv


def normal_back(upstream, gain, normal_rows, inv):
    scaled = upstream * gain
    mean = jnp.mean(scaled, axis=1, keepdims=True)
    cross = jnp.mean(scaled * normal_rows, axis=1, keepdims=True)
    return inv * (scaled - mean - normal_rows * cross)


def shards(
    layer_input,
    w_qkv,
    w_out,
    w_up,
    w_down,
    b_qkv,
    b_out,
    b_up,
    b_down,
    norm_gains,
    norm_shifts,
    hidden_gain,
    hidden_shift,
    seq_ids,
    positions,
    d_out,
):
    z, c, f = g_place()
    x, h = t_place()
    zc = z * 2 + c
    me = zc * 2 + f
    head_at = f * 1024 + zc * 128
    hidden_at = f * 4096 + zc * 512

    def head_part(vector):
        return lax.dynamic_slice_in_dim(vector, head_at, 128, axis=vector.ndim - 1)

    def hidden_part(vector):
        return lax.dynamic_slice_in_dim(vector, hidden_at, 512, axis=vector.ndim - 1)

    def my_rows(rows):
        return lax.dynamic_slice_in_dim(rows, me * 64, 64, axis=0)

    rank_here = seq_ids.reshape(2, RUN)[:, 0] * 64 + positions.reshape(2, RUN)[:, 0] // RUN
    rank = lax.all_gather(rank_here, SEQ, axis=0, tiled=True)
    group_rank = lax.dynamic_slice_in_dim(rank, (x * 2 + h) * 16, 16)
    slot = jnp.sum((group_rank[None, :] < group_rank[:, None]).astype(jnp.int32), axis=1)
    hit = slot[None, :] == jnp.arange(16, dtype=jnp.int32)[:, None]
    srank = jnp.sum(jnp.where(hit, group_rank[None, :], 0), axis=1)
    srun = jnp.sum(jnp.where(hit, jnp.arange(16, dtype=jnp.int32)[None, :], 0), axis=1)
    order = (rank, srun, srank)
    places = ((group_rank % 64) * RUN)[:, None] + jnp.arange(RUN, dtype=jnp.int32)[None, :]
    cosine, sine, growth = lane_tables(places.reshape(1024), 4096)

    packed = jnp.concatenate(
        [
            w_up.reshape(32, 8, 512),
            w_down.reshape(32, 8, 512),
            w_qkv.reshape(32, 3, 8, 128).transpose(0, 2, 1, 3).reshape(32, 8, 384),
            w_out.reshape(32, 8, 128),
        ],
        axis=2,
    ).transpose(1, 0, 2)
    packed = lax.all_to_all(packed, ("z", "c"), 0, 0, tiled=True).reshape(256, 1536)
    w_attn = gather_t(packed[:, 1024:], 1, "gather_attn_weights")
    w_ffn = lax.all_gather(packed[:, :1024], TOK, axis=0, tiled=True)
    qkv_w, out_w = w_attn[:, :384], w_attn[:, 384:]
    up_w, down_w = w_ffn[:, :512], w_ffn[:, 512:]

    input_all = gather_g(layer_input, 2, "gather_input")
    normal_all, unused = normal(input_all.astype(F32))
    in_low = (normal_all * norm_gains[0] + norm_shifts[0]).astype(BF)
    qkv = jnp.dot(in_low, qkv_w, preferred_element_type=F32) + head_part(b_qkv).reshape(384)
    queries, keys, values = qkv[:, :128], qkv[:, 128:256], qkv[:, 256:]
    query_low = ((queries * cosine + swap_halves(queries) * sine) * growth).astype(BF)
    query_low = query_low * jnp.bfloat16(0.125)
    shrink = 1.0 / growth
    key_low = ((keys * cosine + swap_halves(keys) * sine) * shrink).astype(BF)
    kv = gather_t(jnp.concatenate([key_low, values.astype(BF)], axis=1), 3, "gather_kv")
    attended, log_total = attend(order, query_low, kv)

    part_sum = jnp.sum(attended, axis=1)
    part_mean = part_sum / 128
    part_spread = jnp.sum(jnp.square(attended - part_mean[:, None]), axis=1)
    stats = stats_g(jnp.stack([part_sum, part_spread]), 4, "stats_attn")
    center = jnp.sum(stats[:, 0], axis=0) / 2048
    spread = jnp.sum(stats[:, 1] + 128 * jnp.square(stats[:, 0] / 128 - center[None]), axis=0)
    scale_attn = lax.rsqrt(spread / 2048 + EPS)[:, None]
    normal_attn = (attended - center[:, None]) * scale_attn
    attn_low = (normal_attn * head_part(norm_gains[1]) + head_part(norm_shifts[1])).astype(BF)
    branch = scatter_g(
        lax.dot_general(attn_low, out_w, NT, preferred_element_type=F32), 5, "scatter_branch"
    )
    input_rows = my_rows(input_all).astype(F32)
    mid = input_rows + (branch + b_out)

    normal_mid, scale_mid = normal(mid)
    mid_rows = (normal_mid * norm_gains[2] + norm_shifts[2]).astype(BF)
    mid_low = gather_g(mid_rows, 6, "gather_mid")
    grad_all = gather_g(d_out, 7, "gather_grad")
    grad_hidden = jnp.dot(grad_all, down_w, preferred_element_type=F32)
    pre_act = jnp.dot(mid_low, up_w, preferred_element_type=F32) + hidden_part(b_up)
    below = 0.5 * (1.0 + lax.erf(pre_act * math.sqrt(0.5)))
    activated = pre_act * below
    slope = below + pre_act * jnp.exp(-0.5 * pre_act * pre_act) * (1.0 / math.sqrt(2.0 * math.pi))
    gain_hidden = hidden_part(hidden_gain)
    part_sum = jnp.sum(activated, axis=1)
    part_centered = activated - (part_sum / 512)[:, None]
    part_spread = jnp.sum(jnp.square(part_centered), axis=1)
    scaled = grad_hidden * gain_hidden
    stats = stats_g(
        jnp.stack(
            [
                part_sum,
                part_spread,
                jnp.sum(scaled, axis=1),
                jnp.sum(scaled * part_centered, axis=1),
            ]
        ),
        8,
        "stats_hidden",
    )
    center = jnp.sum(stats[:, 0], axis=0) / 8192
    apart = stats[:, 0] / 512 - center[None]
    spread = jnp.sum(stats[:, 1] + 512 * jnp.square(apart), axis=0)
    scale_hidden = lax.rsqrt(spread / 8192 + EPS)
    back_mean = jnp.sum(stats[:, 2], axis=0) / 8192
    back_cross = scale_hidden * jnp.sum(stats[:, 3] + apart * stats[:, 2], axis=0) / 8192
    normal_hidden = (activated - center[:, None]) * scale_hidden[:, None]
    hidden_low = (normal_hidden * gain_hidden + hidden_part(hidden_shift)).astype(BF)
    grad_act = scale_hidden[:, None] * (
        scaled - back_mean[:, None] - normal_hidden * back_cross[:, None]
    )
    pre_low = (grad_act * slope).astype(BF)
    grad_mid_norm = scatter_g(
        lax.dot_general(pre_low, up_w, NT, preferred_element_type=F32), 9, "scatter_mid"
    )
    ffn_rows = scatter_g(
        lax.dot_general(hidden_low, down_w, NT, preferred_element_type=F32), 10, "scatter_ffn"
    )
    output_rows = mid + (ffn_rows + b_down)
    up_term = lax.dot_general(mid_low, pre_low, TN, preferred_element_type=F32)
    down_term = lax.dot_general(grad_all, hidden_low, TN, preferred_element_type=F32)
    ffn_term = jnp.concatenate([up_term.astype(BF), down_term.astype(BF)], axis=1)
    ffn_grads = lax.psum_scatter(ffn_term, TOK, scatter_dimension=0, tiled=True)

    grad_out_rows = my_rows(grad_all).astype(F32)
    grad_mid = grad_out_rows + normal_back(grad_mid_norm, norm_gains[2], normal_mid, scale_mid)
    branch_rows = grad_mid.astype(BF)
    branch_all = gather_g(branch_rows, 11, "gather_branch_grad")
    grad_attn_norm = jnp.dot(branch_all, out_w, preferred_element_type=F32)
    scaled = grad_attn_norm * head_part(norm_gains[1])
    stats = stats_g(
        jnp.stack([jnp.sum(scaled, axis=1), jnp.sum(scaled * normal_attn, axis=1)]),
        12,
        "stats_attn_back",
    )
    stats = jnp.sum(stats, axis=0) / 2048
    grad_attended = (
        scale_attn * (scaled - stats[0][:, None] - normal_attn * stats[1][:, None])
    ).astype(BF)
    query_grad, kv_part = attend_back(order, query_low, kv, grad_attended, attended, log_total)
    kv_grad = scatter_t(kv_part, 13, "scatter_kv")

    def unrotate(grads, factor):
        grads = grads * factor
        return grads * cosine - swap_halves(grads) * sine

    grad_qkv = jnp.concatenate(
        [unrotate(query_grad, growth), unrotate(kv_grad[:, :128], shrink), kv_grad[:, 128:]],
        axis=1,
    ).astype(BF)
    grad_in_norm = scatter_g(
        lax.dot_general(grad_qkv, qkv_w, NT, preferred_element_type=F32), 14, "scatter_in"
    )
    normal_in, scale_in = normal(input_rows)
    input_grad_rows = grad_mid + normal_back(grad_in_norm, norm_gains[0], normal_in, scale_in)

    qkv_term = lax.dot_general(in_low, grad_qkv, TN, preferred_element_type=F32)
    out_term = lax.dot_general(branch_all, attn_low, TN, preferred_element_type=F32)
    attn_grads = scatter_t(
        jnp.concatenate([qkv_term.astype(BF), out_term.astype(BF)], axis=1), 15, "scatter_attn_grads"
    )

    r_parts = jnp.stack(
        [
            jnp.sum(grad_in_norm * normal_in, axis=0),
            jnp.sum(grad_mid_norm * normal_mid, axis=0),
            jnp.sum(grad_in_norm, axis=0),
            jnp.sum(grad_mid_norm, axis=0),
            jnp.sum(branch_rows.astype(F32), axis=0),
            jnp.sum(grad_out_rows, axis=0),
            jnp.zeros((2048,), F32),
            jnp.zeros((2048,), F32),
        ]
    )
    r_parts = r_parts.reshape(8, 16, 128).transpose(1, 0, 2)
    s_parts = jnp.concatenate(
        [
            jnp.sum(grad_qkv.astype(F32), axis=0),
            jnp.sum(grad_attn_norm * normal_attn, axis=0),
            jnp.sum(grad_attn_norm, axis=0),
            jnp.sum(pre_low.astype(F32), axis=0),
            jnp.sum(grad_hidden * normal_hidden, axis=0),
            jnp.sum(grad_hidden, axis=0),
            jnp.zeros((896,), F32),
        ]
    ).reshape(24, 128)
    sums = sum_small(r_parts, s_parts, 16)
    by_rows = sums[:, :6].transpose(1, 0, 2).reshape(6, 2048)

    def by_heads(first, count):
        part = sums[:, 8 + first : 8 + first + count].reshape(8, 2, count, 128)
        return part.transpose(2, 1, 0, 3).reshape(count, 2048)

    def by_hidden(first):
        part = sums[:, 8 + first : 12 + first].reshape(8, 2, 512)
        return part.transpose(1, 0, 2).reshape(8192)

    head_sums = by_heads(0, 5)
    gains_grad = jnp.stack([by_rows[0], head_sums[3], by_rows[1]])
    shifts_grad = jnp.stack([by_rows[2], head_sums[4], by_rows[3]])

    both = jnp.stack([output_rows, input_grad_rows]).reshape(2, 64, 2, 1024)
    both = lax.all_to_all(both, "f", 2, 1, tiled=True).reshape(2, 128, 1024)
    grads = jnp.concatenate([ffn_grads.astype(F32), attn_grads], axis=1).reshape(8, 32, 1536)
    grads = lax.all_to_all(grads, ("z", "c"), 0, 0, tiled=True)
    grads = grads.transpose(1, 0, 2)
    return (
        both[0],
        both[1],
        grads[:, :, 1024:1408].reshape(32, 8, 3, 128).transpose(0, 2, 1, 3).reshape(32, 3, 1024),
        grads[:, :, 1408:].reshape(32, 1024),
        grads[:, :, :512].reshape(32, 4096),
        grads[:, :, 512:1024].reshape(32, 4096),
        head_sums[:3],
        by_rows[4],
        by_hidden(5),
        by_rows[5],
        gains_grad,
        shifts_grad,
        by_hidden(9),
        by_hidden(13),
    )


def solution(mesh):
    fine = Mesh(mesh.devices.reshape(4, 2, 4, 2, 2), SEQ + ("f",))
    both = P(SEQ, "f")
    return jax.shard_map(
        shards,
        mesh=fine,
        in_specs=(both, P(SEQ, None, "f"), both, both, both)
        + (P(),) * 8
        + (P(SEQ), P(SEQ), both),
        out_specs=(both, both, P(SEQ, None, "f"), both, both, both) + (P(),) * 8,
        check_vma=False,
    )
```

```python
import math

import jax
import jax.numpy as jnp
from jax import lax
from jax.experimental import pallas as pl
from jax.experimental.pallas import tpu as pltpu
from jax.sharding import Mesh
from jax.sharding import PartitionSpec as P

SEQ = ("x", "h", "z", "c")
TOK = ("x", "h")
HEAD = 64
RUN = 64
CHUNK = 512
EPS = 1e-05
MESH = pl.DeviceIdType.MESH
BF = jnp.bfloat16
F32 = jnp.float32
DMA = pltpu.SemaphoreType.DMA
ANY = pl.BlockSpec(memory_space=pl.ANY)
VMEM = pl.BlockSpec(memory_space=pltpu.VMEM)
NT = (((1,), (1,)), ((), ()))
TN = (((0,), (0,)), ((), ()))
NN = (((1,), (0,)), ((), ()))


def sds(shape, dtype):
    return jax.ShapeDtypeStruct(shape, dtype)


AXES = {"x": 4, "h": 2, "z": 4, "c": 2, "f": 2}
RING_G, PAIR_G = "z", "f"
RING_T, PAIR_T = "x", "h"


class Net:
    def __init__(self, send, recv):
        self.send, self.recv, self.copies = send, recv, []
        self.at = {axis: lax.axis_index(axis) for axis in AXES}

    def device(self, offset):
        return {a: lax.rem(self.at[a] + d + AXES[a], AXES[a]) for a, d in offset.items()}

    def place(self, offset, *axes):
        index = 0
        for a in axes:
            d = offset.get(a, 0)
            at = lax.rem(self.at[a] + d + AXES[a], AXES[a]) if d else self.at[a]
            index = index * AXES[a] + at
        return index

    def greet(self, *groups):
        offsets = {
            tuple((a, o[a]) for a in AXES if o.get(a, 0)) for group in groups for o in group
        }
        barrier = pltpu.get_barrier_semaphore()
        for offset in sorted(offsets):
            pl.semaphore_signal(
                barrier, inc=1, device_id=self.device(dict(offset)), device_id_type=MESH
            )
        pl.semaphore_wait(barrier, len(offsets))

    def push(self, src, dst, offset):
        k = len(self.copies)
        copy = pltpu.make_async_remote_copy(
            src_ref=src,
            dst_ref=dst,
            send_sem=self.send.at[k],
            recv_sem=self.recv.at[k],
            device_id=self.device(offset),
            device_id_type=MESH,
        )
        copy.start()
        self.copies.append(copy)
        return copy

    def finish(self):
        for copy in self.copies:
            copy.wait_send()


SIBLING = {"c": 1}
NEAR_G = [{"z": 1}, {"z": 3}, {"f": 1}, SIBLING]
NEAR_T = [{"x": 1}, {"x": 3}, {"h": 1}]
ALL_T = [{"x": i, "h": j} for i in range(4) for j in range(2)][1:]
ALL_ZC = [{"z": i, "c": j} for i in range(4) for j in range(2)][1:]
ALL_G = [{"z": i, "c": j, "f": k} for i in range(4) for j in range(2) for k in range(2)][1:]


def run_flows(*flows):
    left = list(flows)
    while left:
        left = [flow for flow in left if next(flow, "end") != "end"]


def half_rows(ref, which):
    rows = ref.shape[0] // 2
    return ref.at[pl.ds(which * rows, rows)]


def gather_flow(net, src, slot, ring, pair, local, sibling):
    up, down, across = {ring: 1}, {ring: 3}, {pair: 1}
    passed = []

    def to_sibling(ref):
        if sibling:
            passed.append(net.push(ref, ref, SIBLING))

    mine = slot({})
    from_down = net.push(src, mine, up)
    from_up = net.push(src, mine, down)
    from_across = net.push(src, mine, across)
    if sibling:
        passed.append(net.push(src, mine, SIBLING))
    here = pltpu.make_async_copy(src, mine, local)
    here.start()
    yield
    from_down.wait_recv()
    below = slot({ring: 3})
    first = net.push(half_rows(below, 0), half_rows(below, 0), up)
    to_sibling(below)
    yield
    from_up.wait_recv()
    above = slot({ring: 1})
    second = net.push(half_rows(above, 1), half_rows(above, 1), down)
    to_sibling(above)
    yield
    from_across.wait_recv()
    beside = slot({pair: 1})
    beside_down = net.push(beside, beside, up)
    beside_up = net.push(beside, beside, down)
    to_sibling(beside)
    yield
    first.wait_recv()
    second.wait_recv()
    far = slot({ring: 2})
    beside_far = net.push(far, far, across)
    to_sibling(far)
    yield
    beside_down.wait_recv()
    to_sibling(slot({ring: 3, pair: 1}))
    yield
    beside_up.wait_recv()
    to_sibling(slot({ring: 1, pair: 1}))
    yield
    beside_far.wait_recv()
    to_sibling(slot({ring: 2, pair: 1}))
    yield
    here.wait()
    for copy in passed:
        copy.wait_recv()


def add_into(target, *sources):
    rows = 16

    def step(i, carry):
        at = pl.ds(pl.multiple_of(i * rows, rows), rows)
        total = target[at, :].astype(F32)
        for source in sources:
            total = total + source[at, :].astype(F32)
        target[at, :] = total.astype(target.dtype)
        return carry

    lax.fori_loop(0, target.shape[0] // rows, step, 0)


ROOTS = ((2, 1), (1, 1), (3, 1), (2, 0), (1, 0), (3, 0), (0, 1), (0, 0))


def scatter_flow(net, chunk, out, mine, other, landed, local, ring, pair, sibling):
    up, down, across = {ring: 1}, {ring: 3}, {pair: 1}
    loads, shared = [], []
    for k, (i, j) in enumerate(ROOTS):
        if sibling:
            shared.append(net.push(chunk({ring: i, pair: j, "c": 1}), other.at[k], SIBLING))
        load = pltpu.make_async_copy(chunk({ring: i, pair: j}), mine.at[k], local.at[k])
        load.start()
        loads.append(load)

    def ready(k):
        loads[k].wait()
        if sibling:
            shared[k].wait_recv()
            add_into(mine.at[k], other.at[k])

    yield
    ready(0)
    beside_far = net.push(mine.at[0], landed.at[0], across)
    ready(1)
    beside_down = net.push(mine.at[1], landed.at[1], up)
    ready(2)
    beside_up = net.push(mine.at[2], landed.at[2], down)
    ready(3)
    yield
    beside_far.wait_recv()
    add_into(mine.at[3], landed.at[0])
    first = net.push(half_rows(mine.at[3], 0), half_rows(landed.at[3], 0), down)
    second = net.push(half_rows(mine.at[3], 1), half_rows(landed.at[3], 1), up)
    ready(6)
    yield
    beside_down.wait_recv()
    beside_up.wait_recv()
    add_into(mine.at[6], landed.at[1], landed.at[2])
    from_across = net.push(mine.at[6], landed.at[4], across)
    ready(5)
    yield
    first.wait_recv()
    add_into(half_rows(mine.at[5], 0), half_rows(landed.at[3], 0))
    from_up = net.push(mine.at[5], landed.at[5], down)
    ready(4)
    yield
    second.wait_recv()
    add_into(half_rows(mine.at[4], 1), half_rows(landed.at[3], 1))
    from_down = net.push(mine.at[4], landed.at[6], up)
    ready(7)
    yield
    from_across.wait_recv()
    yield
    from_up.wait_recv()
    from_down.wait_recv()

    def total(i, carry):
        at = pl.ds(pl.multiple_of(i * 16, 16), 16)
        value = mine[7, at, :].astype(F32) + landed[4, at, :].astype(F32)
        out[at, :] = value + (landed[5, at, :].astype(F32) + landed[6, at, :].astype(F32))
        return carry

    lax.fori_loop(0, out.shape[0] // 16, total, 0)


def gather_slot(net, out, rows, ring, pair):
    order = ("z", "c", "f") if ring == "z" else ("x", "h")

    def slot(offset):
        at = net.place(offset, *order)
        return out.at[pl.ds(pl.multiple_of(at * rows, rows), rows)]

    return slot


def input_slot(net, out):
    def slot(offset):
        row = pl.multiple_of(net.place(offset, "z", "c") * 128, 128)
        column = pl.multiple_of(net.place(offset, "f") * 1024, 1024)
        return out.at[pl.ds(row, 128), pl.ds(column, 1024)]

    return slot


def scatter_chunk(net, ref, ring):
    order = ("z", "c", "f") if ring == "z" else ("x", "h")
    return lambda offset: ref.at[net.place(offset, *order)]


def comm_call(kernel, name, number, pushes, locals_, out_shape, scratch, in_specs, out_specs, *args):
    return pl.pallas_call(
        kernel,
        out_shape=out_shape,
        in_specs=in_specs,
        out_specs=out_specs,
        scratch_shapes=[DMA((pushes,)), DMA((pushes,)), DMA((locals_,))] + scratch,
        name=name,
        compiler_params=pltpu.CompilerParams(
            collective_id=number, has_side_effects=True, vmem_limit_bytes=48 << 20
        ),
    )(*args)


def scatter_scratch(rows, width, sibling):
    shapes = [pltpu.VMEM((8, rows, width), BF), pltpu.VMEM((7, rows, width), BF)]
    return shapes + ([pltpu.VMEM((8, rows, width), BF)] if sibling else [])


def g_place():
    return lax.axis_index("z"), lax.axis_index("c"), lax.axis_index("f")


def t_place():
    return lax.axis_index("x"), lax.axis_index("h")


def gather_g(values, number, name):
    def kernel(x_ref, o_ref, send, recv, local):
        net = Net(send, recv)
        net.greet(NEAR_G)
        slot = gather_slot(net, o_ref, 64, "z", "f")
        run_flows(gather_flow(net, x_ref, slot, "z", "f", local.at[0], True))
        net.finish()

    return comm_call(
        kernel, name, number, 16, 1, sds((1024, 2048), values.dtype), [], [ANY], ANY, values
    )


def scatter_g(partial_rows, number, name):
    def kernel(x_ref, o_ref, send, recv, local, mine, landed, other):
        net = Net(send, recv)
        net.greet(NEAR_G)
        chunk = scatter_chunk(net, x_ref, "z")
        run_flows(scatter_flow(net, chunk, o_ref, mine, other, landed, local, "z", "f", True))
        net.finish()

    return comm_call(
        kernel,
        name,
        number,
        16,
        8,
        sds((64, 2048), F32),
        scatter_scratch(64, 2048, True),
        [ANY],
        VMEM,
        partial_rows.astype(BF).reshape(16, 64, 2048),
    )


def start_all(layer_input, packed, ranks, number):
    def kernel(x_ref, w_ref, r_ref, xo, ao, fo, ro, send, recv, local, blocks, near):
        net = Net(send, recv)
        net.greet(NEAR_G, ALL_ZC, ALL_T)
        me = net.place({}, "z", "c")
        group = net.place({}, "x", "h")

        def weights():
            near_sent, attn_sent, ffn_sent = [], [], []
            for offset in ALL_ZC:
                to = net.place(offset, "z", "c")
                attn_sent.append(
                    net.push(
                        w_ref.at[to, :, pl.ds(1024, 512)], blocks.at[pl.ds(pl.multiple_of(me * 32, 32), 32)], offset
                    )
                )
            for offset in ALL_ZC:
                near_sent.append(net.push(r_ref, near.at[me], offset))
            rows = pl.ds(pl.multiple_of(me * 32, 32), 32)
            own = pltpu.make_async_copy(w_ref.at[me, :, pl.ds(1024, 512)], blocks.at[rows], local.at[1])
            own.start()
            own_ffn = pltpu.make_async_copy(w_ref.at[me, :, pl.ds(0, 1024)], fo.at[rows], local.at[2])
            own_ffn.start()
            near[me] = r_ref[...]
            own.wait()
            yield
            for copy in attn_sent:
                copy.wait_recv()
            slot = gather_slot(net, ao, 256, "x", "h")
            gathering = gather_flow(net, blocks, slot, "x", "h", local.at[3], False)
            yield next(gathering)
            for copy in near_sent:
                copy.wait_recv()
            rank_sent = [net.push(near, ro.at[group], offset) for offset in ALL_T]
            ro[group] = near[...]
            for offset in ALL_ZC:
                to = net.place(offset, "z", "c")
                ffn_sent.append(net.push(w_ref.at[to, :, pl.ds(0, 1024)], fo.at[rows], offset))
            yield from gathering
            for copy in rank_sent + ffn_sent:
                copy.wait_recv()
            own_ffn.wait()

        rows_flow = gather_flow(net, x_ref, input_slot(net, xo), "z", "f", local.at[0], True)
        run_flows(weights(), rows_flow)
        net.finish()

    return comm_call(
        kernel,
        "start_all",
        number,
        16 + 8 + 28,
        4,
        (sds((1024, 2048), BF), sds((2048, 512), BF), sds((256, 1024), BF), sds((8, 8, 8, 128), jnp.int32)),
        [pltpu.VMEM((256, 512), BF), pltpu.VMEM((8, 8, 128), jnp.int32)],
        [ANY, ANY, VMEM],
        (ANY, ANY, ANY, VMEM),
        layer_input,
        packed,
        ranks,
    )


def gather_both(kv_here, grad_here, number):
    def kernel(k_ref, g_ref, ko, go, send, recv, local):
        net = Net(send, recv)
        net.greet(NEAR_G, NEAR_T)
        run_flows(
            gather_flow(net, k_ref, gather_slot(net, ko, 1024, "x", "h"), "x", "h", local.at[0], False),
            gather_flow(net, g_ref, input_slot(net, go), "z", "f", local.at[1], True),
        )
        net.finish()

    return comm_call(
        kernel,
        "gather_kv_and_grad",
        number,
        24,
        2,
        (sds((8192, 256), BF), sds((1024, 2048), BF)),
        [],
        [ANY, ANY],
        (ANY, ANY),
        kv_here,
        grad_here,
    )


def scatter_both(t_part, g_part, number, name):
    total, width = t_part.shape
    rows = total // 8

    def kernel(t_ref, g_ref, to, go, send, recv, local, t_mine, t_landed, mine, landed, other):
        net = Net(send, recv)
        net.greet(NEAR_G, NEAR_T)
        t_local = local.at[pl.ds(0, 8)]
        g_local = local.at[pl.ds(8, 8)]
        run_flows(
            scatter_flow(
                net, scatter_chunk(net, t_ref, "x"), to, t_mine, None, t_landed, t_local, "x", "h", False
            ),
            scatter_flow(net, scatter_chunk(net, g_ref, "z"), go, mine, other, landed, g_local, "z", "f", True),
        )
        net.finish()

    return comm_call(
        kernel,
        name,
        number,
        24,
        16,
        (sds((rows, width), F32), sds((64, 2048), F32)),
        scatter_scratch(rows, width, False) + scatter_scratch(64, 2048, True),
        [ANY, ANY],
        (VMEM, VMEM),
        t_part.astype(BF).reshape(8, rows, width),
        g_part.astype(BF).reshape(16, 64, 2048),
    )


def stats_g(stats, number, name):
    count, tokens = stats.shape
    sent = stats.reshape(count * tokens // 128, 128)

    def kernel(x_ref, o_ref, send, recv, local):
        net = Net(send, recv)
        net.greet(ALL_G)
        me = net.place({}, "z", "c", "f")
        for offset in ALL_G:
            net.push(x_ref, o_ref.at[me], offset)
        o_ref[me] = x_ref[...]
        for copy in net.copies:
            copy.wait_recv()
        net.finish()

    out = comm_call(
        kernel, name, number, 15, 1, sds((16,) + sent.shape, F32), [], [VMEM], VMEM, sent
    )
    return out.reshape(16, count, tokens)


def finish_all(grads, r_parts, s_parts, output_rows, input_rows, number):
    def kernel(w_ref, r_ref, s_ref, y_ref, i_ref, wo, so, yo, io, send, recv, local, rbuf, packed, tbuf):
        net = Net(send, recv)
        net.greet(ALL_G, ALL_T)
        me = net.place({}, "z", "c", "f")
        here = net.place({}, "z", "c")
        f = net.at["f"]

        def rows_flow(k, source, target):
            rows = target.at[pl.ds(pl.multiple_of(f * 64, 64), 64)]
            theirs = source.at[:, pl.ds(pl.multiple_of((1 - f) * 1024, 1024), 1024)]
            own = source.at[:, pl.ds(pl.multiple_of(f * 1024, 1024), 1024)]
            copy = net.push(theirs, rows, {"f": 1})
            load = pltpu.make_async_copy(own, rows, local.at[k])
            load.start()
            yield
            yield
            yield
            copy.wait_recv()
            load.wait()

        def weights_flow():
            copies = []
            for offset in ALL_ZC:
                to = net.place(offset, "z", "c")
                copies.append(net.push(w_ref.at[to], wo.at[here], offset))
            load = pltpu.make_async_copy(w_ref.at[here], wo.at[here], local.at[2])
            load.start()
            yield
            yield
            yield
            for copy in copies:
                copy.wait_recv()
            load.wait()

        def vectors_flow():
            copies = []
            for k, offset in enumerate(ALL_G):
                to = net.place(offset, "z", "c", "f")
                copies.append(net.push(r_ref.at[to], rbuf.at[k], offset))
            yield
            for copy in copies:
                copy.wait_recv()
            total = r_ref[me]
            for k in range(15):
                total = total + rbuf[k]
            packed[0:8] = total
            packed[8:32] = s_ref[...]
            copies = [net.push(packed, tbuf.at[k], offset) for k, offset in enumerate(ALL_T)]
            yield
            for copy in copies:
                copy.wait_recv()
            total = packed[...]
            for k in range(7):
                total = total + tbuf[k]
            so[me] = total
            copies = [net.push(so.at[me], so.at[me], offset) for offset in ALL_G]
            yield
            for copy in copies:
                copy.wait_recv()

        run_flows(vectors_flow(), rows_flow(0, y_ref, yo), rows_flow(1, i_ref, io), weights_flow())
        net.finish()

    return comm_call(
        kernel,
        "finish_all",
        number,
        15 + 7 + 15 + 2 + 7,
        3,
        (sds((8, 32, 512), F32), sds((16, 32, 128), F32), sds((128, 1024), F32), sds((128, 1024), F32)),
        [pltpu.VMEM((15, 8, 128), F32), pltpu.VMEM((32, 128), F32), pltpu.VMEM((7, 32, 128), F32)],
        [ANY, VMEM, VMEM, ANY, ANY],
        (ANY, VMEM, ANY, ANY),
        grads,
        r_parts,
        s_parts,
        output_rows,
        input_rows,
    )


def both_heads(rows, zero):
    lanes = lax.broadcasted_iota(jnp.int32, rows.shape, 1)
    return jnp.where(lanes < HEAD, rows, zero), jnp.where(lanes >= HEAD, rows, zero)


def run_rows(ref, run):
    return ref[pl.ds(pl.multiple_of(run * RUN, RUN), RUN), :]


def pair_rows(ref, run_a, run_b, dtype):
    zero = jnp.zeros((), dtype)
    a = both_heads(run_rows(ref, run_a).astype(dtype), zero)
    b = both_heads(run_rows(ref, run_b).astype(dtype), zero)
    return jnp.concatenate(a + b, axis=0)


def pair_bounds(rank_a, rank_b):
    lanes = lax.broadcasted_iota(jnp.int32, (1, 256), 1)
    rank = jnp.where(lanes < 128, rank_a, rank_b)
    last = rank * RUN + lax.rem(lanes, RUN)
    return (rank // 64) * 4096, last


def seen(chunk, low, last):
    keys = chunk * CHUNK + lax.broadcasted_iota(jnp.int32, (CHUNK, 256), 0)
    return (keys >= low) & (keys <= last)


def sort_keys(rank, kv_ref, keys, values):
    def move(r, carry):
        to = pl.ds(pl.multiple_of(rank[r] * RUN, RUN), RUN)
        rows = run_rows(kv_ref, r)
        keys[to, :] = rows[:, :128]
        values[to, :] = rows[:, 128:]
        return carry

    lax.fori_loop(0, 128, move, 0)


def flip(source, target):
    def one(i, carry):
        rows = source[pl.ds(pl.multiple_of(i * CHUNK, CHUNK), CHUNK), :]
        target[i] = rows.T
        return carry

    lax.fori_loop(0, 16, one, 0)


def chunk_rows(ref, i):
    return ref[pl.ds(pl.multiple_of(i * CHUNK, CHUNK), CHUNK), :]


def lane_heads(total):
    turned = total.T
    lanes = lax.broadcasted_iota(jnp.int32, (RUN, 128), 1)
    a = jnp.where(lanes < HEAD, turned[0:64], turned[64:128])
    b = jnp.where(lanes < HEAD, turned[128:192], turned[192:256])
    return a, b


def attend_kernel(rank, srun, srank, q_ref, kv_ref, o_ref, lse_ref, keys, values, flipped):
    sort_keys(rank, kv_ref, keys, values)
    flip(values, flipped)

    def pair(p, carry):
        run_a, run_b = srun[2 * p], srun[2 * p + 1]
        rank_a, rank_b = srank[2 * p], srank[2 * p + 1]
        queries = pair_rows(q_ref, run_a, run_b, BF)
        low, last = pair_bounds(rank_a, rank_b)

        def step(i, state):
            peak, total, mixed = state
            scores = lax.dot_general(
                chunk_rows(keys, i), queries, NT, preferred_element_type=F32
            )
            scores = jnp.where(seen(i, low, last), scores, -1e30)
            new_peak = jnp.maximum(peak, jnp.max(scores, axis=0, keepdims=True))
            weights = jnp.exp(scores - new_peak)
            shrink = jnp.exp(peak - new_peak)
            total = total * shrink + jnp.sum(weights, axis=0, keepdims=True)
            mixed = mixed * shrink + lax.dot_general(
                flipped[i], weights.astype(BF), NN, preferred_element_type=F32
            )
            return new_peak, total, mixed

        start = (
            jnp.full((1, 256), -1e20, F32),
            jnp.zeros((1, 256), F32),
            jnp.zeros((128, 256), F32),
        )
        peak, total, mixed = lax.fori_loop((rank_a // 64) * 8, rank_b // 8 + 1, step, start)
        a, b = lane_heads(mixed / total)
        o_ref[pl.ds(pl.multiple_of(run_a * RUN, RUN), RUN), :] = a
        o_ref[pl.ds(pl.multiple_of(run_b * RUN, RUN), RUN), :] = b
        lse_ref[p] = peak + jnp.log(total)
        return carry

    lax.fori_loop(0, 8, pair, 0)


def attend(order, queries, kv):
    return pl.pallas_call(
        attend_kernel,
        out_shape=(sds((1024, 128), F32), sds((8, 1, 256), F32)),
        grid_spec=pltpu.PrefetchScalarGridSpec(
            num_scalar_prefetch=3,
            grid=(1,),
            in_specs=[VMEM, VMEM],
            out_specs=(VMEM, VMEM),
            scratch_shapes=[
                pltpu.VMEM((8192, 128), BF),
                pltpu.VMEM((8192, 128), BF),
                pltpu.VMEM((16, 128, CHUNK), BF),
            ],
        ),
        name="attend",
        compiler_params=pltpu.CompilerParams(vmem_limit_bytes=48 << 20),
    )(*order, queries, kv)


def attend_back_kernel(
    rank, srun, srank, q_ref, kv_ref, g_ref, a_ref, lse_ref, dq_ref, dkv_ref, keys, values, flipped, dkeys, dvalues
):
    sort_keys(rank, kv_ref, keys, values)
    flip(keys, flipped)

    def clear(i, carry):
        rows = pl.ds(pl.multiple_of(i * CHUNK, CHUNK), CHUNK)
        dkeys[rows, :] = jnp.zeros((CHUNK, 128), F32)
        dvalues[rows, :] = jnp.zeros((CHUNK, 128), F32)
        return carry

    lax.fori_loop(0, 16, clear, 0)

    def pair(p, carry):
        run_a, run_b = srun[2 * p], srun[2 * p + 1]
        rank_a, rank_b = srank[2 * p], srank[2 * p + 1]
        queries = pair_rows(q_ref, run_a, run_b, BF)
        grads = pair_rows(g_ref, run_a, run_b, BF)
        low, last = pair_bounds(rank_a, rank_b)
        product = pair_rows(g_ref, run_a, run_b, F32) * pair_rows(a_ref, run_a, run_b, F32)
        delta = lax.dot_general(
            jnp.ones((8, 128), F32),
            product,
            NT,
            preferred_element_type=F32,
            precision=lax.Precision.HIGHEST,
        )[0:1]
        log_total = lse_ref[p]

        def step(i, dq):
            rows = pl.ds(pl.multiple_of(i * CHUNK, CHUNK), CHUNK)
            scores = lax.dot_general(keys[rows, :], queries, NT, preferred_element_type=F32)
            probs = jnp.where(seen(i, low, last), jnp.exp(scores - log_total), 0.0)
            dprobs = lax.dot_general(values[rows, :], grads, NT, preferred_element_type=F32)
            dscores = (probs * (dprobs - delta)).astype(BF)
            dvalues[rows, :] += lax.dot_general(
                probs.astype(BF), grads, NN, preferred_element_type=F32
            )
            dkeys[rows, :] += lax.dot_general(dscores, queries, NN, preferred_element_type=F32)
            return dq + lax.dot_general(flipped[i], dscores, NN, preferred_element_type=F32)

        dq = lax.fori_loop(
            (rank_a // 64) * 8, rank_b // 8 + 1, step, jnp.zeros((128, 256), F32)
        )
        a, b = lane_heads(dq)
        dq_ref[pl.ds(pl.multiple_of(run_a * RUN, RUN), RUN), :] = a * 0.125
        dq_ref[pl.ds(pl.multiple_of(run_b * RUN, RUN), RUN), :] = b * 0.125
        return carry

    lax.fori_loop(0, 8, pair, 0)

    def back(r, carry):
        source = pl.ds(pl.multiple_of(rank[r] * RUN, RUN), RUN)
        to = pl.ds(pl.multiple_of(r * RUN, RUN), RUN)
        dkv_ref[to, 0:128] = dkeys[source, :].astype(BF)
        dkv_ref[to, 128:256] = dvalues[source, :].astype(BF)
        return carry

    lax.fori_loop(0, 128, back, 0)


def attend_back(order, queries, kv, grads, attended, log_total):
    return pl.pallas_call(
        attend_back_kernel,
        out_shape=(sds((1024, 128), F32), sds((8192, 256), BF)),
        grid_spec=pltpu.PrefetchScalarGridSpec(
            num_scalar_prefetch=3,
            grid=(1,),
            in_specs=[VMEM] * 5,
            out_specs=(VMEM, VMEM),
            scratch_shapes=[
                pltpu.VMEM((8192, 128), BF),
                pltpu.VMEM((8192, 128), BF),
                pltpu.VMEM((16, 128, CHUNK), BF),
                pltpu.VMEM((8192, 128), F32),
                pltpu.VMEM((8192, 128), F32),
            ],
        ),
        name="attend_back",
        compiler_params=pltpu.CompilerParams(vmem_limit_bytes=56 << 20),
    )(*order, queries, kv, grads, attended, log_total)


def lane_tables(places, seq_length):
    half = HEAD // 2
    lanes = jnp.arange(128, dtype=jnp.int32)
    indices = (lanes % half).astype(F32)
    inverse_freq = jnp.exp(-jnp.log(10000.0) * indices / half)
    spots = places.astype(F32)
    angles = spots[:, None] * inverse_freq[None, :]
    ratios = (2.0 * indices + 0.4 * HEAD) / (1.4 * HEAD)
    powers = (spots - seq_length // 2) / 512.0
    growth = jnp.exp(powers[:, None] * jnp.log(ratios)[None, :])
    sign = jnp.where(lanes % HEAD < half, -1.0, 1.0)
    return jnp.cos(angles), jnp.sin(angles) * sign[None, :], growth


def swap_halves(values):
    half = HEAD // 2
    first = (jnp.arange(128) % HEAD < half)[None, :]
    return jnp.where(first, jnp.roll(values, -half, axis=1), jnp.roll(values, half, axis=1))


def normal(values):
    center = jnp.mean(values, axis=1, keepdims=True)
    centered = values - center
    variance = jnp.mean(centered * centered, axis=1, keepdims=True)
    inv = lax.rsqrt(variance + EPS)
    return centered * inv, inv


def normal_back(upstream, gain, normal_rows, inv):
    scaled = upstream * gain
    mean = jnp.mean(scaled, axis=1, keepdims=True)
    cross = jnp.mean(scaled * normal_rows, axis=1, keepdims=True)
    return inv * (scaled - mean - normal_rows * cross)


def shards(
    layer_input,
    w_qkv,
    w_out,
    w_up,
    w_down,
    b_qkv,
    b_out,
    b_up,
    b_down,
    norm_gains,
    norm_shifts,
    hidden_gain,
    hidden_shift,
    seq_ids,
    positions,
    d_out,
):
    z, c, f = g_place()
    x, h = t_place()
    zc = z * 2 + c
    me = zc * 2 + f
    head_at = f * 1024 + zc * 128
    hidden_at = f * 4096 + zc * 512

    def head_part(vector):
        return lax.dynamic_slice_in_dim(vector, head_at, 128, axis=vector.ndim - 1)

    def hidden_part(vector):
        return lax.dynamic_slice_in_dim(vector, hidden_at, 512, axis=vector.ndim - 1)

    def my_rows(rows):
        return lax.dynamic_slice_in_dim(rows, me * 64, 64, axis=0)

    packed = jnp.concatenate(
        [
            w_up.reshape(32, 8, 512),
            w_down.reshape(32, 8, 512),
            w_qkv.reshape(32, 3, 8, 128).transpose(0, 2, 1, 3).reshape(32, 8, 384),
            w_out.reshape(32, 8, 128),
        ],
        axis=2,
    ).transpose(1, 0, 2)
    rank_here = seq_ids.reshape(2, RUN)[:, 0] * 64 + positions.reshape(2, RUN)[:, 0] // RUN
    rank_tile = jnp.zeros((8, 128), jnp.int32).at[0, :2].set(rank_here)
    input_all, w_attn, ffn_block, ranks = start_all(layer_input, packed, rank_tile, 1)
    qkv_w, out_w = w_attn[:, :384], w_attn[:, 384:]

    rank = ranks[:, :, 0, :2].reshape(128)
    group_rank = lax.dynamic_slice_in_dim(rank, (x * 2 + h) * 16, 16)
    slot = jnp.sum((group_rank[None, :] < group_rank[:, None]).astype(jnp.int32), axis=1)
    hit = slot[None, :] == jnp.arange(16, dtype=jnp.int32)[:, None]
    srank = jnp.sum(jnp.where(hit, group_rank[None, :], 0), axis=1)
    srun = jnp.sum(jnp.where(hit, jnp.arange(16, dtype=jnp.int32)[None, :], 0), axis=1)
    order = (rank, srun, srank)
    places = ((group_rank % 64) * RUN)[:, None] + jnp.arange(RUN, dtype=jnp.int32)[None, :]
    cosine, sine, growth = lane_tables(places.reshape(1024), 4096)

    normal_all, unused = normal(input_all.astype(F32))
    in_low = (normal_all * norm_gains[0] + norm_shifts[0]).astype(BF)
    qkv = jnp.dot(in_low, qkv_w, preferred_element_type=F32) + head_part(b_qkv).reshape(384)
    queries, keys, values = qkv[:, :128], qkv[:, 128:256], qkv[:, 256:]
    query_low = ((queries * cosine + swap_halves(queries) * sine) * growth).astype(BF)
    query_low = query_low * jnp.bfloat16(0.125)
    shrink = 1.0 / growth
    key_low = ((keys * cosine + swap_halves(keys) * sine) * shrink).astype(BF)
    kv, grad_all = gather_both(
        jnp.concatenate([key_low, values.astype(BF)], axis=1), d_out, 2
    )
    ffn_block, unused = lax.optimization_barrier((ffn_block, kv))
    w_ffn = lax.all_gather(ffn_block, TOK, axis=0, tiled=True)
    up_w, down_w = w_ffn[:, :512], w_ffn[:, 512:]
    attended, log_total = attend(order, query_low, kv)

    part_sum = jnp.sum(attended, axis=1)
    part_mean = part_sum / 128
    part_spread = jnp.sum(jnp.square(attended - part_mean[:, None]), axis=1)
    stats = stats_g(jnp.stack([part_sum, part_spread]), 4, "stats_attn")
    center = jnp.sum(stats[:, 0], axis=0) / 2048
    spread = jnp.sum(stats[:, 1] + 128 * jnp.square(stats[:, 0] / 128 - center[None]), axis=0)
    scale_attn = lax.rsqrt(spread / 2048 + EPS)[:, None]
    normal_attn = (attended - center[:, None]) * scale_attn
    attn_low = (normal_attn * head_part(norm_gains[1]) + head_part(norm_shifts[1])).astype(BF)
    branch = scatter_g(
        lax.dot_general(attn_low, out_w, NT, preferred_element_type=F32), 5, "scatter_branch"
    )
    input_rows = my_rows(input_all).astype(F32)
    mid = input_rows + (branch + b_out)

    normal_mid, scale_mid = normal(mid)
    mid_rows = (normal_mid * norm_gains[2] + norm_shifts[2]).astype(BF)
    mid_low = gather_g(mid_rows, 6, "gather_mid")
    grad_hidden = jnp.dot(grad_all, down_w, preferred_element_type=F32)
    pre_act = jnp.dot(mid_low, up_w, preferred_element_type=F32) + hidden_part(b_up)
    below = 0.5 * (1.0 + lax.erf(pre_act * math.sqrt(0.5)))
    activated = pre_act * below
    slope = below + pre_act * jnp.exp(-0.5 * pre_act * pre_act) * (1.0 / math.sqrt(2.0 * math.pi))
    gain_hidden = hidden_part(hidden_gain)
    part_sum = jnp.sum(activated, axis=1)
    part_centered = activated - (part_sum / 512)[:, None]
    part_spread = jnp.sum(jnp.square(part_centered), axis=1)
    scaled = grad_hidden * gain_hidden
    stats = stats_g(
        jnp.stack(
            [
                part_sum,
                part_spread,
                jnp.sum(scaled, axis=1),
                jnp.sum(scaled * part_centered, axis=1),
            ]
        ),
        8,
        "stats_hidden",
    )
    center = jnp.sum(stats[:, 0], axis=0) / 8192
    apart = stats[:, 0] / 512 - center[None]
    spread = jnp.sum(stats[:, 1] + 512 * jnp.square(apart), axis=0)
    scale_hidden = lax.rsqrt(spread / 8192 + EPS)
    back_mean = jnp.sum(stats[:, 2], axis=0) / 8192
    back_cross = scale_hidden * jnp.sum(stats[:, 3] + apart * stats[:, 2], axis=0) / 8192
    normal_hidden = (activated - center[:, None]) * scale_hidden[:, None]
    hidden_low = (normal_hidden * gain_hidden + hidden_part(hidden_shift)).astype(BF)
    grad_act = scale_hidden[:, None] * (
        scaled - back_mean[:, None] - normal_hidden * back_cross[:, None]
    )
    pre_low = (grad_act * slope).astype(BF)
    grad_mid_norm = scatter_g(
        lax.dot_general(pre_low, up_w, NT, preferred_element_type=F32), 9, "scatter_mid"
    )
    ffn_part = lax.dot_general(hidden_low, down_w, NT, preferred_element_type=F32).astype(BF)
    up_term = lax.dot_general(mid_low, pre_low, TN, preferred_element_type=F32)
    down_term = lax.dot_general(grad_all, hidden_low, TN, preferred_element_type=F32)
    ffn_term = jnp.concatenate([up_term.astype(BF), down_term.astype(BF)], axis=1)
    ffn_grads = lax.psum_scatter(ffn_term, TOK, scatter_dimension=0, tiled=True)
    ffn_grads = lax.all_to_all(ffn_grads.reshape(8, 32, 1024), ("z", "c"), 0, 0, tiled=True)
    ffn_grads = ffn_grads.astype(F32).transpose(1, 0, 2)

    grad_out_rows = my_rows(grad_all).astype(F32)
    grad_mid = grad_out_rows + normal_back(grad_mid_norm, norm_gains[2], normal_mid, scale_mid)
    branch_rows = grad_mid.astype(BF)
    branch_all = gather_g(branch_rows, 11, "gather_branch_grad")
    grad_attn_norm = jnp.dot(branch_all, out_w, preferred_element_type=F32)
    scaled = grad_attn_norm * head_part(norm_gains[1])
    stats = stats_g(
        jnp.stack([jnp.sum(scaled, axis=1), jnp.sum(scaled * normal_attn, axis=1)]),
        12,
        "stats_attn_back",
    )
    stats = jnp.sum(stats, axis=0) / 2048
    grad_attended = (
        scale_attn * (scaled - stats[0][:, None] - normal_attn * stats[1][:, None])
    ).astype(BF)
    query_grad, kv_part = attend_back(order, query_low, kv, grad_attended, attended, log_total)
    kv_grad, ffn_rows = scatter_both(kv_part, ffn_part, 13, "scatter_kv_and_ffn")
    output_rows = mid + (ffn_rows + b_down)

    def unrotate(grads, factor):
        grads = grads * factor
        return grads * cosine - swap_halves(grads) * sine

    grad_qkv = jnp.concatenate(
        [unrotate(query_grad, growth), unrotate(kv_grad[:, :128], shrink), kv_grad[:, 128:]],
        axis=1,
    ).astype(BF)
    qkv_term = lax.dot_general(in_low, grad_qkv, TN, preferred_element_type=F32)
    out_term = lax.dot_general(branch_all, attn_low, TN, preferred_element_type=F32)
    attn_grads, grad_in_norm = scatter_both(
        jnp.concatenate([qkv_term.astype(BF), out_term.astype(BF)], axis=1),
        lax.dot_general(grad_qkv, qkv_w, NT, preferred_element_type=F32),
        14,
        "scatter_weights_and_in",
    )
    normal_in, scale_in = normal(input_rows)
    input_grad_rows = grad_mid + normal_back(grad_in_norm, norm_gains[0], normal_in, scale_in)

    r_parts = jnp.stack(
        [
            jnp.sum(grad_in_norm * normal_in, axis=0),
            jnp.sum(grad_mid_norm * normal_mid, axis=0),
            jnp.sum(grad_in_norm, axis=0),
            jnp.sum(grad_mid_norm, axis=0),
            jnp.sum(branch_rows.astype(F32), axis=0),
            jnp.sum(grad_out_rows, axis=0),
            jnp.zeros((2048,), F32),
            jnp.zeros((2048,), F32),
        ]
    )
    r_parts = r_parts.reshape(8, 16, 128).transpose(1, 0, 2)
    s_parts = jnp.concatenate(
        [
            jnp.sum(grad_qkv.astype(F32), axis=0),
            jnp.sum(grad_attn_norm * normal_attn, axis=0),
            jnp.sum(grad_attn_norm, axis=0),
            jnp.sum(pre_low.astype(F32), axis=0),
            jnp.sum(grad_hidden * normal_hidden, axis=0),
            jnp.sum(grad_hidden, axis=0),
            jnp.zeros((896,), F32),
        ]
    ).reshape(24, 128)
    grads, sums, layer_output, input_grad = finish_all(
        attn_grads.reshape(8, 32, 512), r_parts, s_parts, output_rows, input_grad_rows, 16
    )
    grads = grads.transpose(1, 0, 2)
    by_rows = sums[:, :6].transpose(1, 0, 2).reshape(6, 2048)

    def by_heads(first, count):
        part = sums[:, 8 + first : 8 + first + count].reshape(8, 2, count, 128)
        return part.transpose(2, 1, 0, 3).reshape(count, 2048)

    def by_hidden(first):
        part = sums[:, 8 + first : 12 + first].reshape(8, 2, 512)
        return part.transpose(1, 0, 2).reshape(8192)

    head_sums = by_heads(0, 5)
    gains_grad = jnp.stack([by_rows[0], head_sums[3], by_rows[1]])
    shifts_grad = jnp.stack([by_rows[2], head_sums[4], by_rows[3]])

    return (
        layer_output,
        input_grad,
        grads[:, :, :384].reshape(32, 8, 3, 128).transpose(0, 2, 1, 3).reshape(32, 3, 1024),
        grads[:, :, 384:].reshape(32, 1024),
        ffn_grads[:, :, :512].reshape(32, 4096),
        ffn_grads[:, :, 512:].reshape(32, 4096),
        head_sums[:3],
        by_rows[4],
        by_hidden(5),
        by_rows[5],
        gains_grad,
        shifts_grad,
        by_hidden(9),
        by_hidden(13),
    )


def solution(mesh):
    fine = Mesh(mesh.devices.reshape(4, 2, 4, 2, 2), SEQ + ("f",))
    both = P(SEQ, "f")
    return jax.shard_map(
        shards,
        mesh=fine,
        in_specs=(both, P(SEQ, None, "f"), both, both, both)
        + (P(),) * 8
        + (P(SEQ), P(SEQ), both),
        out_specs=(both, both, P(SEQ, None, "f"), both, both, both) + (P(),) * 8,
        check_vma=False,
    )
```

```python
import math

import jax
import jax.numpy as jnp
from jax import lax
from jax.experimental import pallas as pl
from jax.experimental.pallas import tpu as pltpu
from jax.sharding import Mesh
from jax.sharding import PartitionSpec as P

SEQ = ("x", "h", "z", "c")
TOK = ("x", "h")
HEAD = 64
RUN = 64
CHUNK = 512
EPS = 1e-05
MESH = pl.DeviceIdType.MESH
BF = jnp.bfloat16
F32 = jnp.float32
DMA = pltpu.SemaphoreType.DMA
ANY = pl.BlockSpec(memory_space=pl.ANY)
VMEM = pl.BlockSpec(memory_space=pltpu.VMEM)
NT = (((1,), (1,)), ((), ()))
TN = (((0,), (0,)), ((), ()))
NN = (((1,), (0,)), ((), ()))


def sds(shape, dtype):
    return jax.ShapeDtypeStruct(shape, dtype)


AXES = {"x": 4, "h": 2, "z": 4, "c": 2, "f": 2}
RING_G, PAIR_G = "z", "f"
RING_T, PAIR_T = "x", "h"


class Net:
    def __init__(self, send, recv):
        self.send, self.recv, self.copies, self.drained = send, recv, [], 0
        self.at = {axis: lax.axis_index(axis) for axis in AXES}

    def device(self, offset):
        return {a: lax.rem(self.at[a] + d + AXES[a], AXES[a]) for a, d in offset.items()}

    def place(self, offset, *axes):
        index = 0
        for a in axes:
            d = offset.get(a, 0)
            at = lax.rem(self.at[a] + d + AXES[a], AXES[a]) if d else self.at[a]
            index = index * AXES[a] + at
        return index

    def greet(self, *groups):
        offsets = {
            tuple((a, o[a]) for a in AXES if o.get(a, 0)) for group in groups for o in group
        }
        barrier = pltpu.get_barrier_semaphore()
        for offset in sorted(offsets):
            pl.semaphore_signal(
                barrier, inc=1, device_id=self.device(dict(offset)), device_id_type=MESH
            )
        pl.semaphore_wait(barrier, len(offsets))

    def push(self, src, dst, offset):
        k = len(self.copies)
        copy = pltpu.make_async_remote_copy(
            src_ref=src,
            dst_ref=dst,
            send_sem=self.send.at[k],
            recv_sem=self.recv.at[k],
            device_id=self.device(offset),
            device_id_type=MESH,
        )
        copy.start()
        self.copies.append(copy)
        return copy

    def finish(self):
        for copy in self.copies[self.drained :]:
            copy.wait_send()
        self.drained = len(self.copies)


SIBLING = {"c": 1}
NEAR_G = [{"z": 1}, {"z": 3}, {"f": 1}, SIBLING]
NEAR_T = [{"x": 1}, {"x": 3}, {"h": 1}]
ALL_T = [{"x": i, "h": j} for i in range(4) for j in range(2)][1:]
ALL_ZC = [{"z": i, "c": j} for i in range(4) for j in range(2)][1:]
ALL_G = [{"z": i, "c": j, "f": k} for i in range(4) for j in range(2) for k in range(2)][1:]


def run_flows(*flows):
    left = list(flows)
    while left:
        left = [flow for flow in left if next(flow, "end") != "end"]


def half_rows(ref, which):
    rows = ref.shape[0] // 2
    return ref.at[pl.ds(which * rows, rows)]


def gather_flow(net, src, slot, ring, pair, local, sibling, light=False):
    up, down, across = {ring: 1}, {ring: 3}, {pair: 1}
    passed = []

    def to_sibling(ref):
        if sibling:
            passed.append(net.push(ref, ref, SIBLING))

    mine = slot({})
    from_down = net.push(src, mine, up)
    from_up = net.push(src, mine, down)
    from_across = net.push(src, mine, across)
    if sibling:
        passed.append(net.push(src, mine, SIBLING))
    here = pltpu.make_async_copy(src, mine, local)
    here.start()
    yield
    from_down.wait_recv()
    below = slot({ring: 3})
    first = net.push(half_rows(below, 0), half_rows(below, 0), up)
    to_sibling(below)
    yield
    from_up.wait_recv()
    above = slot({ring: 1})
    second = net.push(half_rows(above, 1), half_rows(above, 1), down)
    to_sibling(above)
    yield
    from_across.wait_recv()
    beside = slot({pair: 1})
    beside_down = net.push(beside, beside, up)
    beside_up = net.push(beside, beside, down)
    to_sibling(beside)
    yield
    first.wait_recv()
    second.wait_recv()
    far = slot({ring: 2})
    if not light:
        beside_far = [net.push(far, far, across)]
    to_sibling(far)
    yield
    beside_down.wait_recv()
    below = slot({ring: 3, pair: 1})
    if light:
        beside_far = [net.push(half_rows(below, 0), half_rows(below, 0), up)]
    to_sibling(below)
    yield
    beside_up.wait_recv()
    above = slot({ring: 1, pair: 1})
    if light:
        beside_far.append(net.push(half_rows(above, 1), half_rows(above, 1), down))
    to_sibling(above)
    yield
    for copy in beside_far:
        copy.wait_recv()
    to_sibling(slot({ring: 2, pair: 1}))
    yield
    here.wait()
    for copy in passed:
        copy.wait_recv()


def add_into(target, *sources):
    rows = min(32768 // target.shape[1], target.shape[0])

    def step(i, carry):
        at = pl.ds(pl.multiple_of(i * rows, rows), rows)
        total = target[at, :].astype(F32)
        for source in sources:
            total = total + source[at, :].astype(F32)
        target[at, :] = total.astype(target.dtype)
        return carry

    lax.fori_loop(0, target.shape[0] // rows, step, 0)


ROOTS = ((2, 1), (1, 1), (3, 1), (2, 0), (1, 0), (3, 0), (0, 1), (0, 0))


def scatter_flow(
    net, chunk, out, mine, other, landed, local, ring, pair, sibling, light=False
):
    up, down, across = {ring: 1}, {ring: 3}, {pair: 1}
    loads, shared = [], []
    for k, (i, j) in enumerate(ROOTS):
        if sibling:
            shared.append(net.push(chunk({ring: i, pair: j, "c": 1}), other.at[k], SIBLING))
        load = pltpu.make_async_copy(chunk({ring: i, pair: j}), mine.at[k], local.at[k])
        load.start()
        loads.append(load)

    def ready(k):
        loads[k].wait()
        if sibling:
            shared[k].wait_recv()
            add_into(mine.at[k], other.at[k])

    def halves(k, to):
        return (
            net.push(half_rows(mine.at[k], 0), half_rows(landed.at[to], 0), down),
            net.push(half_rows(mine.at[k], 1), half_rows(landed.at[to], 1), up),
        )

    yield
    ready(0)
    if light:
        beside_first, beside_second = halves(0, 0)
        ready(3)
        first, second = halves(3, 3)
        ready(2)
        ready(1)
        yield
        beside_first.wait_recv()
        add_into(half_rows(mine.at[2], 0), half_rows(landed.at[0], 0))
        beside_up = net.push(mine.at[2], landed.at[2], down)
        beside_second.wait_recv()
        add_into(half_rows(mine.at[1], 1), half_rows(landed.at[0], 1))
        beside_down = net.push(mine.at[1], landed.at[1], up)
    else:
        beside_far = net.push(mine.at[0], landed.at[0], across)
        ready(1)
        beside_down = net.push(mine.at[1], landed.at[1], up)
        ready(2)
        beside_up = net.push(mine.at[2], landed.at[2], down)
        ready(3)
        yield
        beside_far.wait_recv()
        add_into(mine.at[3], landed.at[0])
        first, second = halves(3, 3)
    ready(6)
    yield
    beside_down.wait_recv()
    beside_up.wait_recv()
    add_into(mine.at[6], landed.at[1], landed.at[2])
    from_across = net.push(mine.at[6], landed.at[4], across)
    ready(5)
    yield
    first.wait_recv()
    add_into(half_rows(mine.at[5], 0), half_rows(landed.at[3], 0))
    from_up = net.push(mine.at[5], landed.at[5], down)
    ready(4)
    yield
    second.wait_recv()
    add_into(half_rows(mine.at[4], 1), half_rows(landed.at[3], 1))
    from_down = net.push(mine.at[4], landed.at[6], up)
    ready(7)
    yield
    from_across.wait_recv()
    yield
    from_up.wait_recv()
    from_down.wait_recv()

    rows = 32768 // out.shape[1]

    def total(i, carry):
        at = pl.ds(pl.multiple_of(i * rows, rows), rows)
        value = mine[7, at, :].astype(F32) + landed[4, at, :].astype(F32)
        out[at, :] = value + (landed[5, at, :].astype(F32) + landed[6, at, :].astype(F32))
        return carry

    lax.fori_loop(0, out.shape[0] // rows, total, 0)


def gather_slot(net, out, rows, ring, pair):
    order = ("z", "c", "f") if ring == "z" else ("x", "h")

    def slot(offset):
        at = net.place(offset, *order)
        return out.at[pl.ds(pl.multiple_of(at * rows, rows), rows)]

    return slot


def input_slot(net, out):
    def slot(offset):
        row = pl.multiple_of(net.place(offset, "z", "c") * 128, 128)
        column = pl.multiple_of(net.place(offset, "f") * 1024, 1024)
        return out.at[pl.ds(row, 128), pl.ds(column, 1024)]

    return slot


def scatter_chunk(net, ref, ring):
    order = ("z", "c", "f") if ring == "z" else ("x", "h")
    return lambda offset: ref.at[net.place(offset, *order)]


def comm_call(kernel, name, number, pushes, locals_, out_shape, scratch, in_specs, out_specs, *args):
    return pl.pallas_call(
        kernel,
        out_shape=out_shape,
        in_specs=in_specs,
        out_specs=out_specs,
        scratch_shapes=[DMA((pushes,)), DMA((pushes,)), DMA((locals_,))] + scratch,
        name=name,
        compiler_params=pltpu.CompilerParams(
            collective_id=number, has_side_effects=True, vmem_limit_bytes=56 << 20
        ),
    )(*args)


def scatter_scratch(rows, width, sibling):
    shapes = [pltpu.VMEM((8, rows, width), BF), pltpu.VMEM((7, rows, width), BF)]
    return shapes + ([pltpu.VMEM((8, rows, width), BF)] if sibling else [])


def g_place():
    return lax.axis_index("z"), lax.axis_index("c"), lax.axis_index("f")


def t_place():
    return lax.axis_index("x"), lax.axis_index("h")


def start_all(layer_input, packed, ranks, number):
    def kernel(x_ref, w_ref, r_ref, xo, ao, fo, ro, send, recv, local, blocks, near):
        net = Net(send, recv)
        net.greet(NEAR_G, ALL_ZC, ALL_T)
        me = net.place({}, "z", "c")
        group = net.place({}, "x", "h")

        def weights():
            near_sent, attn_sent, ffn_sent = [], [], []
            for offset in ALL_ZC:
                to = net.place(offset, "z", "c")
                attn_sent.append(
                    net.push(
                        w_ref.at[to, :, pl.ds(1024, 512)], blocks.at[pl.ds(pl.multiple_of(me * 32, 32), 32)], offset
                    )
                )
            for offset in ALL_ZC:
                near_sent.append(net.push(r_ref, near.at[me], offset))
            rows = pl.ds(pl.multiple_of(me * 32, 32), 32)
            own = pltpu.make_async_copy(w_ref.at[me, :, pl.ds(1024, 512)], blocks.at[rows], local.at[1])
            own.start()
            own_ffn = pltpu.make_async_copy(w_ref.at[me, :, pl.ds(0, 1024)], fo.at[rows], local.at[2])
            own_ffn.start()
            near[me] = r_ref[...]
            own.wait()
            yield
            for copy in attn_sent:
                copy.wait_recv()
            slot = gather_slot(net, ao, 256, "x", "h")
            gathering = gather_flow(net, blocks, slot, "x", "h", local.at[3], False)
            yield next(gathering)
            for copy in near_sent:
                copy.wait_recv()
            rank_sent = [net.push(near, ro.at[group], offset) for offset in ALL_T]
            ro[group] = near[...]
            for offset in ALL_ZC:
                to = net.place(offset, "z", "c")
                ffn_sent.append(net.push(w_ref.at[to, :, pl.ds(0, 1024)], fo.at[rows], offset))
            yield from gathering
            for copy in rank_sent + ffn_sent:
                copy.wait_recv()
            own_ffn.wait()

        rows_flow = gather_flow(net, x_ref, input_slot(net, xo), "z", "f", local.at[0], True, True)
        run_flows(weights(), rows_flow)
        net.finish()

    return comm_call(
        kernel,
        "start_all",
        number,
        17 + 8 + 28,
        4,
        (sds((1024, 2048), BF), sds((2048, 512), BF), sds((256, 1024), BF), sds((8, 8, 8, 128), jnp.int32)),
        [pltpu.VMEM((256, 512), BF), pltpu.VMEM((8, 8, 128), jnp.int32)],
        [ANY, ANY, VMEM],
        (ANY, ANY, ANY, VMEM),
        layer_input,
        packed,
        ranks,
    )


def gather_both(kv_here, grad_here, number):
    def kernel(k_ref, g_ref, ko, go, send, recv, local):
        net = Net(send, recv)
        net.greet(NEAR_G, NEAR_T)
        run_flows(
            gather_flow(net, k_ref, gather_slot(net, ko, 1024, "x", "h"), "x", "h", local.at[0], False),
            gather_flow(net, g_ref, input_slot(net, go), "z", "f", local.at[1], True, True),
        )
        net.finish()

    return comm_call(
        kernel,
        "gather_kv_and_grad",
        number,
        25,
        2,
        (sds((8192, 256), BF), sds((1024, 2048), BF)),
        [],
        [ANY, ANY],
        (ANY, ANY),
        kv_here,
        grad_here,
    )


def scatter_both(t_part, g_part, number, name):
    total, width = t_part.shape
    rows = total // 8

    def kernel(t_ref, g_ref, to, go, send, recv, local, t_mine, t_landed, mine, landed, other):
        net = Net(send, recv)
        net.greet(NEAR_G, NEAR_T)
        t_local = local.at[pl.ds(0, 8)]
        g_local = local.at[pl.ds(8, 8)]
        run_flows(
            scatter_flow(
                net, scatter_chunk(net, t_ref, "x"), to, t_mine, None, t_landed, t_local, "x", "h", False
            ),
            scatter_flow(
                net, scatter_chunk(net, g_ref, "z"), go, mine, other, landed, g_local, "z", "f", True, True
            ),
        )
        net.finish()

    return comm_call(
        kernel,
        name,
        number,
        25,
        16,
        (sds((rows, width), F32), sds((64, 2048), F32)),
        scatter_scratch(rows, width, False) + scatter_scratch(64, 2048, True),
        [ANY, ANY],
        (VMEM, VMEM),
        t_part.astype(BF).reshape(8, rows, width),
        g_part.astype(BF).reshape(16, 64, 2048),
    )


def row_sums(values):
    ones = jnp.ones((8, values.shape[1]), F32)
    return lax.dot_general(
        ones, values, NT, preferred_element_type=F32, precision=lax.Precision.HIGHEST
    )[0:1]


def tile(i, rows=128):
    return pl.ds(pl.multiple_of(i * rows, rows), rows)


def columns_of(rows_ref, i):
    return rows_ref[i].T


def put_rows(rows_ref, *values):
    for k, value in enumerate(values):
        for i in range(8):
            rows_ref[i, k : k + 1, :] = value[i : i + 1]


def middle_kernel(
    att,
    w_attn,
    w_ffn,
    grad_all,
    input_all,
    b_out,
    b_up,
    gains,
    shifts,
    hid_gain,
    hid_shift,
    mid,
    grad_mid,
    mid_low,
    hidden_low,
    pre_low,
    ffn_part,
    branch_all,
    grad_att,
    attn_low,
    hid_vec,
    head_vec,
    row_vec,
    send,
    recv,
    local,
    input_rows,
    low_rows,
    partial_rows,
    mine,
    landed_a,
    other_a,
    landed_b,
    other_b,
    grad_hidden,
    activated,
    slope,
    normal_attn,
    normal_mid,
    scale_mid,
    sent_a,
    stats_a,
    rows_a,
    sent_b,
    stats_b,
    rows_b,
    sent_c,
    stats_c,
    rows_c,
):
    net = Net(send, recv)
    net.greet(ALL_G)
    me = net.place({}, "z", "c", "f")
    head_at = pl.ds(
        pl.multiple_of(net.at["f"] * 1024 + net.place({}, "z", "c") * 128, 128), 128
    )
    hidden_at = pl.ds(
        pl.multiple_of(net.at["f"] * 4096 + net.place({}, "z", "c") * 512, 512), 512
    )
    my_rows = pl.ds(pl.multiple_of(me * 64, 64), 64)
    load = pltpu.make_async_copy(input_all.at[my_rows], input_rows, local.at[8])
    load.start()
    head_gain, head_shift = gains[1:2, head_at], shifts[1:2, head_at]
    gain_here, shift_here, bias_here = hid_gain[:, hidden_at], hid_shift[:, hidden_at], b_up[:, hidden_at]

    def exchange(sent, stats):
        copies = [net.push(sent, stats.at[me], offset) for offset in ALL_G]
        stats[me] = sent[...]
        for copy in copies:
            copy.wait_recv()

    def chunk(offset):
        at = net.place(offset, "z", "c", "f")
        return partial_rows.at[pl.ds(pl.multiple_of(at * 64, 64), 64)]

    def measure(i, carry):
        here = att[tile(i), :]
        centered = here - jnp.mean(here, axis=1, keepdims=True)
        sent_a[pl.ds(i, 1), :] = row_sums(here)
        sent_a[pl.ds(8 + i, 1), :] = row_sums(centered * centered)
        return carry

    lax.fori_loop(0, 8, measure, 0)
    exchange(sent_a, stats_a)
    center = jnp.sum(stats_a[:, 0:8], axis=0) / 2048
    spread = jnp.sum(
        stats_a[:, 8:16] + 128 * jnp.square(stats_a[:, 0:8] / 128 - center[None]), axis=0
    )
    put_rows(rows_a, center, lax.rsqrt(spread / 2048 + EPS))

    def norm_heads(i, carry):
        columns = columns_of(rows_a, i)
        normal_rows = (att[tile(i), :] - columns[:, 0:1]) * columns[:, 1:2]
        normal_attn[tile(i), :] = normal_rows
        attn_low[tile(i), :] = (normal_rows * head_gain + head_shift).astype(BF)
        return carry

    lax.fori_loop(0, 8, norm_heads, 0)

    def project(i, carry):
        partial_rows[:, tile(i, 256)] = lax.dot_general(
            attn_low[...], w_attn[tile(i, 256), 384:512], NT, preferred_element_type=F32
        ).astype(BF)
        return carry

    lax.fori_loop(0, 8, project, 0)
    run_flows(
        scatter_flow(net, chunk, mid, mine, other_a, landed_a, local, "z", "f", True)
    )
    net.finish()

    load.wait()

    def mid_norm(i, carry):
        at = tile(i, 16)
        rows = input_rows[at, :].astype(F32) + (mid[at, :] + b_out[...])
        mid[at, :] = rows
        centered = rows - jnp.mean(rows, axis=1, keepdims=True)
        scale = lax.rsqrt(jnp.mean(centered * centered, axis=1, keepdims=True) + EPS)
        rows = centered * scale
        normal_mid[at, :] = rows
        scale_mid[at, :] = jnp.broadcast_to(scale, (16, 128))
        low_rows[at, :] = (rows * gains[2:3, :] + shifts[2:3, :]).astype(BF)
        return carry

    lax.fori_loop(0, 4, mid_norm, 0)

    def hidden_grads():
        for i in range(4):
            yield
            grad_hidden[tile(i, 256), :] = jnp.dot(
                grad_all[tile(i, 256), :], w_ffn[:, 512:1024], preferred_element_type=F32
            )

    run_flows(
        gather_flow(net, low_rows, gather_slot(net, mid_low, 64, "z", "f"), "z", "f", local.at[0], True),
        hidden_grads(),
    )
    net.finish()

    def up(i, carry):
        at = tile(i)
        pre = jnp.dot(mid_low[at, :], w_ffn[:, 0:512], preferred_element_type=F32) + bias_here
        below = 0.5 + 0.5 * lax.erf(pre * math.sqrt(0.5))
        act = pre * below
        activated[at, :] = act
        slope[at, :] = below + pre * jnp.exp(-0.5 * pre * pre) * (1.0 / math.sqrt(2.0 * math.pi))
        centered = act - jnp.mean(act, axis=1, keepdims=True)
        scaled = grad_hidden[at, :] * gain_here
        sent_b[pl.ds(i, 1), :] = row_sums(act)
        sent_b[pl.ds(8 + i, 1), :] = row_sums(centered * centered)
        sent_b[pl.ds(16 + i, 1), :] = row_sums(scaled)
        sent_b[pl.ds(24 + i, 1), :] = row_sums(scaled * centered)
        return carry

    lax.fori_loop(0, 8, up, 0)
    exchange(sent_b, stats_b)
    center = jnp.sum(stats_b[:, 0:8], axis=0) / 8192
    apart = stats_b[:, 0:8] / 512 - center[None]
    spread = jnp.sum(stats_b[:, 8:16] + 512 * jnp.square(apart), axis=0)
    scale = lax.rsqrt(spread / 8192 + EPS)
    mean_back = jnp.sum(stats_b[:, 16:24], axis=0) / 8192
    cross_back = scale * jnp.sum(stats_b[:, 24:32] + apart * stats_b[:, 16:24], axis=0) / 8192
    put_rows(rows_b, center, scale, mean_back, cross_back)

    def hidden(i, carry):
        at = tile(i)
        columns = columns_of(rows_b, i)
        scale = columns[:, 1:2]
        normal_rows = (activated[at, :] - columns[:, 0:1]) * scale
        hidden_low[at, :] = (normal_rows * gain_here + shift_here).astype(BF)
        upstream = grad_hidden[at, :]
        back = scale * (upstream * gain_here - columns[:, 2:3] - normal_rows * columns[:, 3:4])
        low = (back * slope[at, :]).astype(BF)
        pre_low[at, :] = low
        return (
            carry[0] + jnp.sum(low.astype(F32), axis=0, keepdims=True),
            carry[1] + jnp.sum(upstream * normal_rows, axis=0, keepdims=True),
            carry[2] + jnp.sum(upstream, axis=0, keepdims=True),
        )

    sums = lax.fori_loop(0, 8, hidden, (jnp.zeros((1, 512), F32),) * 3)
    for k in range(3):
        hid_vec[k : k + 1, :] = sums[k]

    def project_back(i, carry):
        partial_rows[:, tile(i, 256)] = lax.dot_general(
            pre_low[...], w_ffn[tile(i, 256), 0:512], NT, preferred_element_type=F32
        ).astype(BF)
        return carry

    lax.fori_loop(0, 8, project_back, 0)

    def down():
        for i in range(8):
            yield
            ffn_part[:, tile(i, 256)] = lax.dot_general(
                hidden_low[...], w_ffn[tile(i, 256), 512:1024], NT, preferred_element_type=F32
            ).astype(BF)

    run_flows(
        scatter_flow(net, chunk, grad_mid, mine, other_b, landed_b, local, "z", "f", True), down()
    )
    net.finish()

    def mid_back(i, carry):
        at = tile(i, 16)
        upstream = grad_mid[at, :]
        normal_rows = normal_mid[at, :]
        scaled = upstream * gains[2:3, :]
        mean = jnp.mean(scaled, axis=1, keepdims=True)
        cross = jnp.mean(scaled * normal_rows, axis=1, keepdims=True)
        out_rows = grad_all[pl.ds(pl.multiple_of(me * 64 + i * 16, 16), 16), :].astype(F32)
        rows = out_rows + scale_mid[at, 0:1] * (scaled - mean - normal_rows * cross)
        grad_mid[at, :] = rows
        low = rows.astype(BF)
        low_rows[at, :] = low
        row_vec[0:1, :] += jnp.sum(upstream * normal_rows, axis=0, keepdims=True)
        row_vec[1:2, :] += jnp.sum(upstream, axis=0, keepdims=True)
        row_vec[2:3, :] += jnp.sum(low.astype(F32), axis=0, keepdims=True)
        row_vec[3:4, :] += jnp.sum(out_rows, axis=0, keepdims=True)
        return carry

    row_vec[...] = jnp.zeros_like(row_vec)
    lax.fori_loop(0, 4, mid_back, 0)
    run_flows(
        gather_flow(
            net, low_rows, gather_slot(net, branch_all, 64, "z", "f"), "z", "f", local.at[0], True
        )
    )
    net.finish()

    def attn_back(i, carry):
        at = tile(i)
        upstream = jnp.dot(branch_all[at, :], w_attn[:, 384:512], preferred_element_type=F32)
        normal_rows = normal_attn[at, :]
        scaled = upstream * head_gain
        activated[at, 0:128] = scaled
        sent_c[pl.ds(i, 1), :] = row_sums(scaled)
        sent_c[pl.ds(8 + i, 1), :] = row_sums(scaled * normal_rows)
        return (
            carry[0] + jnp.sum(upstream * normal_rows, axis=0, keepdims=True),
            carry[1] + jnp.sum(upstream, axis=0, keepdims=True),
        )

    sums = lax.fori_loop(0, 8, attn_back, (jnp.zeros((1, 128), F32),) * 2)
    for k in range(2):
        head_vec[k : k + 1, :] = sums[k]
    exchange(sent_c, stats_c)
    totals = jnp.sum(stats_c[...], axis=0) / 2048
    put_rows(rows_c, totals[0:8], totals[8:16])

    def heads_back(i, carry):
        at = tile(i)
        columns = columns_of(rows_c, i)
        scale = columns_of(rows_a, i)[:, 1:2]
        grad_att[at, :] = (
            scale
            * (activated[at, 0:128] - columns[:, 0:1] - normal_attn[at, :] * columns[:, 1:2])
        ).astype(BF)
        return carry

    lax.fori_loop(0, 8, heads_back, 0)
    net.finish()


def middle(number, *args):
    wide = pltpu.VMEM((1024, 512), F32)
    return comm_call(
        middle_kernel,
        "middle",
        number,
        15 * 3 + 16 * 4,
        9,
        (
            sds((64, 2048), F32),
            sds((64, 2048), F32),
            sds((1024, 2048), BF),
            sds((1024, 512), BF),
            sds((1024, 512), BF),
            sds((1024, 2048), BF),
            sds((1024, 2048), BF),
            sds((1024, 128), BF),
            sds((1024, 128), BF),
            sds((8, 512), F32),
            sds((8, 128), F32),
            sds((8, 2048), F32),
        ),
        [
            pltpu.VMEM((64, 2048), BF),
            pltpu.VMEM((64, 2048), BF),
            pltpu.VMEM((1024, 2048), BF),
            pltpu.VMEM((8, 64, 2048), BF),
            pltpu.VMEM((7, 64, 2048), BF),
            pltpu.VMEM((8, 64, 2048), BF),
            pltpu.VMEM((7, 64, 2048), BF),
            pltpu.VMEM((8, 64, 2048), BF),
            wide,
            wide,
            wide,
            pltpu.VMEM((1024, 128), F32),
            pltpu.VMEM((64, 2048), F32),
            pltpu.VMEM((64, 128), F32),
            pltpu.VMEM((16, 128), F32),
            pltpu.VMEM((16, 16, 128), F32),
            pltpu.VMEM((8, 8, 128), F32),
            pltpu.VMEM((32, 128), F32),
            pltpu.VMEM((16, 32, 128), F32),
            pltpu.VMEM((8, 8, 128), F32),
            pltpu.VMEM((16, 128), F32),
            pltpu.VMEM((16, 16, 128), F32),
            pltpu.VMEM((8, 8, 128), F32),
        ],
        [VMEM] * 4 + [ANY] + [VMEM] * 6,
        (VMEM,) * 12,
        *args,
    )


def finish_all(attn_grads, ffn_grads, r_parts, s_parts, output_rows, input_rows, number):
    def kernel(
        a_ref,
        w_ref,
        r_ref,
        s_ref,
        y_ref,
        i_ref,
        yo,
        io,
        qkv_out,
        out_out,
        up_out,
        down_out,
        qkv_bias,
        gains_out,
        shifts_out,
        out_bias,
        down_bias,
        up_bias,
        hid_gain_out,
        hid_shift_out,
        send,
        recv,
        local,
        rbuf,
        packed,
        tbuf,
        sums,
        abuf,
        wbuf,
    ):
        net = Net(send, recv)
        net.greet(ALL_G, ALL_T)
        me = net.place({}, "z", "c", "f")
        here = net.place({}, "z", "c")
        f = net.at["f"]

        def rows_flow(k, source, target):
            rows = target.at[pl.ds(pl.multiple_of(f * 64, 64), 64)]
            theirs = source.at[:, pl.ds(pl.multiple_of((1 - f) * 1024, 1024), 1024)]
            own = source.at[:, pl.ds(pl.multiple_of(f * 1024, 1024), 1024)]
            copy = net.push(theirs, rows, {"f": 1})
            load = pltpu.make_async_copy(own, rows, local.at[k])
            load.start()
            for _ in range(5):
                yield
            copy.wait_recv()
            load.wait()

        def weights_flow():
            copies = []
            for offset in ALL_ZC:
                to = net.place(offset, "z", "c")
                copies.append(net.push(a_ref.at[to], abuf.at[here], offset))
                copies.append(net.push(w_ref.at[to], wbuf.at[here], offset))
            loads = [
                pltpu.make_async_copy(a_ref.at[here], abuf.at[here], local.at[2]),
                pltpu.make_async_copy(w_ref.at[here], wbuf.at[here], local.at[3]),
            ]
            for load in loads:
                load.start()
            yield
            yield
            for copy in copies:
                copy.wait_recv()
            for load in loads:
                load.wait()

            def place(i, carry):
                small, large = tile(i, 128), tile(i, 512)
                for j in range(3):
                    at = pl.ds(pl.multiple_of(j * 1024 + i * 128, 128), 128)
                    qkv_out[:, at] = abuf[i, :, j * 128 : j * 128 + 128]
                out_out[:, small] = abuf[i, :, 384:512]
                up_out[:, large] = wbuf[i, :, 0:512].astype(F32)
                down_out[:, large] = wbuf[i, :, 512:1024].astype(F32)
                return carry

            lax.fori_loop(0, 8, place, 0)

        def vectors_flow():
            copies = []
            for k, offset in enumerate(ALL_G):
                to = net.place(offset, "z", "c", "f")
                copies.append(net.push(r_ref.at[to], rbuf.at[k], offset))
            yield
            for copy in copies:
                copy.wait_recv()
            total = r_ref[me]
            for k in range(15):
                total = total + rbuf[k]
            packed[0:8] = total
            packed[8:32] = s_ref[...]
            copies = [net.push(packed, tbuf.at[k], offset) for k, offset in enumerate(ALL_T)]
            yield
            for copy in copies:
                copy.wait_recv()
            total = packed[...]
            for k in range(7):
                total = total + tbuf[k]
            sums[me] = total
            copies = [net.push(sums.at[me], sums.at[me], offset) for offset in ALL_G]
            yield
            yield
            for copy in copies:
                copy.wait_recv()

            def place(g, carry):
                by_rows = pl.ds(g, 1)
                by_heads = pl.ds(lax.rem(g, 2) * 8 + g // 2, 1)
                gains_out[0, by_rows, :] = sums[g, 0:1, :]
                shifts_out[0, by_rows, :] = sums[g, 1:2, :]
                gains_out[2, by_rows, :] = sums[g, 2:3, :]
                shifts_out[2, by_rows, :] = sums[g, 3:4, :]
                out_bias[by_rows, :] = sums[g, 4:5, :]
                down_bias[by_rows, :] = sums[g, 5:6, :]
                for j in range(3):
                    qkv_bias[j, by_heads, :] = sums[g, 8 + j : 9 + j, :]
                gains_out[1, by_heads, :] = sums[g, 11:12, :]
                shifts_out[1, by_heads, :] = sums[g, 12:13, :]
                for k, target in enumerate((up_bias, hid_gain_out, hid_shift_out)):
                    for j in range(4):
                        at = pl.ds((lax.rem(g, 2) * 8 + g // 2) * 4 + j, 1)
                        target[at, :] = sums[g, 13 + 4 * k + j : 14 + 4 * k + j, :]
                return carry

            lax.fori_loop(0, 16, place, 0)

        run_flows(vectors_flow(), rows_flow(0, i_ref, io), rows_flow(1, y_ref, yo), weights_flow())
        net.finish()

    vector, hidden = sds((16, 128), F32), sds((64, 128), F32)
    triple = sds((3, 16, 128), F32)
    half = sds((128, 1024), F32)
    return comm_call(
        kernel,
        "finish_all",
        number,
        15 + 7 + 15 + 2 + 14,
        4,
        (
            half,
            half,
            sds((32, 3072), F32),
            sds((32, 1024), F32),
            sds((32, 4096), F32),
            sds((32, 4096), F32),
            triple,
            triple,
            triple,
            vector,
            vector,
            hidden,
            hidden,
            hidden,
        ),
        [
            pltpu.VMEM((15, 8, 128), F32),
            pltpu.VMEM((32, 128), F32),
            pltpu.VMEM((7, 32, 128), F32),
            pltpu.VMEM((16, 32, 128), F32),
            pltpu.VMEM((8, 32, 512), F32),
            pltpu.VMEM((8, 32, 1024), BF),
        ],
        [VMEM] * 6,
        (VMEM,) * 14,
        attn_grads,
        ffn_grads,
        r_parts,
        s_parts,
        output_rows,
        input_rows,
    )


def both_heads(rows, zero):
    lanes = lax.broadcasted_iota(jnp.int32, rows.shape, 1)
    return jnp.where(lanes < HEAD, rows, zero), jnp.where(lanes >= HEAD, rows, zero)


def run_rows(ref, run):
    return ref[pl.ds(pl.multiple_of(run * RUN, RUN), RUN), :]


def pair_rows(ref, run_a, run_b, dtype):
    zero = jnp.zeros((), dtype)
    a = both_heads(run_rows(ref, run_a).astype(dtype), zero)
    b = both_heads(run_rows(ref, run_b).astype(dtype), zero)
    return jnp.concatenate(a + b, axis=0)


def pair_bounds(rank_a, rank_b):
    lanes = lax.broadcasted_iota(jnp.int32, (1, 256), 1)
    rank = jnp.where(lanes < 128, rank_a, rank_b)
    last = rank * RUN + lax.rem(lanes, RUN)
    return (rank // 64) * 4096, last


def seen(chunk, low, last):
    keys = chunk * CHUNK + lax.broadcasted_iota(jnp.int32, (CHUNK, 256), 0)
    return (keys >= low) & (keys <= last)


def sort_keys(rank, kv_ref, keys, values):
    def move(r, carry):
        to = pl.ds(pl.multiple_of(rank[r] * RUN, RUN), RUN)
        rows = run_rows(kv_ref, r)
        keys[to, :] = rows[:, :128]
        values[to, :] = rows[:, 128:]
        return carry

    lax.fori_loop(0, 128, move, 0)


def flip(source, target):
    def one(i, carry):
        rows = source[pl.ds(pl.multiple_of(i * CHUNK, CHUNK), CHUNK), :]
        target[i] = rows.T
        return carry

    lax.fori_loop(0, 16, one, 0)


def chunk_rows(ref, i):
    return ref[pl.ds(pl.multiple_of(i * CHUNK, CHUNK), CHUNK), :]


def lane_heads(total):
    turned = total.T
    lanes = lax.broadcasted_iota(jnp.int32, (RUN, 128), 1)
    a = jnp.where(lanes < HEAD, turned[0:64], turned[64:128])
    b = jnp.where(lanes < HEAD, turned[128:192], turned[192:256])
    return a, b


def attend_kernel(rank, srun, srank, q_ref, kv_ref, o_ref, lse_ref, keys, values, flipped):
    sort_keys(rank, kv_ref, keys, values)
    flip(values, flipped)

    def pair(p, carry):
        run_a, run_b = srun[2 * p], srun[2 * p + 1]
        rank_a, rank_b = srank[2 * p], srank[2 * p + 1]
        queries = pair_rows(q_ref, run_a, run_b, BF)
        low, last = pair_bounds(rank_a, rank_b)

        def step(i, state):
            peak, total, mixed = state
            scores = lax.dot_general(
                chunk_rows(keys, i), queries, NT, preferred_element_type=F32
            )
            scores = jnp.where(seen(i, low, last), scores, -1e30)
            new_peak = jnp.maximum(peak, jnp.max(scores, axis=0, keepdims=True))
            weights = jnp.exp(scores - new_peak)
            shrink = jnp.exp(peak - new_peak)
            total = total * shrink + jnp.sum(weights, axis=0, keepdims=True)
            mixed = mixed * shrink + lax.dot_general(
                flipped[i], weights.astype(BF), NN, preferred_element_type=F32
            )
            return new_peak, total, mixed

        start = (
            jnp.full((1, 256), -1e20, F32),
            jnp.zeros((1, 256), F32),
            jnp.zeros((128, 256), F32),
        )
        peak, total, mixed = lax.fori_loop((rank_a // 64) * 8, rank_b // 8 + 1, step, start)
        a, b = lane_heads(mixed / total)
        o_ref[pl.ds(pl.multiple_of(run_a * RUN, RUN), RUN), :] = a
        o_ref[pl.ds(pl.multiple_of(run_b * RUN, RUN), RUN), :] = b
        lse_ref[p] = peak + jnp.log(total)
        return carry

    lax.fori_loop(0, 8, pair, 0)


def attend(order, queries, kv):
    return pl.pallas_call(
        attend_kernel,
        out_shape=(sds((1024, 128), F32), sds((8, 1, 256), F32)),
        grid_spec=pltpu.PrefetchScalarGridSpec(
            num_scalar_prefetch=3,
            grid=(1,),
            in_specs=[VMEM, VMEM],
            out_specs=(VMEM, VMEM),
            scratch_shapes=[
                pltpu.VMEM((8192, 128), BF),
                pltpu.VMEM((8192, 128), BF),
                pltpu.VMEM((16, 128, CHUNK), BF),
            ],
        ),
        name="attend",
        compiler_params=pltpu.CompilerParams(vmem_limit_bytes=48 << 20),
    )(*order, queries, kv)


def attend_back_kernel(
    rank, srun, srank, q_ref, kv_ref, g_ref, a_ref, lse_ref, dq_ref, dkv_ref, keys, values, flipped, dkeys, dvalues
):
    sort_keys(rank, kv_ref, keys, values)
    flip(keys, flipped)

    def clear(i, carry):
        rows = pl.ds(pl.multiple_of(i * CHUNK, CHUNK), CHUNK)
        dkeys[rows, :] = jnp.zeros((CHUNK, 128), F32)
        dvalues[rows, :] = jnp.zeros((CHUNK, 128), F32)
        return carry

    lax.fori_loop(0, 16, clear, 0)

    def pair(p, carry):
        run_a, run_b = srun[2 * p], srun[2 * p + 1]
        rank_a, rank_b = srank[2 * p], srank[2 * p + 1]
        queries = pair_rows(q_ref, run_a, run_b, BF)
        grads = pair_rows(g_ref, run_a, run_b, BF)
        low, last = pair_bounds(rank_a, rank_b)
        product = pair_rows(g_ref, run_a, run_b, F32) * pair_rows(a_ref, run_a, run_b, F32)
        delta = lax.dot_general(
            jnp.ones((8, 128), F32),
            product,
            NT,
            preferred_element_type=F32,
            precision=lax.Precision.HIGHEST,
        )[0:1]
        log_total = lse_ref[p]

        def step(i, dq):
            rows = pl.ds(pl.multiple_of(i * CHUNK, CHUNK), CHUNK)
            scores = lax.dot_general(keys[rows, :], queries, NT, preferred_element_type=F32)
            probs = jnp.where(seen(i, low, last), jnp.exp(scores - log_total), 0.0)
            dprobs = lax.dot_general(values[rows, :], grads, NT, preferred_element_type=F32)
            dscores = (probs * (dprobs - delta)).astype(BF)
            dvalues[rows, :] += lax.dot_general(
                probs.astype(BF), grads, NN, preferred_element_type=F32
            )
            dkeys[rows, :] += lax.dot_general(dscores, queries, NN, preferred_element_type=F32)
            return dq + lax.dot_general(flipped[i], dscores, NN, preferred_element_type=F32)

        dq = lax.fori_loop(
            (rank_a // 64) * 8, rank_b // 8 + 1, step, jnp.zeros((128, 256), F32)
        )
        a, b = lane_heads(dq)
        dq_ref[pl.ds(pl.multiple_of(run_a * RUN, RUN), RUN), :] = a * 0.125
        dq_ref[pl.ds(pl.multiple_of(run_b * RUN, RUN), RUN), :] = b * 0.125
        return carry

    lax.fori_loop(0, 8, pair, 0)

    def back(r, carry):
        source = pl.ds(pl.multiple_of(rank[r] * RUN, RUN), RUN)
        to = pl.ds(pl.multiple_of(r * RUN, RUN), RUN)
        dkv_ref[to, 0:128] = dkeys[source, :].astype(BF)
        dkv_ref[to, 128:256] = dvalues[source, :].astype(BF)
        return carry

    lax.fori_loop(0, 128, back, 0)


def attend_back(order, queries, kv, grads, attended, log_total):
    return pl.pallas_call(
        attend_back_kernel,
        out_shape=(sds((1024, 128), F32), sds((8192, 256), BF)),
        grid_spec=pltpu.PrefetchScalarGridSpec(
            num_scalar_prefetch=3,
            grid=(1,),
            in_specs=[VMEM] * 5,
            out_specs=(VMEM, VMEM),
            scratch_shapes=[
                pltpu.VMEM((8192, 128), BF),
                pltpu.VMEM((8192, 128), BF),
                pltpu.VMEM((16, 128, CHUNK), BF),
                pltpu.VMEM((8192, 128), F32),
                pltpu.VMEM((8192, 128), F32),
            ],
        ),
        name="attend_back",
        compiler_params=pltpu.CompilerParams(vmem_limit_bytes=56 << 20),
    )(*order, queries, kv, grads, attended, log_total)


def lane_tables(places, seq_length):
    half = HEAD // 2
    lanes = jnp.arange(128, dtype=jnp.int32)
    indices = (lanes % half).astype(F32)
    inverse_freq = jnp.exp(-jnp.log(10000.0) * indices / half)
    spots = places.astype(F32)
    angles = spots[:, None] * inverse_freq[None, :]
    ratios = (2.0 * indices + 0.4 * HEAD) / (1.4 * HEAD)
    powers = (spots - seq_length // 2) / 512.0
    growth = jnp.exp(powers[:, None] * jnp.log(ratios)[None, :])
    sign = jnp.where(lanes % HEAD < half, -1.0, 1.0)
    return jnp.cos(angles), jnp.sin(angles) * sign[None, :], growth


def swap_halves(values):
    half = HEAD // 2
    first = (jnp.arange(128) % HEAD < half)[None, :]
    return jnp.where(first, jnp.roll(values, -half, axis=1), jnp.roll(values, half, axis=1))


def normal(values):
    center = jnp.mean(values, axis=1, keepdims=True)
    centered = values - center
    variance = jnp.mean(centered * centered, axis=1, keepdims=True)
    inv = lax.rsqrt(variance + EPS)
    return centered * inv, inv


def normal_back(upstream, gain, normal_rows, inv):
    scaled = upstream * gain
    mean = jnp.mean(scaled, axis=1, keepdims=True)
    cross = jnp.mean(scaled * normal_rows, axis=1, keepdims=True)
    return inv * (scaled - mean - normal_rows * cross)


def shards(
    layer_input,
    w_qkv,
    w_out,
    w_up,
    w_down,
    b_qkv,
    b_out,
    b_up,
    b_down,
    norm_gains,
    norm_shifts,
    hidden_gain,
    hidden_shift,
    seq_ids,
    positions,
    d_out,
):
    z, c, f = g_place()
    x, h = t_place()
    zc = z * 2 + c
    me = zc * 2 + f
    head_at = f * 1024 + zc * 128
    hidden_at = f * 4096 + zc * 512

    def head_part(vector):
        return lax.dynamic_slice_in_dim(vector, head_at, 128, axis=vector.ndim - 1)

    def hidden_part(vector):
        return lax.dynamic_slice_in_dim(vector, hidden_at, 512, axis=vector.ndim - 1)

    def my_rows(rows):
        return lax.dynamic_slice_in_dim(rows, me * 64, 64, axis=0)

    packed = jnp.concatenate(
        [
            w_up.reshape(32, 8, 512),
            w_down.reshape(32, 8, 512),
            w_qkv.reshape(32, 3, 8, 128).transpose(0, 2, 1, 3).reshape(32, 8, 384),
            w_out.reshape(32, 8, 128),
        ],
        axis=2,
    ).transpose(1, 0, 2)
    rank_here = seq_ids.reshape(2, RUN)[:, 0] * 64 + positions.reshape(2, RUN)[:, 0] // RUN
    rank_tile = jnp.zeros((8, 128), jnp.int32).at[0, :2].set(rank_here)
    input_all, w_attn, ffn_block, ranks = start_all(layer_input, packed, rank_tile, 1)
    qkv_w = w_attn[:, :384]

    rank = ranks[:, :, 0, :2].reshape(128)
    group_rank = lax.dynamic_slice_in_dim(rank, (x * 2 + h) * 16, 16)
    slot = jnp.sum((group_rank[None, :] < group_rank[:, None]).astype(jnp.int32), axis=1)
    hit = slot[None, :] == jnp.arange(16, dtype=jnp.int32)[:, None]
    srank = jnp.sum(jnp.where(hit, group_rank[None, :], 0), axis=1)
    srun = jnp.sum(jnp.where(hit, jnp.arange(16, dtype=jnp.int32)[None, :], 0), axis=1)
    order = (rank, srun, srank)
    places = ((group_rank % 64) * RUN)[:, None] + jnp.arange(RUN, dtype=jnp.int32)[None, :]
    cosine, sine, growth = lane_tables(places.reshape(1024), 4096)

    normal_all, unused = normal(input_all.astype(F32))
    in_low = (normal_all * norm_gains[0] + norm_shifts[0]).astype(BF)
    qkv = jnp.dot(in_low, qkv_w, preferred_element_type=F32) + head_part(b_qkv).reshape(384)
    queries, keys, values = qkv[:, :128], qkv[:, 128:256], qkv[:, 256:]
    query_low = ((queries * cosine + swap_halves(queries) * sine) * growth).astype(BF)
    query_low = query_low * jnp.bfloat16(0.125)
    shrink = 1.0 / growth
    key_low = ((keys * cosine + swap_halves(keys) * sine) * shrink).astype(BF)
    kv, grad_all = gather_both(
        jnp.concatenate([key_low, values.astype(BF)], axis=1), d_out, 2
    )
    w_ffn = lax.all_gather(ffn_block, TOK, axis=0, tiled=True)
    attended, log_total = attend(order, query_low, kv)

    (
        mid,
        grad_mid,
        mid_low,
        hidden_low,
        pre_low,
        ffn_part,
        branch_all,
        grad_attended,
        attn_low,
        hid_vec,
        head_vec,
        row_vec,
    ) = middle(
        3,
        attended,
        w_attn,
        w_ffn,
        grad_all,
        input_all,
        b_out.reshape(1, 2048),
        b_up.reshape(1, 8192),
        norm_gains,
        norm_shifts,
        hidden_gain.reshape(1, 8192),
        hidden_shift.reshape(1, 8192),
    )
    input_rows = my_rows(input_all).astype(F32)
    up_term = lax.dot_general(mid_low, pre_low, TN, preferred_element_type=F32)
    down_term = lax.dot_general(grad_all, hidden_low, TN, preferred_element_type=F32)
    ffn_term = jnp.concatenate([up_term.astype(BF), down_term.astype(BF)], axis=1)
    ffn_grads = lax.psum_scatter(ffn_term, TOK, scatter_dimension=0, tiled=True)
    query_grad, kv_part = attend_back(order, query_low, kv, grad_attended, attended, log_total)
    kv_grad, ffn_rows = scatter_both(kv_part, ffn_part, 13, "scatter_kv_and_ffn")
    output_rows = mid + (ffn_rows + b_down)

    def unrotate(grads, factor):
        grads = grads * factor
        return grads * cosine - swap_halves(grads) * sine

    grad_qkv = jnp.concatenate(
        [unrotate(query_grad, growth), unrotate(kv_grad[:, :128], shrink), kv_grad[:, 128:]],
        axis=1,
    ).astype(BF)
    qkv_term = lax.dot_general(in_low, grad_qkv, TN, preferred_element_type=F32)
    out_term = lax.dot_general(branch_all, attn_low, TN, preferred_element_type=F32)
    attn_grads, grad_in_norm = scatter_both(
        jnp.concatenate([qkv_term.astype(BF), out_term.astype(BF)], axis=1),
        lax.dot_general(grad_qkv, qkv_w, NT, preferred_element_type=F32),
        14,
        "scatter_weights_and_in",
    )
    normal_in, scale_in = normal(input_rows)
    input_grad_rows = grad_mid + normal_back(grad_in_norm, norm_gains[0], normal_in, scale_in)

    zero_row = jnp.zeros((2, 2048), F32)
    r_parts = jnp.concatenate(
        [
            jnp.sum(grad_in_norm * normal_in, axis=0)[None],
            jnp.sum(grad_in_norm, axis=0)[None],
            row_vec[:4],
            zero_row,
        ]
    )
    r_parts = r_parts.reshape(8, 16, 128).transpose(1, 0, 2)
    s_parts = jnp.concatenate(
        [
            jnp.sum(grad_qkv.astype(F32), axis=0).reshape(3, 128),
            head_vec[:2],
            hid_vec[:3].reshape(12, 128),
            jnp.zeros((7, 128), F32),
        ]
    )
    (
        layer_output,
        input_grad,
        qkv_grad,
        out_grad,
        up_grad,
        down_grad,
        qkv_bias,
        gains_grad,
        shifts_grad,
        out_bias,
        down_bias,
        up_bias,
        hid_gain_grad,
        hid_shift_grad,
    ) = finish_all(
        attn_grads.reshape(8, 32, 512),
        ffn_grads.reshape(8, 32, 1024),
        r_parts,
        s_parts,
        output_rows,
        input_grad_rows,
        16,
    )
    return (
        layer_output,
        input_grad,
        qkv_grad.reshape(32, 3, 1024),
        out_grad,
        up_grad,
        down_grad,
        qkv_bias.reshape(3, 2048),
        out_bias.reshape(2048),
        up_bias.reshape(8192),
        down_bias.reshape(2048),
        gains_grad.reshape(3, 2048),
        shifts_grad.reshape(3, 2048),
        hid_gain_grad.reshape(8192),
        hid_shift_grad.reshape(8192),
    )


def solution(mesh):
    fine = Mesh(mesh.devices.reshape(4, 2, 4, 2, 2), SEQ + ("f",))
    both = P(SEQ, "f")
    return jax.shard_map(
        shards,
        mesh=fine,
        in_specs=(both, P(SEQ, None, "f"), both, both, both)
        + (P(),) * 8
        + (P(SEQ), P(SEQ), both),
        out_specs=(both, both, P(SEQ, None, "f"), both, both, both) + (P(),) * 8,
        check_vma=False,
    )
```

```python
import math

import jax
import jax.numpy as jnp
from jax import lax
from jax.experimental import pallas as pl
from jax.experimental.pallas import tpu as pltpu
from jax.sharding import Mesh
from jax.sharding import PartitionSpec as P

SEQ = ("x", "h", "z", "c")
TOK = ("x", "h")
HEAD = 64
RUN = 64
CHUNK = 512
EPS = 1e-05
MESH = pl.DeviceIdType.MESH
BF = jnp.bfloat16
F32 = jnp.float32
DMA = pltpu.SemaphoreType.DMA
ANY = pl.BlockSpec(memory_space=pl.ANY)
VMEM = pl.BlockSpec(memory_space=pltpu.VMEM)
NT = (((1,), (1,)), ((), ()))
TN = (((0,), (0,)), ((), ()))
NN = (((1,), (0,)), ((), ()))


def sds(shape, dtype):
    return jax.ShapeDtypeStruct(shape, dtype)


AXES = {"x": 4, "h": 2, "z": 4, "c": 2, "f": 2}
RING_G, PAIR_G = "z", "f"
RING_T, PAIR_T = "x", "h"


class Net:
    def __init__(self, send, recv):
        self.send, self.recv, self.copies, self.drained = send, recv, [], 0
        self.at = {axis: lax.axis_index(axis) for axis in AXES}

    def device(self, offset):
        return {a: lax.rem(self.at[a] + d + AXES[a], AXES[a]) for a, d in offset.items()}

    def place(self, offset, *axes):
        index = 0
        for a in axes:
            d = offset.get(a, 0)
            at = lax.rem(self.at[a] + d + AXES[a], AXES[a]) if d else self.at[a]
            index = index * AXES[a] + at
        return index

    def greet(self, *groups):
        offsets = {
            tuple((a, o[a]) for a in AXES if o.get(a, 0)) for group in groups for o in group
        }
        barrier = pltpu.get_barrier_semaphore()
        for offset in sorted(offsets):
            pl.semaphore_signal(
                barrier, inc=1, device_id=self.device(dict(offset)), device_id_type=MESH
            )
        pl.semaphore_wait(barrier, len(offsets))

    def push(self, src, dst, offset):
        k = len(self.copies)
        copy = pltpu.make_async_remote_copy(
            src_ref=src,
            dst_ref=dst,
            send_sem=self.send.at[k],
            recv_sem=self.recv.at[k],
            device_id=self.device(offset),
            device_id_type=MESH,
        )
        copy.start()
        self.copies.append(copy)
        return copy

    def finish(self):
        for copy in self.copies[self.drained :]:
            copy.wait_send()
        self.drained = len(self.copies)


SIBLING = {"c": 1}
NEAR_G = [{"z": 1}, {"z": 3}, {"f": 1}, SIBLING]
NEAR_T = [{"x": 1}, {"x": 3}, {"h": 1}]
ALL_T = [{"x": i, "h": j} for i in range(4) for j in range(2)][1:]
ALL_ZC = [{"z": i, "c": j} for i in range(4) for j in range(2)][1:]
ALL_G = [{"z": i, "c": j, "f": k} for i in range(4) for j in range(2) for k in range(2)][1:]


def run_flows(*flows):
    left = list(flows)
    while left:
        left = [flow for flow in left if next(flow, "end") != "end"]


def advance(flow, steps=1):
    for _ in range(steps):
        next(flow, None)


def run_with(main, *others):
    for _ in main:
        for other in others:
            next(other, None)


def half_rows(ref, which):
    rows = ref.shape[0] // 2
    return ref.at[pl.ds(which * rows, rows)]


def gather_flow(net, src, slot, ring, pair, local, sibling, light=False):
    up, down, across = {ring: 1}, {ring: 3}, {pair: 1}
    passed = []

    def to_sibling(ref):
        if sibling:
            passed.append(net.push(ref, ref, SIBLING))

    mine = slot({})
    from_down = net.push(src, mine, up)
    from_up = net.push(src, mine, down)
    from_across = net.push(src, mine, across)
    if sibling:
        passed.append(net.push(src, mine, SIBLING))
    here = pltpu.make_async_copy(src, mine, local)
    here.start()
    yield
    from_down.wait_recv()
    below = slot({ring: 3})
    first = net.push(half_rows(below, 0), half_rows(below, 0), up)
    to_sibling(below)
    yield
    from_up.wait_recv()
    above = slot({ring: 1})
    second = net.push(half_rows(above, 1), half_rows(above, 1), down)
    to_sibling(above)
    yield
    from_across.wait_recv()
    beside = slot({pair: 1})
    beside_down = net.push(beside, beside, up)
    beside_up = net.push(beside, beside, down)
    to_sibling(beside)
    yield
    first.wait_recv()
    second.wait_recv()
    far = slot({ring: 2})
    if not light:
        beside_far = [net.push(far, far, across)]
    to_sibling(far)
    yield
    beside_down.wait_recv()
    below = slot({ring: 3, pair: 1})
    if light:
        beside_far = [net.push(half_rows(below, 0), half_rows(below, 0), up)]
    to_sibling(below)
    yield
    beside_up.wait_recv()
    above = slot({ring: 1, pair: 1})
    if light:
        beside_far.append(net.push(half_rows(above, 1), half_rows(above, 1), down))
    to_sibling(above)
    yield
    for copy in beside_far:
        copy.wait_recv()
    to_sibling(slot({ring: 2, pair: 1}))
    yield
    here.wait()
    for copy in passed:
        copy.wait_recv()


def add_into(target, *sources):
    rows = min(32768 // target.shape[1], target.shape[0])

    def step(i, carry):
        at = pl.ds(pl.multiple_of(i * rows, rows), rows)
        total = target[at, :].astype(F32)
        for source in sources:
            total = total + source[at, :].astype(F32)
        target[at, :] = total.astype(target.dtype)
        return carry

    lax.fori_loop(0, target.shape[0] // rows, step, 0)


ROOTS = ((2, 1), (1, 1), (3, 1), (2, 0), (1, 0), (3, 0), (0, 1), (0, 0))


def scatter_flow(
    net, chunk, out, mine, other, landed, local, ring, pair, sibling, light=False
):
    up, down, across = {ring: 1}, {ring: 3}, {pair: 1}
    loads, shared = [], []
    for k, (i, j) in enumerate(ROOTS):
        if sibling:
            shared.append(net.push(chunk({ring: i, pair: j, "c": 1}), other.at[k], SIBLING))
        if chunk is not None:
            load = pltpu.make_async_copy(chunk({ring: i, pair: j}), mine.at[k], local.at[k])
            load.start()
            loads.append(load)

    def ready(k):
        if chunk is not None:
            loads[k].wait()
        if sibling:
            shared[k].wait_recv()
            add_into(mine.at[k], other.at[k])

    def halves(k, to):
        return (
            net.push(half_rows(mine.at[k], 0), half_rows(landed.at[to], 0), down),
            net.push(half_rows(mine.at[k], 1), half_rows(landed.at[to], 1), up),
        )

    if chunk is not None:
        yield
    ready(0)
    if light:
        beside_first, beside_second = halves(0, 0)
        ready(3)
        first, second = halves(3, 3)
        ready(2)
        ready(1)
        yield
        beside_first.wait_recv()
        add_into(half_rows(mine.at[2], 0), half_rows(landed.at[0], 0))
        beside_up = net.push(mine.at[2], landed.at[2], down)
        beside_second.wait_recv()
        add_into(half_rows(mine.at[1], 1), half_rows(landed.at[0], 1))
        beside_down = net.push(mine.at[1], landed.at[1], up)
    else:
        beside_far = net.push(mine.at[0], landed.at[0], across)
        ready(1)
        beside_down = net.push(mine.at[1], landed.at[1], up)
        ready(2)
        beside_up = net.push(mine.at[2], landed.at[2], down)
        ready(3)
        yield
        beside_far.wait_recv()
        add_into(mine.at[3], landed.at[0])
        first, second = halves(3, 3)
    ready(6)
    yield
    beside_down.wait_recv()
    beside_up.wait_recv()
    add_into(mine.at[6], landed.at[1], landed.at[2])
    from_across = net.push(mine.at[6], landed.at[4], across)
    ready(5)
    yield
    first.wait_recv()
    add_into(half_rows(mine.at[5], 0), half_rows(landed.at[3], 0))
    from_up = net.push(mine.at[5], landed.at[5], down)
    ready(4)
    yield
    second.wait_recv()
    add_into(half_rows(mine.at[4], 1), half_rows(landed.at[3], 1))
    from_down = net.push(mine.at[4], landed.at[6], up)
    ready(7)
    yield
    from_across.wait_recv()
    yield
    from_up.wait_recv()
    from_down.wait_recv()

    rows = 32768 // out.shape[1]

    def total(i, carry):
        at = pl.ds(pl.multiple_of(i * rows, rows), rows)
        value = mine[7, at, :].astype(F32) + landed[4, at, :].astype(F32)
        out[at, :] = value + (landed[5, at, :].astype(F32) + landed[6, at, :].astype(F32))
        return carry

    lax.fori_loop(0, out.shape[0] // rows, total, 0)


def gather_slot(net, out, rows, ring, pair):
    order = ("z", "c", "f") if ring == "z" else ("x", "h")

    def slot(offset):
        at = net.place(offset, *order)
        return out.at[pl.ds(pl.multiple_of(at * rows, rows), rows)]

    return slot


def input_slot(net, out):
    def slot(offset):
        row = pl.multiple_of(net.place(offset, "z", "c") * 128, 128)
        column = pl.multiple_of(net.place(offset, "f") * 1024, 1024)
        return out.at[pl.ds(row, 128), pl.ds(column, 1024)]

    return slot


def scatter_chunk(net, ref, ring):
    order = ("z", "c", "f") if ring == "z" else ("x", "h")
    return lambda offset: ref.at[net.place(offset, *order)]


def comm_call(kernel, name, number, pushes, locals_, out_shape, scratch, in_specs, out_specs, *args):
    return pl.pallas_call(
        kernel,
        out_shape=out_shape,
        in_specs=in_specs,
        out_specs=out_specs,
        scratch_shapes=[DMA((pushes,)), DMA((pushes,)), DMA((locals_,))] + scratch,
        name=name,
        compiler_params=pltpu.CompilerParams(
            collective_id=number, has_side_effects=True, vmem_limit_bytes=60 << 20
        ),
    )(*args)


def scatter_scratch(rows, width, sibling):
    shapes = [pltpu.VMEM((8, rows, width), BF), pltpu.VMEM((7, rows, width), BF)]
    return shapes + ([pltpu.VMEM((8, rows, width), BF)] if sibling else [])


def g_place():
    return lax.axis_index("z"), lax.axis_index("c"), lax.axis_index("f")


def t_place():
    return lax.axis_index("x"), lax.axis_index("h")


def start_all(layer_input, packed, ranks, number):
    def kernel(x_ref, w_ref, r_ref, xo, ao, fo, ro, send, recv, local, blocks, near):
        net = Net(send, recv)
        net.greet(NEAR_G, ALL_ZC, ALL_T)
        me = net.place({}, "z", "c")
        group = net.place({}, "x", "h")

        def weights():
            near_sent, attn_sent, ffn_sent = [], [], []
            for offset in ALL_ZC:
                to = net.place(offset, "z", "c")
                attn_sent.append(
                    net.push(
                        w_ref.at[to, :, pl.ds(1024, 512)], blocks.at[pl.ds(pl.multiple_of(me * 32, 32), 32)], offset
                    )
                )
            for offset in ALL_ZC:
                near_sent.append(net.push(r_ref, near.at[me], offset))
            rows = pl.ds(pl.multiple_of(me * 32, 32), 32)
            own = pltpu.make_async_copy(w_ref.at[me, :, pl.ds(1024, 512)], blocks.at[rows], local.at[1])
            own.start()
            own_ffn = pltpu.make_async_copy(w_ref.at[me, :, pl.ds(0, 1024)], fo.at[rows], local.at[2])
            own_ffn.start()
            near[me] = r_ref[...]
            own.wait()
            yield
            for copy in attn_sent:
                copy.wait_recv()
            slot = gather_slot(net, ao, 256, "x", "h")
            gathering = gather_flow(net, blocks, slot, "x", "h", local.at[3], False)
            yield next(gathering)
            for copy in near_sent:
                copy.wait_recv()
            rank_sent = [net.push(near, ro.at[group], offset) for offset in ALL_T]
            ro[group] = near[...]
            for offset in ALL_ZC:
                to = net.place(offset, "z", "c")
                ffn_sent.append(net.push(w_ref.at[to, :, pl.ds(0, 1024)], fo.at[rows], offset))
            yield from gathering
            for copy in rank_sent + ffn_sent:
                copy.wait_recv()
            own_ffn.wait()

        rows_flow = gather_flow(net, x_ref, input_slot(net, xo), "z", "f", local.at[0], True, True)
        run_flows(weights(), rows_flow)
        net.finish()

    return comm_call(
        kernel,
        "start_all",
        number,
        17 + 8 + 28,
        4,
        (sds((1024, 2048), BF), sds((2048, 512), BF), sds((256, 1024), BF), sds((8, 8, 8, 128), jnp.int32)),
        [pltpu.VMEM((256, 512), BF), pltpu.VMEM((8, 8, 128), jnp.int32)],
        [ANY, ANY, VMEM],
        (ANY, ANY, ANY, VMEM),
        layer_input,
        packed,
        ranks,
    )


def gather_both(kv_here, grad_here, number):
    def kernel(k_ref, g_ref, ko, go, send, recv, local):
        net = Net(send, recv)
        net.greet(NEAR_G, NEAR_T)
        run_flows(
            gather_flow(net, k_ref, gather_slot(net, ko, 1024, "x", "h"), "x", "h", local.at[0], False),
            gather_flow(net, g_ref, input_slot(net, go), "z", "f", local.at[1], True, True),
        )
        net.finish()

    return comm_call(
        kernel,
        "gather_kv_and_grad",
        number,
        25,
        2,
        (sds((8192, 256), BF), sds((1024, 2048), BF)),
        [],
        [ANY, ANY],
        (ANY, ANY),
        kv_here,
        grad_here,
    )


def row_sums(values):
    ones = jnp.ones((8, values.shape[1]), F32)
    return lax.dot_general(
        ones, values, NT, preferred_element_type=F32, precision=lax.Precision.HIGHEST
    )[0:1]


def tile(i, rows=128):
    return pl.ds(pl.multiple_of(i * rows, rows), rows)


def columns_of(rows_ref, i):
    return rows_ref[i].T


def put_rows(rows_ref, *values):
    for k, value in enumerate(values):
        for i in range(8):
            rows_ref[i, k : k + 1, :] = value[i : i + 1]


def fold_lanes(values):
    return (values[:, 0:128] + values[:, 128:256]) + (values[:, 256:384] + values[:, 384:512])


def middle_kernel(
    att,
    w_attn,
    ffn_block,
    grad_all_in,
    input_all,
    b_out,
    b_up,
    gains,
    shifts,
    hid_gain,
    hid_shift,
    mid,
    grad_mid,
    ffn_part,
    grad_att,
    ffn_grad,
    out_term,
    hid_vec,
    head_vec,
    row_vec,
    send,
    recv,
    local,
    grad_all,
    out_w,
    w_ffn,
    mid_low,
    branch_all,
    hidden_low,
    pre_low,
    hidden_turned,
    pre_turned,
    attn_low,
    input_rows,
    low_rows,
    partial_rows,
    mine,
    landed,
    other,
    t_mine,
    t_landed,
    grad_hidden,
    activated,
    slope,
    normal_attn,
    normal_mid,
    scale_mid,
    sent_a,
    stats_a,
    rows_a,
    sent_b,
    stats_b,
    rows_b,
    sent_c,
    stats_c,
    rows_c,
):
    net = Net(send, recv)
    me = net.place({}, "z", "c", "f")
    my_rows = pl.ds(pl.multiple_of(me * 64, 64), 64)
    load_w = pltpu.make_async_copy(w_attn.at[:, pl.ds(384, 128)], out_w, local.at[10])
    load_w.start()
    load_rows = pltpu.make_async_copy(input_all.at[my_rows], input_rows, local.at[8])
    load_rows.start()
    load_grad = pltpu.make_async_copy(grad_all_in, grad_all, local.at[11])
    load_grad.start()
    net.greet(ALL_G, NEAR_T)
    weights = gather_flow(
        net, ffn_block, gather_slot(net, w_ffn, 256, "x", "h"), "x", "h", local.at[9], False, True
    )
    advance(weights)
    head_at = pl.ds(
        pl.multiple_of(net.at["f"] * 1024 + net.place({}, "z", "c") * 128, 128), 128
    )
    hidden_at = pl.ds(
        pl.multiple_of(net.at["f"] * 4096 + net.place({}, "z", "c") * 512, 512), 512
    )
    head_gain, head_shift = gains[1:2, head_at], shifts[1:2, head_at]
    gain_here, shift_here, bias_here = hid_gain[:, hidden_at], hid_shift[:, hidden_at], b_up[:, hidden_at]

    def exchange(sent, stats):
        copies = [net.push(sent, stats.at[me], offset) for offset in ALL_G]
        stats[me] = sent[...]
        for copy in copies:
            copy.wait_recv()

    def chunk(offset):
        at = net.place(offset, "z", "c", "f")
        return partial_rows.at[pl.ds(pl.multiple_of(at * 64, 64), 64)]

    def measure(i, carry):
        here = att[tile(i), :]
        centered = here - jnp.mean(here, axis=1, keepdims=True)
        sent_a[pl.ds(i, 1), :] = row_sums(here)
        sent_a[pl.ds(8 + i, 1), :] = row_sums(centered * centered)
        return carry

    lax.fori_loop(0, 8, measure, 0)
    exchange(sent_a, stats_a)
    center = jnp.sum(stats_a[:, 0:8], axis=0) / 2048
    spread = jnp.sum(
        stats_a[:, 8:16] + 128 * jnp.square(stats_a[:, 0:8] / 128 - center[None]), axis=0
    )
    put_rows(rows_a, center, lax.rsqrt(spread / 2048 + EPS))

    def norm_heads(i, carry):
        columns = columns_of(rows_a, i)
        normal_rows = (att[tile(i), :] - columns[:, 0:1]) * columns[:, 1:2]
        normal_attn[tile(i), :] = normal_rows
        attn_low[tile(i), :] = (normal_rows * head_gain + head_shift).astype(BF)
        return carry

    lax.fori_loop(0, 8, norm_heads, 0)
    load_w.wait()

    def project(i, carry):
        partial_rows[:, tile(i, 256)] = lax.dot_general(
            attn_low[...], out_w[tile(i, 256), :], NT, preferred_element_type=F32
        ).astype(BF)
        return carry

    lax.fori_loop(0, 8, project, 0)
    advance(weights, 3)
    run_with(scatter_flow(net, chunk, mid, mine, other, landed, local, "z", "f", True))
    advance(weights, 3)
    net.finish()

    load_rows.wait()

    def mid_norm(i, carry):
        at = tile(i, 16)
        rows = input_rows[at, :].astype(F32) + (mid[at, :] + b_out[...])
        mid[at, :] = rows
        centered = rows - jnp.mean(rows, axis=1, keepdims=True)
        scale = lax.rsqrt(jnp.mean(centered * centered, axis=1, keepdims=True) + EPS)
        rows = centered * scale
        normal_mid[at, :] = rows
        scale_mid[at, :] = jnp.broadcast_to(scale, (16, 128))
        low_rows[at, :] = (rows * gains[2:3, :] + shifts[2:3, :]).astype(BF)
        return carry

    lax.fori_loop(0, 4, mid_norm, 0)
    gathering = gather_flow(
        net, low_rows, gather_slot(net, mid_low, 64, "z", "f"), "z", "f", local.at[0], True
    )
    advance(gathering, 6)
    advance(weights, 2)
    load_grad.wait()
    for i in range(4):
        grad_hidden[tile(i, 256), :] = jnp.dot(
            grad_all[tile(i, 256), :], w_ffn[:, 512:1024], preferred_element_type=F32
        )
        advance(gathering)
    net.finish()

    def up(i, carry):
        at = tile(i)
        pre = jnp.dot(mid_low[at, :], w_ffn[:, 0:512], preferred_element_type=F32) + bias_here
        below = 0.5 + 0.5 * lax.erf(pre * math.sqrt(0.5))
        act = pre * below
        activated[at, :] = act
        slope[at, :] = below + pre * jnp.exp(-0.5 * pre * pre) * (1.0 / math.sqrt(2.0 * math.pi))
        centered = act - jnp.mean(act, axis=1, keepdims=True)
        scaled = grad_hidden[at, :] * gain_here
        sent_b[pl.ds(i, 1), :] = row_sums(fold_lanes(act))
        sent_b[pl.ds(8 + i, 1), :] = row_sums(fold_lanes(centered * centered))
        sent_b[pl.ds(16 + i, 1), :] = row_sums(fold_lanes(scaled))
        sent_b[pl.ds(24 + i, 1), :] = row_sums(fold_lanes(scaled * centered))
        return carry

    lax.fori_loop(0, 8, up, 0)
    exchange(sent_b, stats_b)
    center = jnp.sum(stats_b[:, 0:8], axis=0) / 8192
    apart = stats_b[:, 0:8] / 512 - center[None]
    spread = jnp.sum(stats_b[:, 8:16] + 512 * jnp.square(apart), axis=0)
    scale = lax.rsqrt(spread / 8192 + EPS)
    mean_back = jnp.sum(stats_b[:, 16:24], axis=0) / 8192
    cross_back = scale * jnp.sum(stats_b[:, 24:32] + apart * stats_b[:, 16:24], axis=0) / 8192
    put_rows(rows_b, center, scale, mean_back, cross_back)

    def hidden(i, carry):
        at = tile(i)
        columns = columns_of(rows_b, i)
        scale = columns[:, 1:2]
        normal_rows = (activated[at, :] - columns[:, 0:1]) * scale
        hidden_low[at, :] = (normal_rows * gain_here + shift_here).astype(BF)
        upstream = grad_hidden[at, :]
        back = scale * (upstream * gain_here - columns[:, 2:3] - normal_rows * columns[:, 3:4])
        low = (back * slope[at, :]).astype(BF)
        pre_low[at, :] = low
        return (
            carry[0] + jnp.sum(low.astype(F32), axis=0, keepdims=True),
            carry[1] + jnp.sum(upstream * normal_rows, axis=0, keepdims=True),
            carry[2] + jnp.sum(upstream, axis=0, keepdims=True),
        )

    sums = lax.fori_loop(0, 8, hidden, (jnp.zeros((1, 512), F32),) * 3)
    for k in range(3):
        hid_vec[k : k + 1, :] = sums[k]

    def project_back(i, carry):
        partial_rows[:, tile(i, 256)] = lax.dot_general(
            pre_low[...], w_ffn[tile(i, 256), 0:512], NT, preferred_element_type=F32
        ).astype(BF)
        return carry

    lax.fori_loop(0, 8, project_back, 0)

    def weight_terms():
        def turn(i, carry):
            pre_turned[:, tile(i)] = pre_low[tile(i), :].T
            hidden_turned[:, tile(i)] = hidden_low[tile(i), :].T
            return carry

        lax.fori_loop(0, 8, turn, 0)
        yield
        for k, (i, j) in enumerate(ROOTS):
            columns = tile(net.place({"x": i, "h": j}, "x", "h"), 256)
            t_mine[k, 0:512, :] = jnp.dot(
                pre_turned[...], mid_low[:, columns], preferred_element_type=F32
            ).astype(BF)
            t_mine[k, 512:1024, :] = jnp.dot(
                hidden_turned[...], grad_all[:, columns], preferred_element_type=F32
            ).astype(BF)
            yield

    terms = weight_terms()
    run_with(scatter_flow(net, chunk, grad_mid, mine, other, landed, local, "z", "f", True), terms)
    advance(terms, 9)
    net.finish()
    weights = scatter_flow(
        net, None, ffn_grad, t_mine, None, t_landed, local, "x", "h", False, True
    )
    advance(weights)

    def mid_back(i, carry):
        at = tile(i, 16)
        upstream = grad_mid[at, :]
        normal_rows = normal_mid[at, :]
        scaled = upstream * gains[2:3, :]
        mean = jnp.mean(scaled, axis=1, keepdims=True)
        cross = jnp.mean(scaled * normal_rows, axis=1, keepdims=True)
        out_rows = grad_all[pl.ds(pl.multiple_of(me * 64 + i * 16, 16), 16), :].astype(F32)
        rows = out_rows + scale_mid[at, 0:1] * (scaled - mean - normal_rows * cross)
        grad_mid[at, :] = rows
        low = rows.astype(BF)
        low_rows[at, :] = low
        row_vec[0:1, :] += jnp.sum(upstream * normal_rows, axis=0, keepdims=True)
        row_vec[1:2, :] += jnp.sum(upstream, axis=0, keepdims=True)
        row_vec[2:3, :] += jnp.sum(low.astype(F32), axis=0, keepdims=True)
        row_vec[3:4, :] += jnp.sum(out_rows, axis=0, keepdims=True)
        return carry

    row_vec[...] = jnp.zeros_like(row_vec)
    lax.fori_loop(0, 4, mid_back, 0)
    gathering = gather_flow(
        net, low_rows, gather_slot(net, branch_all, 64, "z", "f"), "z", "f", local.at[0], True
    )
    advance(gathering)
    for i in range(8):
        partial_rows[:, tile(i, 256)] = lax.dot_general(
            hidden_low[...], w_ffn[tile(i, 256), 512:1024], NT, preferred_element_type=F32
        ).astype(BF)
        advance(gathering)
        if i == 3:
            advance(weights)
    advance(gathering)
    advance(weights, 3)
    store = pltpu.make_async_copy(partial_rows, ffn_part, local.at[8])
    store.start()

    def attn_back(i, carry):
        at = tile(i)
        upstream = jnp.dot(branch_all[at, :], out_w[...], preferred_element_type=F32)
        normal_rows = normal_attn[at, :]
        scaled = upstream * head_gain
        activated[at, 0:128] = scaled
        sent_c[pl.ds(i, 1), :] = row_sums(scaled)
        sent_c[pl.ds(8 + i, 1), :] = row_sums(scaled * normal_rows)
        return (
            carry[0] + jnp.sum(upstream * normal_rows, axis=0, keepdims=True),
            carry[1] + jnp.sum(upstream, axis=0, keepdims=True),
        )

    sums = lax.fori_loop(0, 8, attn_back, (jnp.zeros((1, 128), F32),) * 2)
    for k in range(2):
        head_vec[k : k + 1, :] = sums[k]
    exchange(sent_c, stats_c)
    totals = jnp.sum(stats_c[...], axis=0) / 2048
    put_rows(rows_c, totals[0:8], totals[8:16])

    def heads_back(i, carry):
        at = tile(i)
        columns = columns_of(rows_c, i)
        scale = columns_of(rows_a, i)[:, 1:2]
        grad_att[at, :] = (
            scale
            * (activated[at, 0:128] - columns[:, 0:1] - normal_attn[at, :] * columns[:, 1:2])
        ).astype(BF)
        pre_turned[0:128, at] = attn_low[at, :].T
        return carry

    lax.fori_loop(0, 8, heads_back, 0)

    def out_terms(i, carry):
        out_term[:, tile(i, 256)] = jnp.dot(
            pre_turned[0:128, :], branch_all[:, tile(i, 256)], preferred_element_type=F32
        ).astype(BF)
        return carry

    lax.fori_loop(0, 8, out_terms, 0)
    run_with(weights)
    store.wait()
    net.finish()


def middle(number, *args):
    wide = pltpu.VMEM((1024, 512), F32)
    low = pltpu.VMEM((1024, 512), BF)
    tall = pltpu.VMEM((512, 1024), BF)
    whole = pltpu.VMEM((1024, 2048), BF)
    return comm_call(
        middle_kernel,
        "middle",
        number,
        15 * 3 + 16 * 4 + 9 * 2,
        12,
        (
            sds((64, 2048), F32),
            sds((64, 2048), F32),
            sds((1024, 2048), BF),
            sds((1024, 128), BF),
            sds((1024, 256), F32),
            sds((128, 2048), BF),
            sds((8, 512), F32),
            sds((8, 128), F32),
            sds((8, 2048), F32),
        ),
        [
            whole,
            pltpu.VMEM((2048, 128), BF),
            pltpu.VMEM((2048, 1024), BF),
            whole,
            whole,
            low,
            low,
            tall,
            tall,
            pltpu.VMEM((1024, 128), BF),
            pltpu.VMEM((64, 2048), BF),
            pltpu.VMEM((64, 2048), BF),
            whole,
            pltpu.VMEM((8, 64, 2048), BF),
            pltpu.VMEM((7, 64, 2048), BF),
            pltpu.VMEM((8, 64, 2048), BF),
            pltpu.VMEM((8, 1024, 256), BF),
            pltpu.VMEM((7, 1024, 256), BF),
            wide,
            wide,
            wide,
            pltpu.VMEM((1024, 128), F32),
            pltpu.VMEM((64, 2048), F32),
            pltpu.VMEM((64, 128), F32),
            pltpu.VMEM((16, 128), F32),
            pltpu.VMEM((16, 16, 128), F32),
            pltpu.VMEM((8, 8, 128), F32),
            pltpu.VMEM((32, 128), F32),
            pltpu.VMEM((16, 32, 128), F32),
            pltpu.VMEM((8, 8, 128), F32),
            pltpu.VMEM((16, 128), F32),
            pltpu.VMEM((16, 16, 128), F32),
            pltpu.VMEM((8, 8, 128), F32),
        ],
        [VMEM] + [ANY] * 4 + [VMEM] * 6,
        (VMEM, VMEM, ANY) + (VMEM,) * 6,
        *args,
    )


def turn_halves(values):
    lanes = lax.broadcasted_iota(jnp.int32, values.shape, 1)
    first = lax.rem(lanes, HEAD) < HEAD // 2
    return jnp.where(first, pltpu.roll(values, 96, axis=1), pltpu.roll(values, 32, axis=1))


def tail_kernel(
    kv_part,
    ffn_part,
    ffn_grad,
    query_grad,
    cosine,
    sine,
    growth,
    w_attn,
    in_low,
    out_term,
    mid,
    grad_mid,
    input_all,
    b_down,
    gains,
    hid_vec,
    head_vec,
    row_vec,
    out_half,
    in_half,
    attn_got,
    ffn_got,
    vectors,
    send,
    recv,
    local,
    kv_mine,
    kv_landed,
    kv_grad,
    f_mine,
    f_landed,
    f_other,
    i_mine,
    i_landed,
    i_other,
    w_mine,
    w_landed,
    w_grad,
    w_rows,
    attn_rows,
    ffn_rows,
    out_rows,
    in_rows,
    grad_qkv,
    turned,
    partial_rows,
    input_rows,
    row_parts,
    row_got,
    packed,
    packed_got,
):
    net = Net(send, recv)
    me = net.place({}, "z", "c", "f")
    here = net.place({}, "z", "c")
    f = net.at["f"]
    load = pltpu.make_async_copy(
        input_all.at[pl.ds(pl.multiple_of(me * 64, 64), 64)], input_rows, local.at[16]
    )
    load.start()
    net.greet(ALL_G, ALL_T)

    def to_halves(source, target, k):
        rows = target.at[pl.ds(pl.multiple_of(f * 64, 64), 64)]
        theirs = source.at[:, pl.ds(pl.multiple_of((1 - f) * 1024, 1024), 1024)]
        own = source.at[:, pl.ds(pl.multiple_of(f * 1024, 1024), 1024)]
        copy = net.push(theirs, rows, {"f": 1})
        keep = pltpu.make_async_copy(own, rows, local.at[k])
        keep.start()
        return copy, keep

    def to_rows(source, got, k):
        copies = []
        for offset in ALL_ZC:
            at = net.place(offset, "z", "c")
            copies.append(
                net.push(source.at[pl.ds(pl.multiple_of(at * 32, 32), 32)], got.at[here], offset)
            )
        keep = pltpu.make_async_copy(
            source.at[pl.ds(pl.multiple_of(here * 32, 32), 32)], got.at[here], local.at[k]
        )
        keep.start()
        return copies, keep

    def ffn_weights():
        def turn(i, carry):
            for j in range(2):
                block = ffn_grad[tile(i), j * 128 : j * 128 + 128].T
                w_rows[j * 128 : j * 128 + 128, tile(i)] = block.astype(BF)
            return carry

        lax.fori_loop(0, 8, turn, 0)
        yield to_rows(w_rows, ffn_got, 17)

    kv_flow = scatter_flow(
        net,
        scatter_chunk(net, kv_part, "x"),
        kv_grad,
        kv_mine,
        None,
        kv_landed,
        local.at[pl.ds(0, 8)],
        "x",
        "h",
        False,
    )
    ffn_flow = scatter_flow(
        net,
        scatter_chunk(net, ffn_part, "z"),
        ffn_rows,
        f_mine,
        f_other,
        f_landed,
        local.at[pl.ds(8, 8)],
        "z",
        "f",
        True,
        True,
    )
    advance(kv_flow, 2)
    advance(ffn_flow, 2)
    ffn_copies, ffn_keep = next(ffn_weights())
    run_flows(kv_flow, ffn_flow)

    def finish_rows(i, carry):
        at = tile(i, 16)
        out_rows[at, :] = mid[at, :] + (ffn_rows[at, :] + b_down[...])
        return carry

    lax.fori_loop(0, 4, finish_rows, 0)
    out_copy, out_keep = to_halves(out_rows, out_half, 18)

    def unrotate(i, carry):
        at = tile(i)
        cos, sin, grow = cosine[at, :], sine[at, :], growth[at, :]
        queries = query_grad[at, :] * grow
        queries = (queries * cos - turn_halves(queries) * sin).astype(BF)
        keys = kv_grad[at, 0:128] / grow
        keys = (keys * cos - turn_halves(keys) * sin).astype(BF)
        values = kv_grad[at, 128:256].astype(BF)
        grad_qkv[at, 0:128] = queries
        grad_qkv[at, 128:256] = keys
        grad_qkv[at, 256:384] = values
        return tuple(
            total + jnp.sum(part.astype(F32), axis=0, keepdims=True)
            for total, part in zip(carry, (queries, keys, values))
        )

    bias = lax.fori_loop(0, 8, unrotate, (jnp.zeros((1, 128), F32),) * 3)
    for k in range(3):
        packed[8 + k : 9 + k, :] = bias[k]

    def project(i, carry):
        partial_rows[:, tile(i, 256)] = lax.dot_general(
            grad_qkv[...], w_attn[tile(i, 256), 0:384], NT, preferred_element_type=F32
        ).astype(BF)
        return carry

    lax.fori_loop(0, 8, project, 0)

    def chunk(offset):
        at = net.place(offset, "z", "c", "f")
        return partial_rows.at[pl.ds(pl.multiple_of(at * 64, 64), 64)]

    in_flow = scatter_flow(
        net, chunk, in_rows, i_mine, i_other, i_landed, local, "z", "f", True, True
    )
    advance(in_flow)

    def turn_grads(i, carry):
        turned[:, tile(i)] = grad_qkv[tile(i), :].T
        return carry

    lax.fori_loop(0, 8, turn_grads, 0)
    advance(in_flow)
    for k, (i, j) in enumerate(ROOTS):
        columns = tile(net.place({"x": i, "h": j}, "x", "h"), 256)
        w_mine[k, 0:384, :] = jnp.dot(
            turned[...], in_low[:, columns], preferred_element_type=F32
        ).astype(BF)
        w_mine[k, 384:512, :] = out_term[:, columns]
        if k in (3, 7):
            advance(in_flow)
    w_flow = scatter_flow(net, None, w_grad, w_mine, None, w_landed, None, "x", "h", False)
    advance(w_flow)
    run_flows(in_flow, w_flow)

    load.wait()

    def in_back(i, carry):
        at = tile(i, 16)
        rows = input_rows[at, :].astype(F32)
        centered = rows - jnp.mean(rows, axis=1, keepdims=True)
        scale = lax.rsqrt(jnp.mean(centered * centered, axis=1, keepdims=True) + EPS)
        normal_rows = centered * scale
        upstream = in_rows[at, :]
        scaled = upstream * gains[0:1, :]
        mean = jnp.mean(scaled, axis=1, keepdims=True)
        cross = jnp.mean(scaled * normal_rows, axis=1, keepdims=True)
        in_rows[at, :] = grad_mid[at, :] + scale * (scaled - mean - normal_rows * cross)
        return (
            carry[0] + jnp.sum(upstream * normal_rows, axis=0, keepdims=True),
            carry[1] + jnp.sum(upstream, axis=0, keepdims=True),
        )

    sums = lax.fori_loop(0, 4, in_back, (jnp.zeros((1, 2048), F32),) * 2)
    in_copy, in_keep = to_halves(in_rows, in_half, 19)

    def turn_weights(i, carry):
        for j in range(2):
            w_grad_rows = w_grad[tile(i), j * 128 : j * 128 + 128].T
            attn_rows[j * 128 : j * 128 + 128, tile(i)] = w_grad_rows
        return carry

    for g in range(16):
        at = slice(g * 128, g * 128 + 128)
        for k in range(2):
            row_parts[g, k : k + 1, :] = sums[k][:, at]
        row_parts[g, 2:6, :] = row_vec[0:4, at]
        row_parts[g, 6:8, :] = jnp.zeros((2, 128), F32)
    copies = []
    for k, offset in enumerate(ALL_G):
        to = net.place(offset, "z", "c", "f")
        copies.append(net.push(row_parts.at[to], row_got.at[k], offset))
    lax.fori_loop(0, 4, turn_weights, 0)
    attn_copies, attn_keep = to_rows(attn_rows, attn_got, 20)
    packed[11:13, :] = head_vec[0:2, :]
    for k in range(3):
        for j in range(4):
            at = 13 + 4 * k + j
            packed[at : at + 1, :] = hid_vec[k : k + 1, j * 128 : j * 128 + 128]
    packed[25:32, :] = jnp.zeros((7, 128), F32)
    for copy in copies:
        copy.wait_recv()
    total = row_parts[me]
    for k in range(15):
        total = total + row_got[k]
    packed[0:8, :] = total
    copies = [net.push(packed, packed_got.at[k], offset) for k, offset in enumerate(ALL_T)]
    for copy in copies:
        copy.wait_recv()
    total = packed[...]
    for k in range(7):
        total = total + packed_got[k]
    vectors[me] = total
    copies = [net.push(vectors.at[me], vectors.at[me], offset) for offset in ALL_G]
    for copy in ffn_copies + attn_copies + copies + [out_copy, in_copy]:
        copy.wait_recv()
    for keep in (ffn_keep, attn_keep, out_keep, in_keep):
        keep.wait()
    net.finish()


def tail(number, *args):
    half = sds((128, 1024), F32)
    rows = pltpu.VMEM((64, 2048), F32)
    return comm_call(
        tail_kernel,
        "tail",
        number,
        8 + 17 + 7 + 17 + 8 + 2 + 7 + 37,
        21,
        (
            half,
            half,
            sds((8, 32, 512), F32),
            sds((8, 32, 1024), BF),
            sds((16, 32, 128), F32),
        ),
        scatter_scratch(1024, 256, False)
        + [pltpu.VMEM((1024, 256), F32)]
        + scatter_scratch(64, 2048, True)
        + scatter_scratch(64, 2048, True)
        + scatter_scratch(512, 256, False)
        + [
            pltpu.VMEM((512, 256), F32),
            pltpu.VMEM((256, 1024), BF),
            pltpu.VMEM((256, 512), F32),
            rows,
            rows,
            rows,
            pltpu.VMEM((1024, 384), BF),
            pltpu.VMEM((384, 1024), BF),
            pltpu.VMEM((1024, 2048), BF),
            pltpu.VMEM((64, 2048), BF),
            pltpu.VMEM((16, 8, 128), F32),
            pltpu.VMEM((15, 8, 128), F32),
            pltpu.VMEM((32, 128), F32),
            pltpu.VMEM((7, 32, 128), F32),
        ],
        [ANY, ANY] + [VMEM] * 10 + [ANY] + [VMEM] * 5,
        (VMEM,) * 5,
        *args,
    )


def assemble_kernel(
    out_in,
    in_in,
    attn_got,
    ffn_got,
    sums,
    out_half,
    in_half,
    qkv_out,
    out_out,
    up_out,
    down_out,
    qkv_bias,
    gains_out,
    shifts_out,
    out_bias,
    down_bias,
    up_bias,
    hid_gain_out,
    hid_shift_out,
):
    out_half[...] = out_in[...]
    in_half[...] = in_in[...]

    def weights(i, carry):
        small, large = tile(i, 128), tile(i, 512)
        for j in range(3):
            at = pl.ds(pl.multiple_of(j * 1024 + i * 128, 128), 128)
            qkv_out[:, at] = attn_got[i, :, j * 128 : j * 128 + 128]
        out_out[:, small] = attn_got[i, :, 384:512]
        up_out[:, large] = ffn_got[i, :, 0:512].astype(F32)
        down_out[:, large] = ffn_got[i, :, 512:1024].astype(F32)
        return carry

    lax.fori_loop(0, 8, weights, 0)

    def place(g, carry):
        by_rows = pl.ds(g, 1)
        head = lax.rem(g, 2) * 8 + g // 2
        by_heads = pl.ds(head, 1)
        for k, (target, j) in enumerate(
            ((gains_out, 0), (shifts_out, 0), (gains_out, 2), (shifts_out, 2))
        ):
            target[j, by_rows, :] = sums[g, k : k + 1, :]
        out_bias[by_rows, :] = sums[g, 4:5, :]
        down_bias[by_rows, :] = sums[g, 5:6, :]
        for j in range(3):
            qkv_bias[j, by_heads, :] = sums[g, 8 + j : 9 + j, :]
        gains_out[1, by_heads, :] = sums[g, 11:12, :]
        shifts_out[1, by_heads, :] = sums[g, 12:13, :]
        for k, target in enumerate((up_bias, hid_gain_out, hid_shift_out)):
            for j in range(4):
                at = 13 + 4 * k + j
                target[pl.ds(head * 4 + j, 1), :] = sums[g, at : at + 1, :]
        return carry

    lax.fori_loop(0, 16, place, 0)


def assemble(*args):
    vector, hidden = sds((16, 128), F32), sds((64, 128), F32)
    triple = sds((3, 16, 128), F32)
    half = sds((128, 1024), F32)
    return pl.pallas_call(
        assemble_kernel,
        out_shape=(
            half,
            half,
            sds((32, 3072), F32),
            sds((32, 1024), F32),
            sds((32, 4096), F32),
            sds((32, 4096), F32),
            triple,
            triple,
            triple,
            vector,
            vector,
            hidden,
            hidden,
            hidden,
        ),
        in_specs=[VMEM] * 5,
        out_specs=(VMEM,) * 14,
        name="assemble",
        compiler_params=pltpu.CompilerParams(vmem_limit_bytes=32 << 20),
    )(*args)


def both_heads(rows, zero):
    lanes = lax.broadcasted_iota(jnp.int32, rows.shape, 1)
    return jnp.where(lanes < HEAD, rows, zero), jnp.where(lanes >= HEAD, rows, zero)


def run_rows(ref, run):
    return ref[pl.ds(pl.multiple_of(run * RUN, RUN), RUN), :]


def pair_rows(ref, run_a, run_b, dtype):
    zero = jnp.zeros((), dtype)
    a = both_heads(run_rows(ref, run_a).astype(dtype), zero)
    b = both_heads(run_rows(ref, run_b).astype(dtype), zero)
    return jnp.concatenate(a + b, axis=0)


def pair_bounds(rank_a, rank_b):
    lanes = lax.broadcasted_iota(jnp.int32, (1, 256), 1)
    rank = jnp.where(lanes < 128, rank_a, rank_b)
    last = rank * RUN + lax.rem(lanes, RUN)
    return (rank // 64) * 4096, last


def seen(chunk, low, last):
    keys = chunk * CHUNK + lax.broadcasted_iota(jnp.int32, (CHUNK, 256), 0)
    return (keys >= low) & (keys <= last)


def sort_keys(rank, kv_ref, keys, values):
    def move(r, carry):
        to = pl.ds(pl.multiple_of(rank[r] * RUN, RUN), RUN)
        rows = run_rows(kv_ref, r)
        keys[to, :] = rows[:, :128]
        values[to, :] = rows[:, 128:]
        return carry

    lax.fori_loop(0, 128, move, 0)


def flip(source, target):
    def one(i, carry):
        rows = source[pl.ds(pl.multiple_of(i * CHUNK, CHUNK), CHUNK), :]
        target[i] = rows.T
        return carry

    lax.fori_loop(0, 16, one, 0)


def chunk_rows(ref, i):
    return ref[pl.ds(pl.multiple_of(i * CHUNK, CHUNK), CHUNK), :]


def lane_heads(total):
    turned = total.T
    lanes = lax.broadcasted_iota(jnp.int32, (RUN, 128), 1)
    a = jnp.where(lanes < HEAD, turned[0:64], turned[64:128])
    b = jnp.where(lanes < HEAD, turned[128:192], turned[192:256])
    return a, b


def attend_kernel(rank, srun, srank, q_ref, kv_ref, o_ref, lse_ref, keys, values, flipped):
    sort_keys(rank, kv_ref, keys, values)
    flip(values, flipped)

    def pair(p, carry):
        run_a, run_b = srun[2 * p], srun[2 * p + 1]
        rank_a, rank_b = srank[2 * p], srank[2 * p + 1]
        queries = pair_rows(q_ref, run_a, run_b, BF)
        low, last = pair_bounds(rank_a, rank_b)

        def step(i, state):
            peak, total, mixed = state
            scores = lax.dot_general(
                chunk_rows(keys, i), queries, NT, preferred_element_type=F32
            )
            scores = jnp.where(seen(i, low, last), scores, -1e30)
            new_peak = jnp.maximum(peak, jnp.max(scores, axis=0, keepdims=True))
            weights = jnp.exp(scores - new_peak)
            shrink = jnp.exp(peak - new_peak)
            total = total * shrink + jnp.sum(weights, axis=0, keepdims=True)
            mixed = mixed * shrink + lax.dot_general(
                flipped[i], weights.astype(BF), NN, preferred_element_type=F32
            )
            return new_peak, total, mixed

        start = (
            jnp.full((1, 256), -1e20, F32),
            jnp.zeros((1, 256), F32),
            jnp.zeros((128, 256), F32),
        )
        peak, total, mixed = lax.fori_loop((rank_a // 64) * 8, rank_b // 8 + 1, step, start)
        a, b = lane_heads(mixed / total)
        o_ref[pl.ds(pl.multiple_of(run_a * RUN, RUN), RUN), :] = a
        o_ref[pl.ds(pl.multiple_of(run_b * RUN, RUN), RUN), :] = b
        lse_ref[p] = peak + jnp.log(total)
        return carry

    lax.fori_loop(0, 8, pair, 0)


def attend(order, queries, kv):
    return pl.pallas_call(
        attend_kernel,
        out_shape=(sds((1024, 128), F32), sds((8, 1, 256), F32)),
        grid_spec=pltpu.PrefetchScalarGridSpec(
            num_scalar_prefetch=3,
            grid=(1,),
            in_specs=[VMEM, VMEM],
            out_specs=(VMEM, VMEM),
            scratch_shapes=[
                pltpu.VMEM((8192, 128), BF),
                pltpu.VMEM((8192, 128), BF),
                pltpu.VMEM((16, 128, CHUNK), BF),
            ],
        ),
        name="attend",
        compiler_params=pltpu.CompilerParams(vmem_limit_bytes=48 << 20),
    )(*order, queries, kv)


def attend_back_kernel(
    rank, srun, srank, q_ref, kv_ref, g_ref, a_ref, lse_ref, dq_ref, dkv_ref, keys, values, flipped, dkeys, dvalues
):
    sort_keys(rank, kv_ref, keys, values)
    flip(keys, flipped)

    def clear(i, carry):
        rows = pl.ds(pl.multiple_of(i * CHUNK, CHUNK), CHUNK)
        dkeys[rows, :] = jnp.zeros((CHUNK, 128), F32)
        dvalues[rows, :] = jnp.zeros((CHUNK, 128), F32)
        return carry

    lax.fori_loop(0, 16, clear, 0)

    def pair(p, carry):
        run_a, run_b = srun[2 * p], srun[2 * p + 1]
        rank_a, rank_b = srank[2 * p], srank[2 * p + 1]
        queries = pair_rows(q_ref, run_a, run_b, BF)
        grads = pair_rows(g_ref, run_a, run_b, BF)
        low, last = pair_bounds(rank_a, rank_b)
        product = pair_rows(g_ref, run_a, run_b, F32) * pair_rows(a_ref, run_a, run_b, F32)
        delta = lax.dot_general(
            jnp.ones((8, 128), F32),
            product,
            NT,
            preferred_element_type=F32,
            precision=lax.Precision.HIGHEST,
        )[0:1]
        log_total = lse_ref[p]

        def step(i, dq):
            rows = pl.ds(pl.multiple_of(i * CHUNK, CHUNK), CHUNK)
            scores = lax.dot_general(keys[rows, :], queries, NT, preferred_element_type=F32)
            probs = jnp.where(seen(i, low, last), jnp.exp(scores - log_total), 0.0)
            dprobs = lax.dot_general(values[rows, :], grads, NT, preferred_element_type=F32)
            dscores = (probs * (dprobs - delta)).astype(BF)
            dvalues[rows, :] += lax.dot_general(
                probs.astype(BF), grads, NN, preferred_element_type=F32
            )
            dkeys[rows, :] += lax.dot_general(dscores, queries, NN, preferred_element_type=F32)
            return dq + lax.dot_general(flipped[i], dscores, NN, preferred_element_type=F32)

        dq = lax.fori_loop(
            (rank_a // 64) * 8, rank_b // 8 + 1, step, jnp.zeros((128, 256), F32)
        )
        a, b = lane_heads(dq)
        dq_ref[pl.ds(pl.multiple_of(run_a * RUN, RUN), RUN), :] = a * 0.125
        dq_ref[pl.ds(pl.multiple_of(run_b * RUN, RUN), RUN), :] = b * 0.125
        return carry

    lax.fori_loop(0, 8, pair, 0)

    def back(r, carry):
        source = pl.ds(pl.multiple_of(rank[r] * RUN, RUN), RUN)
        to = pl.ds(pl.multiple_of(r * RUN, RUN), RUN)
        dkv_ref[to, 0:128] = dkeys[source, :].astype(BF)
        dkv_ref[to, 128:256] = dvalues[source, :].astype(BF)
        return carry

    lax.fori_loop(0, 128, back, 0)


def attend_back(order, queries, kv, grads, attended, log_total):
    return pl.pallas_call(
        attend_back_kernel,
        out_shape=(sds((1024, 128), F32), sds((8192, 256), BF)),
        grid_spec=pltpu.PrefetchScalarGridSpec(
            num_scalar_prefetch=3,
            grid=(1,),
            in_specs=[VMEM] * 5,
            out_specs=(VMEM, VMEM),
            scratch_shapes=[
                pltpu.VMEM((8192, 128), BF),
                pltpu.VMEM((8192, 128), BF),
                pltpu.VMEM((16, 128, CHUNK), BF),
                pltpu.VMEM((8192, 128), F32),
                pltpu.VMEM((8192, 128), F32),
            ],
        ),
        name="attend_back",
        compiler_params=pltpu.CompilerParams(vmem_limit_bytes=56 << 20),
    )(*order, queries, kv, grads, attended, log_total)


def lane_tables(places, seq_length):
    half = HEAD // 2
    lanes = jnp.arange(128, dtype=jnp.int32)
    indices = (lanes % half).astype(F32)
    inverse_freq = jnp.exp(-jnp.log(10000.0) * indices / half)
    spots = places.astype(F32)
    angles = spots[:, None] * inverse_freq[None, :]
    ratios = (2.0 * indices + 0.4 * HEAD) / (1.4 * HEAD)
    powers = (spots - seq_length // 2) / 512.0
    growth = jnp.exp(powers[:, None] * jnp.log(ratios)[None, :])
    sign = jnp.where(lanes % HEAD < half, -1.0, 1.0)
    return jnp.cos(angles), jnp.sin(angles) * sign[None, :], growth


def swap_halves(values):
    half = HEAD // 2
    first = (jnp.arange(128) % HEAD < half)[None, :]
    return jnp.where(first, jnp.roll(values, -half, axis=1), jnp.roll(values, half, axis=1))


def normal(values):
    center = jnp.mean(values, axis=1, keepdims=True)
    centered = values - center
    variance = jnp.mean(centered * centered, axis=1, keepdims=True)
    inv = lax.rsqrt(variance + EPS)
    return centered * inv, inv


def shards(
    layer_input,
    w_qkv,
    w_out,
    w_up,
    w_down,
    b_qkv,
    b_out,
    b_up,
    b_down,
    norm_gains,
    norm_shifts,
    hidden_gain,
    hidden_shift,
    seq_ids,
    positions,
    d_out,
):
    z, c, f = g_place()
    x, h = t_place()
    zc = z * 2 + c
    head_at = f * 1024 + zc * 128

    def head_part(vector):
        return lax.dynamic_slice_in_dim(vector, head_at, 128, axis=vector.ndim - 1)

    packed = jnp.concatenate(
        [
            w_up.reshape(32, 8, 512),
            w_down.reshape(32, 8, 512),
            w_qkv.reshape(32, 3, 8, 128).transpose(0, 2, 1, 3).reshape(32, 8, 384),
            w_out.reshape(32, 8, 128),
        ],
        axis=2,
    ).transpose(1, 0, 2)
    rank_here = seq_ids.reshape(2, RUN)[:, 0] * 64 + positions.reshape(2, RUN)[:, 0] // RUN
    rank_tile = jnp.zeros((8, 128), jnp.int32).at[0, :2].set(rank_here)
    input_all, w_attn, ffn_block, ranks = start_all(layer_input, packed, rank_tile, 1)
    qkv_w = w_attn[:, :384]

    rank = ranks[:, :, 0, :2].reshape(128)
    group_rank = lax.dynamic_slice_in_dim(rank, (x * 2 + h) * 16, 16)
    slot = jnp.sum((group_rank[None, :] < group_rank[:, None]).astype(jnp.int32), axis=1)
    hit = slot[None, :] == jnp.arange(16, dtype=jnp.int32)[:, None]
    srank = jnp.sum(jnp.where(hit, group_rank[None, :], 0), axis=1)
    srun = jnp.sum(jnp.where(hit, jnp.arange(16, dtype=jnp.int32)[None, :], 0), axis=1)
    order = (rank, srun, srank)
    places = ((group_rank % 64) * RUN)[:, None] + jnp.arange(RUN, dtype=jnp.int32)[None, :]
    cosine, sine, growth = lane_tables(places.reshape(1024), 4096)

    normal_all, unused = normal(input_all.astype(F32))
    in_low = (normal_all * norm_gains[0] + norm_shifts[0]).astype(BF)
    qkv = jnp.dot(in_low, qkv_w, preferred_element_type=F32) + head_part(b_qkv).reshape(384)
    queries, keys, values = qkv[:, :128], qkv[:, 128:256], qkv[:, 256:]
    query_low = ((queries * cosine + swap_halves(queries) * sine) * growth).astype(BF)
    query_low = query_low * jnp.bfloat16(0.125)
    shrink = 1.0 / growth
    key_low = ((keys * cosine + swap_halves(keys) * sine) * shrink).astype(BF)
    kv, grad_all = gather_both(
        jnp.concatenate([key_low, values.astype(BF)], axis=1), d_out, 2
    )
    attended, log_total = attend(order, query_low, kv)

    (
        mid,
        grad_mid,
        ffn_part,
        grad_attended,
        ffn_grad,
        out_term,
        hid_vec,
        head_vec,
        row_vec,
    ) = middle(
        3,
        attended,
        w_attn,
        ffn_block,
        grad_all,
        input_all,
        b_out.reshape(1, 2048),
        b_up.reshape(1, 8192),
        norm_gains,
        norm_shifts,
        hidden_gain.reshape(1, 8192),
        hidden_shift.reshape(1, 8192),
    )
    query_grad, kv_part = attend_back(order, query_low, kv, grad_attended, attended, log_total)
    parts = tail(
        4,
        kv_part.reshape(8, 1024, 256),
        ffn_part.reshape(16, 64, 2048),
        ffn_grad,
        query_grad,
        cosine,
        sine,
        growth,
        w_attn,
        in_low,
        out_term,
        mid,
        grad_mid,
        input_all,
        b_down.reshape(1, 2048),
        norm_gains,
        hid_vec,
        head_vec,
        row_vec,
    )
    (
        layer_output,
        input_grad,
        qkv_grad,
        out_grad,
        up_grad,
        down_grad,
        qkv_bias,
        gains_grad,
        shifts_grad,
        out_bias,
        down_bias,
        up_bias,
        hid_gain_grad,
        hid_shift_grad,
    ) = assemble(*parts)
    return (
        layer_output,
        input_grad,
        qkv_grad.reshape(32, 3, 1024),
        out_grad,
        up_grad,
        down_grad,
        qkv_bias.reshape(3, 2048),
        out_bias.reshape(2048),
        up_bias.reshape(8192),
        down_bias.reshape(2048),
        gains_grad.reshape(3, 2048),
        shifts_grad.reshape(3, 2048),
        hid_gain_grad.reshape(8192),
        hid_shift_grad.reshape(8192),
    )


def solution(mesh):
    fine = Mesh(mesh.devices.reshape(4, 2, 4, 2, 2), SEQ + ("f",))
    both = P(SEQ, "f")
    return jax.shard_map(
        shards,
        mesh=fine,
        in_specs=(both, P(SEQ, None, "f"), both, both, both)
        + (P(),) * 8
        + (P(SEQ), P(SEQ), both),
        out_specs=(both, both, P(SEQ, None, "f"), both, both, both) + (P(),) * 8,
        check_vma=False,
    )
```

```python
import math

import jax
import jax.numpy as jnp
import numpy as np
from jax import lax
from jax.experimental import pallas as pl
from jax.experimental.pallas import tpu as pltpu
from jax.sharding import Mesh
from jax.sharding import PartitionSpec as P

SEQ = ("x", "h", "z", "c")
TOK = ("x", "h")
HEAD = 64
RUN = 64
CHUNK = 512
EPS = 1e-05
MESH = pl.DeviceIdType.MESH
BF = jnp.bfloat16
F32 = jnp.float32
DMA = pltpu.SemaphoreType.DMA
ANY = pl.BlockSpec(memory_space=pl.ANY)
VMEM = pl.BlockSpec(memory_space=pltpu.VMEM)
NT = (((1,), (1,)), ((), ()))
TN = (((0,), (0,)), ((), ()))
NN = (((1,), (0,)), ((), ()))


def sds(shape, dtype):
    return jax.ShapeDtypeStruct(shape, dtype)


AXES = {"x": 4, "h": 2, "z": 4, "c": 2, "f": 2}
RING_G, PAIR_G = "z", "f"
RING_T, PAIR_T = "x", "h"


class Net:
    def __init__(self, send, recv):
        self.send, self.recv, self.copies, self.drained = send, recv, [], 0
        self.at = {axis: lax.axis_index(axis) for axis in AXES}

    def device(self, offset):
        return {a: lax.rem(self.at[a] + d + AXES[a], AXES[a]) for a, d in offset.items()}

    def place(self, offset, *axes):
        index = 0
        for a in axes:
            d = offset.get(a, 0)
            at = lax.rem(self.at[a] + d + AXES[a], AXES[a]) if d else self.at[a]
            index = index * AXES[a] + at
        return index

    def greet(self, *groups):
        offsets = {
            tuple((a, o[a]) for a in AXES if o.get(a, 0)) for group in groups for o in group
        }
        barrier = pltpu.get_barrier_semaphore()
        for offset in sorted(offsets):
            pl.semaphore_signal(
                barrier, inc=1, device_id=self.device(dict(offset)), device_id_type=MESH
            )
        pl.semaphore_wait(barrier, len(offsets))

    def push(self, src, dst, offset):
        k = len(self.copies)
        copy = pltpu.make_async_remote_copy(
            src_ref=src,
            dst_ref=dst,
            send_sem=self.send.at[k],
            recv_sem=self.recv.at[k],
            device_id=self.device(offset),
            device_id_type=MESH,
        )
        copy.start()
        self.copies.append(copy)
        return copy

    def finish(self):
        for copy in self.copies[self.drained :]:
            copy.wait_send()
        self.drained = len(self.copies)


SIBLING = {"c": 1}
NEAR_G = [{"z": 1}, {"z": 3}, {"f": 1}, SIBLING]
NEAR_T = [{"x": 1}, {"x": 3}, {"h": 1}]
ALL_T = [{"x": i, "h": j} for i in range(4) for j in range(2)][1:]
ALL_ZC = [{"z": i, "c": j} for i in range(4) for j in range(2)][1:]
ALL_G = [{"z": i, "c": j, "f": k} for i in range(4) for j in range(2) for k in range(2)][1:]


class Flow:
    def __init__(self, steps):
        self.steps = steps
        self.step()

    def step(self):
        self.time = next(self.steps, None)


def run_until(main, *others):
    while main.time is not None:
        ready = [flow for flow in (main,) + others if flow.time is not None]
        min(ready, key=lambda flow: flow.time).step()


def run_flows(*flows):
    for flow in flows:
        run_until(flow, *flows)


def run_flows_but(kept, *flows):
    for flow in flows:
        run_until(flow, kept, *flows)


def half_rows(ref, which):
    rows = ref.shape[0] // 2
    return ref.at[pl.ds(which * rows, rows)]


def gather_flow(net, src, slot, ring, pair, local, sibling, light, at, unit, hold=0):
    up, down, across = {ring: 1}, {ring: 3}, {pair: 1}
    passed = []

    def to_sibling(ref):
        if sibling:
            passed.append(net.push(ref, ref, SIBLING))

    def both_ways(ref, target):
        return [
            [net.push(half_rows(ref, k), half_rows(target, k), to) for k in order]
            for to, order in ((up, (0, 1)), (down, (1, 0)))
        ]

    mine = slot({})
    from_down, from_up = both_ways(src, mine)
    if hold:
        yield at + hold
    from_across = net.push(src, mine, across)
    if sibling:
        passed.append(net.push(src, mine, SIBLING))
    here = pltpu.make_async_copy(src, mine, local)
    here.start()
    below, above, beside, far = (slot({ring: 3}), slot({ring: 1}), slot({pair: 1}), slot({ring: 2}))
    yield at + 0.5 * unit
    from_down[0].wait_recv()
    first = net.push(half_rows(below, 0), half_rows(below, 0), up)
    from_up[0].wait_recv()
    second = net.push(half_rows(above, 1), half_rows(above, 1), down)
    yield at + unit
    from_across.wait_recv()
    if light:
        beside_down, beside_up = both_ways(beside, beside)
    else:
        beside_down = [net.push(beside, beside, up)]
        beside_up = [net.push(beside, beside, down)]
    to_sibling(beside)
    yield at + unit
    from_down[1].wait_recv()
    to_sibling(below)
    from_up[1].wait_recv()
    to_sibling(above)
    yield at + 1.5 * unit
    first.wait_recv()
    if not light:
        beside_far = [net.push(half_rows(far, 0), half_rows(far, 0), across)]
    second.wait_recv()
    if not light:
        beside_far.append(net.push(half_rows(far, 1), half_rows(far, 1), across))
    to_sibling(far)
    yield at + (2 if light else 2.5) * unit
    below, above = slot({ring: 3, pair: 1}), slot({ring: 1, pair: 1})
    if light:
        beside_down[0].wait_recv()
        beside_far = [net.push(half_rows(below, 0), half_rows(below, 0), up)]
        beside_up[0].wait_recv()
        beside_far.append(net.push(half_rows(above, 1), half_rows(above, 1), down))
        yield at + 2.5 * unit
    beside_down[-1].wait_recv()
    to_sibling(below)
    beside_up[-1].wait_recv()
    to_sibling(above)
    yield at + (3 if light else 2.5) * unit
    for copy in beside_far:
        copy.wait_recv()
    to_sibling(slot({ring: 2, pair: 1}))
    yield at + (3 if light else 2.5) * unit
    here.wait()
    for copy in passed:
        copy.wait_recv()


def add_into(target, *sources):
    rows = min(32768 // target.shape[1], target.shape[0])

    def step(i, carry):
        at = pl.ds(pl.multiple_of(i * rows, rows), rows)
        total = target[at, :].astype(F32)
        for source in sources:
            total = total + source[at, :].astype(F32)
        target[at, :] = total.astype(target.dtype)
        return carry

    lax.fori_loop(0, target.shape[0] // rows, step, 0)


ROOTS = ((2, 1), (1, 1), (3, 1), (2, 0), (1, 0), (3, 0), (0, 1), (0, 0))


def scatter_flow(
    net, chunk, out, mine, other, landed, local, ring, pair, sibling, light, at, unit
):
    up, down, across = {ring: 1}, {ring: 3}, {pair: 1}
    loads, shared = [], []
    for k, (i, j) in enumerate(ROOTS):
        if sibling:
            shared.append(net.push(chunk({ring: i, pair: j, "c": 1}), other.at[k], SIBLING))
        if chunk is not None:
            load = pltpu.make_async_copy(chunk({ring: i, pair: j}), mine.at[k], local.at[k])
            load.start()
            loads.append(load)

    def ready(k):
        if chunk is not None:
            loads[k].wait()
        if sibling:
            shared[k].wait_recv()
            add_into(mine.at[k], other.at[k])

    def halves(k, to):
        return (
            net.push(half_rows(mine.at[k], 0), half_rows(landed.at[to], 0), down),
            net.push(half_rows(mine.at[k], 1), half_rows(landed.at[to], 1), up),
        )

    def add_half(k, source, which):
        add_into(half_rows(mine.at[k], which), half_rows(landed.at[source], which))

    def send_half(k, to, which, offset):
        return net.push(half_rows(mine.at[k], which), half_rows(landed.at[to], which), offset)

    if chunk is not None:
        yield at + 0.5
    ready(0)
    if light:
        beside_first, beside_second = halves(0, 0)
        ready(3)
        first, second = halves(3, 3)
        ready(2)
        beside_up = [send_half(2, 2, 1, down)]
        ready(1)
        beside_down = [send_half(1, 1, 0, up)]
        yield at + 0.5 * unit
        beside_first.wait_recv()
        add_half(2, 0, 0)
        beside_up.append(send_half(2, 2, 0, down))
        beside_second.wait_recv()
        add_half(1, 0, 1)
        beside_down.append(send_half(1, 1, 1, up))
    else:
        beside_far = [send_half(0, 0, k, across) for k in range(2)]
        ready(1)
        beside_down = [net.push(mine.at[1], landed.at[1], up)]
        ready(2)
        beside_up = [net.push(mine.at[2], landed.at[2], down)]
        ready(3)
        yield at + 0.6 * unit
        beside_far[0].wait_recv()
        add_half(3, 0, 0)
        first = send_half(3, 3, 0, down)
        yield at + unit
        beside_far[1].wait_recv()
        add_half(3, 0, 1)
        second = send_half(3, 3, 1, up)
    ready(5)
    from_up = [send_half(5, 5, 1, down)]
    ready(4)
    from_down = [send_half(4, 6, 0, up)]
    if not light:
        ready(6)
        yield at + 1.1 * unit
        for copy in beside_down + beside_up:
            copy.wait_recv()
        add_into(mine.at[6], landed.at[1], landed.at[2])
        from_across = net.push(mine.at[6], landed.at[4], across)
    yield at + (1.1 if light else 1.6) * unit
    first.wait_recv()
    add_half(5, 3, 0)
    from_up.append(send_half(5, 5, 0, down))
    yield at + (1.1 if light else 1.8) * unit
    second.wait_recv()
    add_half(4, 3, 1)
    from_down.append(send_half(4, 6, 1, up))
    if light:
        ready(6)
        yield at + 2 * unit
        for copy in beside_down + beside_up:
            copy.wait_recv()
        add_into(mine.at[6], landed.at[1], landed.at[2])
        from_across = net.push(mine.at[6], landed.at[4], across)
    ready(7)
    yield at + (3 if light else 2.5) * unit
    for copy in from_up + from_down + [from_across]:
        copy.wait_recv()
    rows = 32768 // out.shape[1]

    def total(i, carry):
        at = pl.ds(pl.multiple_of(i * rows, rows), rows)
        value = mine[7, at, :].astype(F32) + landed[4, at, :].astype(F32)
        out[at, :] = value + (landed[5, at, :].astype(F32) + landed[6, at, :].astype(F32))
        return carry

    lax.fori_loop(0, out.shape[0] // rows, total, 0)


def gather_slot(net, out, rows, ring, pair):
    order = ("z", "c", "f") if ring == "z" else ("x", "h")

    def slot(offset):
        at = net.place(offset, *order)
        return out.at[pl.ds(pl.multiple_of(at * rows, rows), rows)]

    return slot


def input_slot(net, out):
    def slot(offset):
        row = pl.multiple_of(net.place(offset, "z", "c") * 128, 128)
        column = pl.multiple_of(net.place(offset, "f") * 1024, 1024)
        return out.at[pl.ds(row, 128), pl.ds(column, 1024)]

    return slot


def scatter_chunk(net, ref, ring):
    order = ("z", "c", "f") if ring == "z" else ("x", "h")
    return lambda offset: ref.at[net.place(offset, *order)]


def comm_call(kernel, name, number, pushes, locals_, out_shape, scratch, in_specs, out_specs, *args):
    return pl.pallas_call(
        kernel,
        out_shape=out_shape,
        in_specs=in_specs,
        out_specs=out_specs,
        scratch_shapes=[DMA((pushes,)), DMA((pushes,)), DMA((locals_,))] + scratch,
        name=name,
        compiler_params=pltpu.CompilerParams(
            collective_id=number, has_side_effects=True, vmem_limit_bytes=60 << 20
        ),
    )(*args)


def scatter_scratch(rows, width, sibling):
    shapes = [pltpu.VMEM((8, rows, width), BF), pltpu.VMEM((7, rows, width), BF)]
    return shapes + ([pltpu.VMEM((8, rows, width), BF)] if sibling else [])


def g_place():
    return lax.axis_index("z"), lax.axis_index("c"), lax.axis_index("f")


def t_place():
    return lax.axis_index("x"), lax.axis_index("h")


def turn_halves(values):
    lanes = lax.broadcasted_iota(jnp.int32, values.shape, 1)
    first = lax.rem(lanes, HEAD) < HEAD // 2
    return jnp.where(first, pltpu.roll(values, 96, axis=1), pltpu.roll(values, 32, axis=1))


def front_kernel(
    x_ref,
    d_ref,
    w_ref,
    up_ref,
    down_ref,
    rank_ref,
    gains,
    shifts,
    bias,
    run_tables,
    token_tables,
    rows_out,
    low_out,
    w_out,
    ffn_out,
    q_out,
    kv_out,
    grad_out,
    cosine,
    sine,
    growth,
    order,
    send,
    recv,
    local,
    x_all,
    in_low,
    w_all,
    blocks,
    near,
    near_sum,
    far,
    kv_here,
):
    net = Net(send, recv)
    net.greet(NEAR_G, ALL_ZC, ALL_T)
    me = net.place({}, "z", "c")
    group = net.place({}, "x", "h")
    f = net.at["f"]
    rows = pl.ds(pl.multiple_of(me * 32, 32), 32)
    stores = []

    def store(src, dst, k):
        copy = pltpu.make_async_copy(src, dst, local.at[k])
        copy.start()
        stores.append(copy)

    def norm_rows(i, carry):
        at = tile(i, 16)
        values = x_all[at, :].astype(F32)
        centered = values - jnp.mean(values, axis=1, keepdims=True)
        scale = lax.rsqrt(jnp.mean(centered * centered, axis=1, keepdims=True) + EPS)
        in_low[at, :] = (centered * scale * gains[0:1, :] + shifts[0:1, :]).astype(BF)
        return carry

    def activations():
        yield from gather_flow(
            net, x_ref, input_slot(net, x_all), "z", "f", local.at[0], True, True, 0, 5.5
        )
        ffn_sent = []
        for offset in ALL_ZC:
            to = net.place(offset, "z", "c")
            at = pl.ds(pl.multiple_of(to * 512, 512), 512)
            ffn_sent.append(net.push(up_ref.at[:, at], ffn_out.at[rows, pl.ds(0, 512)], offset))
            ffn_sent.append(net.push(down_ref.at[:, at], ffn_out.at[rows, pl.ds(512, 512)], offset))
        at = pl.ds(pl.multiple_of(me * 512, 512), 512)
        store(up_ref.at[:, at], ffn_out.at[rows, pl.ds(0, 512)], 4)
        store(down_ref.at[:, at], ffn_out.at[rows, pl.ds(512, 512)], 5)
        lax.fori_loop(0, 64, norm_rows, 0, unroll=2)
        store(in_low, low_out, 6)
        store(x_all.at[pl.ds(pl.multiple_of((me * 2 + f) * 64, 64), 64)], rows_out, 7)
        yield from gather_flow(
            net, d_ref, input_slot(net, grad_out), "z", "f", local.at[1], True, True, 24, 8
        )
        for copy in ffn_sent:
            copy.wait_recv()

    def run_rank(index):
        lanes = lax.broadcasted_iota(jnp.int32, (1, 128), 1)
        return jnp.sum(jnp.where(lanes == index, near_sum[0:1, :], 0.0), axis=1, keepdims=True)

    def tables(i, carry):
        at = tile(i, RUN)
        block = run_rank(group * 16 + i)
        block = block - jnp.floor(block / 64) * 64
        mask = lax.broadcasted_iota(jnp.int32, (64, 128), 0).astype(F32) == block
        cos_a, sin_a, grow_a = (
            jnp.sum(jnp.where(mask, run_tables[k], 0.0), axis=0, keepdims=True) for k in range(3)
        )
        cos_b, sin_b, grow_b = token_tables[0], token_tables[1], token_tables[2]
        lanes = lax.broadcasted_iota(jnp.int32, (RUN, 128), 1)
        sin = sin_a * cos_b + cos_a * sin_b
        cosine[at, :] = cos_a * cos_b - sin_a * sin_b
        sine[at, :] = jnp.where(lax.rem(lanes, HEAD) < HEAD // 2, -sin, sin)
        growth[at, :] = grow_a * grow_b
        return carry

    def put_order():
        lanes = lax.broadcasted_iota(jnp.int32, (16, 128), 1)
        places = lax.broadcasted_iota(jnp.int32, (16, 128), 0)
        ranks = jnp.zeros((16, 128), F32)
        by_lane = jnp.full((16, 128), 1e9, F32)
        for k in range(16):
            rank = run_rank(group * 16 + k)
            ranks = jnp.where(places == k, rank, ranks)
            by_lane = jnp.where(lanes == k, rank, by_lane)
        slot = jnp.sum((by_lane < ranks).astype(F32), axis=1, keepdims=True)
        hit = lanes.astype(F32) == slot
        runs = jnp.sum(jnp.where(hit, places.astype(F32), 0.0), axis=0, keepdims=True)
        ranks = jnp.sum(jnp.where(hit, ranks, 0.0), axis=0, keepdims=True)
        total = jnp.sum(far[...], axis=0)[0:1]
        order[0:1, :] = total.astype(jnp.int32)
        order[1:2, :] = runs.astype(jnp.int32)
        order[2:3, :] = ranks.astype(jnp.int32)
        order[3:8, :] = jnp.zeros((5, 128), jnp.int32)

    head_at = pl.ds(pl.multiple_of(f * 1024 + me * 128, 128), 128)

    def project(i, carry):
        at = tile(i, 256)
        values = jnp.dot(in_low[at, :], w_all[:, 0:384], preferred_element_type=F32)
        queries = values[:, 0:128] + bias[0:1, head_at]
        keys = values[:, 128:256] + bias[1:2, head_at]
        cos, sin, grow = cosine[at, :], sine[at, :], growth[at, :]
        queries = ((queries * cos + turn_halves(queries) * sin) * grow).astype(BF)
        q_out[at, :] = queries * jnp.bfloat16(0.125)
        keys = (keys * cos + turn_halves(keys) * sin) * (1.0 / grow)
        kv_here[at, 0:128] = keys.astype(BF)
        kv_here[at, 128:256] = (values[:, 256:384] + bias[2:3, head_at]).astype(BF)
        return carry

    def attention():
        attn_sent, near_sent = [], []
        for offset in ALL_ZC:
            to = net.place(offset, "z", "c")
            attn_sent.append(net.push(w_ref.at[to], blocks.at[rows], offset))
        for offset in ALL_ZC:
            near_sent.append(net.push(rank_ref, near.at[me], offset))
        own = pltpu.make_async_copy(w_ref.at[me], blocks.at[rows], local.at[2])
        own.start()
        near[me] = rank_ref[...]
        own.wait()
        yield 5
        for copy in attn_sent:
            copy.wait_recv()
        weights = gather_flow(
            net, blocks, gather_slot(net, w_all, 256, "x", "h"), "x", "h", local.at[3], False, False, 6, 5.5
        )
        yield next(weights)
        for copy in near_sent:
            copy.wait_recv()
        near_sum[...] = jnp.sum(near[...], axis=0)
        far_sent = [net.push(near_sum, far.at[group], offset) for offset in ALL_T]
        far[group] = near_sum[...]
        lax.fori_loop(0, 16, tables, 0)
        yield from weights
        store(w_all, w_out, 8)
        yield 26
        lax.fori_loop(0, 4, project, 0)
        sending = gather_flow(
            net, kv_here, gather_slot(net, kv_out, 1024, "x", "h"), "x", "h", local.at[9], False, False, 29, 11
        )
        yield next(sending)
        for copy in far_sent:
            copy.wait_recv()
        put_order()
        yield from sending

    run_flows(Flow(attention()), Flow(activations()))
    for copy in stores:
        copy.wait()
    net.finish()


def front(number, *args):
    table = sds((1024, 128), F32)
    return comm_call(
        front_kernel,
        "front",
        number,
        23 * 2 + 14 + 7 * 3 + 12 * 2,
        10,
        (
            sds((64, 2048), BF),
            sds((1024, 2048), BF),
            sds((2048, 512), BF),
            sds((256, 1024), BF),
            sds((1024, 128), BF),
            sds((8192, 256), BF),
            sds((1024, 2048), BF),
            table,
            table,
            table,
            sds((8, 128), jnp.int32),
        ),
        [
            pltpu.VMEM((1024, 2048), BF),
            pltpu.VMEM((1024, 2048), BF),
            pltpu.VMEM((2048, 512), BF),
            pltpu.VMEM((256, 512), BF),
            pltpu.VMEM((8, 8, 128), F32),
            pltpu.VMEM((8, 128), F32),
            pltpu.VMEM((8, 8, 128), F32),
            pltpu.VMEM((1024, 256), BF),
        ],
        [ANY] * 5 + [VMEM] * 6,
        (ANY,) * 4 + (VMEM, ANY, ANY) + (VMEM,) * 4,
        *args,
    )


def row_sums(values):
    ones = jnp.ones((8, values.shape[1]), F32)
    return lax.dot_general(
        ones, values, NT, preferred_element_type=F32, precision=lax.Precision.HIGHEST
    )[0:1]


def put_sums(target, i, *values):
    sums = row_sums(jnp.concatenate(values, axis=0))
    for k in range(len(values)):
        target[pl.ds(8 * k + i, 1), :] = sums[:, k * 128 : k * 128 + 128]


def tile(i, rows=128):
    return pl.ds(pl.multiple_of(i * rows, rows), rows)


def columns_of(rows_ref, i):
    return rows_ref[i].T


def put_rows(rows_ref, *values):
    for k, value in enumerate(values):
        for i in range(8):
            rows_ref[i, k : k + 1, :] = value[i : i + 1]


def fold_lanes(values):
    return (values[:, 0:128] + values[:, 128:256]) + (values[:, 256:384] + values[:, 384:512])


def middle_kernel(
    att,
    w_attn,
    ffn_block,
    grad_all_in,
    input_rows,
    b_out,
    b_up,
    gains,
    shifts,
    hid_gain,
    hid_shift,
    mid,
    grad_mid,
    ffn_part,
    grad_att,
    ffn_grad,
    out_term,
    hid_vec,
    head_vec,
    row_vec,
    send,
    recv,
    local,
    grad_all,
    out_w,
    w_ffn,
    mid_low,
    branch_all,
    hidden_low,
    pre_low,
    hidden_turned,
    pre_turned,
    attn_low,
    low_rows,
    partial_rows,
    mine,
    landed,
    other,
    t_mine,
    t_landed,
    grad_hidden,
    activated,
    slope,
    normal_attn,
    normal_mid,
    scale_mid,
    sent_a,
    stats_a,
    rows_a,
    sent_b,
    stats_b,
    rows_b,
    sent_c,
    stats_c,
    rows_c,
):
    net = Net(send, recv)
    me = net.place({}, "z", "c", "f")
    load_w = pltpu.make_async_copy(w_attn.at[:, pl.ds(384, 128)], out_w, local.at[10])
    load_w.start()
    load_grad = pltpu.make_async_copy(grad_all_in, grad_all, local.at[11])
    load_grad.start()
    net.greet(ALL_G, NEAR_T)
    weights = Flow(
        gather_flow(
            net, ffn_block, gather_slot(net, w_ffn, 256, "x", "h"), "x", "h", local.at[9], False, True, 2, 11, 7
        )
    )
    head_at = pl.ds(
        pl.multiple_of(net.at["f"] * 1024 + net.place({}, "z", "c") * 128, 128), 128
    )
    hidden_at = pl.ds(
        pl.multiple_of(net.at["f"] * 4096 + net.place({}, "z", "c") * 512, 512), 512
    )
    head_gain, head_shift = gains[1:2, head_at], shifts[1:2, head_at]
    gain_here, shift_here, bias_here = hid_gain[:, hidden_at], hid_shift[:, hidden_at], b_up[:, hidden_at]

    def exchange(sent, stats):
        copies = [net.push(sent, stats.at[me], offset) for offset in ALL_G]
        stats[me] = sent[...]
        for copy in copies:
            copy.wait_recv()

    def chunk(offset):
        at = net.place(offset, "z", "c", "f")
        return partial_rows.at[pl.ds(pl.multiple_of(at * 64, 64), 64)]

    def measure(i, carry):
        here = att[tile(i), :]
        centered = here - jnp.mean(here, axis=1, keepdims=True)
        put_sums(sent_a, i, here, centered * centered)
        return carry

    lax.fori_loop(0, 8, measure, 0, unroll=2)
    exchange(sent_a, stats_a)
    center = jnp.sum(stats_a[:, 0:8], axis=0) / 2048
    spread = jnp.sum(
        stats_a[:, 8:16] + 128 * jnp.square(stats_a[:, 0:8] / 128 - center[None]), axis=0
    )
    put_rows(rows_a, center, lax.rsqrt(spread / 2048 + EPS))

    def norm_heads(i, carry):
        columns = columns_of(rows_a, i)
        normal_rows = (att[tile(i), :] - columns[:, 0:1]) * columns[:, 1:2]
        normal_attn[tile(i), :] = normal_rows
        attn_low[tile(i), :] = (normal_rows * head_gain + head_shift).astype(BF)
        return carry

    lax.fori_loop(0, 8, norm_heads, 0, unroll=2)
    load_w.wait()

    def project(i, carry):
        partial_rows[:, tile(i, 256)] = lax.dot_general(
            attn_low[...], out_w[tile(i, 256), :], NT, preferred_element_type=F32
        ).astype(BF)
        return carry

    lax.fori_loop(0, 8, project, 0)
    run_until(
        Flow(scatter_flow(net, chunk, mid, mine, other, landed, local, "z", "f", True, False, 13, 5.5)),
        weights,
    )
    net.finish()

    def mid_norm(i, carry):
        at = tile(i, 16)
        rows = input_rows[at, :].astype(F32) + (mid[at, :] + b_out[...])
        mid[at, :] = rows
        centered = rows - jnp.mean(rows, axis=1, keepdims=True)
        scale = lax.rsqrt(jnp.mean(centered * centered, axis=1, keepdims=True) + EPS)
        rows = centered * scale
        normal_mid[at, :] = rows
        scale_mid[at, :] = jnp.broadcast_to(scale, (16, 128))
        low_rows[at, :] = (rows * gains[2:3, :] + shifts[2:3, :]).astype(BF)
        return carry

    lax.fori_loop(0, 4, mid_norm, 0)
    def hidden_grads():
        yield 43
        run_until(weights)
        load_grad.wait()
        for i in range(4):
            grad_hidden[tile(i, 256), :] = jnp.dot(
                grad_all[tile(i, 256), :], w_ffn[:, 512:1024], preferred_element_type=F32
            )
            yield 44

    run_flows(
        Flow(
            gather_flow(
                net, low_rows, gather_slot(net, mid_low, 64, "z", "f"), "z", "f", local.at[0], True, False, 31, 5.5
            )
        ),
        Flow(hidden_grads()),
        weights,
    )
    net.finish()

    def up(i, carry):
        at = tile(i)
        pre = jnp.dot(mid_low[at, :], w_ffn[:, 0:512], preferred_element_type=F32) + bias_here
        below = 0.5 + 0.5 * lax.erf(pre * math.sqrt(0.5))
        act = pre * below
        activated[at, :] = act
        slope[at, :] = below + pre * jnp.exp(-0.5 * pre * pre) * (1.0 / math.sqrt(2.0 * math.pi))
        centered = act - jnp.mean(act, axis=1, keepdims=True)
        scaled = grad_hidden[at, :] * gain_here
        put_sums(
            sent_b,
            i,
            fold_lanes(act),
            fold_lanes(centered * centered),
            fold_lanes(scaled),
            fold_lanes(scaled * centered),
        )
        return carry

    lax.fori_loop(0, 8, up, 0, unroll=2)
    exchange(sent_b, stats_b)
    center = jnp.sum(stats_b[:, 0:8], axis=0) / 8192
    apart = stats_b[:, 0:8] / 512 - center[None]
    spread = jnp.sum(stats_b[:, 8:16] + 512 * jnp.square(apart), axis=0)
    scale = lax.rsqrt(spread / 8192 + EPS)
    mean_back = jnp.sum(stats_b[:, 16:24], axis=0) / 8192
    cross_back = scale * jnp.sum(stats_b[:, 24:32] + apart * stats_b[:, 16:24], axis=0) / 8192
    put_rows(rows_b, center, scale, mean_back, cross_back)

    def hidden(i, carry):
        at = tile(i)
        columns = columns_of(rows_b, i)
        scale = columns[:, 1:2]
        normal_rows = (activated[at, :] - columns[:, 0:1]) * scale
        hidden_low[at, :] = (normal_rows * gain_here + shift_here).astype(BF)
        upstream = grad_hidden[at, :]
        back = scale * (upstream * gain_here - columns[:, 2:3] - normal_rows * columns[:, 3:4])
        low = (back * slope[at, :]).astype(BF)
        pre_low[at, :] = low
        return (
            carry[0] + jnp.sum(low.astype(F32), axis=0, keepdims=True),
            carry[1] + jnp.sum(upstream * normal_rows, axis=0, keepdims=True),
            carry[2] + jnp.sum(upstream, axis=0, keepdims=True),
        )

    sums = lax.fori_loop(0, 8, hidden, (jnp.zeros((1, 512), F32),) * 3)
    for k in range(3):
        hid_vec[k : k + 1, :] = sums[k]

    def project_back(i, carry):
        partial_rows[:, tile(i, 256)] = lax.dot_general(
            pre_low[...], w_ffn[tile(i, 256), 0:512], NT, preferred_element_type=F32
        ).astype(BF)
        return carry

    lax.fori_loop(0, 8, project_back, 0)

    def weight_terms():
        def turn(i, carry):
            pre_turned[:, tile(i)] = pre_low[tile(i), :].T
            hidden_turned[:, tile(i)] = hidden_low[tile(i), :].T
            return carry

        yield 69
        lax.fori_loop(0, 8, turn, 0)
        for k, (i, j) in enumerate(ROOTS):
            yield 70 + k
            columns = tile(net.place({"x": i, "h": j}, "x", "h"), 256)
            t_mine[k, 0:512, :] = jnp.dot(
                pre_turned[...], mid_low[:, columns], preferred_element_type=F32
            ).astype(BF)
            t_mine[k, 512:1024, :] = jnp.dot(
                hidden_turned[...], grad_all[:, columns], preferred_element_type=F32
            ).astype(BF)

    def weight_scatter():
        yield from weight_terms()
        yield from scatter_flow(
            net, None, ffn_grad, t_mine, None, t_landed, local, "x", "h", False, False, 82, 11
        )

    weights = Flow(weight_scatter())
    run_until(
        Flow(scatter_flow(net, chunk, grad_mid, mine, other, landed, local, "z", "f", True, False, 68, 5.5)),
        weights,
    )
    net.finish()

    def mid_back(i, carry):
        at = tile(i, 16)
        upstream = grad_mid[at, :]
        normal_rows = normal_mid[at, :]
        scaled = upstream * gains[2:3, :]
        mean = jnp.mean(scaled, axis=1, keepdims=True)
        cross = jnp.mean(scaled * normal_rows, axis=1, keepdims=True)
        out_rows = grad_all[pl.ds(pl.multiple_of(me * 64 + i * 16, 16), 16), :].astype(F32)
        rows = out_rows + scale_mid[at, 0:1] * (scaled - mean - normal_rows * cross)
        grad_mid[at, :] = rows
        low = rows.astype(BF)
        low_rows[at, :] = low
        row_vec[0:1, :] += jnp.sum(upstream * normal_rows, axis=0, keepdims=True)
        row_vec[1:2, :] += jnp.sum(upstream, axis=0, keepdims=True)
        row_vec[2:3, :] += jnp.sum(low.astype(F32), axis=0, keepdims=True)
        row_vec[3:4, :] += jnp.sum(out_rows, axis=0, keepdims=True)
        return carry

    row_vec[...] = jnp.zeros_like(row_vec)
    lax.fori_loop(0, 4, mid_back, 0)
    def down():
        for i in range(8):
            yield 87 + i
            partial_rows[:, tile(i, 256)] = lax.dot_general(
                hidden_low[...], w_ffn[tile(i, 256), 512:1024], NT, preferred_element_type=F32
            ).astype(BF)

    run_flows_but(
        weights,
        Flow(
            gather_flow(
                net, low_rows, gather_slot(net, branch_all, 64, "z", "f"), "z", "f", local.at[0], True, True, 86, 5.5
            )
        ),
        Flow(down()),
    )
    store = pltpu.make_async_copy(partial_rows, ffn_part, local.at[8])
    store.start()

    def attn_back(i, carry):
        at = tile(i)
        upstream = jnp.dot(branch_all[at, :], out_w[...], preferred_element_type=F32)
        normal_rows = normal_attn[at, :]
        scaled = upstream * head_gain
        activated[at, 0:128] = scaled
        put_sums(sent_c, i, scaled, scaled * normal_rows)
        return (
            carry[0] + jnp.sum(upstream * normal_rows, axis=0, keepdims=True),
            carry[1] + jnp.sum(upstream, axis=0, keepdims=True),
        )

    sums = lax.fori_loop(0, 8, attn_back, (jnp.zeros((1, 128), F32),) * 2, unroll=2)
    for k in range(2):
        head_vec[k : k + 1, :] = sums[k]
    exchange(sent_c, stats_c)
    totals = jnp.sum(stats_c[...], axis=0) / 2048
    put_rows(rows_c, totals[0:8], totals[8:16])

    def heads_back(i, carry):
        at = tile(i)
        columns = columns_of(rows_c, i)
        scale = columns_of(rows_a, i)[:, 1:2]
        grad_att[at, :] = (
            scale
            * (activated[at, 0:128] - columns[:, 0:1] - normal_attn[at, :] * columns[:, 1:2])
        ).astype(BF)
        pre_turned[0:128, at] = attn_low[at, :].T
        return carry

    lax.fori_loop(0, 8, heads_back, 0, unroll=2)

    def out_terms(i, carry):
        out_term[:, tile(i, 256)] = jnp.dot(
            pre_turned[0:128, :], branch_all[:, tile(i, 256)], preferred_element_type=F32
        ).astype(BF)
        return carry

    lax.fori_loop(0, 8, out_terms, 0)
    run_until(weights)
    store.wait()
    net.finish()


def middle(number, *args):
    wide = pltpu.VMEM((1024, 512), F32)
    low = pltpu.VMEM((1024, 512), BF)
    tall = pltpu.VMEM((512, 1024), BF)
    whole = pltpu.VMEM((1024, 2048), BF)
    return comm_call(
        middle_kernel,
        "middle",
        number,
        15 * 3 + 20 * 4 + 14 * 2,
        12,
        (
            sds((64, 2048), F32),
            sds((64, 2048), F32),
            sds((1024, 2048), BF),
            sds((1024, 128), BF),
            sds((1024, 256), F32),
            sds((128, 2048), BF),
            sds((8, 512), F32),
            sds((8, 128), F32),
            sds((8, 2048), F32),
        ),
        [
            whole,
            pltpu.VMEM((2048, 128), BF),
            pltpu.VMEM((2048, 1024), BF),
            whole,
            whole,
            low,
            low,
            tall,
            tall,
            pltpu.VMEM((1024, 128), BF),
            pltpu.VMEM((64, 2048), BF),
            whole,
            pltpu.VMEM((8, 64, 2048), BF),
            pltpu.VMEM((7, 64, 2048), BF),
            pltpu.VMEM((8, 64, 2048), BF),
            pltpu.VMEM((8, 1024, 256), BF),
            pltpu.VMEM((7, 1024, 256), BF),
            wide,
            wide,
            wide,
            pltpu.VMEM((1024, 128), F32),
            pltpu.VMEM((64, 2048), F32),
            pltpu.VMEM((64, 128), F32),
            pltpu.VMEM((16, 128), F32),
            pltpu.VMEM((16, 16, 128), F32),
            pltpu.VMEM((8, 8, 128), F32),
            pltpu.VMEM((32, 128), F32),
            pltpu.VMEM((16, 32, 128), F32),
            pltpu.VMEM((8, 8, 128), F32),
            pltpu.VMEM((16, 128), F32),
            pltpu.VMEM((16, 16, 128), F32),
            pltpu.VMEM((8, 8, 128), F32),
        ],
        [VMEM] + [ANY] * 3 + [VMEM] * 7,
        (VMEM, VMEM, ANY) + (VMEM,) * 6,
        *args,
    )


def tail_kernel(
    kv_part,
    ffn_part,
    ffn_grad,
    query_grad,
    cosine,
    sine,
    growth,
    w_attn_in,
    in_low_in,
    out_term,
    mid,
    grad_mid,
    input_rows,
    b_down,
    gains,
    hid_vec,
    head_vec,
    row_vec,
    out_half,
    in_half,
    attn_got,
    ffn_got,
    vectors,
    send,
    recv,
    local,
    kv_mine,
    kv_landed,
    kv_grad,
    f_mine,
    f_landed,
    f_other,
    i_mine,
    i_landed,
    i_other,
    w_mine,
    w_landed,
    w_grad,
    w_rows,
    attn_rows,
    ffn_rows,
    out_rows,
    in_rows,
    grad_qkv,
    turned,
    partial_rows,
    w_attn,
    in_low,
    row_parts,
    row_got,
    packed,
    packed_got,
):
    net = Net(send, recv)
    me = net.place({}, "z", "c", "f")
    here = net.place({}, "z", "c")
    f = net.at["f"]
    load_w = pltpu.make_async_copy(w_attn_in, w_attn, local.at[16])
    load_w.start()
    load_in = pltpu.make_async_copy(in_low_in, in_low, local.at[21])
    load_in.start()
    net.greet(ALL_G, ALL_T)

    def to_halves(source, target, k):
        rows = target.at[pl.ds(pl.multiple_of(f * 64, 64), 64)]
        theirs = source.at[:, pl.ds(pl.multiple_of((1 - f) * 1024, 1024), 1024)]
        own = source.at[:, pl.ds(pl.multiple_of(f * 1024, 1024), 1024)]
        copy = net.push(theirs, rows, {"f": 1})
        keep = pltpu.make_async_copy(own, rows, local.at[k])
        keep.start()
        return copy, keep

    def to_rows(source, got, k):
        copies = []
        for offset in ALL_ZC:
            at = net.place(offset, "z", "c")
            copies.append(
                net.push(source.at[pl.ds(pl.multiple_of(at * 32, 32), 32)], got.at[here], offset)
            )
        keep = pltpu.make_async_copy(
            source.at[pl.ds(pl.multiple_of(here * 32, 32), 32)], got.at[here], local.at[k]
        )
        keep.start()
        return copies, keep

    def ffn_weights():
        def turn(i, carry):
            for j in range(2):
                block = ffn_grad[tile(i), j * 128 : j * 128 + 128].T
                w_rows[j * 128 : j * 128 + 128, tile(i)] = block.astype(BF)
            return carry

        lax.fori_loop(0, 8, turn, 0)
        yield to_rows(w_rows, ffn_got, 17)

    kv_flow = Flow(
        scatter_flow(
            net,
            scatter_chunk(net, kv_part, "x"),
            kv_grad,
            kv_mine,
            None,
            kv_landed,
            local.at[pl.ds(0, 8)],
            "x",
            "h",
            False,
            False,
            0,
            11,
        )
    )
    ffn_flow = Flow(
        scatter_flow(
            net,
            scatter_chunk(net, ffn_part, "z"),
            ffn_rows,
            f_mine,
            f_other,
            f_landed,
            local.at[pl.ds(8, 8)],
            "z",
            "f",
            True,
            True,
            4,
            7,
        )
    )
    kv_flow.step()
    ffn_flow.step()
    ffn_copies, ffn_keep = next(ffn_weights())
    run_until(kv_flow, ffn_flow)
    run_until(ffn_flow)

    def finish_rows(i, carry):
        at = tile(i, 16)
        out_rows[at, :] = mid[at, :] + (ffn_rows[at, :] + b_down[...])
        return carry

    lax.fori_loop(0, 4, finish_rows, 0)
    out_copy, out_keep = to_halves(out_rows, out_half, 18)

    def unrotate(i, carry):
        at = tile(i)
        cos, sin, grow = cosine[at, :], sine[at, :], growth[at, :]
        queries = query_grad[at, :] * grow
        queries = (queries * cos - turn_halves(queries) * sin).astype(BF)
        keys = kv_grad[at, 0:128] / grow
        keys = (keys * cos - turn_halves(keys) * sin).astype(BF)
        values = kv_grad[at, 128:256].astype(BF)
        grad_qkv[at, 0:128] = queries
        grad_qkv[at, 128:256] = keys
        grad_qkv[at, 256:384] = values
        return tuple(
            total + jnp.sum(part.astype(F32), axis=0, keepdims=True)
            for total, part in zip(carry, (queries, keys, values))
        )

    bias = lax.fori_loop(0, 8, unrotate, (jnp.zeros((1, 128), F32),) * 3)
    for k in range(3):
        packed[8 + k : 9 + k, :] = bias[k]
    load_w.wait()

    def project(i, carry):
        partial_rows[:, tile(i, 256)] = lax.dot_general(
            grad_qkv[...], w_attn[tile(i, 256), 0:384], NT, preferred_element_type=F32
        ).astype(BF)
        return carry

    lax.fori_loop(0, 8, project, 0)

    def chunk(offset):
        at = net.place(offset, "z", "c", "f")
        return partial_rows.at[pl.ds(pl.multiple_of(at * 64, 64), 64)]

    def weight_scatter():
        def turn_grads(i, carry):
            turned[:, tile(i)] = grad_qkv[tile(i), :].T
            return carry

        yield 0.6
        lax.fori_loop(0, 8, turn_grads, 0)
        load_in.wait()
        for k, (i, j) in enumerate(ROOTS):
            yield 1 + k
            columns = tile(net.place({"x": i, "h": j}, "x", "h"), 256)
            w_mine[k, 0:384, :] = jnp.dot(
                turned[...], in_low[:, columns], preferred_element_type=F32
            ).astype(BF)
            w_mine[k, 384:512, :] = out_term[:, columns]
        yield from scatter_flow(
            net, None, w_grad, w_mine, None, w_landed, None, "x", "h", False, False, 5, 5.5
        )

    in_flow = Flow(
        scatter_flow(net, chunk, in_rows, i_mine, i_other, i_landed, local, "z", "f", True, False, 0, 5.5)
    )
    w_flow = Flow(weight_scatter())
    run_until(in_flow, w_flow)

    def in_back(i, carry):
        at = tile(i, 16)
        rows = input_rows[at, :].astype(F32)
        centered = rows - jnp.mean(rows, axis=1, keepdims=True)
        scale = lax.rsqrt(jnp.mean(centered * centered, axis=1, keepdims=True) + EPS)
        normal_rows = centered * scale
        upstream = in_rows[at, :]
        scaled = upstream * gains[0:1, :]
        mean = jnp.mean(scaled, axis=1, keepdims=True)
        cross = jnp.mean(scaled * normal_rows, axis=1, keepdims=True)
        in_rows[at, :] = grad_mid[at, :] + scale * (scaled - mean - normal_rows * cross)
        return (
            carry[0] + jnp.sum(upstream * normal_rows, axis=0, keepdims=True),
            carry[1] + jnp.sum(upstream, axis=0, keepdims=True),
        )

    sums = lax.fori_loop(0, 4, in_back, (jnp.zeros((1, 2048), F32),) * 2)
    in_copy, in_keep = to_halves(in_rows, in_half, 19)
    run_until(w_flow)

    def turn_weights(i, carry):
        for j in range(2):
            w_grad_rows = w_grad[tile(i), j * 128 : j * 128 + 128].T
            attn_rows[j * 128 : j * 128 + 128, tile(i)] = w_grad_rows
        return carry

    for g in range(16):
        at = slice(g * 128, g * 128 + 128)
        for k in range(2):
            row_parts[g, k : k + 1, :] = sums[k][:, at]
        row_parts[g, 2:6, :] = row_vec[0:4, at]
        row_parts[g, 6:8, :] = jnp.zeros((2, 128), F32)
    copies = []
    for k, offset in enumerate(ALL_G):
        to = net.place(offset, "z", "c", "f")
        copies.append(net.push(row_parts.at[to], row_got.at[k], offset))
    lax.fori_loop(0, 4, turn_weights, 0)
    attn_copies, attn_keep = to_rows(attn_rows, attn_got, 20)
    packed[11:13, :] = head_vec[0:2, :]
    for k in range(3):
        for j in range(4):
            at = 13 + 4 * k + j
            packed[at : at + 1, :] = hid_vec[k : k + 1, j * 128 : j * 128 + 128]
    packed[25:32, :] = jnp.zeros((7, 128), F32)
    for copy in copies:
        copy.wait_recv()
    total = row_parts[me]
    for k in range(15):
        total = total + row_got[k]
    packed[0:8, :] = total
    copies = [net.push(packed, packed_got.at[k], offset) for k, offset in enumerate(ALL_T)]
    for copy in copies:
        copy.wait_recv()
    total = packed[...]
    for k in range(7):
        total = total + packed_got[k]
    vectors[me] = total
    copies = [net.push(vectors.at[me], vectors.at[me], offset) for offset in ALL_G]
    for copy in ffn_copies + attn_copies + copies + [out_copy, in_copy]:
        copy.wait_recv()
    for keep in (ffn_keep, attn_keep, out_keep, in_keep):
        keep.wait()
    net.finish()


def tail(number, *args):
    half = sds((128, 1024), F32)
    rows = pltpu.VMEM((64, 2048), F32)
    return comm_call(
        tail_kernel,
        "tail",
        number,
        12 + 22 + 7 + 20 + 12 + 2 + 7 + 37,
        22,
        (
            half,
            half,
            sds((8, 32, 512), F32),
            sds((8, 32, 1024), BF),
            sds((16, 32, 128), F32),
        ),
        scatter_scratch(1024, 256, False)
        + [pltpu.VMEM((1024, 256), F32)]
        + scatter_scratch(64, 2048, True)
        + scatter_scratch(64, 2048, True)
        + scatter_scratch(512, 256, False)
        + [
            pltpu.VMEM((512, 256), F32),
            pltpu.VMEM((256, 1024), BF),
            pltpu.VMEM((256, 512), F32),
            rows,
            rows,
            rows,
            pltpu.VMEM((1024, 384), BF),
            pltpu.VMEM((384, 1024), BF),
            pltpu.VMEM((1024, 2048), BF),
            pltpu.VMEM((2048, 512), BF),
            pltpu.VMEM((1024, 2048), BF),
            pltpu.VMEM((16, 8, 128), F32),
            pltpu.VMEM((15, 8, 128), F32),
            pltpu.VMEM((32, 128), F32),
            pltpu.VMEM((7, 32, 128), F32),
        ],
        [ANY, ANY] + [VMEM] * 5 + [ANY, ANY] + [VMEM] * 9,
        (VMEM,) * 5,
        *args,
    )


def assemble_kernel(
    out_in,
    in_in,
    attn_got,
    ffn_got,
    sums,
    out_half,
    in_half,
    qkv_out,
    out_out,
    up_out,
    down_out,
    qkv_bias,
    gains_out,
    shifts_out,
    out_bias,
    down_bias,
    up_bias,
    hid_gain_out,
    hid_shift_out,
):
    out_half[...] = out_in[...]
    in_half[...] = in_in[...]

    def weights(i, carry):
        small, large = tile(i, 128), tile(i, 512)
        for j in range(3):
            at = pl.ds(pl.multiple_of(j * 1024 + i * 128, 128), 128)
            qkv_out[:, at] = attn_got[i, :, j * 128 : j * 128 + 128]
        out_out[:, small] = attn_got[i, :, 384:512]
        up_out[:, large] = ffn_got[i, :, 0:512].astype(F32)
        down_out[:, large] = ffn_got[i, :, 512:1024].astype(F32)
        return carry

    lax.fori_loop(0, 8, weights, 0)

    def place(g, carry):
        by_rows = pl.ds(g, 1)
        head = lax.rem(g, 2) * 8 + g // 2
        by_heads = pl.ds(head, 1)
        for k, (target, j) in enumerate(
            ((gains_out, 0), (shifts_out, 0), (gains_out, 2), (shifts_out, 2))
        ):
            target[j, by_rows, :] = sums[g, k : k + 1, :]
        out_bias[by_rows, :] = sums[g, 4:5, :]
        down_bias[by_rows, :] = sums[g, 5:6, :]
        for j in range(3):
            qkv_bias[j, by_heads, :] = sums[g, 8 + j : 9 + j, :]
        gains_out[1, by_heads, :] = sums[g, 11:12, :]
        shifts_out[1, by_heads, :] = sums[g, 12:13, :]
        for k, target in enumerate((up_bias, hid_gain_out, hid_shift_out)):
            for j in range(4):
                at = 13 + 4 * k + j
                target[pl.ds(head * 4 + j, 1), :] = sums[g, at : at + 1, :]
        return carry

    lax.fori_loop(0, 16, place, 0)


def assemble(*args):
    vector, hidden = sds((16, 128), F32), sds((64, 128), F32)
    triple = sds((3, 16, 128), F32)
    half = sds((128, 1024), F32)
    return pl.pallas_call(
        assemble_kernel,
        out_shape=(
            half,
            half,
            sds((32, 3072), F32),
            sds((32, 1024), F32),
            sds((32, 4096), F32),
            sds((32, 4096), F32),
            triple,
            triple,
            triple,
            vector,
            vector,
            hidden,
            hidden,
            hidden,
        ),
        in_specs=[VMEM] * 5,
        out_specs=(VMEM,) * 14,
        name="assemble",
        compiler_params=pltpu.CompilerParams(vmem_limit_bytes=32 << 20),
    )(*args)


def both_heads(rows, zero):
    lanes = lax.broadcasted_iota(jnp.int32, rows.shape, 1)
    return jnp.where(lanes < HEAD, rows, zero), jnp.where(lanes >= HEAD, rows, zero)


def run_rows(ref, run):
    return ref[pl.ds(pl.multiple_of(run * RUN, RUN), RUN), :]


def pair_rows(ref, run_a, run_b, dtype):
    zero = jnp.zeros((), dtype)
    a = both_heads(run_rows(ref, run_a).astype(dtype), zero)
    b = both_heads(run_rows(ref, run_b).astype(dtype), zero)
    return jnp.concatenate(a + b, axis=0)


def pair_bounds(rank_a, rank_b):
    lanes = lax.broadcasted_iota(jnp.int32, (1, 256), 1)
    rank = jnp.where(lanes < 128, rank_a, rank_b)
    last = rank * RUN + lax.rem(lanes, RUN)
    return (rank // 64) * 4096, last


def seen(chunk, low, last):
    keys = chunk * CHUNK + lax.broadcasted_iota(jnp.int32, (CHUNK, 256), 0)
    return (keys >= low) & (keys <= last)


def sort_keys(order, kv_ref, keys, values):
    def move(r, carry):
        to = pl.ds(pl.multiple_of(order[0, r] * RUN, RUN), RUN)
        rows = run_rows(kv_ref, r)
        keys[to, :] = rows[:, :128]
        values[to, :] = rows[:, 128:]
        return carry

    lax.fori_loop(0, 128, move, 0)


def flip(source, target):
    def one(i, carry):
        rows = source[pl.ds(pl.multiple_of(i * CHUNK, CHUNK), CHUNK), :]
        target[i] = rows.T
        return carry

    lax.fori_loop(0, 16, one, 0)


def chunk_rows(ref, i):
    return ref[pl.ds(pl.multiple_of(i * CHUNK, CHUNK), CHUNK), :]


def lane_heads(total):
    turned = total.T
    lanes = lax.broadcasted_iota(jnp.int32, (RUN, 128), 1)
    a = jnp.where(lanes < HEAD, turned[0:64], turned[64:128])
    b = jnp.where(lanes < HEAD, turned[128:192], turned[192:256])
    return a, b


def attend_kernel(order, q_ref, kv_ref, o_ref, lse_ref, keys, values, flipped):
    sort_keys(order, kv_ref, keys, values)
    flip(values, flipped)

    def pair(p, carry):
        run_a, run_b = order[1, 2 * p], order[1, 2 * p + 1]
        rank_a, rank_b = order[2, 2 * p], order[2, 2 * p + 1]
        queries = pair_rows(q_ref, run_a, run_b, BF)
        low, last = pair_bounds(rank_a, rank_b)

        def step(i, state):
            peak, total, mixed = state
            scores = lax.dot_general(
                chunk_rows(keys, i), queries, NT, preferred_element_type=F32
            )
            scores = jnp.where(seen(i, low, last), scores, -1e30)
            new_peak = jnp.maximum(peak, jnp.max(scores, axis=0, keepdims=True))
            weights = jnp.exp(scores - new_peak)
            shrink = jnp.exp(peak - new_peak)
            total = total * shrink + jnp.sum(weights, axis=0, keepdims=True)
            mixed = mixed * shrink + lax.dot_general(
                flipped[i], weights.astype(BF), NN, preferred_element_type=F32
            )
            return new_peak, total, mixed

        start = (
            jnp.full((1, 256), -1e20, F32),
            jnp.zeros((1, 256), F32),
            jnp.zeros((128, 256), F32),
        )
        peak, total, mixed = lax.fori_loop((rank_a // 64) * 8, rank_b // 8 + 1, step, start)
        a, b = lane_heads(mixed / total)
        o_ref[pl.ds(pl.multiple_of(run_a * RUN, RUN), RUN), :] = a
        o_ref[pl.ds(pl.multiple_of(run_b * RUN, RUN), RUN), :] = b
        lse_ref[p] = peak + jnp.log(total)
        return carry

    lax.fori_loop(0, 8, pair, 0)


def attend(order, queries, kv):
    return pl.pallas_call(
        attend_kernel,
        out_shape=(sds((1024, 128), F32), sds((8, 1, 256), F32)),
        grid_spec=pltpu.PrefetchScalarGridSpec(
            num_scalar_prefetch=1,
            grid=(1,),
            in_specs=[VMEM, VMEM],
            out_specs=(VMEM, VMEM),
            scratch_shapes=[
                pltpu.VMEM((8192, 128), BF),
                pltpu.VMEM((8192, 128), BF),
                pltpu.VMEM((16, 128, CHUNK), BF),
            ],
        ),
        name="attend",
        compiler_params=pltpu.CompilerParams(vmem_limit_bytes=48 << 20),
    )(order, queries, kv)


def attend_back_kernel(
    order, q_ref, kv_ref, g_ref, a_ref, lse_ref, dq_ref, dkv_ref, keys, values, flipped, dkeys, dvalues
):
    sort_keys(order, kv_ref, keys, values)
    flip(keys, flipped)

    def clear(i, carry):
        rows = pl.ds(pl.multiple_of(i * CHUNK, CHUNK), CHUNK)
        dkeys[rows, :] = jnp.zeros((CHUNK, 128), F32)
        dvalues[rows, :] = jnp.zeros((CHUNK, 128), F32)
        return carry

    lax.fori_loop(0, 16, clear, 0)

    def pair(p, carry):
        run_a, run_b = order[1, 2 * p], order[1, 2 * p + 1]
        rank_a, rank_b = order[2, 2 * p], order[2, 2 * p + 1]
        queries = pair_rows(q_ref, run_a, run_b, BF)
        grads = pair_rows(g_ref, run_a, run_b, BF)
        low, last = pair_bounds(rank_a, rank_b)
        product = pair_rows(g_ref, run_a, run_b, F32) * pair_rows(a_ref, run_a, run_b, F32)
        delta = lax.dot_general(
            jnp.ones((8, 128), F32),
            product,
            NT,
            preferred_element_type=F32,
            precision=lax.Precision.HIGHEST,
        )[0:1]
        log_total = lse_ref[p]

        def step(i, dq):
            rows = pl.ds(pl.multiple_of(i * CHUNK, CHUNK), CHUNK)
            scores = lax.dot_general(keys[rows, :], queries, NT, preferred_element_type=F32)
            probs = jnp.where(seen(i, low, last), jnp.exp(scores - log_total), 0.0)
            dprobs = lax.dot_general(values[rows, :], grads, NT, preferred_element_type=F32)
            dscores = (probs * (dprobs - delta)).astype(BF)
            dvalues[rows, :] += lax.dot_general(
                probs.astype(BF), grads, NN, preferred_element_type=F32
            )
            dkeys[rows, :] += lax.dot_general(dscores, queries, NN, preferred_element_type=F32)
            return dq + lax.dot_general(flipped[i], dscores, NN, preferred_element_type=F32)

        dq = lax.fori_loop(
            (rank_a // 64) * 8, rank_b // 8 + 1, step, jnp.zeros((128, 256), F32)
        )
        a, b = lane_heads(dq)
        dq_ref[pl.ds(pl.multiple_of(run_a * RUN, RUN), RUN), :] = a * 0.125
        dq_ref[pl.ds(pl.multiple_of(run_b * RUN, RUN), RUN), :] = b * 0.125
        return carry

    lax.fori_loop(0, 8, pair, 0)

    def back(r, carry):
        source = pl.ds(pl.multiple_of(order[0, r] * RUN, RUN), RUN)
        to = pl.ds(pl.multiple_of(r * RUN, RUN), RUN)
        dkv_ref[to, 0:128] = dkeys[source, :].astype(BF)
        dkv_ref[to, 128:256] = dvalues[source, :].astype(BF)
        return carry

    lax.fori_loop(0, 128, back, 0)


def attend_back(order, queries, kv, grads, attended, log_total):
    return pl.pallas_call(
        attend_back_kernel,
        out_shape=(sds((1024, 128), F32), sds((8192, 256), BF)),
        grid_spec=pltpu.PrefetchScalarGridSpec(
            num_scalar_prefetch=1,
            grid=(1,),
            in_specs=[VMEM] * 5,
            out_specs=(VMEM, VMEM),
            scratch_shapes=[
                pltpu.VMEM((8192, 128), BF),
                pltpu.VMEM((8192, 128), BF),
                pltpu.VMEM((16, 128, CHUNK), BF),
                pltpu.VMEM((8192, 128), F32),
                pltpu.VMEM((8192, 128), F32),
            ],
        ),
        name="attend_back",
        compiler_params=pltpu.CompilerParams(vmem_limit_bytes=56 << 20),
    )(order, queries, kv, grads, attended, log_total)


def lane_tables(seq_length):
    half = HEAD // 2
    indices = (np.arange(128) % half).astype(np.float32)
    inverse_freq = np.exp(-np.log(np.float32(10000.0)) * indices / np.float32(half)).astype(np.float64)
    ratios = np.log((2.0 * indices + 0.4 * HEAD) / (1.4 * HEAD)).astype(np.float64)

    def tables(places, powers):
        angles = places[:, None] * inverse_freq[None, :]
        growth = np.exp(powers[:, None] * ratios[None, :])
        return np.stack([np.cos(angles), np.sin(angles), growth]).astype(np.float32)

    runs = np.arange(64) * float(RUN)
    tokens = np.arange(RUN).astype(np.float64)
    return (
        jnp.asarray(tables(runs, (runs - seq_length // 2) / 512.0)),
        jnp.asarray(tables(tokens, tokens / 512.0)),
    )


def shards(
    layer_input,
    w_qkv,
    w_out,
    w_up,
    w_down,
    b_qkv,
    b_out,
    b_up,
    b_down,
    norm_gains,
    norm_shifts,
    hidden_gain,
    hidden_shift,
    seq_ids,
    positions,
    d_out,
):
    packed = jnp.concatenate(
        [
            w_qkv.reshape(32, 3, 8, 128).transpose(2, 0, 1, 3).reshape(8, 32, 384),
            w_out.reshape(32, 8, 128).transpose(1, 0, 2),
        ],
        axis=2,
    )
    here = lax.axis_index(SEQ) * 2
    lanes = jnp.arange(128, dtype=jnp.int32)
    ranks = seq_ids * 64 + positions // RUN
    first, second = ranks[0], ranks[RUN]
    ranks = jnp.where(lanes == here, first, jnp.where(lanes == here + 1, second, 0))
    ranks = jnp.broadcast_to(ranks.astype(F32)[None], (8, 128))
    run_tables, token_tables = lane_tables(4096)
    (
        input_rows,
        in_low,
        w_attn,
        ffn_block,
        query_low,
        kv,
        grad_all,
        cosine,
        sine,
        growth,
        order,
    ) = front(
        1,
        layer_input,
        d_out,
        packed,
        w_up,
        w_down,
        ranks,
        norm_gains,
        norm_shifts,
        b_qkv,
        run_tables,
        token_tables,
    )
    attended, log_total = attend(order, query_low, kv)
    (
        mid,
        grad_mid,
        ffn_part,
        grad_attended,
        ffn_grad,
        out_term,
        hid_vec,
        head_vec,
        row_vec,
    ) = middle(
        3,
        attended,
        w_attn,
        ffn_block,
        grad_all,
        input_rows,
        b_out.reshape(1, 2048),
        b_up.reshape(1, 8192),
        norm_gains,
        norm_shifts,
        hidden_gain.reshape(1, 8192),
        hidden_shift.reshape(1, 8192),
    )
    query_grad, kv_part = attend_back(order, query_low, kv, grad_attended, attended, log_total)
    parts = tail(
        4,
        kv_part.reshape(8, 1024, 256),
        ffn_part.reshape(16, 64, 2048),
        ffn_grad,
        query_grad,
        cosine,
        sine,
        growth,
        w_attn,
        in_low,
        out_term,
        mid,
        grad_mid,
        input_rows,
        b_down.reshape(1, 2048),
        norm_gains,
        hid_vec,
        head_vec,
        row_vec,
    )
    (
        layer_output,
        input_grad,
        qkv_grad,
        out_grad,
        up_grad,
        down_grad,
        qkv_bias,
        gains_grad,
        shifts_grad,
        out_bias,
        down_bias,
        up_bias,
        hid_gain_grad,
        hid_shift_grad,
    ) = assemble(*parts)
    return (
        layer_output,
        input_grad,
        qkv_grad.reshape(32, 3, 1024),
        out_grad,
        up_grad,
        down_grad,
        qkv_bias.reshape(3, 2048),
        out_bias.reshape(2048),
        up_bias.reshape(8192),
        down_bias.reshape(2048),
        gains_grad.reshape(3, 2048),
        shifts_grad.reshape(3, 2048),
        hid_gain_grad.reshape(8192),
        hid_shift_grad.reshape(8192),
    )


def solution(mesh):
    fine = Mesh(mesh.devices.reshape(4, 2, 4, 2, 2), SEQ + ("f",))
    both = P(SEQ, "f")
    return jax.shard_map(
        shards,
        mesh=fine,
        in_specs=(both, P(SEQ, None, "f"), both, both, both)
        + (P(),) * 8
        + (P(SEQ), P(SEQ), both),
        out_specs=(both, both, P(SEQ, None, "f"), both, both, both) + (P(),) * 8,
        check_vma=False,
    )
```

```python
import math

import jax
import jax.numpy as jnp
import numpy as np
from jax import lax
from jax.experimental import pallas as pl
from jax.experimental.pallas import tpu as pltpu
from jax.sharding import Mesh
from jax.sharding import PartitionSpec as P

SEQ = ("x", "h", "z", "c")
TOK = ("x", "h")
HEAD = 64
RUN = 64
CHUNK = 512
EPS = 1e-05
MESH = pl.DeviceIdType.MESH
BF = jnp.bfloat16
F32 = jnp.float32
DMA = pltpu.SemaphoreType.DMA
ANY = pl.BlockSpec(memory_space=pl.ANY)
VMEM = pl.BlockSpec(memory_space=pltpu.VMEM)
NT = (((1,), (1,)), ((), ()))
TN = (((0,), (0,)), ((), ()))
NN = (((1,), (0,)), ((), ()))


def sds(shape, dtype):
    return jax.ShapeDtypeStruct(shape, dtype)


AXES = {"x": 4, "h": 2, "z": 4, "c": 2, "f": 2}
RING_G, PAIR_G = "z", "f"
RING_T, PAIR_T = "x", "h"


class Net:
    def __init__(self, send, recv):
        self.send, self.recv, self.copies, self.drained = send, recv, [], 0
        self.at = {axis: lax.axis_index(axis) for axis in AXES}

    def device(self, offset):
        return {a: lax.rem(self.at[a] + d + AXES[a], AXES[a]) for a, d in offset.items()}

    def place(self, offset, *axes):
        index = 0
        for a in axes:
            d = offset.get(a, 0)
            at = lax.rem(self.at[a] + d + AXES[a], AXES[a]) if d else self.at[a]
            index = index * AXES[a] + at
        return index

    def greet(self, *groups):
        offsets = {
            tuple((a, o[a]) for a in AXES if o.get(a, 0)) for group in groups for o in group
        }
        barrier = pltpu.get_barrier_semaphore()
        for offset in sorted(offsets):
            pl.semaphore_signal(
                barrier, inc=1, device_id=self.device(dict(offset)), device_id_type=MESH
            )
        pl.semaphore_wait(barrier, len(offsets))

    def push(self, src, dst, offset):
        k = len(self.copies)
        copy = pltpu.make_async_remote_copy(
            src_ref=src,
            dst_ref=dst,
            send_sem=self.send.at[k],
            recv_sem=self.recv.at[k],
            device_id=self.device(offset),
            device_id_type=MESH,
        )
        copy.start()
        self.copies.append(copy)
        return copy

    def finish(self):
        for copy in self.copies[self.drained :]:
            copy.wait_send()
        self.drained = len(self.copies)


UP = [(i, (i + 1) % 4) for i in range(4)]
DOWN = [(i, (i + 3) % 4) for i in range(4)]
ACROSS = [(0, 1), (1, 0)]
SIBLING = {"c": 1}
NEAR_G = [{"z": 1}, {"z": 3}, {"f": 1}, SIBLING]
NEAR_T = [{"x": 1}, {"x": 3}, {"h": 1}]
ALL_T = [{"x": i, "h": j} for i in range(4) for j in range(2)][1:]
ALL_ZC = [{"z": i, "c": j} for i in range(4) for j in range(2)][1:]
ALL_G = [{"z": i, "c": j, "f": k} for i in range(4) for j in range(2) for k in range(2)][1:]


class Flow:
    def __init__(self, steps):
        self.steps = steps
        self.step()

    def step(self):
        self.time = next(self.steps, None)


def run_until(main, *others):
    while main.time is not None:
        ready = [flow for flow in (main,) + others if flow.time is not None]
        min(ready, key=lambda flow: flow.time).step()


def run_flows(*flows):
    for flow in flows:
        run_until(flow, *flows)


def run_flows_but(kept, *flows):
    for flow in flows:
        run_until(flow, kept, *flows)


def half_rows(ref, which):
    rows = ref.shape[0] // 2
    return ref.at[pl.ds(which * rows, rows)]


def gather_flow(
    net, src, slot, ring, pair, local, sibling, light, at, unit, hold=0, arrived=None
):
    up, down, across = {ring: 1}, {ring: 3}, {pair: 1}
    passed = {}

    def to_sibling(ref, i, j):
        if sibling:
            passed[i, j] = net.push(ref, ref, SIBLING)

    def both_ways(ref, target):
        return [
            [net.push(half_rows(ref, k), half_rows(target, k), to) for k in order]
            for to, order in ((up, (0, 1)), (down, (1, 0)))
        ]

    def show(*places):
        if arrived is not None:
            for i in places:
                arrived({ring: i})

    def show_sibling(*places):
        if arrived is not None:
            for i in places:
                for j in range(2):
                    passed.pop((i, j)).wait_recv()
                arrived({ring: i, "c": 1})

    mine = slot({})
    from_down, from_up = both_ways(src, mine)
    if hold:
        yield at + hold
    from_across = net.push(src, mine, across)
    if sibling:
        passed[0, 0] = net.push(src, mine, SIBLING)
    here = pltpu.make_async_copy(src, mine, local)
    here.start()
    below, above, beside, far = (slot({ring: 3}), slot({ring: 1}), slot({pair: 1}), slot({ring: 2}))
    yield at + 0.5 * unit
    from_down[0].wait_recv()
    first = net.push(half_rows(below, 0), half_rows(below, 0), up)
    from_up[0].wait_recv()
    second = net.push(half_rows(above, 1), half_rows(above, 1), down)
    yield at + unit + hold
    from_across.wait_recv()
    if light:
        beside_down, beside_up = both_ways(beside, beside)
    else:
        beside_down = [net.push(beside, beside, up)]
        beside_up = [net.push(beside, beside, down)]
    to_sibling(beside, 0, 1)
    yield at + unit + hold
    from_down[1].wait_recv()
    to_sibling(below, 3, 0)
    from_up[1].wait_recv()
    to_sibling(above, 1, 0)
    here.wait()
    show(0)
    yield at + 1.5 * unit + hold
    first.wait_recv()
    if not light:
        beside_far = [net.push(half_rows(far, 0), half_rows(far, 0), across)]
    second.wait_recv()
    if not light:
        beside_far.append(net.push(half_rows(far, 1), half_rows(far, 1), across))
    to_sibling(far, 2, 0)
    show_sibling(0)
    yield at + (1.7 if light and hold else 2 if light else 2.5) * unit + hold
    below, above = slot({ring: 3, pair: 1}), slot({ring: 1, pair: 1})
    if light:
        beside_down[0].wait_recv()
        beside_far = [net.push(half_rows(below, 0), half_rows(below, 0), up)]
        beside_up[0].wait_recv()
        beside_far.append(net.push(half_rows(above, 1), half_rows(above, 1), down))
        yield at + 2.5 * unit + hold
    beside_down[-1].wait_recv()
    to_sibling(below, 3, 1)
    beside_up[-1].wait_recv()
    to_sibling(above, 1, 1)
    show(3, 1)
    yield at + (3 if light else 2.5) * unit + hold
    for copy in beside_far:
        copy.wait_recv()
    to_sibling(slot({ring: 2, pair: 1}), 2, 1)
    show_sibling(3, 1)
    show(2)
    yield at + (3 if light else 2.5) * unit + hold
    show_sibling(2)
    for copy in passed.values():
        copy.wait_recv()


def gather_rest_flow(net, blocks, slot, ring, pair, local, at, unit):
    up, down = {ring: 1}, {ring: 3}
    mine, below, above, beside = (slot(o) for o in ({}, {ring: 3}, {ring: 1}, {pair: 1}))
    beside_down = [net.push(half_rows(blocks[3], k), half_rows(beside, k), up) for k in (0, 1)]
    beside_up = [net.push(half_rows(blocks[3], k), half_rows(beside, k), down) for k in (1, 0)]
    far = [
        net.push(half_rows(blocks[1], 0), half_rows(below, 0), up),
        net.push(half_rows(blocks[2], 1), half_rows(above, 1), down),
    ]
    here = [
        pltpu.make_async_copy(block, target, local.at[k])
        for k, (block, target) in enumerate(zip(blocks, (mine, below, above, beside)))
    ]
    for copy in here:
        copy.start()
    yield at + 0.7 * unit
    below, above = slot({ring: 3, pair: 1}), slot({ring: 1, pair: 1})
    beside_down[0].wait_recv()
    far.append(net.push(half_rows(below, 0), half_rows(below, 0), up))
    beside_up[0].wait_recv()
    far.append(net.push(half_rows(above, 1), half_rows(above, 1), down))
    yield at + 2.1 * unit
    for copy in far + beside_down[1:] + beside_up[1:]:
        copy.wait_recv()
    for copy in here:
        copy.wait()


def add_into(target, *sources):
    rows = min(32768 // target.shape[1], target.shape[0])

    def step(i, carry):
        at = pl.ds(pl.multiple_of(i * rows, rows), rows)
        total = target[at, :].astype(F32)
        for source in sources:
            total = total + source[at, :].astype(F32)
        target[at, :] = total.astype(target.dtype)
        return carry

    lax.fori_loop(0, target.shape[0] // rows, step, 0)


ROOTS = ((2, 1), (1, 1), (3, 1), (2, 0), (1, 0), (3, 0), (0, 1), (0, 0))


def scatter_flow(
    net, chunk, out, mine, other, landed, local, ring, pair, sibling, light, at, unit, last=True
):
    up, down, across = {ring: 1}, {ring: 3}, {pair: 1}
    loads, shared = [], []
    for k, (i, j) in enumerate(ROOTS):
        if sibling:
            shared.append(net.push(chunk({ring: i, pair: j, "c": 1}), other.at[k], SIBLING))
        if chunk is not None:
            load = pltpu.make_async_copy(chunk({ring: i, pair: j}), mine.at[k], local.at[k])
            load.start()
            loads.append(load)

    def ready(k):
        if chunk is not None:
            loads[k].wait()
        if sibling:
            shared[k].wait_recv()
            add_into(mine.at[k], other.at[k])

    def halves(k, to):
        return (
            net.push(half_rows(mine.at[k], 0), half_rows(landed.at[to], 0), down),
            net.push(half_rows(mine.at[k], 1), half_rows(landed.at[to], 1), up),
        )

    def add_half(k, source, which):
        add_into(half_rows(mine.at[k], which), half_rows(landed.at[source], which))

    def send_half(k, to, which, offset):
        return net.push(half_rows(mine.at[k], which), half_rows(landed.at[to], which), offset)

    if chunk is not None:
        yield at + 0.5
    ready(0)
    if light:
        beside_first, beside_second = halves(0, 0)
        ready(3)
        first, second = halves(3, 3)
        ready(2)
        beside_up = [send_half(2, 2, 1, down)]
        ready(1)
        beside_down = [send_half(1, 1, 0, up)]
        yield at + 0.5 * unit
        beside_first.wait_recv()
        add_half(2, 0, 0)
        beside_up.append(send_half(2, 2, 0, down))
        beside_second.wait_recv()
        add_half(1, 0, 1)
        beside_down.append(send_half(1, 1, 1, up))
    else:
        beside_far = [send_half(0, 0, k, across) for k in range(2)]
        ready(1)
        beside_down = [net.push(mine.at[1], landed.at[1], up)]
        ready(2)
        beside_up = [net.push(mine.at[2], landed.at[2], down)]
        ready(3)
        yield at + 0.6 * unit
        beside_far[0].wait_recv()
        add_half(3, 0, 0)
        first = send_half(3, 3, 0, down)
        yield at + unit
        beside_far[1].wait_recv()
        add_half(3, 0, 1)
        second = send_half(3, 3, 1, up)
    ready(5)
    ready(4)
    if last:
        from_up = [send_half(5, 5, 1, down)]
        from_down = [send_half(4, 6, 0, up)]
    if not light:
        ready(6)
        yield at + 1.1 * unit
        for copy in beside_down + beside_up:
            copy.wait_recv()
        add_into(mine.at[6], landed.at[1], landed.at[2])
        if last:
            from_across = net.push(mine.at[6], landed.at[4], across)
    yield at + (1.1 if light else 1.6) * unit
    first.wait_recv()
    add_half(5, 3, 0)
    if last:
        from_up.append(send_half(5, 5, 0, down))
    yield at + (1.1 if light else 1.8) * unit
    second.wait_recv()
    add_half(4, 3, 1)
    if not last:
        return
    from_down.append(send_half(4, 6, 1, up))
    if light:
        ready(6)
        yield at + 2 * unit
        for copy in beside_down + beside_up:
            copy.wait_recv()
        add_into(mine.at[6], landed.at[1], landed.at[2])
        from_across = net.push(mine.at[6], landed.at[4], across)
    ready(7)
    yield at + (3 if light else 2.5) * unit
    for copy in from_up + from_down + [from_across]:
        copy.wait_recv()
    rows = 32768 // out.shape[1]

    def total(i, carry):
        at = pl.ds(pl.multiple_of(i * rows, rows), rows)
        value = mine[7, at, :].astype(F32) + landed[4, at, :].astype(F32)
        out[at, :] = value + (landed[5, at, :].astype(F32) + landed[6, at, :].astype(F32))
        return carry

    lax.fori_loop(0, out.shape[0] // rows, total, 0)


def gather_slot(net, out, rows, ring, pair):
    order = ("z", "c", "f") if ring == "z" else ("x", "h")

    def slot(offset):
        at = net.place(offset, *order)
        return out.at[pl.ds(pl.multiple_of(at * rows, rows), rows)]

    return slot


def input_slot(net, out):
    def slot(offset):
        row = pl.multiple_of(net.place(offset, "z", "c") * 128, 128)
        column = pl.multiple_of(net.place(offset, "f") * 1024, 1024)
        return out.at[pl.ds(row, 128), pl.ds(column, 1024)]

    return slot


def scatter_chunk(net, ref, ring):
    order = ("z", "c", "f") if ring == "z" else ("x", "h")
    return lambda offset: ref.at[net.place(offset, *order)]


def comm_call(kernel, name, number, pushes, locals_, out_shape, scratch, in_specs, out_specs, *args):
    return pl.pallas_call(
        kernel,
        out_shape=out_shape,
        in_specs=in_specs,
        out_specs=out_specs,
        scratch_shapes=[DMA((pushes,)), DMA((pushes,)), DMA((locals_,))] + scratch,
        name=name,
        compiler_params=pltpu.CompilerParams(
            collective_id=number, has_side_effects=True, vmem_limit_bytes=60 << 20
        ),
    )(*args)


def scatter_scratch(rows, width, sibling):
    shapes = [pltpu.VMEM((8, rows, width), BF), pltpu.VMEM((7, rows, width), BF)]
    return shapes + ([pltpu.VMEM((8, rows, width), BF)] if sibling else [])


def turn_halves(values):
    lanes = lax.broadcasted_iota(jnp.int32, values.shape, 1)
    first = lax.rem(lanes, HEAD) < HEAD // 2
    return jnp.where(first, pltpu.roll(values, 96, axis=1), pltpu.roll(values, 32, axis=1))


def front_kernel(
    x_ref,
    d_ref,
    w_ref,
    up_ref,
    down_ref,
    rank_ref,
    gains,
    shifts,
    bias,
    run_tables,
    token_tables,
    rows_out,
    low_out,
    w_out,
    ffn_out,
    q_out,
    kv_out,
    grad_out,
    cosine,
    sine,
    growth,
    order,
    send,
    recv,
    local,
    x_all,
    in_low,
    w_all,
    blocks,
    near,
    near_sum,
    far,
    kv_here,
):
    net = Net(send, recv)
    net.greet(NEAR_G, ALL_ZC, ALL_T)
    me = net.place({}, "z", "c")
    group = net.place({}, "x", "h")
    f = net.at["f"]
    rows = pl.ds(pl.multiple_of(me * 32, 32), 32)
    stores = []

    def store(src, dst, k):
        copy = pltpu.make_async_copy(src, dst, local.at[k])
        copy.start()
        stores.append(copy)

    def norm_block(offset):
        first = net.place(offset, "z", "c") * 128

        def norm_rows(i, carry):
            at = pl.ds(pl.multiple_of(first + i * 16, 16), 16)
            values = x_all[at, :].astype(F32)
            centered = values - jnp.mean(values, axis=1, keepdims=True)
            scale = lax.rsqrt(jnp.mean(centered * centered, axis=1, keepdims=True) + EPS)
            in_low[at, :] = (centered * scale * gains[0:1, :] + shifts[0:1, :]).astype(BF)
            return carry

        lax.fori_loop(0, 8, norm_rows, 0, unroll=4)

    def activations():
        yield from gather_flow(
            net, x_ref, input_slot(net, x_all), "z", "f", local.at[0], True, True, 0, 5.5, 0, norm_block
        )
        ffn_sent = []
        for offset in ALL_ZC:
            to = net.place(offset, "z", "c")
            at = pl.ds(pl.multiple_of(to * 512, 512), 512)
            ffn_sent.append(net.push(up_ref.at[:, at], ffn_out.at[rows, pl.ds(0, 512)], offset))
            ffn_sent.append(net.push(down_ref.at[:, at], ffn_out.at[rows, pl.ds(512, 512)], offset))
        at = pl.ds(pl.multiple_of(me * 512, 512), 512)
        store(up_ref.at[:, at], ffn_out.at[rows, pl.ds(0, 512)], 4)
        store(down_ref.at[:, at], ffn_out.at[rows, pl.ds(512, 512)], 5)
        store(in_low, low_out, 6)
        store(x_all.at[pl.ds(pl.multiple_of((me * 2 + f) * 64, 64), 64)], rows_out, 7)
        yield from gather_flow(
            net, d_ref, input_slot(net, grad_out), "z", "f", local.at[1], True, True, 24, 8
        )
        for copy in ffn_sent:
            copy.wait_recv()

    def run_rank(index):
        lanes = lax.broadcasted_iota(jnp.int32, (1, 128), 1)
        return jnp.sum(jnp.where(lanes == index, near_sum[0:1, :], 0.0), axis=1, keepdims=True)

    def tables(i, carry):
        at = tile(i, RUN)
        block = run_rank(group * 16 + i)
        block = block - jnp.floor(block / 64) * 64
        mask = lax.broadcasted_iota(jnp.int32, (64, 128), 0).astype(F32) == block
        cos_a, sin_a, grow_a = (
            jnp.sum(jnp.where(mask, run_tables[k], 0.0), axis=0, keepdims=True) for k in range(3)
        )
        cos_b, sin_b, grow_b = token_tables[0], token_tables[1], token_tables[2]
        lanes = lax.broadcasted_iota(jnp.int32, (RUN, 128), 1)
        sin = sin_a * cos_b + cos_a * sin_b
        cosine[at, :] = cos_a * cos_b - sin_a * sin_b
        sine[at, :] = jnp.where(lax.rem(lanes, HEAD) < HEAD // 2, -sin, sin)
        growth[at, :] = grow_a * grow_b
        return carry

    def put_order():
        lanes = lax.broadcasted_iota(jnp.int32, (16, 128), 1)
        places = lax.broadcasted_iota(jnp.int32, (16, 128), 0)
        ranks = jnp.zeros((16, 128), F32)
        by_lane = jnp.full((16, 128), 1e9, F32)
        for k in range(16):
            rank = run_rank(group * 16 + k)
            ranks = jnp.where(places == k, rank, ranks)
            by_lane = jnp.where(lanes == k, rank, by_lane)
        slot = jnp.sum((by_lane < ranks).astype(F32), axis=1, keepdims=True)
        hit = lanes.astype(F32) == slot
        runs = jnp.sum(jnp.where(hit, places.astype(F32), 0.0), axis=0, keepdims=True)
        ranks = jnp.sum(jnp.where(hit, ranks, 0.0), axis=0, keepdims=True)
        total = jnp.sum(far[...], axis=0)[0:1]
        order[0:1, :] = total.astype(jnp.int32)
        order[1:2, :] = runs.astype(jnp.int32)
        order[2:3, :] = ranks.astype(jnp.int32)
        order[3:8, :] = jnp.zeros((5, 128), jnp.int32)

    head_at = pl.ds(pl.multiple_of(f * 1024 + me * 128, 128), 128)

    def project(i, carry):
        at = tile(i, 256)
        values = jnp.dot(in_low[at, :], w_all[:, 0:384], preferred_element_type=F32)
        queries = values[:, 0:128] + bias[0:1, head_at]
        keys = values[:, 128:256] + bias[1:2, head_at]
        cos, sin, grow = cosine[at, :], sine[at, :], growth[at, :]
        queries = ((queries * cos + turn_halves(queries) * sin) * grow).astype(BF)
        q_out[at, :] = queries * jnp.bfloat16(0.125)
        keys = (keys * cos + turn_halves(keys) * sin) * (1.0 / grow)
        kv_here[at, 0:128] = keys.astype(BF)
        kv_here[at, 128:256] = (values[:, 256:384] + bias[2:3, head_at]).astype(BF)
        return carry

    def attention():
        attn_sent, near_sent = [], []
        for offset in ALL_ZC:
            to = net.place(offset, "z", "c")
            attn_sent.append(net.push(w_ref.at[to], blocks.at[rows], offset))
        for offset in ALL_ZC:
            near_sent.append(net.push(rank_ref, near.at[me], offset))
        own = pltpu.make_async_copy(w_ref.at[me], blocks.at[rows], local.at[2])
        own.start()
        near[me] = rank_ref[...]
        own.wait()
        yield 5
        for copy in attn_sent:
            copy.wait_recv()
        weights = gather_flow(
            net, blocks, gather_slot(net, w_all, 256, "x", "h"), "x", "h", local.at[3], False, False, 6, 5.5
        )
        yield next(weights)
        for copy in near_sent:
            copy.wait_recv()
        near_sum[...] = jnp.sum(near[...], axis=0)
        far_sent = [net.push(near_sum, far.at[group], offset) for offset in ALL_T]
        far[group] = near_sum[...]
        lax.fori_loop(0, 16, tables, 0)
        yield from weights
        store(w_all, w_out, 8)
        yield 26
        lax.fori_loop(0, 4, project, 0)
        sending = gather_flow(
            net, kv_here, gather_slot(net, kv_out, 1024, "x", "h"), "x", "h", local.at[9], False, False, 29, 11
        )
        yield next(sending)
        for copy in far_sent:
            copy.wait_recv()
        put_order()
        yield from sending

    run_flows(Flow(attention()), Flow(activations()))
    for copy in stores:
        copy.wait()
    net.finish()


def front(number, *args):
    table = sds((1024, 128), F32)
    return comm_call(
        front_kernel,
        "front",
        number,
        23 * 2 + 14 + 7 * 3 + 12 * 2,
        10,
        (
            sds((64, 2048), BF),
            sds((1024, 2048), BF),
            sds((2048, 512), BF),
            sds((256, 1024), BF),
            sds((1024, 128), BF),
            sds((8192, 256), BF),
            sds((1024, 2048), BF),
            table,
            table,
            table,
            sds((8, 128), jnp.int32),
        ),
        [
            pltpu.VMEM((1024, 2048), BF),
            pltpu.VMEM((1024, 2048), BF),
            pltpu.VMEM((2048, 512), BF),
            pltpu.VMEM((256, 512), BF),
            pltpu.VMEM((8, 8, 128), F32),
            pltpu.VMEM((8, 128), F32),
            pltpu.VMEM((8, 8, 128), F32),
            pltpu.VMEM((1024, 256), BF),
        ],
        [ANY] * 5 + [VMEM] * 6,
        (ANY,) * 4 + (VMEM, ANY, ANY) + (VMEM,) * 4,
        *args,
    )


def row_sums(values):
    ones = jnp.ones((8, values.shape[1]), F32)
    return lax.dot_general(
        ones, values, NT, preferred_element_type=F32, precision=lax.Precision.HIGHEST
    )[0:1]


def put_sums(target, i, *values):
    sums = row_sums(jnp.concatenate(values, axis=0))
    for k in range(len(values)):
        target[pl.ds(8 * k + i, 1), :] = sums[:, k * 128 : k * 128 + 128]


def tile(i, rows=128):
    return pl.ds(pl.multiple_of(i * rows, rows), rows)


def columns_of(rows_ref, i):
    return rows_ref[i].T


def put_rows(rows_ref, *values):
    for k, value in enumerate(values):
        for i in range(8):
            rows_ref[i, k : k + 1, :] = value[i : i + 1]


def fold_lanes(values):
    return (values[:, 0:128] + values[:, 128:256]) + (values[:, 256:384] + values[:, 384:512])


def middle_kernel(
    att,
    w_attn,
    ffn_block,
    ffn_below,
    ffn_above,
    ffn_beside,
    grad_all_in,
    input_rows,
    b_out,
    b_up,
    gains,
    shifts,
    hid_gain,
    hid_shift,
    mid,
    grad_mid,
    ffn_part,
    grad_att,
    ffn_up,
    ffn_down,
    ffn_across,
    ffn_own,
    out_term,
    hid_vec,
    head_vec,
    row_vec,
    send,
    recv,
    local,
    grad_all,
    out_w,
    w_ffn,
    mid_low,
    branch_all,
    hidden_low,
    pre_low,
    hidden_turned,
    pre_turned,
    attn_low,
    low_rows,
    partial_rows,
    mine,
    landed,
    other,
    t_mine,
    t_landed,
    grad_hidden,
    activated,
    slope,
    normal_attn,
    normal_mid,
    scale_mid,
    sent_a,
    stats_a,
    rows_a,
    sent_b,
    stats_b,
    rows_b,
    sent_c,
    stats_c,
    rows_c,
):
    net = Net(send, recv)
    me = net.place({}, "z", "c", "f")
    load_w = pltpu.make_async_copy(w_attn.at[:, pl.ds(384, 128)], out_w, local.at[10])
    load_w.start()
    load_grad = pltpu.make_async_copy(grad_all_in, grad_all, local.at[11])
    load_grad.start()
    net.greet(ALL_G, NEAR_T)
    weights = Flow(
        gather_rest_flow(
            net,
            (ffn_block, ffn_below, ffn_above, ffn_beside),
            gather_slot(net, w_ffn, 256, "x", "h"),
            "x",
            "h",
            local.at[pl.ds(12, 4)],
            0,
            11,
        )
    )
    head_at = pl.ds(
        pl.multiple_of(net.at["f"] * 1024 + net.place({}, "z", "c") * 128, 128), 128
    )
    hidden_at = pl.ds(
        pl.multiple_of(net.at["f"] * 4096 + net.place({}, "z", "c") * 512, 512), 512
    )
    head_gain, head_shift = gains[1:2, head_at], shifts[1:2, head_at]
    gain_here, shift_here, bias_here = hid_gain[:, hidden_at], hid_shift[:, hidden_at], b_up[:, hidden_at]

    def exchange(sent, stats):
        copies = [net.push(sent, stats.at[me], offset) for offset in ALL_G]
        stats[me] = sent[...]
        for copy in copies:
            copy.wait_recv()

    def chunk(offset):
        at = net.place(offset, "z", "c", "f")
        return partial_rows.at[pl.ds(pl.multiple_of(at * 64, 64), 64)]

    def measure(i, carry):
        here = att[tile(i), :]
        centered = here - jnp.mean(here, axis=1, keepdims=True)
        put_sums(sent_a, i, here, centered * centered)
        return carry

    lax.fori_loop(0, 8, measure, 0, unroll=2)
    exchange(sent_a, stats_a)
    center = jnp.sum(stats_a[:, 0:8], axis=0) / 2048
    spread = jnp.sum(
        stats_a[:, 8:16] + 128 * jnp.square(stats_a[:, 0:8] / 128 - center[None]), axis=0
    )
    put_rows(rows_a, center, lax.rsqrt(spread / 2048 + EPS))

    def norm_heads(i, carry):
        columns = columns_of(rows_a, i)
        normal_rows = (att[tile(i), :] - columns[:, 0:1]) * columns[:, 1:2]
        normal_attn[tile(i), :] = normal_rows
        attn_low[tile(i), :] = (normal_rows * head_gain + head_shift).astype(BF)
        return carry

    lax.fori_loop(0, 8, norm_heads, 0, unroll=2)
    load_w.wait()

    def project(i, carry):
        partial_rows[:, tile(i, 256)] = lax.dot_general(
            attn_low[...], out_w[tile(i, 256), :], NT, preferred_element_type=F32
        ).astype(BF)
        return carry

    lax.fori_loop(0, 8, project, 0)
    run_until(
        Flow(scatter_flow(net, chunk, mid, mine, other, landed, local, "z", "f", True, False, 13, 5.5)),
        weights,
    )
    net.finish()

    def mid_norm(i, carry):
        at = tile(i, 16)
        rows = input_rows[at, :].astype(F32) + (mid[at, :] + b_out[...])
        mid[at, :] = rows
        centered = rows - jnp.mean(rows, axis=1, keepdims=True)
        scale = lax.rsqrt(jnp.mean(centered * centered, axis=1, keepdims=True) + EPS)
        rows = centered * scale
        normal_mid[at, :] = rows
        scale_mid[at, :] = jnp.broadcast_to(scale, (16, 128))
        low_rows[at, :] = (rows * gains[2:3, :] + shifts[2:3, :]).astype(BF)
        return carry

    lax.fori_loop(0, 4, mid_norm, 0)
    def hidden_grads():
        yield 43
        run_until(weights)
        load_grad.wait()
        for i in range(4):
            grad_hidden[tile(i, 256), :] = jnp.dot(
                grad_all[tile(i, 256), :], w_ffn[:, 512:1024], preferred_element_type=F32
            )
            yield 44

    run_flows(
        Flow(
            gather_flow(
                net, low_rows, gather_slot(net, mid_low, 64, "z", "f"), "z", "f", local.at[0], True, False, 31, 5.5
            )
        ),
        Flow(hidden_grads()),
        weights,
    )
    net.finish()

    def up(i, carry):
        at = tile(i)
        pre = jnp.dot(mid_low[at, :], w_ffn[:, 0:512], preferred_element_type=F32) + bias_here
        below = 0.5 + 0.5 * lax.erf(pre * math.sqrt(0.5))
        act = pre * below
        activated[at, :] = act
        slope[at, :] = below + pre * jnp.exp(-0.5 * pre * pre) * (1.0 / math.sqrt(2.0 * math.pi))
        centered = act - jnp.mean(act, axis=1, keepdims=True)
        scaled = grad_hidden[at, :] * gain_here
        put_sums(
            sent_b,
            i,
            fold_lanes(act),
            fold_lanes(centered * centered),
            fold_lanes(scaled),
            fold_lanes(scaled * centered),
        )
        return carry

    lax.fori_loop(0, 8, up, 0, unroll=2)
    exchange(sent_b, stats_b)
    center = jnp.sum(stats_b[:, 0:8], axis=0) / 8192
    apart = stats_b[:, 0:8] / 512 - center[None]
    spread = jnp.sum(stats_b[:, 8:16] + 512 * jnp.square(apart), axis=0)
    scale = lax.rsqrt(spread / 8192 + EPS)
    mean_back = jnp.sum(stats_b[:, 16:24], axis=0) / 8192
    cross_back = scale * jnp.sum(stats_b[:, 24:32] + apart * stats_b[:, 16:24], axis=0) / 8192
    put_rows(rows_b, center, scale, mean_back, cross_back)

    def hidden(i, carry):
        at = tile(i)
        columns = columns_of(rows_b, i)
        scale = columns[:, 1:2]
        normal_rows = (activated[at, :] - columns[:, 0:1]) * scale
        hidden_low[at, :] = (normal_rows * gain_here + shift_here).astype(BF)
        upstream = grad_hidden[at, :]
        back = scale * (upstream * gain_here - columns[:, 2:3] - normal_rows * columns[:, 3:4])
        low = (back * slope[at, :]).astype(BF)
        pre_low[at, :] = low
        return (
            carry[0] + jnp.sum(low.astype(F32), axis=0, keepdims=True),
            carry[1] + jnp.sum(upstream * normal_rows, axis=0, keepdims=True),
            carry[2] + jnp.sum(upstream, axis=0, keepdims=True),
        )

    sums = lax.fori_loop(0, 8, hidden, (jnp.zeros((1, 512), F32),) * 3)
    for k in range(3):
        hid_vec[k : k + 1, :] = sums[k]

    def project_back(i, carry):
        partial_rows[:, tile(i, 256)] = lax.dot_general(
            pre_low[...], w_ffn[tile(i, 256), 0:512], NT, preferred_element_type=F32
        ).astype(BF)
        return carry

    lax.fori_loop(0, 8, project_back, 0)

    def weight_terms():
        def turn(i, carry):
            pre_turned[:, tile(i)] = pre_low[tile(i), :].T
            hidden_turned[:, tile(i)] = hidden_low[tile(i), :].T
            return carry

        yield 69
        lax.fori_loop(0, 8, turn, 0)
        for k, (i, j) in enumerate(ROOTS):
            yield 70 + k
            columns = tile(net.place({"x": i, "h": j}, "x", "h"), 256)
            t_mine[k, 0:512, :] = jnp.dot(
                pre_turned[...], mid_low[:, columns], preferred_element_type=F32
            ).astype(BF)
            t_mine[k, 512:1024, :] = jnp.dot(
                hidden_turned[...], grad_all[:, columns], preferred_element_type=F32
            ).astype(BF)

    stores = []

    def weight_scatter():
        yield from weight_terms()
        yield from scatter_flow(
            net, None, None, t_mine, None, t_landed, local, "x", "h", False, False, 82, 11, False
        )
        for k in range(4):
            target = (ffn_up, ffn_down, ffn_across, ffn_own)[k]
            sums_store = pltpu.make_async_copy(t_mine.at[4 + k], target, local.at[16 + k])
            sums_store.start()
            stores.append(sums_store)

    weights = Flow(weight_scatter())
    run_until(
        Flow(scatter_flow(net, chunk, grad_mid, mine, other, landed, local, "z", "f", True, False, 68, 5.5)),
        weights,
    )
    net.finish()

    def mid_back(i, carry):
        at = tile(i, 16)
        upstream = grad_mid[at, :]
        normal_rows = normal_mid[at, :]
        scaled = upstream * gains[2:3, :]
        mean = jnp.mean(scaled, axis=1, keepdims=True)
        cross = jnp.mean(scaled * normal_rows, axis=1, keepdims=True)
        out_rows = grad_all[pl.ds(pl.multiple_of(me * 64 + i * 16, 16), 16), :].astype(F32)
        rows = out_rows + scale_mid[at, 0:1] * (scaled - mean - normal_rows * cross)
        grad_mid[at, :] = rows
        low = rows.astype(BF)
        low_rows[at, :] = low
        row_vec[0:1, :] += jnp.sum(upstream * normal_rows, axis=0, keepdims=True)
        row_vec[1:2, :] += jnp.sum(upstream, axis=0, keepdims=True)
        row_vec[2:3, :] += jnp.sum(low.astype(F32), axis=0, keepdims=True)
        row_vec[3:4, :] += jnp.sum(out_rows, axis=0, keepdims=True)
        return carry

    row_vec[...] = jnp.zeros_like(row_vec)
    lax.fori_loop(0, 4, mid_back, 0)
    def down():
        for i in range(8):
            yield 87 + i
            partial_rows[:, tile(i, 256)] = lax.dot_general(
                hidden_low[...], w_ffn[tile(i, 256), 512:1024], NT, preferred_element_type=F32
            ).astype(BF)

    run_flows_but(
        weights,
        Flow(
            gather_flow(
                net, low_rows, gather_slot(net, branch_all, 64, "z", "f"), "z", "f", local.at[0], True, True, 86, 5.5
            )
        ),
        Flow(down()),
    )
    store = pltpu.make_async_copy(partial_rows, ffn_part, local.at[8])
    store.start()

    def attn_back(i, carry):
        at = tile(i)
        upstream = jnp.dot(branch_all[at, :], out_w[...], preferred_element_type=F32)
        normal_rows = normal_attn[at, :]
        scaled = upstream * head_gain
        activated[at, 0:128] = scaled
        put_sums(sent_c, i, scaled, scaled * normal_rows)
        return (
            carry[0] + jnp.sum(upstream * normal_rows, axis=0, keepdims=True),
            carry[1] + jnp.sum(upstream, axis=0, keepdims=True),
        )

    sums = lax.fori_loop(0, 8, attn_back, (jnp.zeros((1, 128), F32),) * 2, unroll=2)
    for k in range(2):
        head_vec[k : k + 1, :] = sums[k]
    exchange(sent_c, stats_c)
    totals = jnp.sum(stats_c[...], axis=0) / 2048
    put_rows(rows_c, totals[0:8], totals[8:16])

    def heads_back(i, carry):
        at = tile(i)
        columns = columns_of(rows_c, i)
        scale = columns_of(rows_a, i)[:, 1:2]
        grad_att[at, :] = (
            scale
            * (activated[at, 0:128] - columns[:, 0:1] - normal_attn[at, :] * columns[:, 1:2])
        ).astype(BF)
        pre_turned[0:128, at] = attn_low[at, :].T
        return carry

    lax.fori_loop(0, 8, heads_back, 0, unroll=2)

    def out_terms(i, carry):
        out_term[:, tile(i, 256)] = jnp.dot(
            pre_turned[0:128, :], branch_all[:, tile(i, 256)], preferred_element_type=F32
        ).astype(BF)
        return carry

    lax.fori_loop(0, 8, out_terms, 0)
    run_until(weights)
    for copy in stores:
        copy.wait()
    store.wait()
    net.finish()


def middle(number, *args):
    wide = pltpu.VMEM((1024, 512), F32)
    low = pltpu.VMEM((1024, 512), BF)
    tall = pltpu.VMEM((512, 1024), BF)
    whole = pltpu.VMEM((1024, 2048), BF)
    return comm_call(
        middle_kernel,
        "middle",
        number,
        15 * 3 + 20 * 4 + 14 * 2,
        20,
        (
            sds((64, 2048), F32),
            sds((64, 2048), F32),
            sds((1024, 2048), BF),
            sds((1024, 128), BF),
            *(sds((1024, 256), BF),) * 4,
            sds((128, 2048), BF),
            sds((8, 512), F32),
            sds((8, 128), F32),
            sds((8, 2048), F32),
        ),
        [
            whole,
            pltpu.VMEM((2048, 128), BF),
            pltpu.VMEM((2048, 1024), BF),
            whole,
            whole,
            low,
            low,
            tall,
            tall,
            pltpu.VMEM((1024, 128), BF),
            pltpu.VMEM((64, 2048), BF),
            whole,
            pltpu.VMEM((8, 64, 2048), BF),
            pltpu.VMEM((7, 64, 2048), BF),
            pltpu.VMEM((8, 64, 2048), BF),
            pltpu.VMEM((8, 1024, 256), BF),
            pltpu.VMEM((7, 1024, 256), BF),
            wide,
            wide,
            wide,
            pltpu.VMEM((1024, 128), F32),
            pltpu.VMEM((64, 2048), F32),
            pltpu.VMEM((64, 128), F32),
            pltpu.VMEM((16, 128), F32),
            pltpu.VMEM((16, 16, 128), F32),
            pltpu.VMEM((8, 8, 128), F32),
            pltpu.VMEM((32, 128), F32),
            pltpu.VMEM((16, 32, 128), F32),
            pltpu.VMEM((8, 8, 128), F32),
            pltpu.VMEM((16, 128), F32),
            pltpu.VMEM((16, 16, 128), F32),
            pltpu.VMEM((8, 8, 128), F32),
        ],
        [VMEM] + [ANY] * 6 + [VMEM] * 7,
        (VMEM, VMEM, ANY, VMEM) + (ANY,) * 4 + (VMEM,) * 4,
        *args,
    )


def tail_kernel(
    kv_part,
    ffn_part,
    ffn_own,
    ffn_up,
    ffn_down,
    ffn_across,
    query_grad,
    cosine,
    sine,
    growth,
    w_attn_in,
    in_low_in,
    out_term,
    mid,
    grad_mid,
    input_rows,
    b_down,
    gains,
    hid_vec,
    head_vec,
    row_vec,
    out_half,
    in_half,
    attn_got,
    ffn_got,
    vectors,
    send,
    recv,
    local,
    kv_mine,
    kv_landed,
    kv_grad,
    f_mine,
    f_landed,
    f_other,
    i_mine,
    i_landed,
    i_other,
    w_mine,
    w_landed,
    w_grad,
    w_rows,
    attn_rows,
    ffn_rows,
    out_rows,
    in_rows,
    grad_qkv,
    turned,
    partial_rows,
    w_attn,
    in_low,
    row_parts,
    row_got,
    packed,
    packed_got,
):
    net = Net(send, recv)
    me = net.place({}, "z", "c", "f")
    here = net.place({}, "z", "c")
    f = net.at["f"]
    load_w = pltpu.make_async_copy(w_attn_in, w_attn, local.at[16])
    load_w.start()
    load_in = pltpu.make_async_copy(in_low_in, in_low, local.at[21])
    load_in.start()
    net.greet(ALL_G, ALL_T)

    def to_halves(source, target, k):
        rows = target.at[pl.ds(pl.multiple_of(f * 64, 64), 64)]
        theirs = source.at[:, pl.ds(pl.multiple_of((1 - f) * 1024, 1024), 1024)]
        own = source.at[:, pl.ds(pl.multiple_of(f * 1024, 1024), 1024)]
        copy = net.push(theirs, rows, {"f": 1})
        keep = pltpu.make_async_copy(own, rows, local.at[k])
        keep.start()
        return copy, keep

    def to_rows(source, got, k):
        copies = []
        for offset in ALL_ZC:
            at = net.place(offset, "z", "c")
            copies.append(
                net.push(source.at[pl.ds(pl.multiple_of(at * 32, 32), 32)], got.at[here], offset)
            )
        keep = pltpu.make_async_copy(
            source.at[pl.ds(pl.multiple_of(here * 32, 32), 32)], got.at[here], local.at[k]
        )
        keep.start()
        return copies, keep

    def ffn_weights():
        def turn(i, carry):
            for j in range(2):
                at = slice(j * 128, j * 128 + 128)
                block = ffn_own[tile(i), at].astype(F32) + ffn_up[tile(i), at].astype(F32)
                block = block + (ffn_down[tile(i), at].astype(F32) + ffn_across[tile(i), at].astype(F32))
                block = block.T
                w_rows[j * 128 : j * 128 + 128, tile(i)] = block.astype(BF)
            return carry

        lax.fori_loop(0, 8, turn, 0)
        yield to_rows(w_rows, ffn_got, 17)

    kv_flow = Flow(
        scatter_flow(
            net,
            scatter_chunk(net, kv_part, "x"),
            kv_grad,
            kv_mine,
            None,
            kv_landed,
            local.at[pl.ds(0, 8)],
            "x",
            "h",
            False,
            False,
            0,
            11,
        )
    )
    ffn_flow = Flow(
        scatter_flow(
            net,
            scatter_chunk(net, ffn_part, "z"),
            ffn_rows,
            f_mine,
            f_other,
            f_landed,
            local.at[pl.ds(8, 8)],
            "z",
            "f",
            True,
            True,
            4,
            7,
        )
    )
    kv_flow.step()
    ffn_flow.step()
    ffn_copies, ffn_keep = next(ffn_weights())
    run_until(kv_flow, ffn_flow)
    run_until(ffn_flow)

    def finish_rows(i, carry):
        at = tile(i, 16)
        out_rows[at, :] = mid[at, :] + (ffn_rows[at, :] + b_down[...])
        return carry

    lax.fori_loop(0, 4, finish_rows, 0)
    out_copy, out_keep = to_halves(out_rows, out_half, 18)

    def unrotate(i, carry):
        at = tile(i)
        cos, sin, grow = cosine[at, :], sine[at, :], growth[at, :]
        queries = query_grad[at, :] * grow
        queries = (queries * cos - turn_halves(queries) * sin).astype(BF)
        keys = kv_grad[at, 0:128] / grow
        keys = (keys * cos - turn_halves(keys) * sin).astype(BF)
        values = kv_grad[at, 128:256].astype(BF)
        grad_qkv[at, 0:128] = queries
        grad_qkv[at, 128:256] = keys
        grad_qkv[at, 256:384] = values
        return tuple(
            total + jnp.sum(part.astype(F32), axis=0, keepdims=True)
            for total, part in zip(carry, (queries, keys, values))
        )

    bias = lax.fori_loop(0, 8, unrotate, (jnp.zeros((1, 128), F32),) * 3)
    for k in range(3):
        packed[8 + k : 9 + k, :] = bias[k]
    load_w.wait()

    def project(i, carry):
        partial_rows[:, tile(i, 256)] = lax.dot_general(
            grad_qkv[...], w_attn[tile(i, 256), 0:384], NT, preferred_element_type=F32
        ).astype(BF)
        return carry

    lax.fori_loop(0, 8, project, 0)

    def chunk(offset):
        at = net.place(offset, "z", "c", "f")
        return partial_rows.at[pl.ds(pl.multiple_of(at * 64, 64), 64)]

    def weight_scatter():
        def turn_grads(i, carry):
            turned[:, tile(i)] = grad_qkv[tile(i), :].T
            return carry

        yield 0.6
        lax.fori_loop(0, 8, turn_grads, 0)
        load_in.wait()
        for k, (i, j) in enumerate(ROOTS):
            yield 1 + k
            columns = tile(net.place({"x": i, "h": j}, "x", "h"), 256)
            w_mine[k, 0:384, :] = jnp.dot(
                turned[...], in_low[:, columns], preferred_element_type=F32
            ).astype(BF)
            w_mine[k, 384:512, :] = out_term[:, columns]
        yield from scatter_flow(
            net, None, w_grad, w_mine, None, w_landed, None, "x", "h", False, False, 5, 5.5
        )

    in_flow = Flow(
        scatter_flow(net, chunk, in_rows, i_mine, i_other, i_landed, local, "z", "f", True, False, 0, 5.5)
    )
    w_flow = Flow(weight_scatter())
    run_until(in_flow, w_flow)

    def in_back(i, carry):
        at = tile(i, 16)
        rows = input_rows[at, :].astype(F32)
        centered = rows - jnp.mean(rows, axis=1, keepdims=True)
        scale = lax.rsqrt(jnp.mean(centered * centered, axis=1, keepdims=True) + EPS)
        normal_rows = centered * scale
        upstream = in_rows[at, :]
        scaled = upstream * gains[0:1, :]
        mean = jnp.mean(scaled, axis=1, keepdims=True)
        cross = jnp.mean(scaled * normal_rows, axis=1, keepdims=True)
        in_rows[at, :] = grad_mid[at, :] + scale * (scaled - mean - normal_rows * cross)
        return (
            carry[0] + jnp.sum(upstream * normal_rows, axis=0, keepdims=True),
            carry[1] + jnp.sum(upstream, axis=0, keepdims=True),
        )

    sums = lax.fori_loop(0, 4, in_back, (jnp.zeros((1, 2048), F32),) * 2)
    in_copy, in_keep = to_halves(in_rows, in_half, 19)
    run_until(w_flow)

    def turn_weights(i, carry):
        for j in range(2):
            w_grad_rows = w_grad[tile(i), j * 128 : j * 128 + 128].T
            attn_rows[j * 128 : j * 128 + 128, tile(i)] = w_grad_rows
        return carry

    for g in range(16):
        at = slice(g * 128, g * 128 + 128)
        for k in range(2):
            row_parts[g, k : k + 1, :] = sums[k][:, at]
        row_parts[g, 2:6, :] = row_vec[0:4, at]
        row_parts[g, 6:8, :] = jnp.zeros((2, 128), F32)
    copies = []
    for k, offset in enumerate(ALL_G):
        to = net.place(offset, "z", "c", "f")
        copies.append(net.push(row_parts.at[to], row_got.at[k], offset))
    lax.fori_loop(0, 4, turn_weights, 0)
    attn_copies, attn_keep = to_rows(attn_rows, attn_got, 20)
    packed[11:13, :] = head_vec[0:2, :]
    for k in range(3):
        for j in range(4):
            at = 13 + 4 * k + j
            packed[at : at + 1, :] = hid_vec[k : k + 1, j * 128 : j * 128 + 128]
    packed[25:32, :] = jnp.zeros((7, 128), F32)
    for copy in copies:
        copy.wait_recv()
    total = row_parts[me]
    for k in range(15):
        total = total + row_got[k]
    packed[0:8, :] = total
    copies = [net.push(packed, packed_got.at[k], offset) for k, offset in enumerate(ALL_T)]
    for copy in copies:
        copy.wait_recv()
    total = packed[...]
    for k in range(7):
        total = total + packed_got[k]
    vectors[me] = total
    copies = [net.push(vectors.at[me], vectors.at[me], offset) for offset in ALL_G]
    for copy in ffn_copies + attn_copies + copies + [out_copy, in_copy]:
        copy.wait_recv()
    for keep in (ffn_keep, attn_keep, out_keep, in_keep):
        keep.wait()
    net.finish()


def tail(number, *args):
    half = sds((128, 1024), F32)
    rows = pltpu.VMEM((64, 2048), F32)
    return comm_call(
        tail_kernel,
        "tail",
        number,
        12 + 22 + 7 + 20 + 12 + 2 + 7 + 37,
        22,
        (
            half,
            half,
            sds((8, 32, 512), F32),
            sds((8, 32, 1024), BF),
            sds((16, 32, 128), F32),
        ),
        scatter_scratch(1024, 256, False)
        + [pltpu.VMEM((1024, 256), F32)]
        + scatter_scratch(64, 2048, True)
        + scatter_scratch(64, 2048, True)
        + scatter_scratch(512, 256, False)
        + [
            pltpu.VMEM((512, 256), F32),
            pltpu.VMEM((256, 1024), BF),
            pltpu.VMEM((256, 512), F32),
            rows,
            rows,
            rows,
            pltpu.VMEM((1024, 384), BF),
            pltpu.VMEM((384, 1024), BF),
            pltpu.VMEM((1024, 2048), BF),
            pltpu.VMEM((2048, 512), BF),
            pltpu.VMEM((1024, 2048), BF),
            pltpu.VMEM((16, 8, 128), F32),
            pltpu.VMEM((15, 8, 128), F32),
            pltpu.VMEM((32, 128), F32),
            pltpu.VMEM((7, 32, 128), F32),
        ],
        [ANY, ANY] + [VMEM] * 8 + [ANY, ANY] + [VMEM] * 9,
        (VMEM,) * 5,
        *args,
    )


def assemble_kernel(
    out_in,
    in_in,
    attn_in,
    ffn_in,
    sums_in,
    out_half,
    in_half,
    qkv_out,
    out_out,
    up_out,
    down_out,
    qkv_bias,
    gains_out,
    shifts_out,
    out_bias,
    down_bias,
    up_bias,
    hid_gain_out,
    hid_shift_out,
    attn_got,
    ffn_got,
    sums,
    sems,
):
    pairs = ((out_in, out_half), (in_in, in_half), (sums_in, sums), (attn_in, attn_got), (ffn_in, ffn_got))
    copies = [pltpu.make_async_copy(a, b, sems.at[k]) for k, (a, b) in enumerate(pairs)]
    for copy in copies:
        copy.start()
    for copy in copies:
        copy.wait()

    def weights(i, carry):
        small, large = tile(i, 128), tile(i, 512)
        for j in range(3):
            at = pl.ds(pl.multiple_of(j * 1024 + i * 128, 128), 128)
            qkv_out[:, at] = attn_got[i, :, j * 128 : j * 128 + 128]
        out_out[:, small] = attn_got[i, :, 384:512]
        up_out[:, large] = ffn_got[i, :, 0:512].astype(F32)
        down_out[:, large] = ffn_got[i, :, 512:1024].astype(F32)
        return carry

    lax.fori_loop(0, 8, weights, 0)

    def place(g, carry):
        by_rows = pl.ds(g, 1)
        head = lax.rem(g, 2) * 8 + g // 2
        by_heads = pl.ds(head, 1)
        for k, (target, j) in enumerate(
            ((gains_out, 0), (shifts_out, 0), (gains_out, 2), (shifts_out, 2))
        ):
            target[j, by_rows, :] = sums[g, k : k + 1, :]
        out_bias[by_rows, :] = sums[g, 4:5, :]
        down_bias[by_rows, :] = sums[g, 5:6, :]
        for j in range(3):
            qkv_bias[j, by_heads, :] = sums[g, 8 + j : 9 + j, :]
        gains_out[1, by_heads, :] = sums[g, 11:12, :]
        shifts_out[1, by_heads, :] = sums[g, 12:13, :]
        for k, target in enumerate((up_bias, hid_gain_out, hid_shift_out)):
            for j in range(4):
                at = 13 + 4 * k + j
                target[pl.ds(head * 4 + j, 1), :] = sums[g, at : at + 1, :]
        return carry

    lax.fori_loop(0, 16, place, 0)


def assemble(*args):
    vector, hidden = sds((16, 128), F32), sds((64, 128), F32)
    triple = sds((3, 16, 128), F32)
    half = sds((128, 1024), F32)
    return pl.pallas_call(
        assemble_kernel,
        out_shape=(
            half,
            half,
            sds((32, 3072), F32),
            sds((32, 1024), F32),
            sds((32, 4096), F32),
            sds((32, 4096), F32),
            triple,
            triple,
            triple,
            vector,
            vector,
            hidden,
            hidden,
            hidden,
        ),
        in_specs=[ANY] * 5,
        out_specs=(VMEM,) * 14,
        scratch_shapes=[
            pltpu.VMEM((8, 32, 512), F32),
            pltpu.VMEM((8, 32, 1024), BF),
            pltpu.VMEM((16, 32, 128), F32),
            DMA((5,)),
        ],
        name="assemble",
        compiler_params=pltpu.CompilerParams(vmem_limit_bytes=60 << 20),
    )(*args)


def both_heads(rows, zero):
    lanes = lax.broadcasted_iota(jnp.int32, rows.shape, 1)
    return jnp.where(lanes < HEAD, rows, zero), jnp.where(lanes >= HEAD, rows, zero)


def run_rows(ref, run):
    return ref[pl.ds(pl.multiple_of(run * RUN, RUN), RUN), :]


def pair_rows(ref, run_a, run_b, dtype):
    zero = jnp.zeros((), dtype)
    a = both_heads(run_rows(ref, run_a).astype(dtype), zero)
    b = both_heads(run_rows(ref, run_b).astype(dtype), zero)
    return jnp.concatenate(a + b, axis=0)


def pair_bounds(rank_a, rank_b):
    lanes = lax.broadcasted_iota(jnp.int32, (1, 256), 1)
    rank = jnp.where(lanes < 128, rank_a, rank_b)
    last = rank * RUN + lax.rem(lanes, RUN)
    return (rank // 64) * 4096, last


def seen(chunk, low, last):
    keys = chunk * CHUNK + lax.broadcasted_iota(jnp.int32, (CHUNK, 256), 0)
    return (keys >= low) & (keys <= last)


def sort_keys(order, kv_ref, kv):
    def move(r, carry):
        target = pl.ds(pl.multiple_of(order[0, r] * RUN, RUN), RUN)
        kv[target, :] = run_rows(kv_ref, r)
        return carry

    lax.fori_loop(0, 128, move, 0, unroll=4)


def flip(kv, columns, target):
    def one(i, carry):
        target[i] = kv[tile(i, CHUNK), columns].T
        return carry

    lax.fori_loop(0, 16, one, 0, unroll=2)


def over_chunks(rank_a, rank_b, step, start):
    low = (rank_a // 64) * 8
    whole = jnp.where(rank_a // 64 == rank_b // 64, (rank_a // 8 - low) // 2, 0)

    def two(i, state):
        return step(low + 2 * i + 1, step(low + 2 * i, state, False), False)

    state = lax.fori_loop(0, whole, two, start)
    return lax.fori_loop(
        low + 2 * whole, rank_b // 8 + 1, lambda i, state: step(i, state, True), state
    )


def lane_heads(total):
    turned = total.T
    lanes = lax.broadcasted_iota(jnp.int32, (RUN, 128), 1)
    a = jnp.where(lanes < HEAD, turned[0:64], turned[64:128])
    b = jnp.where(lanes < HEAD, turned[128:192], turned[192:256])
    return a, b


def attend_kernel(order, q_ref, kv_ref, o_ref, lse_ref, kv, flipped):
    sort_keys(order, kv_ref, kv)
    flip(kv, slice(128, 256), flipped)

    def pair(p, carry):
        run_a, run_b = order[1, 2 * p], order[1, 2 * p + 1]
        rank_a, rank_b = order[2, 2 * p], order[2, 2 * p + 1]
        queries = pair_rows(q_ref, run_a, run_b, BF)
        low, last = pair_bounds(rank_a, rank_b)

        def step(i, state, masked):
            peak, total, mixed = state
            scores = lax.dot_general(
                kv[tile(i, CHUNK), 0:128], queries, NT, preferred_element_type=F32
            )
            if masked:
                scores = jnp.where(seen(i, low, last), scores, -1e30)
            new_peak = jnp.maximum(peak, jnp.max(scores, axis=0, keepdims=True))
            weights = jnp.exp(scores - new_peak)
            shrink = jnp.exp(peak - new_peak)
            total = total * shrink + jnp.sum(weights, axis=0, keepdims=True)
            mixed = mixed * shrink + lax.dot_general(
                flipped[i], weights.astype(BF), NN, preferred_element_type=F32
            )
            return new_peak, total, mixed

        start = (
            jnp.full((1, 256), -1e20, F32),
            jnp.zeros((1, 256), F32),
            jnp.zeros((128, 256), F32),
        )
        peak, total, mixed = over_chunks(rank_a, rank_b, step, start)
        a, b = lane_heads(mixed / total)
        o_ref[pl.ds(pl.multiple_of(run_a * RUN, RUN), RUN), :] = a
        o_ref[pl.ds(pl.multiple_of(run_b * RUN, RUN), RUN), :] = b
        lse_ref[p] = peak + jnp.log(total)
        return carry

    lax.fori_loop(0, 8, pair, 0)


def attend(order, queries, kv):
    return pl.pallas_call(
        attend_kernel,
        out_shape=(sds((1024, 128), F32), sds((8, 1, 256), F32)),
        grid_spec=pltpu.PrefetchScalarGridSpec(
            num_scalar_prefetch=1,
            grid=(1,),
            in_specs=[VMEM, VMEM],
            out_specs=(VMEM, VMEM),
            scratch_shapes=[
                pltpu.VMEM((8192, 256), BF),
                pltpu.VMEM((16, 128, CHUNK), BF),
            ],
        ),
        name="attend",
        cost_estimate=pl.CostEstimate(flops=30_000_000_000, bytes_accessed=20_000_000, transcendentals=0),
        compiler_params=pltpu.CompilerParams(vmem_limit_bytes=60 << 20),
    )(order, queries, kv)


def attend_back_kernel(
    order, q_ref, kv_ref, g_ref, a_ref, lse_ref, dq_ref, dkv_ref, kv, flipped, dkeys, dvalues
):
    sort_keys(order, kv_ref, kv)
    flip(kv, slice(0, 128), flipped)

    def clear(i, carry):
        dkeys[tile(i, CHUNK), :] = jnp.zeros((CHUNK, 128), F32)
        dvalues[tile(i, CHUNK), :] = jnp.zeros((CHUNK, 128), F32)
        return carry

    lax.fori_loop(0, 16, clear, 0)

    def pair(p, carry):
        run_a, run_b = order[1, 2 * p], order[1, 2 * p + 1]
        rank_a, rank_b = order[2, 2 * p], order[2, 2 * p + 1]
        queries = pair_rows(q_ref, run_a, run_b, BF)
        grads = pair_rows(g_ref, run_a, run_b, BF)
        low, last = pair_bounds(rank_a, rank_b)
        product = pair_rows(g_ref, run_a, run_b, F32) * pair_rows(a_ref, run_a, run_b, F32)
        delta = row_sums(product)
        log_total = lse_ref[p]

        def step(i, dq, masked):
            rows = tile(i, CHUNK)
            scores = lax.dot_general(kv[rows, 0:128], queries, NT, preferred_element_type=F32)
            dprobs = lax.dot_general(kv[rows, 128:256], grads, NT, preferred_element_type=F32)
            probs = jnp.exp(scores - log_total)
            if masked:
                probs = jnp.where(seen(i, low, last), probs, 0.0)
            dscores = (probs * (dprobs - delta)).astype(BF)
            dvalues[rows, :] += lax.dot_general(
                probs.astype(BF), grads, NN, preferred_element_type=F32
            )
            dkeys[rows, :] += lax.dot_general(dscores, queries, NN, preferred_element_type=F32)
            return dq + lax.dot_general(flipped[i], dscores, NN, preferred_element_type=F32)

        dq = over_chunks(rank_a, rank_b, step, jnp.zeros((128, 256), F32))
        a, b = lane_heads(dq)
        dq_ref[pl.ds(pl.multiple_of(run_a * RUN, RUN), RUN), :] = a * 0.125
        dq_ref[pl.ds(pl.multiple_of(run_b * RUN, RUN), RUN), :] = b * 0.125
        return carry

    lax.fori_loop(0, 8, pair, 0)

    def back(r, carry):
        source = pl.ds(pl.multiple_of(order[0, r] * RUN, RUN), RUN)
        to = pl.ds(pl.multiple_of(r * RUN, RUN), RUN)
        dkv_ref[to, 0:128] = dkeys[source, :].astype(BF)
        dkv_ref[to, 128:256] = dvalues[source, :].astype(BF)
        return carry

    lax.fori_loop(0, 128, back, 0, unroll=4)


def attend_back(order, queries, kv, grads, attended, log_total):
    return pl.pallas_call(
        attend_back_kernel,
        out_shape=(sds((1024, 128), F32), sds((8192, 256), BF)),
        grid_spec=pltpu.PrefetchScalarGridSpec(
            num_scalar_prefetch=1,
            grid=(1,),
            in_specs=[VMEM] * 5,
            out_specs=(VMEM, VMEM),
            scratch_shapes=[
                pltpu.VMEM((8192, 256), BF),
                pltpu.VMEM((16, 128, CHUNK), BF),
                pltpu.VMEM((8192, 128), F32),
                pltpu.VMEM((8192, 128), F32),
            ],
        ),
        name="attend_back",
        cost_estimate=pl.CostEstimate(flops=30_000_000_000, bytes_accessed=20_000_000, transcendentals=0),
        compiler_params=pltpu.CompilerParams(vmem_limit_bytes=60 << 20),
    )(order, queries, kv, grads, attended, log_total)


def lane_tables(seq_length):
    half = HEAD // 2
    indices = (np.arange(128) % half).astype(np.float32)
    inverse_freq = np.exp(-np.log(np.float32(10000.0)) * indices / np.float32(half)).astype(np.float64)
    ratios = np.log((2.0 * indices + 0.4 * HEAD) / (1.4 * HEAD)).astype(np.float64)

    def tables(places, powers):
        angles = places[:, None] * inverse_freq[None, :]
        growth = np.exp(powers[:, None] * ratios[None, :])
        return np.stack([np.cos(angles), np.sin(angles), growth]).astype(np.float32)

    runs = np.arange(64) * float(RUN)
    tokens = np.arange(RUN).astype(np.float64)
    return (
        jnp.asarray(tables(runs, (runs - seq_length // 2) / 512.0)),
        jnp.asarray(tables(tokens, tokens / 512.0)),
    )


def shards(
    layer_input,
    w_qkv,
    w_out,
    w_up,
    w_down,
    b_qkv,
    b_out,
    b_up,
    b_down,
    norm_gains,
    norm_shifts,
    hidden_gain,
    hidden_shift,
    seq_ids,
    positions,
    d_out,
):
    packed = jnp.concatenate(
        [
            w_qkv.reshape(32, 3, 8, 128).transpose(2, 0, 1, 3).reshape(8, 32, 384),
            w_out.reshape(32, 8, 128).transpose(1, 0, 2),
        ],
        axis=2,
    )
    here = lax.axis_index(SEQ) * 2
    lanes = jnp.arange(128, dtype=jnp.int32)
    ranks = seq_ids * 64 + positions // RUN
    first, second = ranks[0], ranks[RUN]
    ranks = jnp.where(lanes == here, first, jnp.where(lanes == here + 1, second, 0))
    ranks = jnp.broadcast_to(ranks.astype(F32)[None], (8, 128))
    run_tables, token_tables = lane_tables(4096)
    (
        input_rows,
        in_low,
        w_attn,
        ffn_block,
        query_low,
        kv,
        grad_all,
        cosine,
        sine,
        growth,
        order,
    ) = front(
        1,
        layer_input,
        d_out,
        packed,
        w_up,
        w_down,
        ranks,
        norm_gains,
        norm_shifts,
        b_qkv,
        run_tables,
        token_tables,
    )
    ffn_near = (
        lax.ppermute(ffn_block, "x", UP),
        lax.ppermute(ffn_block, "x", DOWN),
        lax.ppermute(ffn_block, "h", ACROSS),
    )
    attended, log_total = attend(order, query_low, kv)
    (
        mid,
        grad_mid,
        ffn_part,
        grad_attended,
        ffn_up,
        ffn_down,
        ffn_across,
        ffn_own,
        out_term,
        hid_vec,
        head_vec,
        row_vec,
    ) = middle(
        3,
        attended,
        w_attn,
        ffn_block,
        *ffn_near,
        grad_all,
        input_rows,
        b_out.reshape(1, 2048),
        b_up.reshape(1, 8192),
        norm_gains,
        norm_shifts,
        hidden_gain.reshape(1, 8192),
        hidden_shift.reshape(1, 8192),
    )
    ffn_got = (
        lax.ppermute(ffn_up, "x", UP),
        lax.ppermute(ffn_down, "x", DOWN),
        lax.ppermute(ffn_across, "h", ACROSS),
    )
    query_grad, kv_part = attend_back(order, query_low, kv, grad_attended, attended, log_total)
    parts = tail(
        4,
        kv_part.reshape(8, 1024, 256),
        ffn_part.reshape(16, 64, 2048),
        ffn_own,
        *ffn_got,
        query_grad,
        cosine,
        sine,
        growth,
        w_attn,
        in_low,
        out_term,
        mid,
        grad_mid,
        input_rows,
        b_down.reshape(1, 2048),
        norm_gains,
        hid_vec,
        head_vec,
        row_vec,
    )
    (
        layer_output,
        input_grad,
        qkv_grad,
        out_grad,
        up_grad,
        down_grad,
        qkv_bias,
        gains_grad,
        shifts_grad,
        out_bias,
        down_bias,
        up_bias,
        hid_gain_grad,
        hid_shift_grad,
    ) = assemble(*parts)
    return (
        layer_output,
        input_grad,
        qkv_grad.reshape(32, 3, 1024),
        out_grad,
        up_grad,
        down_grad,
        qkv_bias.reshape(3, 2048),
        out_bias.reshape(2048),
        up_bias.reshape(8192),
        down_bias.reshape(2048),
        gains_grad.reshape(3, 2048),
        shifts_grad.reshape(3, 2048),
        hid_gain_grad.reshape(8192),
        hid_shift_grad.reshape(8192),
    )


def solution(mesh):
    fine = Mesh(mesh.devices.reshape(4, 2, 4, 2, 2), SEQ + ("f",))
    both = P(SEQ, "f")
    return jax.shard_map(
        shards,
        mesh=fine,
        in_specs=(both, P(SEQ, None, "f"), both, both, both)
        + (P(),) * 8
        + (P(SEQ), P(SEQ), both),
        out_specs=(both, both, P(SEQ, None, "f"), both, both, both) + (P(),) * 8,
        check_vma=False,
    )
```

```python
import math

import jax
import jax.numpy as jnp
import numpy as np
from jax import lax
from jax.experimental import pallas as pl
from jax.experimental.pallas import tpu as pltpu
from jax.sharding import Mesh
from jax.sharding import PartitionSpec as P

SEQ = ("x", "h", "z", "c")
TOK = ("x", "h")
HEAD = 64
RUN = 64
CHUNK = 512
EPS = 1e-05
MESH = pl.DeviceIdType.MESH
BF = jnp.bfloat16
F32 = jnp.float32
DMA = pltpu.SemaphoreType.DMA
ANY = pl.BlockSpec(memory_space=pl.ANY)
VMEM = pl.BlockSpec(memory_space=pltpu.VMEM)
NT = (((1,), (1,)), ((), ()))
TN = (((0,), (0,)), ((), ()))
NN = (((1,), (0,)), ((), ()))


def sds(shape, dtype):
    return jax.ShapeDtypeStruct(shape, dtype)


AXES = {"x": 4, "h": 2, "z": 4, "c": 2, "f": 2}
RING_G, PAIR_G = "z", "f"
RING_T, PAIR_T = "x", "h"


class Net:
    def __init__(self, send, recv):
        self.send, self.recv, self.copies, self.drained = send, recv, [], 0
        self.at = {axis: lax.axis_index(axis) for axis in AXES}

    def device(self, offset):
        return {a: lax.rem(self.at[a] + d + AXES[a], AXES[a]) for a, d in offset.items()}

    def place(self, offset, *axes):
        index = 0
        for a in axes:
            d = offset.get(a, 0)
            at = lax.rem(self.at[a] + d + AXES[a], AXES[a]) if d else self.at[a]
            index = index * AXES[a] + at
        return index

    def greet(self, *groups):
        offsets = {
            tuple((a, o[a]) for a in AXES if o.get(a, 0)) for group in groups for o in group
        }
        barrier = pltpu.get_barrier_semaphore()
        for offset in sorted(offsets):
            pl.semaphore_signal(
                barrier, inc=1, device_id=self.device(dict(offset)), device_id_type=MESH
            )
        pl.semaphore_wait(barrier, len(offsets))

    def push(self, src, dst, offset):
        k = len(self.copies)
        copy = pltpu.make_async_remote_copy(
            src_ref=src,
            dst_ref=dst,
            send_sem=self.send.at[k],
            recv_sem=self.recv.at[k],
            device_id=self.device(offset),
            device_id_type=MESH,
        )
        copy.start()
        self.copies.append(copy)
        return copy

    def finish(self):
        for copy in self.copies[self.drained :]:
            copy.wait_send()
        self.drained = len(self.copies)


UP = [(i, (i + 1) % 4) for i in range(4)]
DOWN = [(i, (i + 3) % 4) for i in range(4)]
ACROSS = [(0, 1), (1, 0)]
SIBLING = {"c": 1}
NEAR_G = [{"z": 1}, {"z": 3}, {"f": 1}, SIBLING]
NEAR_T = [{"x": 1}, {"x": 3}, {"h": 1}]
ALL_T = [{"x": i, "h": j} for i in range(4) for j in range(2)][1:]
ALL_ZC = [{"z": i, "c": j} for i in range(4) for j in range(2)][1:]
ALL_G = [{"z": i, "c": j, "f": k} for i in range(4) for j in range(2) for k in range(2)][1:]


class Flow:
    def __init__(self, steps):
        self.steps = steps
        self.step()

    def step(self):
        self.time = next(self.steps, None)


def run_until(main, *others):
    while main.time is not None:
        ready = [flow for flow in (main,) + others if flow.time is not None]
        min(ready, key=lambda flow: flow.time).step()


def run_flows(*flows):
    for flow in flows:
        run_until(flow, *flows)


def run_flows_but(kept, *flows):
    for flow in flows:
        run_until(flow, kept, *flows)


def half_rows(ref, which):
    rows = ref.shape[0] // 2
    return ref.at[pl.ds(which * rows, rows)]


def gather_flow(
    net, src, slot, ring, pair, local, sibling, light, at, unit, hold=0, arrived=None
):
    up, down, across = {ring: 1}, {ring: 3}, {pair: 1}
    passed = {}

    def to_sibling(ref, i, j):
        if sibling:
            passed[i, j] = net.push(ref, ref, SIBLING)

    def both_ways(ref, target):
        return [
            [net.push(half_rows(ref, k), half_rows(target, k), to) for k in order]
            for to, order in ((up, (0, 1)), (down, (1, 0)))
        ]

    def show(*places):
        if arrived is not None:
            for i in places:
                arrived({ring: i})

    def show_sibling(*places):
        if arrived is not None:
            for i in places:
                for j in range(2):
                    passed.pop((i, j)).wait_recv()
                arrived({ring: i, "c": 1})

    mine = slot({})
    from_down, from_up = both_ways(src, mine)
    if hold:
        yield at + hold
    from_across = net.push(src, mine, across)
    if sibling:
        passed[0, 0] = net.push(src, mine, SIBLING)
    here = pltpu.make_async_copy(src, mine, local)
    here.start()
    below, above, beside, far = (slot({ring: 3}), slot({ring: 1}), slot({pair: 1}), slot({ring: 2}))
    yield at + 0.5 * unit
    from_down[0].wait_recv()
    first = net.push(half_rows(below, 0), half_rows(below, 0), up)
    from_up[0].wait_recv()
    second = net.push(half_rows(above, 1), half_rows(above, 1), down)
    yield at + unit + hold
    from_across.wait_recv()
    if light:
        beside_down, beside_up = both_ways(beside, beside)
    else:
        beside_down = [net.push(beside, beside, up)]
        beside_up = [net.push(beside, beside, down)]
    to_sibling(beside, 0, 1)
    yield at + unit + hold
    from_down[1].wait_recv()
    to_sibling(below, 3, 0)
    from_up[1].wait_recv()
    to_sibling(above, 1, 0)
    here.wait()
    show(0)
    yield at + 1.5 * unit + hold
    first.wait_recv()
    if not light:
        beside_far = [net.push(half_rows(far, 0), half_rows(far, 0), across)]
    second.wait_recv()
    if not light:
        beside_far.append(net.push(half_rows(far, 1), half_rows(far, 1), across))
    to_sibling(far, 2, 0)
    show_sibling(0)
    yield at + (1.7 if light and hold else 2 if light else 2.5) * unit + hold
    below, above = slot({ring: 3, pair: 1}), slot({ring: 1, pair: 1})
    if light:
        beside_down[0].wait_recv()
        beside_far = [net.push(half_rows(below, 0), half_rows(below, 0), up)]
        beside_up[0].wait_recv()
        beside_far.append(net.push(half_rows(above, 1), half_rows(above, 1), down))
        yield at + 2.5 * unit + hold
    beside_down[-1].wait_recv()
    to_sibling(below, 3, 1)
    beside_up[-1].wait_recv()
    to_sibling(above, 1, 1)
    show(3, 1)
    yield at + (3 if light else 2.5) * unit + hold
    for copy in beside_far:
        copy.wait_recv()
    to_sibling(slot({ring: 2, pair: 1}), 2, 1)
    show_sibling(3, 1)
    show(2)
    yield at + (3 if light else 2.5) * unit + hold
    show_sibling(2)
    for copy in passed.values():
        copy.wait_recv()


def gather_rest_flow(net, blocks, slot, ring, pair, local, at, unit):
    up, down = {ring: 1}, {ring: 3}
    mine, below, above, beside = (slot(o) for o in ({}, {ring: 3}, {ring: 1}, {pair: 1}))
    beside_down = [net.push(half_rows(blocks[3], k), half_rows(beside, k), up) for k in (0, 1)]
    beside_up = [net.push(half_rows(blocks[3], k), half_rows(beside, k), down) for k in (1, 0)]
    far = [
        net.push(half_rows(blocks[1], 0), half_rows(below, 0), up),
        net.push(half_rows(blocks[2], 1), half_rows(above, 1), down),
    ]
    here = [
        pltpu.make_async_copy(block, target, local.at[k])
        for k, (block, target) in enumerate(zip(blocks, (mine, below, above, beside)))
    ]
    for copy in here:
        copy.start()
    yield at + 0.7 * unit
    below, above = slot({ring: 3, pair: 1}), slot({ring: 1, pair: 1})
    beside_down[0].wait_recv()
    far.append(net.push(half_rows(below, 0), half_rows(below, 0), up))
    beside_up[0].wait_recv()
    far.append(net.push(half_rows(above, 1), half_rows(above, 1), down))
    yield at + 2.1 * unit
    for copy in far + beside_down[1:] + beside_up[1:]:
        copy.wait_recv()
    for copy in here:
        copy.wait()


def add_into(target, *sources):
    rows = min(32768 // target.shape[1], target.shape[0])

    def step(i, carry):
        at = pl.ds(pl.multiple_of(i * rows, rows), rows)
        total = target[at, :].astype(F32)
        for source in sources:
            total = total + source[at, :].astype(F32)
        target[at, :] = total.astype(target.dtype)
        return carry

    lax.fori_loop(0, target.shape[0] // rows, step, 0)


ROOTS = ((2, 1), (1, 1), (3, 1), (2, 0), (1, 0), (3, 0), (0, 1), (0, 0))


def scatter_flow(
    net, chunk, out, mine, other, landed, local, ring, pair, sibling, light, at, unit, last=True
):
    up, down, across = {ring: 1}, {ring: 3}, {pair: 1}
    loads, shared = [], []
    for k, (i, j) in enumerate(ROOTS):
        if sibling:
            shared.append(net.push(chunk({ring: i, pair: j, "c": 1}), other.at[k], SIBLING))
        if chunk is not None:
            load = pltpu.make_async_copy(chunk({ring: i, pair: j}), mine.at[k], local.at[k])
            load.start()
            loads.append(load)

    def ready(k):
        if chunk is not None:
            loads[k].wait()
        if sibling:
            shared[k].wait_recv()
            add_into(mine.at[k], other.at[k])

    def halves(k, to):
        return (
            net.push(half_rows(mine.at[k], 0), half_rows(landed.at[to], 0), down),
            net.push(half_rows(mine.at[k], 1), half_rows(landed.at[to], 1), up),
        )

    def add_half(k, source, which):
        add_into(half_rows(mine.at[k], which), half_rows(landed.at[source], which))

    def send_half(k, to, which, offset):
        return net.push(half_rows(mine.at[k], which), half_rows(landed.at[to], which), offset)

    if chunk is not None:
        yield at + 0.5
    ready(0)
    if light:
        beside_first, beside_second = halves(0, 0)
        ready(3)
        first, second = halves(3, 3)
        ready(2)
        beside_up = [send_half(2, 2, 1, down)]
        ready(1)
        beside_down = [send_half(1, 1, 0, up)]
        yield at + 0.5 * unit
        beside_first.wait_recv()
        add_half(2, 0, 0)
        beside_up.append(send_half(2, 2, 0, down))
        beside_second.wait_recv()
        add_half(1, 0, 1)
        beside_down.append(send_half(1, 1, 1, up))
    else:
        beside_far = [send_half(0, 0, k, across) for k in range(2)]
        ready(1)
        beside_down = [net.push(mine.at[1], landed.at[1], up)]
        ready(2)
        beside_up = [net.push(mine.at[2], landed.at[2], down)]
        ready(3)
        yield at + 0.6 * unit
        beside_far[0].wait_recv()
        add_half(3, 0, 0)
        first = send_half(3, 3, 0, down)
        yield at + unit
        beside_far[1].wait_recv()
        add_half(3, 0, 1)
        second = send_half(3, 3, 1, up)
    ready(5)
    ready(4)
    if last:
        from_up = [send_half(5, 5, 1, down)]
        from_down = [send_half(4, 6, 0, up)]
    if not light:
        ready(6)
        yield at + 1.1 * unit
        for copy in beside_down + beside_up:
            copy.wait_recv()
        add_into(mine.at[6], landed.at[1], landed.at[2])
        if last:
            from_across = net.push(mine.at[6], landed.at[4], across)
    yield at + (1.1 if light else 1.6) * unit
    first.wait_recv()
    add_half(5, 3, 0)
    if last:
        from_up.append(send_half(5, 5, 0, down))
    yield at + (1.1 if light else 1.8) * unit
    second.wait_recv()
    add_half(4, 3, 1)
    if not last:
        return
    from_down.append(send_half(4, 6, 1, up))
    if light:
        ready(6)
        yield at + 2 * unit
        for copy in beside_down + beside_up:
            copy.wait_recv()
        add_into(mine.at[6], landed.at[1], landed.at[2])
        from_across = net.push(mine.at[6], landed.at[4], across)
    ready(7)
    yield at + (3 if light else 2.5) * unit
    for copy in from_up + from_down + [from_across]:
        copy.wait_recv()
    rows = 32768 // out.shape[1]

    def total(i, carry):
        at = pl.ds(pl.multiple_of(i * rows, rows), rows)
        value = mine[7, at, :].astype(F32) + landed[4, at, :].astype(F32)
        out[at, :] = value + (landed[5, at, :].astype(F32) + landed[6, at, :].astype(F32))
        return carry

    lax.fori_loop(0, out.shape[0] // rows, total, 0)


def gather_slot(net, out, rows, ring, pair):
    order = ("z", "c", "f") if ring == "z" else ("x", "h")

    def slot(offset):
        at = net.place(offset, *order)
        return out.at[pl.ds(pl.multiple_of(at * rows, rows), rows)]

    return slot


def input_slot(net, out):
    def slot(offset):
        row = pl.multiple_of(net.place(offset, "z", "c") * 128, 128)
        column = pl.multiple_of(net.place(offset, "f") * 1024, 1024)
        return out.at[pl.ds(row, 128), pl.ds(column, 1024)]

    return slot


def scatter_chunk(net, ref, ring):
    order = ("z", "c", "f") if ring == "z" else ("x", "h")
    return lambda offset: ref.at[net.place(offset, *order)]


def comm_call(kernel, name, number, pushes, locals_, out_shape, scratch, in_specs, out_specs, *args):
    return pl.pallas_call(
        kernel,
        out_shape=out_shape,
        in_specs=in_specs,
        out_specs=out_specs,
        scratch_shapes=[DMA((pushes,)), DMA((pushes,)), DMA((locals_,))] + scratch,
        name=name,
        compiler_params=pltpu.CompilerParams(
            collective_id=number, has_side_effects=True, vmem_limit_bytes=60 << 20
        ),
    )(*args)


def scatter_scratch(rows, width, sibling):
    shapes = [pltpu.VMEM((8, rows, width), BF), pltpu.VMEM((7, rows, width), BF)]
    return shapes + ([pltpu.VMEM((8, rows, width), BF)] if sibling else [])


def turn_halves(values):
    lanes = lax.broadcasted_iota(jnp.int32, values.shape, 1)
    first = lax.rem(lanes, HEAD) < HEAD // 2
    return jnp.where(first, pltpu.roll(values, 96, axis=1), pltpu.roll(values, 32, axis=1))


def front_kernel(
    x_ref,
    d_ref,
    w_ref,
    up_ref,
    down_ref,
    seq_ref,
    place_ref,
    gains,
    shifts,
    bias,
    run_tables,
    token_tables,
    rows_out,
    low_out,
    w_out,
    ffn_out,
    q_out,
    kv_out,
    grad_out,
    cosine,
    sine,
    growth,
    order,
    w_norm,
    send,
    recv,
    local,
    x_all,
    in_low,
    w_all,
    blocks,
    near,
    near_sum,
    far,
    kv_here,
    norm_parts,
    norm_got,
    ranks_here,
):
    net = Net(send, recv)
    net.greet(ALL_G, ALL_T)
    me = net.place({}, "z", "c")
    group = net.place({}, "x", "h")
    f = net.at["f"]
    rows = pl.ds(pl.multiple_of(me * 32, 32), 32)
    stores = []

    def store(src, dst, k):
        copy = pltpu.make_async_copy(src, dst, local.at[k])
        copy.start()
        stores.append(copy)

    def norm_block(offset):
        first = net.place(offset, "z", "c") * 128

        def norm_rows(i, carry):
            at = pl.ds(pl.multiple_of(first + i * 16, 16), 16)
            values = x_all[at, :].astype(F32)
            centered = values - jnp.mean(values, axis=1, keepdims=True)
            scale = lax.rsqrt(jnp.mean(centered * centered, axis=1, keepdims=True) + EPS)
            in_low[at, :] = (centered * scale * gains[0:1, :] + shifts[0:1, :]).astype(BF)
            return carry

        lax.fori_loop(0, 8, norm_rows, 0, unroll=4)

    def activations():
        yield from gather_flow(
            net, x_ref, input_slot(net, x_all), "z", "f", local.at[0], True, True, 0, 5.5, 0, norm_block
        )
        ffn_sent = []
        for offset in ALL_ZC:
            to = net.place(offset, "z", "c")
            at = pl.ds(pl.multiple_of(to * 512, 512), 512)
            ffn_sent.append(net.push(up_ref.at[:, at], ffn_out.at[rows, pl.ds(0, 512)], offset))
            ffn_sent.append(net.push(down_ref.at[:, at], ffn_out.at[rows, pl.ds(512, 512)], offset))
        at = pl.ds(pl.multiple_of(me * 512, 512), 512)
        store(up_ref.at[:, at], ffn_out.at[rows, pl.ds(0, 512)], 4)
        store(down_ref.at[:, at], ffn_out.at[rows, pl.ds(512, 512)], 5)
        store(in_low, low_out, 6)
        store(x_all.at[pl.ds(pl.multiple_of((me * 2 + f) * 64, 64), 64)], rows_out, 7)
        yield from gather_flow(
            net, d_ref, input_slot(net, grad_out), "z", "f", local.at[1], True, True, 24, 8
        )
        for copy in ffn_sent:
            copy.wait_recv()

    def run_rank(index):
        lanes = lax.broadcasted_iota(jnp.int32, (1, 128), 1)
        return jnp.sum(jnp.where(lanes == index, near_sum[0:1, :], 0.0), axis=1, keepdims=True)

    def tables(i, carry):
        at = tile(i, RUN)
        block = run_rank(group * 16 + i)
        block = block - jnp.floor(block / 64) * 64
        mask = lax.broadcasted_iota(jnp.int32, (64, 128), 0).astype(F32) == block
        cos_a, sin_a, grow_a = (
            jnp.sum(jnp.where(mask, run_tables[k], 0.0), axis=0, keepdims=True) for k in range(3)
        )
        cos_b, sin_b, grow_b = token_tables[0], token_tables[1], token_tables[2]
        lanes = lax.broadcasted_iota(jnp.int32, (RUN, 128), 1)
        sin = sin_a * cos_b + cos_a * sin_b
        cosine[at, :] = cos_a * cos_b - sin_a * sin_b
        sine[at, :] = jnp.where(lax.rem(lanes, HEAD) < HEAD // 2, -sin, sin)
        growth[at, :] = grow_a * grow_b
        return carry

    def put_order():
        lanes = lax.broadcasted_iota(jnp.int32, (16, 128), 1)
        places = lax.broadcasted_iota(jnp.int32, (16, 128), 0)
        ranks = jnp.zeros((16, 128), F32)
        by_lane = jnp.full((16, 128), 1e9, F32)
        for k in range(16):
            rank = run_rank(group * 16 + k)
            ranks = jnp.where(places == k, rank, ranks)
            by_lane = jnp.where(lanes == k, rank, by_lane)
        slot = jnp.sum((by_lane < ranks).astype(F32), axis=1, keepdims=True)
        hit = lanes.astype(F32) == slot
        runs = jnp.sum(jnp.where(hit, places.astype(F32), 0.0), axis=0, keepdims=True)
        ranks = jnp.sum(jnp.where(hit, ranks, 0.0), axis=0, keepdims=True)
        total = jnp.sum(far[...], axis=0)[0:1]
        order[0:1, :] = total.astype(jnp.int32)
        order[1:2, :] = runs.astype(jnp.int32)
        order[2:3, :] = ranks.astype(jnp.int32)
        order[3:8, :] = jnp.zeros((5, 128), jnp.int32)

    head_at = pl.ds(pl.multiple_of(f * 1024 + me * 128, 128), 128)

    def project(i, carry):
        at = tile(i, 256)
        values = jnp.dot(in_low[at, :], w_all[:, 0:384], preferred_element_type=F32)
        queries = values[:, 0:128] + bias[0:1, head_at]
        keys = values[:, 128:256] + bias[1:2, head_at]
        cos, sin, grow = cosine[at, :], sine[at, :], growth[at, :]
        queries = ((queries * cos + turn_halves(queries) * sin) * grow).astype(BF)
        q_out[at, :] = queries * jnp.bfloat16(0.125)
        keys = (keys * cos + turn_halves(keys) * sin) * (1.0 / grow)
        kv_here[at, 0:128] = keys.astype(BF)
        kv_here[at, 128:256] = (values[:, 256:384] + bias[2:3, head_at]).astype(BF)
        return carry

    def put_ranks():
        lanes = lax.broadcasted_iota(jnp.int32, (1, 128), 1)
        ranks = (seq_ref[...] * 64 + place_ref[...] // RUN).astype(F32)
        first, second = (
            jnp.sum(jnp.where(lanes == k * RUN, ranks, 0.0), axis=1, keepdims=True) for k in range(2)
        )
        at = net.place({}, "x", "h", "z", "c") * 2
        row = jnp.where(lanes == at, first, jnp.where(lanes == at + 1, second, 0.0))
        ranks_here[...] = jnp.broadcast_to(row, (8, 128))

    def attention():
        attn_sent, near_sent = [], []
        put_ranks()
        for offset in ALL_ZC:
            to = net.place(offset, "z", "c")
            attn_sent.append(net.push(w_ref.at[to], blocks.at[rows], offset))
        for offset in ALL_ZC:
            near_sent.append(net.push(ranks_here, near.at[me], offset))
        own = pltpu.make_async_copy(w_ref.at[me], blocks.at[rows], local.at[2])
        own.start()
        near[me] = ranks_here[...]
        own.wait()
        yield 5
        for copy in attn_sent:
            copy.wait_recv()
        weights = gather_flow(
            net, blocks, gather_slot(net, w_all, 256, "x", "h"), "x", "h", local.at[3], False, False, 6, 5.5
        )
        yield next(weights)
        for copy in near_sent:
            copy.wait_recv()
        near_sum[...] = jnp.sum(near[...], axis=0)
        far_sent = [net.push(near_sum, far.at[group], offset) for offset in ALL_T]
        far[group] = near_sum[...]
        lax.fori_loop(0, 16, tables, 0)
        yield from weights
        store(w_all, w_out, 8)
        yield 26
        lax.fori_loop(0, 4, project, 0)
        sending = gather_flow(
            net, kv_here, gather_slot(net, kv_out, 1024, "x", "h"), "x", "h", local.at[9], False, False, 29, 11
        )
        yield next(sending)
        for copy in far_sent:
            copy.wait_recv()
        put_order()
        yield from sending

    def norm_sums():
        yield 25
        gain, shift = gains[1:2, head_at], shifts[1:2, head_at]
        high = [gain.astype(BF), shift.astype(BF)]
        low = [(v - h.astype(F32)).astype(BF) for v, h in zip((gain, shift), high)]
        vectors = jnp.concatenate(high + low + [jnp.zeros((12, 128), BF)], axis=0)

        def norm_vectors(i, carry):
            parts = lax.dot_general(
                vectors, w_all[tile(i, 128), 384:512], NT, preferred_element_type=F32
            )
            norm_parts[i] = parts[0:8] + jnp.concatenate([parts[2:8], parts[8:10]], axis=0)
            return carry

        lax.fori_loop(0, 16, norm_vectors, 0)
        mine = net.place({}, "z", "c", "f")
        sent = []
        for k, offset in enumerate(ALL_G):
            to = net.place(offset, "z", "c", "f")
            sent.append(net.push(norm_parts.at[to], norm_got.at[k], offset))
        yield 41
        for copy in sent:
            copy.wait_recv()
        w_norm[mine] = norm_parts[mine] + jnp.sum(norm_got[...], axis=0)
        sent = [net.push(w_norm.at[mine], w_norm.at[mine], offset) for offset in ALL_G]
        yield 58
        for copy in sent:
            copy.wait_recv()

    run_flows(Flow(attention()), Flow(activations()), Flow(norm_sums()))
    for copy in stores:
        copy.wait()
    net.finish()


def front(number, *args):
    table = sds((1024, 128), F32)
    return comm_call(
        front_kernel,
        "front",
        number,
        23 * 2 + 14 + 7 * 3 + 12 * 2 + 30,
        10,
        (
            sds((64, 2048), BF),
            sds((1024, 2048), BF),
            sds((2048, 512), BF),
            sds((256, 1024), BF),
            sds((1024, 128), BF),
            sds((8192, 256), BF),
            sds((1024, 2048), BF),
            table,
            table,
            table,
            sds((8, 128), jnp.int32),
            sds((16, 8, 128), F32),
        ),
        [
            pltpu.VMEM((1024, 2048), BF),
            pltpu.VMEM((1024, 2048), BF),
            pltpu.VMEM((2048, 512), BF),
            pltpu.VMEM((256, 512), BF),
            pltpu.VMEM((8, 8, 128), F32),
            pltpu.VMEM((8, 128), F32),
            pltpu.VMEM((8, 8, 128), F32),
            pltpu.VMEM((1024, 256), BF),
            pltpu.VMEM((16, 8, 128), F32),
            pltpu.VMEM((15, 8, 128), F32),
            pltpu.VMEM((8, 128), F32),
        ],
        [ANY] * 5 + [VMEM] * 7,
        (ANY,) * 4 + (VMEM, ANY, ANY) + (VMEM,) * 5,
        *args,
    )


def row_sums(values):
    ones = jnp.ones((8, values.shape[1]), F32)
    return lax.dot_general(
        ones, values, NT, preferred_element_type=F32, precision=lax.Precision.HIGHEST
    )[0:1]


def put_sums(target, i, *values):
    sums = row_sums(jnp.concatenate(values, axis=0))
    for k in range(len(values)):
        target[pl.ds(8 * k + i, 1), :] = sums[:, k * 128 : k * 128 + 128]


def tile(i, rows=128):
    return pl.ds(pl.multiple_of(i * rows, rows), rows)


def columns_of(rows_ref, i):
    return rows_ref[i].T


def put_rows(rows_ref, *values):
    for k, value in enumerate(values):
        for i in range(8):
            rows_ref[i, k : k + 1, :] = value[i : i + 1]


def fold_groups(values):
    values = values[:, 0:1024] + values[:, 1024:2048]
    return fold_lanes(values[:, 0:512] + values[:, 512:1024])


def fold_lanes(values):
    return (values[:, 0:128] + values[:, 128:256]) + (values[:, 256:384] + values[:, 384:512])


def middle_kernel(
    att,
    w_attn,
    ffn_block,
    ffn_below,
    ffn_above,
    ffn_beside,
    grad_all_in,
    input_rows,
    b_out,
    b_up,
    gains,
    shifts,
    hid_gain,
    hid_shift,
    w_norm,
    mid,
    grad_mid,
    ffn_part,
    grad_att,
    ffn_up,
    ffn_down,
    ffn_across,
    ffn_own,
    branch_out,
    turned_out,
    hid_vec,
    head_vec,
    row_vec,
    send,
    recv,
    local,
    grad_all,
    out_w,
    w_ffn,
    mid_low,
    branch_all,
    hidden_low,
    pre_low,
    hidden_turned,
    pre_turned,
    attn_low,
    low_rows,
    partial_rows,
    mine,
    landed,
    other,
    t_mine,
    t_landed,
    grad_hidden,
    activated,
    slope,
    normal_attn,
    normal_mid,
    scale_mid,
    sent_a,
    stats_a,
    rows_a,
    sent_b,
    stats_b,
    rows_b,
    sent_c,
    stats_c,
    rows_c,
    branch_rows,
    w_rows,
    folded,
):
    net = Net(send, recv)
    me = net.place({}, "z", "c", "f")
    load_w = pltpu.make_async_copy(w_attn.at[:, pl.ds(384, 128)], out_w, local.at[10])
    load_w.start()
    load_grad = pltpu.make_async_copy(grad_all_in, grad_all, local.at[11])
    load_grad.start()
    net.greet(ALL_G, NEAR_T)
    weights = Flow(
        gather_rest_flow(
            net,
            (ffn_block, ffn_below, ffn_above, ffn_beside),
            gather_slot(net, w_ffn, 256, "x", "h"),
            "x",
            "h",
            local.at[pl.ds(12, 4)],
            0,
            11,
        )
    )
    head_at = pl.ds(
        pl.multiple_of(net.at["f"] * 1024 + net.place({}, "z", "c") * 128, 128), 128
    )
    hidden_at = pl.ds(
        pl.multiple_of(net.at["f"] * 4096 + net.place({}, "z", "c") * 512, 512), 512
    )
    head_gain, head_shift = gains[1:2, head_at], shifts[1:2, head_at]
    gain_here, shift_here, bias_here = hid_gain[:, hidden_at], hid_shift[:, hidden_at], b_up[:, hidden_at]

    def exchange(sent, stats):
        copies = [net.push(sent, stats.at[me], offset) for offset in ALL_G]
        stats[me] = sent[...]
        for copy in copies:
            copy.wait_recv()

    def chunk(offset):
        at = net.place(offset, "z", "c", "f")
        return partial_rows.at[pl.ds(pl.multiple_of(at * 64, 64), 64)]

    def measure(i, carry):
        here = att[tile(i), :]
        centered = here - jnp.mean(here, axis=1, keepdims=True)
        put_sums(sent_a, i, here, centered * centered)
        return carry

    lax.fori_loop(0, 8, measure, 0, unroll=2)
    exchange(sent_a, stats_a)
    center = jnp.sum(stats_a[:, 0:8], axis=0) / 2048
    spread = jnp.sum(
        stats_a[:, 8:16] + 128 * jnp.square(stats_a[:, 0:8] / 128 - center[None]), axis=0
    )
    put_rows(rows_a, center, lax.rsqrt(spread / 2048 + EPS))

    def norm_heads(i, carry):
        columns = columns_of(rows_a, i)
        normal_rows = (att[tile(i), :] - columns[:, 0:1]) * columns[:, 1:2]
        normal_attn[tile(i), :] = normal_rows
        attn_low[tile(i), :] = (normal_rows * head_gain + head_shift).astype(BF)
        return carry

    lax.fori_loop(0, 8, norm_heads, 0, unroll=2)
    load_w.wait()

    def project(i, carry):
        partial_rows[:, tile(i, 256)] = lax.dot_general(
            attn_low[...], out_w[tile(i, 256), :], NT, preferred_element_type=F32
        ).astype(BF)
        return carry

    lax.fori_loop(0, 8, project, 0)
    run_until(
        Flow(scatter_flow(net, chunk, mid, mine, other, landed, local, "z", "f", True, False, 13, 5.5)),
        weights,
    )
    net.finish()

    def mid_norm(i, carry):
        at = tile(i, 16)
        branch_rows[at, :] = mid[at, :]
        rows = input_rows[at, :].astype(F32) + (mid[at, :] + b_out[...])
        mid[at, :] = rows
        centered = rows - jnp.mean(rows, axis=1, keepdims=True)
        scale = lax.rsqrt(jnp.mean(centered * centered, axis=1, keepdims=True) + EPS)
        rows = centered * scale
        normal_mid[at, :] = rows
        scale_mid[at, :] = jnp.broadcast_to(scale, (16, 128))
        low_rows[at, :] = (rows * gains[2:3, :] + shifts[2:3, :]).astype(BF)
        return carry

    lax.fori_loop(0, 4, mid_norm, 0)
    def hidden_grads():
        yield 43
        run_until(weights)
        load_grad.wait()
        for i in range(4):
            grad_hidden[tile(i, 256), :] = jnp.dot(
                grad_all[tile(i, 256), :], w_ffn[:, 512:1024], preferred_element_type=F32
            )
            yield 44

    run_flows(
        Flow(
            gather_flow(
                net, low_rows, gather_slot(net, mid_low, 64, "z", "f"), "z", "f", local.at[0], True, False, 31, 5.5
            )
        ),
        Flow(hidden_grads()),
        weights,
    )
    net.finish()

    def up(i, carry):
        at = tile(i)
        pre = jnp.dot(mid_low[at, :], w_ffn[:, 0:512], preferred_element_type=F32) + bias_here
        below = 0.5 + 0.5 * lax.erf(pre * math.sqrt(0.5))
        act = pre * below
        activated[at, :] = act
        slope[at, :] = below + pre * jnp.exp(-0.5 * pre * pre) * (1.0 / math.sqrt(2.0 * math.pi))
        centered = act - jnp.mean(act, axis=1, keepdims=True)
        scaled = grad_hidden[at, :] * gain_here
        put_sums(
            sent_b,
            i,
            fold_lanes(act),
            fold_lanes(centered * centered),
            fold_lanes(scaled),
            fold_lanes(scaled * centered),
        )
        return carry

    lax.fori_loop(0, 8, up, 0, unroll=2)
    exchange(sent_b, stats_b)
    center = jnp.sum(stats_b[:, 0:8], axis=0) / 8192
    apart = stats_b[:, 0:8] / 512 - center[None]
    spread = jnp.sum(stats_b[:, 8:16] + 512 * jnp.square(apart), axis=0)
    scale = lax.rsqrt(spread / 8192 + EPS)
    mean_back = jnp.sum(stats_b[:, 16:24], axis=0) / 8192
    cross_back = scale * jnp.sum(stats_b[:, 24:32] + apart * stats_b[:, 16:24], axis=0) / 8192
    put_rows(rows_b, center, scale, mean_back, cross_back)

    def hidden(i, carry):
        at = tile(i)
        columns = columns_of(rows_b, i)
        scale = columns[:, 1:2]
        normal_rows = (activated[at, :] - columns[:, 0:1]) * scale
        hidden_low[at, :] = (normal_rows * gain_here + shift_here).astype(BF)
        upstream = grad_hidden[at, :]
        back = scale * (upstream * gain_here - columns[:, 2:3] - normal_rows * columns[:, 3:4])
        low = (back * slope[at, :]).astype(BF)
        pre_low[at, :] = low
        return (
            carry[0] + jnp.sum(low.astype(F32), axis=0, keepdims=True),
            carry[1] + jnp.sum(upstream * normal_rows, axis=0, keepdims=True),
            carry[2] + jnp.sum(upstream, axis=0, keepdims=True),
        )

    sums = lax.fori_loop(0, 8, hidden, (jnp.zeros((1, 512), F32),) * 3)
    for k in range(3):
        hid_vec[k : k + 1, :] = sums[k]

    def project_back(i, carry):
        partial_rows[:, tile(i, 256)] = lax.dot_general(
            pre_low[...], w_ffn[tile(i, 256), 0:512], NT, preferred_element_type=F32
        ).astype(BF)
        return carry

    lax.fori_loop(0, 8, project_back, 0)

    def weight_terms():
        def turn(i, carry):
            pre_turned[:, tile(i)] = pre_low[tile(i), :].T
            hidden_turned[:, tile(i)] = hidden_low[tile(i), :].T
            return carry

        yield 69
        lax.fori_loop(0, 8, turn, 0)
        for k, (i, j) in enumerate(ROOTS):
            yield 70 + k
            columns = tile(net.place({"x": i, "h": j}, "x", "h"), 256)
            t_mine[k, 0:512, :] = jnp.dot(
                pre_turned[...], mid_low[:, columns], preferred_element_type=F32
            ).astype(BF)
            t_mine[k, 512:1024, :] = jnp.dot(
                hidden_turned[...], grad_all[:, columns], preferred_element_type=F32
            ).astype(BF)

    stores = []

    def weight_scatter():
        yield from weight_terms()
        yield from scatter_flow(
            net, None, None, t_mine, None, t_landed, local, "x", "h", False, False, 82, 11, False
        )
        for k in range(4):
            target = (ffn_up, ffn_down, ffn_across, ffn_own)[k]
            sums_store = pltpu.make_async_copy(t_mine.at[4 + k], target, local.at[16 + k])
            sums_store.start()
            stores.append(sums_store)

    weights = Flow(weight_scatter())
    run_until(
        Flow(scatter_flow(net, chunk, grad_mid, mine, other, landed, local, "z", "f", True, False, 68, 5.5)),
        weights,
    )
    net.finish()

    def mid_back(i, carry):
        at = tile(i, 16)
        upstream = grad_mid[at, :]
        normal_rows = normal_mid[at, :]
        scaled = upstream * gains[2:3, :]
        mean = jnp.mean(scaled, axis=1, keepdims=True)
        cross = jnp.mean(scaled * normal_rows, axis=1, keepdims=True)
        out_rows = grad_all[pl.ds(pl.multiple_of(me * 64 + i * 16, 16), 16), :].astype(F32)
        rows = out_rows + scale_mid[at, 0:1] * (scaled - mean - normal_rows * cross)
        grad_mid[at, :] = rows
        low = rows.astype(BF)
        low_rows[at, :] = low
        low = low.astype(F32)
        folded[0, at, :] = fold_groups(low * w_rows[0:1, :])
        folded[1, at, :] = fold_groups(low * (branch_rows[at, :] - w_rows[1:2, :]))
        row_vec[0:1, :] += jnp.sum(upstream * normal_rows, axis=0, keepdims=True)
        row_vec[1:2, :] += jnp.sum(upstream, axis=0, keepdims=True)
        row_vec[2:3, :] += jnp.sum(low, axis=0, keepdims=True)
        row_vec[3:4, :] += jnp.sum(out_rows, axis=0, keepdims=True)
        return carry

    row_vec[...] = jnp.zeros_like(row_vec)
    for g in range(16):
        w_rows[:, g * 128 : g * 128 + 128] = w_norm[g]
    lax.fori_loop(0, 4, mid_back, 0)
    def down():
        for i in range(8):
            yield 87 + i
            partial_rows[:, tile(i, 256)] = lax.dot_general(
                hidden_low[...], w_ffn[tile(i, 256), 512:1024], NT, preferred_element_type=F32
            ).astype(BF)

    def norm_sums():
        yield 86.5
        sums = [row_sums(folded[k]) * (1.0 / 2048) for k in range(2)]
        sent_c[...] = jnp.broadcast_to(jnp.concatenate(sums, axis=1), (8, 128))
        copies = [net.push(sent_c, stats_c.at[me], offset) for offset in ALL_G]
        stats_c[me] = sent_c[...]
        yield 99
        for copy in copies:
            copy.wait_recv()

    run_flows_but(
        weights,
        Flow(
            gather_flow(
                net, low_rows, gather_slot(net, branch_all, 64, "z", "f"), "z", "f", local.at[0], True, True, 86, 5.5
            )
        ),
        Flow(norm_sums()),
        Flow(down()),
    )
    store = pltpu.make_async_copy(partial_rows, ffn_part, local.at[8])
    store.start()

    lanes = lax.broadcasted_iota(jnp.int32, (1, 128), 1)
    for i in range(8):
        a, b = stats_c[2 * i, 0:1, :], stats_c[2 * i + 1, 0:1, :]
        rows_c[i, 0:1, :] = jnp.where(lanes < 64, a, pltpu.roll(b, 64, axis=1))
        rows_c[i, 1:2, :] = jnp.where(lanes < 64, pltpu.roll(a, 64, axis=1), b)
    keep = [
        pltpu.make_async_copy(branch_all, branch_out, local.at[20]),
        pltpu.make_async_copy(pre_turned.at[pl.ds(0, 128)], turned_out, local.at[21]),
    ]
    keep[0].start()

    def attn_back(i, carry):
        at = tile(i)
        upstream = jnp.dot(branch_all[at, :], out_w[...], preferred_element_type=F32)
        normal_rows = normal_attn[at, :]
        columns = columns_of(rows_c, i)
        scale = columns_of(rows_a, i)[:, 1:2]
        grad_att[at, :] = (
            scale * (upstream * head_gain - columns[:, 0:1] - normal_rows * columns[:, 1:2])
        ).astype(BF)
        pre_turned[0:128, at] = attn_low[at, :].T
        return (
            carry[0] + jnp.sum(upstream * normal_rows, axis=0, keepdims=True),
            carry[1] + jnp.sum(upstream, axis=0, keepdims=True),
        )

    sums = lax.fori_loop(0, 8, attn_back, (jnp.zeros((1, 128), F32),) * 2, unroll=2)
    for k in range(2):
        head_vec[k : k + 1, :] = sums[k]
    keep[1].start()
    for copy in keep:
        copy.wait()
    run_until(weights)
    for copy in stores:
        copy.wait()
    store.wait()
    net.finish()


def middle(number, *args):
    wide = pltpu.VMEM((1024, 512), F32)
    low = pltpu.VMEM((1024, 512), BF)
    tall = pltpu.VMEM((512, 1024), BF)
    whole = pltpu.VMEM((1024, 2048), BF)
    return comm_call(
        middle_kernel,
        "middle",
        number,
        15 * 3 + 20 * 4 + 14 * 2,
        22,
        (
            sds((64, 2048), F32),
            sds((64, 2048), F32),
            sds((1024, 2048), BF),
            sds((1024, 128), BF),
            *(sds((1024, 256), BF),) * 4,
            sds((1024, 2048), BF),
            sds((128, 1024), BF),
            sds((8, 512), F32),
            sds((8, 128), F32),
            sds((8, 2048), F32),
        ),
        [
            whole,
            pltpu.VMEM((2048, 128), BF),
            pltpu.VMEM((2048, 1024), BF),
            whole,
            whole,
            low,
            low,
            tall,
            tall,
            pltpu.VMEM((1024, 128), BF),
            pltpu.VMEM((64, 2048), BF),
            whole,
            pltpu.VMEM((8, 64, 2048), BF),
            pltpu.VMEM((7, 64, 2048), BF),
            pltpu.VMEM((8, 64, 2048), BF),
            pltpu.VMEM((8, 1024, 256), BF),
            pltpu.VMEM((7, 1024, 256), BF),
            wide,
            wide,
            wide,
            pltpu.VMEM((1024, 128), F32),
            pltpu.VMEM((64, 2048), F32),
            pltpu.VMEM((64, 128), F32),
            pltpu.VMEM((16, 128), F32),
            pltpu.VMEM((16, 16, 128), F32),
            pltpu.VMEM((8, 8, 128), F32),
            pltpu.VMEM((32, 128), F32),
            pltpu.VMEM((16, 32, 128), F32),
            pltpu.VMEM((8, 8, 128), F32),
            pltpu.VMEM((8, 128), F32),
            pltpu.VMEM((16, 8, 128), F32),
            pltpu.VMEM((8, 8, 128), F32),
            pltpu.VMEM((64, 2048), F32),
            pltpu.VMEM((8, 2048), F32),
            pltpu.VMEM((2, 64, 128), F32),
        ],
        [VMEM] + [ANY] * 6 + [VMEM] * 8,
        (VMEM, VMEM, ANY, VMEM) + (ANY,) * 6 + (VMEM,) * 3,
        *args,
    )


def tail_kernel(
    kv_part,
    ffn_part,
    ffn_own,
    ffn_up,
    ffn_down,
    ffn_across,
    query_grad,
    cosine,
    sine,
    growth,
    w_attn_in,
    in_low_in,
    branch_in,
    attn_turned,
    mid,
    grad_mid,
    input_rows,
    b_down,
    gains,
    hid_vec,
    head_vec,
    row_vec,
    out_half,
    in_half,
    attn_got,
    ffn_got,
    vectors,
    send,
    recv,
    local,
    kv_mine,
    kv_landed,
    kv_grad,
    f_mine,
    f_landed,
    f_other,
    i_mine,
    i_landed,
    i_other,
    w_mine,
    w_landed,
    w_grad,
    w_rows,
    attn_rows,
    ffn_rows,
    out_rows,
    in_rows,
    grad_qkv,
    turned,
    partial_rows,
    w_attn,
    in_low,
    branch_all,
    row_parts,
    row_got,
    packed,
    packed_got,
):
    net = Net(send, recv)
    me = net.place({}, "z", "c", "f")
    here = net.place({}, "z", "c")
    f = net.at["f"]
    load_w = pltpu.make_async_copy(w_attn_in, w_attn, local.at[16])
    load_w.start()
    load_in = pltpu.make_async_copy(in_low_in, in_low, local.at[21])
    load_in.start()
    load_branch = pltpu.make_async_copy(branch_in, branch_all, local.at[22])
    load_branch.start()
    net.greet(ALL_G, ALL_T)

    def to_halves(source, target, k):
        rows = target.at[pl.ds(pl.multiple_of(f * 64, 64), 64)]
        theirs = source.at[:, pl.ds(pl.multiple_of((1 - f) * 1024, 1024), 1024)]
        own = source.at[:, pl.ds(pl.multiple_of(f * 1024, 1024), 1024)]
        copy = net.push(theirs, rows, {"f": 1})
        keep = pltpu.make_async_copy(own, rows, local.at[k])
        keep.start()
        return copy, keep

    def to_rows(source, got, k):
        copies = []
        for offset in ALL_ZC:
            at = net.place(offset, "z", "c")
            copies.append(
                net.push(source.at[pl.ds(pl.multiple_of(at * 32, 32), 32)], got.at[here], offset)
            )
        keep = pltpu.make_async_copy(
            source.at[pl.ds(pl.multiple_of(here * 32, 32), 32)], got.at[here], local.at[k]
        )
        keep.start()
        return copies, keep

    def ffn_weights():
        def turn(i, carry):
            for j in range(2):
                at = slice(j * 128, j * 128 + 128)
                block = ffn_own[tile(i), at].astype(F32) + ffn_up[tile(i), at].astype(F32)
                block = block + (ffn_down[tile(i), at].astype(F32) + ffn_across[tile(i), at].astype(F32))
                block = block.T
                w_rows[j * 128 : j * 128 + 128, tile(i)] = block.astype(BF)
            return carry

        lax.fori_loop(0, 8, turn, 0)
        yield to_rows(w_rows, ffn_got, 17)

    kv_flow = Flow(
        scatter_flow(
            net,
            scatter_chunk(net, kv_part, "x"),
            kv_grad,
            kv_mine,
            None,
            kv_landed,
            local.at[pl.ds(0, 8)],
            "x",
            "h",
            False,
            False,
            0,
            11,
        )
    )
    ffn_flow = Flow(
        scatter_flow(
            net,
            scatter_chunk(net, ffn_part, "z"),
            ffn_rows,
            f_mine,
            f_other,
            f_landed,
            local.at[pl.ds(8, 8)],
            "z",
            "f",
            True,
            True,
            4,
            7,
        )
    )
    kv_flow.step()
    ffn_flow.step()
    ffn_copies, ffn_keep = next(ffn_weights())

    def out_terms():
        yield 6
        load_branch.wait()
        for k, (i, j) in enumerate(ROOTS):
            yield 7 + k
            columns = tile(net.place({"x": i, "h": j}, "x", "h"), 256)
            w_mine[k, 384:512, :] = jnp.dot(
                attn_turned[...], branch_all[:, columns], preferred_element_type=F32
            ).astype(BF)

    run_flows(kv_flow, ffn_flow, Flow(out_terms()))

    def finish_rows(i, carry):
        at = tile(i, 16)
        out_rows[at, :] = mid[at, :] + (ffn_rows[at, :] + b_down[...])
        return carry

    lax.fori_loop(0, 4, finish_rows, 0)
    out_copy, out_keep = to_halves(out_rows, out_half, 18)

    def unrotate(i, carry):
        at = tile(i)
        cos, sin, grow = cosine[at, :], sine[at, :], growth[at, :]
        queries = query_grad[at, :] * grow
        queries = (queries * cos - turn_halves(queries) * sin).astype(BF)
        keys = kv_grad[at, 0:128] / grow
        keys = (keys * cos - turn_halves(keys) * sin).astype(BF)
        values = kv_grad[at, 128:256].astype(BF)
        grad_qkv[at, 0:128] = queries
        grad_qkv[at, 128:256] = keys
        grad_qkv[at, 256:384] = values
        return tuple(
            total + jnp.sum(part.astype(F32), axis=0, keepdims=True)
            for total, part in zip(carry, (queries, keys, values))
        )

    bias = lax.fori_loop(0, 8, unrotate, (jnp.zeros((1, 128), F32),) * 3)
    for k in range(3):
        packed[8 + k : 9 + k, :] = bias[k]
    load_w.wait()

    def project(i, carry):
        partial_rows[:, tile(i, 256)] = lax.dot_general(
            grad_qkv[...], w_attn[tile(i, 256), 0:384], NT, preferred_element_type=F32
        ).astype(BF)
        return carry

    lax.fori_loop(0, 8, project, 0)

    def chunk(offset):
        at = net.place(offset, "z", "c", "f")
        return partial_rows.at[pl.ds(pl.multiple_of(at * 64, 64), 64)]

    def weight_scatter():
        def turn_grads(i, carry):
            turned[:, tile(i)] = grad_qkv[tile(i), :].T
            return carry

        yield 0.6
        lax.fori_loop(0, 8, turn_grads, 0)
        load_in.wait()
        for k, (i, j) in enumerate(ROOTS):
            yield 1 + k
            columns = tile(net.place({"x": i, "h": j}, "x", "h"), 256)
            w_mine[k, 0:384, :] = jnp.dot(
                turned[...], in_low[:, columns], preferred_element_type=F32
            ).astype(BF)
        yield from scatter_flow(
            net, None, w_grad, w_mine, None, w_landed, None, "x", "h", False, False, 5, 5.5
        )

    w_flow = Flow(weight_scatter())
    for _ in range(9):
        w_flow.step()
    in_flow = Flow(
        scatter_flow(net, chunk, in_rows, i_mine, i_other, i_landed, local, "z", "f", True, False, 0, 5.5)
    )
    run_until(in_flow, w_flow)

    def in_back(i, carry):
        at = tile(i, 16)
        rows = input_rows[at, :].astype(F32)
        centered = rows - jnp.mean(rows, axis=1, keepdims=True)
        scale = lax.rsqrt(jnp.mean(centered * centered, axis=1, keepdims=True) + EPS)
        normal_rows = centered * scale
        upstream = in_rows[at, :]
        scaled = upstream * gains[0:1, :]
        mean = jnp.mean(scaled, axis=1, keepdims=True)
        cross = jnp.mean(scaled * normal_rows, axis=1, keepdims=True)
        in_rows[at, :] = grad_mid[at, :] + scale * (scaled - mean - normal_rows * cross)
        return (
            carry[0] + jnp.sum(upstream * normal_rows, axis=0, keepdims=True),
            carry[1] + jnp.sum(upstream, axis=0, keepdims=True),
        )

    sums = lax.fori_loop(0, 4, in_back, (jnp.zeros((1, 2048), F32),) * 2)
    in_copy, in_keep = to_halves(in_rows, in_half, 19)
    run_until(w_flow)

    def turn_weights(i, carry):
        for j in range(2):
            w_grad_rows = w_grad[tile(i), j * 128 : j * 128 + 128].T
            attn_rows[j * 128 : j * 128 + 128, tile(i)] = w_grad_rows
        return carry

    for g in range(16):
        at = slice(g * 128, g * 128 + 128)
        for k in range(2):
            row_parts[g, k : k + 1, :] = sums[k][:, at]
        row_parts[g, 2:6, :] = row_vec[0:4, at]
        row_parts[g, 6:8, :] = jnp.zeros((2, 128), F32)
    copies = []
    for k, offset in enumerate(ALL_G):
        to = net.place(offset, "z", "c", "f")
        copies.append(net.push(row_parts.at[to], row_got.at[k], offset))
    lax.fori_loop(0, 4, turn_weights, 0)
    attn_copies, attn_keep = to_rows(attn_rows, attn_got, 20)
    packed[11:13, :] = head_vec[0:2, :]
    for k in range(3):
        for j in range(4):
            at = 13 + 4 * k + j
            packed[at : at + 1, :] = hid_vec[k : k + 1, j * 128 : j * 128 + 128]
    packed[25:32, :] = jnp.zeros((7, 128), F32)
    for copy in copies:
        copy.wait_recv()
    total = row_parts[me]
    for k in range(15):
        total = total + row_got[k]
    packed[0:8, :] = total
    copies = [net.push(packed, packed_got.at[k], offset) for k, offset in enumerate(ALL_T)]
    for copy in copies:
        copy.wait_recv()
    total = packed[...]
    for k in range(7):
        total = total + packed_got[k]
    vectors[me] = total
    copies = [net.push(vectors.at[me], vectors.at[me], offset) for offset in ALL_G]
    for copy in ffn_copies + attn_copies + copies + [out_copy, in_copy]:
        copy.wait_recv()
    for keep in (ffn_keep, attn_keep, out_keep, in_keep):
        keep.wait()
    net.finish()


def tail(number, *args):
    half = sds((128, 1024), F32)
    rows = pltpu.VMEM((64, 2048), F32)
    return comm_call(
        tail_kernel,
        "tail",
        number,
        12 + 22 + 7 + 20 + 12 + 2 + 7 + 37,
        23,
        (
            half,
            half,
            sds((8, 32, 512), F32),
            sds((8, 32, 1024), BF),
            sds((16, 32, 128), F32),
        ),
        scatter_scratch(1024, 256, False)
        + [pltpu.VMEM((1024, 256), F32)]
        + scatter_scratch(64, 2048, True)
        + scatter_scratch(64, 2048, True)
        + scatter_scratch(512, 256, False)
        + [
            pltpu.VMEM((512, 256), F32),
            pltpu.VMEM((256, 1024), BF),
            pltpu.VMEM((256, 512), F32),
            rows,
            rows,
            rows,
            pltpu.VMEM((1024, 384), BF),
            pltpu.VMEM((384, 1024), BF),
            pltpu.VMEM((1024, 2048), BF),
            pltpu.VMEM((2048, 512), BF),
            pltpu.VMEM((1024, 2048), BF),
            pltpu.VMEM((1024, 2048), BF),
            pltpu.VMEM((16, 8, 128), F32),
            pltpu.VMEM((15, 8, 128), F32),
            pltpu.VMEM((32, 128), F32),
            pltpu.VMEM((7, 32, 128), F32),
        ],
        [ANY, ANY] + [VMEM] * 8 + [ANY] * 3 + [VMEM] * 9,
        (VMEM,) * 5,
        *args,
    )


def assemble_kernel(
    out_in,
    in_in,
    attn_in,
    ffn_in,
    sums_in,
    out_half,
    in_half,
    qkv_out,
    out_out,
    up_out,
    down_out,
    qkv_bias,
    gains_out,
    shifts_out,
    out_bias,
    down_bias,
    up_bias,
    hid_gain_out,
    hid_shift_out,
    attn_got,
    ffn_got,
    sums,
    sems,
):
    pairs = ((out_in, out_half), (in_in, in_half), (sums_in, sums), (attn_in, attn_got), (ffn_in, ffn_got))
    copies = [pltpu.make_async_copy(a, b, sems.at[k]) for k, (a, b) in enumerate(pairs)]
    for copy in copies:
        copy.start()
    for copy in copies:
        copy.wait()

    def weights(i, carry):
        small, large = tile(i, 128), tile(i, 512)
        for j in range(3):
            qkv_out[:, j, small] = attn_got[i, :, j * 128 : j * 128 + 128]
        out_out[:, small] = attn_got[i, :, 384:512]
        up_out[:, large] = ffn_got[i, :, 0:512].astype(F32)
        down_out[:, large] = ffn_got[i, :, 512:1024].astype(F32)
        return carry

    lax.fori_loop(0, 8, weights, 0)

    def place(g, carry):
        by_rows, row_lanes = pl.ds(g, 1), tile(g)
        head = lax.rem(g, 2) * 8 + g // 2
        head_lanes = tile(head)
        for k, (target, j) in enumerate(
            ((gains_out, 0), (shifts_out, 0), (gains_out, 2), (shifts_out, 2))
        ):
            target[j : j + 1, row_lanes] = sums[g, k : k + 1, :]
        out_bias[by_rows, :] = sums[g, 4:5, :]
        down_bias[by_rows, :] = sums[g, 5:6, :]
        qkv_bias[:, head_lanes] = sums[g, 8:11, :]
        gains_out[1:2, head_lanes] = sums[g, 11:12, :]
        shifts_out[1:2, head_lanes] = sums[g, 12:13, :]
        for k, target in enumerate((up_bias, hid_gain_out, hid_shift_out)):
            for j in range(4):
                at = 13 + 4 * k + j
                target[pl.ds(head * 4 + j, 1), :] = sums[g, at : at + 1, :]
        return carry

    lax.fori_loop(0, 16, place, 0)


def assemble(*args):
    vector, hidden = sds((16, 128), F32), sds((64, 128), F32)
    triple = sds((3, 2048), F32)
    half = sds((128, 1024), F32)
    return pl.pallas_call(
        assemble_kernel,
        out_shape=(
            half,
            half,
            sds((32, 3, 1024), F32),
            sds((32, 1024), F32),
            sds((32, 4096), F32),
            sds((32, 4096), F32),
            triple,
            triple,
            triple,
            vector,
            vector,
            hidden,
            hidden,
            hidden,
        ),
        in_specs=[ANY] * 5,
        out_specs=(VMEM,) * 14,
        scratch_shapes=[
            pltpu.VMEM((8, 32, 512), F32),
            pltpu.VMEM((8, 32, 1024), BF),
            pltpu.VMEM((16, 32, 128), F32),
            DMA((5,)),
        ],
        name="assemble",
        compiler_params=pltpu.CompilerParams(vmem_limit_bytes=60 << 20),
    )(*args)


def both_heads(rows, zero):
    lanes = lax.broadcasted_iota(jnp.int32, rows.shape, 1)
    return jnp.where(lanes < HEAD, rows, zero), jnp.where(lanes >= HEAD, rows, zero)


def run_rows(ref, run):
    return ref[pl.ds(pl.multiple_of(run * RUN, RUN), RUN), :]


def pair_rows(ref, run_a, run_b, dtype):
    zero = jnp.zeros((), dtype)
    a = both_heads(run_rows(ref, run_a).astype(dtype), zero)
    b = both_heads(run_rows(ref, run_b).astype(dtype), zero)
    return jnp.concatenate(a + b, axis=0)


def pair_bounds(rank_a, rank_b):
    lanes = lax.broadcasted_iota(jnp.int32, (1, 256), 1)
    rank = jnp.where(lanes < 128, rank_a, rank_b)
    last = rank * RUN + lax.rem(lanes, RUN)
    return (rank // 64) * 4096, last


def seen(chunk, low, last):
    keys = chunk * CHUNK + lax.broadcasted_iota(jnp.int32, (CHUNK, 256), 0)
    return (keys >= low) & (keys <= last)


def sort_keys(order, kv_ref, kv):
    def move(r, carry):
        target = pl.ds(pl.multiple_of(order[0, r] * RUN, RUN), RUN)
        kv[target, :] = run_rows(kv_ref, r)
        return carry

    lax.fori_loop(0, 128, move, 0, unroll=4)


def flip(kv, columns, target):
    def one(i, carry):
        target[i] = kv[tile(i, CHUNK), columns].T
        return carry

    lax.fori_loop(0, 16, one, 0, unroll=2)


def over_chunks(rank_a, rank_b, step, start):
    low = (rank_a // 64) * 8
    whole = jnp.where(rank_a // 64 == rank_b // 64, (rank_a // 8 - low) // 2, 0)

    def two(i, state):
        return step(low + 2 * i + 1, step(low + 2 * i, state, False), False)

    state = lax.fori_loop(0, whole, two, start)
    return lax.fori_loop(
        low + 2 * whole, rank_b // 8 + 1, lambda i, state: step(i, state, True), state
    )


def lane_heads(total):
    turned = total.T
    lanes = lax.broadcasted_iota(jnp.int32, (RUN, 128), 1)
    a = jnp.where(lanes < HEAD, turned[0:64], turned[64:128])
    b = jnp.where(lanes < HEAD, turned[128:192], turned[192:256])
    return a, b


def attend_kernel(order, q_ref, kv_ref, o_ref, lse_ref, kv, flipped):
    sort_keys(order, kv_ref, kv)
    flip(kv, slice(128, 256), flipped)

    def pair(p, carry):
        run_a, run_b = order[1, 2 * p], order[1, 2 * p + 1]
        rank_a, rank_b = order[2, 2 * p], order[2, 2 * p + 1]
        queries = pair_rows(q_ref, run_a, run_b, BF)
        low, last = pair_bounds(rank_a, rank_b)

        def step(i, state, masked):
            peak, total, mixed = state
            scores = lax.dot_general(
                kv[tile(i, CHUNK), 0:128], queries, NT, preferred_element_type=F32
            )
            if masked:
                scores = jnp.where(seen(i, low, last), scores, -1e30)
            new_peak = jnp.maximum(peak, jnp.max(scores, axis=0, keepdims=True))
            weights = jnp.exp(scores - new_peak)
            shrink = jnp.exp(peak - new_peak)
            total = total * shrink + jnp.sum(weights, axis=0, keepdims=True)
            mixed = mixed * shrink + lax.dot_general(
                flipped[i], weights.astype(BF), NN, preferred_element_type=F32
            )
            return new_peak, total, mixed

        start = (
            jnp.full((1, 256), -1e20, F32),
            jnp.zeros((1, 256), F32),
            jnp.zeros((128, 256), F32),
        )
        peak, total, mixed = over_chunks(rank_a, rank_b, step, start)
        a, b = lane_heads(mixed / total)
        o_ref[pl.ds(pl.multiple_of(run_a * RUN, RUN), RUN), :] = a
        o_ref[pl.ds(pl.multiple_of(run_b * RUN, RUN), RUN), :] = b
        lse_ref[p] = peak + jnp.log(total)
        return carry

    lax.fori_loop(0, 8, pair, 0)


def attend(order, queries, kv):
    return pl.pallas_call(
        attend_kernel,
        out_shape=(sds((1024, 128), F32), sds((8, 1, 256), F32)),
        grid_spec=pltpu.PrefetchScalarGridSpec(
            num_scalar_prefetch=1,
            grid=(1,),
            in_specs=[VMEM, VMEM],
            out_specs=(VMEM, VMEM),
            scratch_shapes=[
                pltpu.VMEM((8192, 256), BF),
                pltpu.VMEM((16, 128, CHUNK), BF),
            ],
        ),
        name="attend",
        cost_estimate=pl.CostEstimate(flops=30_000_000_000, bytes_accessed=20_000_000, transcendentals=0),
        compiler_params=pltpu.CompilerParams(vmem_limit_bytes=60 << 20),
    )(order, queries, kv)


def attend_back_kernel(
    order, q_ref, kv_ref, g_ref, a_ref, lse_ref, dq_ref, dkv_ref, kv, flipped, dkeys, dvalues
):
    sort_keys(order, kv_ref, kv)
    flip(kv, slice(0, 128), flipped)

    def clear(i, carry):
        dkeys[tile(i, CHUNK), :] = jnp.zeros((CHUNK, 128), F32)
        dvalues[tile(i, CHUNK), :] = jnp.zeros((CHUNK, 128), F32)
        return carry

    lax.fori_loop(0, 16, clear, 0)

    def pair(p, carry):
        run_a, run_b = order[1, 2 * p], order[1, 2 * p + 1]
        rank_a, rank_b = order[2, 2 * p], order[2, 2 * p + 1]
        queries = pair_rows(q_ref, run_a, run_b, BF)
        grads = pair_rows(g_ref, run_a, run_b, BF)
        low, last = pair_bounds(rank_a, rank_b)
        product = pair_rows(g_ref, run_a, run_b, F32) * pair_rows(a_ref, run_a, run_b, F32)
        delta = row_sums(product)
        log_total = lse_ref[p]

        def step(i, dq, masked):
            rows = tile(i, CHUNK)
            scores = lax.dot_general(kv[rows, 0:128], queries, NT, preferred_element_type=F32)
            dprobs = lax.dot_general(kv[rows, 128:256], grads, NT, preferred_element_type=F32)
            probs = jnp.exp(scores - log_total)
            if masked:
                probs = jnp.where(seen(i, low, last), probs, 0.0)
            dscores = (probs * (dprobs - delta)).astype(BF)
            dvalues[rows, :] += lax.dot_general(
                probs.astype(BF), grads, NN, preferred_element_type=F32
            )
            dkeys[rows, :] += lax.dot_general(dscores, queries, NN, preferred_element_type=F32)
            return dq + lax.dot_general(flipped[i], dscores, NN, preferred_element_type=F32)

        dq = over_chunks(rank_a, rank_b, step, jnp.zeros((128, 256), F32))
        a, b = lane_heads(dq)
        dq_ref[pl.ds(pl.multiple_of(run_a * RUN, RUN), RUN), :] = a * 0.125
        dq_ref[pl.ds(pl.multiple_of(run_b * RUN, RUN), RUN), :] = b * 0.125
        return carry

    lax.fori_loop(0, 8, pair, 0)

    def back(r, carry):
        source = pl.ds(pl.multiple_of(order[0, r] * RUN, RUN), RUN)
        to = pl.ds(pl.multiple_of(r * RUN, RUN), RUN)
        dkv_ref[to, 0:128] = dkeys[source, :].astype(BF)
        dkv_ref[to, 128:256] = dvalues[source, :].astype(BF)
        return carry

    lax.fori_loop(0, 128, back, 0, unroll=4)


def attend_back(order, queries, kv, grads, attended, log_total):
    return pl.pallas_call(
        attend_back_kernel,
        out_shape=(sds((1024, 128), F32), sds((8192, 256), BF)),
        grid_spec=pltpu.PrefetchScalarGridSpec(
            num_scalar_prefetch=1,
            grid=(1,),
            in_specs=[VMEM] * 5,
            out_specs=(VMEM, VMEM),
            scratch_shapes=[
                pltpu.VMEM((8192, 256), BF),
                pltpu.VMEM((16, 128, CHUNK), BF),
                pltpu.VMEM((8192, 128), F32),
                pltpu.VMEM((8192, 128), F32),
            ],
        ),
        name="attend_back",
        cost_estimate=pl.CostEstimate(flops=30_000_000_000, bytes_accessed=20_000_000, transcendentals=0),
        compiler_params=pltpu.CompilerParams(vmem_limit_bytes=60 << 20),
    )(order, queries, kv, grads, attended, log_total)


def lane_tables(seq_length):
    half = HEAD // 2
    indices = (np.arange(128) % half).astype(np.float32)
    inverse_freq = np.exp(-np.log(np.float32(10000.0)) * indices / np.float32(half)).astype(np.float64)
    ratios = np.log((2.0 * indices + 0.4 * HEAD) / (1.4 * HEAD)).astype(np.float64)

    def tables(places, powers):
        angles = places[:, None] * inverse_freq[None, :]
        growth = np.exp(powers[:, None] * ratios[None, :])
        return np.stack([np.cos(angles), np.sin(angles), growth]).astype(np.float32)

    runs = np.arange(64) * float(RUN)
    tokens = np.arange(RUN).astype(np.float64)
    return (
        jnp.asarray(tables(runs, (runs - seq_length // 2) / 512.0)),
        jnp.asarray(tables(tokens, tokens / 512.0)),
    )


def shards(
    layer_input,
    w_qkv,
    w_out,
    w_up,
    w_down,
    b_qkv,
    b_out,
    b_up,
    b_down,
    norm_gains,
    norm_shifts,
    hidden_gain,
    hidden_shift,
    seq_ids,
    positions,
    d_out,
):
    packed = jnp.concatenate(
        [
            w_qkv.reshape(32, 3, 8, 128).transpose(2, 0, 1, 3).reshape(8, 32, 384),
            w_out.reshape(32, 8, 128).transpose(1, 0, 2),
        ],
        axis=2,
    )
    run_tables, token_tables = lane_tables(4096)
    (
        input_rows,
        in_low,
        w_attn,
        ffn_block,
        query_low,
        kv,
        grad_all,
        cosine,
        sine,
        growth,
        order,
        w_norm,
    ) = front(
        1,
        layer_input,
        d_out,
        packed,
        w_up,
        w_down,
        seq_ids.reshape(1, 128),
        positions.reshape(1, 128),
        norm_gains,
        norm_shifts,
        b_qkv,
        run_tables,
        token_tables,
    )
    ffn_near = (
        lax.ppermute(ffn_block, "x", UP),
        lax.ppermute(ffn_block, "x", DOWN),
        lax.ppermute(ffn_block, "h", ACROSS),
    )
    attended, log_total = attend(order, query_low, kv)
    (
        mid,
        grad_mid,
        ffn_part,
        grad_attended,
        ffn_up,
        ffn_down,
        ffn_across,
        ffn_own,
        branch_all,
        attn_turned,
        hid_vec,
        head_vec,
        row_vec,
    ) = middle(
        3,
        attended,
        w_attn,
        ffn_block,
        *ffn_near,
        grad_all,
        input_rows,
        b_out.reshape(1, 2048),
        b_up.reshape(1, 8192),
        norm_gains,
        norm_shifts,
        hidden_gain.reshape(1, 8192),
        hidden_shift.reshape(1, 8192),
        w_norm,
    )
    ffn_got = (
        lax.ppermute(ffn_up, "x", UP),
        lax.ppermute(ffn_down, "x", DOWN),
        lax.ppermute(ffn_across, "h", ACROSS),
    )
    query_grad, kv_part = attend_back(order, query_low, kv, grad_attended, attended, log_total)
    parts = tail(
        4,
        kv_part.reshape(8, 1024, 256),
        ffn_part.reshape(16, 64, 2048),
        ffn_own,
        *ffn_got,
        query_grad,
        cosine,
        sine,
        growth,
        w_attn,
        in_low,
        branch_all,
        attn_turned,
        mid,
        grad_mid,
        input_rows,
        b_down.reshape(1, 2048),
        norm_gains,
        hid_vec,
        head_vec,
        row_vec,
    )
    (
        layer_output,
        input_grad,
        qkv_grad,
        out_grad,
        up_grad,
        down_grad,
        qkv_bias,
        gains_grad,
        shifts_grad,
        out_bias,
        down_bias,
        up_bias,
        hid_gain_grad,
        hid_shift_grad,
    ) = assemble(*parts)
    return (
        layer_output,
        input_grad,
        qkv_grad,
        out_grad,
        up_grad,
        down_grad,
        qkv_bias,
        out_bias.reshape(2048),
        up_bias.reshape(8192),
        down_bias.reshape(2048),
        gains_grad,
        shifts_grad,
        hid_gain_grad.reshape(8192),
        hid_shift_grad.reshape(8192),
    )


def solution(mesh):
    fine = Mesh(mesh.devices.reshape(4, 2, 4, 2, 2), SEQ + ("f",))
    both = P(SEQ, "f")
    return jax.shard_map(
        shards,
        mesh=fine,
        in_specs=(both, P(SEQ, None, "f"), both, both, both)
        + (P(),) * 8
        + (P(SEQ), P(SEQ), both),
        out_specs=(both, both, P(SEQ, None, "f"), both, both, both) + (P(),) * 8,
        check_vma=False,
    )
```

```python
import math

import jax
import jax.numpy as jnp
import numpy as np
from jax import lax
from jax.experimental import pallas as pl
from jax.experimental.pallas import tpu as pltpu
from jax.sharding import Mesh
from jax.sharding import PartitionSpec as P

SEQ = ("x", "h", "z", "c")
TOK = ("x", "h")
HEAD = 64
RUN = 64
CHUNK = 1024
EPS = 1e-05
MESH = pl.DeviceIdType.MESH
BF = jnp.bfloat16
F32 = jnp.float32
DMA = pltpu.SemaphoreType.DMA
ANY = pl.BlockSpec(memory_space=pl.ANY)
VMEM = pl.BlockSpec(memory_space=pltpu.VMEM)
NT = (((1,), (1,)), ((), ()))
TN = (((0,), (0,)), ((), ()))
NN = (((1,), (0,)), ((), ()))


def sds(shape, dtype):
    return jax.ShapeDtypeStruct(shape, dtype)


AXES = {"x": 4, "h": 2, "z": 4, "c": 2, "f": 2}
RING_G, PAIR_G = "z", "f"
RING_T, PAIR_T = "x", "h"


class Net:
    loads = []

    def __init__(self, send, recv):
        self.send, self.recv, self.copies, self.drained = send, recv, [], 0
        self.at = {axis: lax.axis_index(axis) for axis in AXES}

    def device(self, offset):
        return {a: lax.rem(self.at[a] + d + AXES[a], AXES[a]) for a, d in offset.items()}

    def place(self, offset, *axes):
        index = 0
        for a in axes:
            d = offset.get(a, 0)
            at = lax.rem(self.at[a] + d + AXES[a], AXES[a]) if d else self.at[a]
            index = index * AXES[a] + at
        return index

    def greet(self, *groups):
        offsets = {
            tuple((a, o[a]) for a in AXES if o.get(a, 0)) for group in groups for o in group
        }
        barrier = pltpu.get_barrier_semaphore()
        for offset in sorted(offsets):
            pl.semaphore_signal(
                barrier, inc=1, device_id=self.device(dict(offset)), device_id_type=MESH
            )
        pl.semaphore_wait(barrier, len(offsets))
        while self.loads:
            self.loads.pop().wait()

    def push(self, src, dst, offset):
        k = len(self.copies)
        copy = pltpu.make_async_remote_copy(
            src_ref=src,
            dst_ref=dst,
            send_sem=self.send.at[k],
            recv_sem=self.recv.at[k],
            device_id=self.device(offset),
            device_id_type=MESH,
        )
        copy.start()
        self.copies.append(copy)
        return copy

    def finish(self):
        for copy in self.copies[self.drained :]:
            copy.wait_send()
        self.drained = len(self.copies)


UP = [(i, (i + 1) % 4) for i in range(4)]
DOWN = [(i, (i + 3) % 4) for i in range(4)]
ACROSS = [(0, 1), (1, 0)]
SIBLING = {"c": 1}
NEAR_G = [{"z": 1}, {"z": 3}, {"f": 1}, SIBLING]
NEAR_T = [{"x": 1}, {"x": 3}, {"h": 1}]
ALL_T = [{"x": i, "h": j} for i in range(4) for j in range(2)][1:]
ALL_ZC = [{"z": i, "c": j} for i in range(4) for j in range(2)][1:]
ALL_G = [{"z": i, "c": j, "f": k} for i in range(4) for j in range(2) for k in range(2)][1:]


class Flow:
    def __init__(self, steps):
        self.steps = steps
        self.step()

    def step(self):
        self.time = next(self.steps, None)


def run_until(main, *others):
    while main.time is not None:
        ready = [flow for flow in (main,) + others if flow.time is not None]
        min(ready, key=lambda flow: flow.time).step()


def run_flows(*flows):
    for flow in flows:
        run_until(flow, *flows)


def run_flows_but(kept, *flows):
    for flow in flows:
        run_until(flow, kept, *flows)


def half_rows(ref, which):
    rows = ref.shape[0] // 2
    return ref.at[pl.ds(which * rows, rows)]


def gather_flow(
    net, src, slot, ring, pair, local, sibling, light, at, unit, hold=0, arrived=None
):
    up, down, across = {ring: 1}, {ring: 3}, {pair: 1}
    passed = {}

    def to_sibling(ref, i, j):
        if sibling:
            passed[i, j] = net.push(ref, ref, SIBLING)

    def both_ways(ref, target):
        return [
            [net.push(half_rows(ref, k), half_rows(target, k), to) for k in order]
            for to, order in ((up, (0, 1)), (down, (1, 0)))
        ]

    def show(*places):
        if arrived is not None:
            for i in places:
                arrived({ring: i})

    def show_sibling(*places):
        if arrived is not None:
            for i in places:
                for j in range(2):
                    passed.pop((i, j)).wait_recv()
                arrived({ring: i, "c": 1})

    mine = slot({})
    from_down, from_up = both_ways(src, mine)
    if hold:
        yield at + hold
    from_across = net.push(src, mine, across)
    if sibling:
        passed[0, 0] = net.push(src, mine, SIBLING)
    here = pltpu.make_async_copy(src, mine, local)
    here.start()
    below, above, beside, far = (slot({ring: 3}), slot({ring: 1}), slot({pair: 1}), slot({ring: 2}))
    yield at + 0.5 * unit
    from_down[0].wait_recv()
    first = net.push(half_rows(below, 0), half_rows(below, 0), up)
    from_up[0].wait_recv()
    second = net.push(half_rows(above, 1), half_rows(above, 1), down)
    yield at + unit + hold
    from_across.wait_recv()
    if light:
        beside_down, beside_up = both_ways(beside, beside)
    else:
        beside_down = [net.push(beside, beside, up)]
        beside_up = [net.push(beside, beside, down)]
    to_sibling(beside, 0, 1)
    yield at + unit + hold
    from_down[1].wait_recv()
    to_sibling(below, 3, 0)
    from_up[1].wait_recv()
    to_sibling(above, 1, 0)
    here.wait()
    show(0)
    yield at + 1.5 * unit + hold
    first.wait_recv()
    if not light:
        beside_far = [net.push(half_rows(far, 0), half_rows(far, 0), across)]
    second.wait_recv()
    if not light:
        beside_far.append(net.push(half_rows(far, 1), half_rows(far, 1), across))
    to_sibling(far, 2, 0)
    show_sibling(0)
    yield at + (1.7 if light and hold else 2 if light else 2.5) * unit + hold
    below, above = slot({ring: 3, pair: 1}), slot({ring: 1, pair: 1})
    if light:
        beside_down[0].wait_recv()
        beside_far = [net.push(half_rows(below, 0), half_rows(below, 0), up)]
        beside_up[0].wait_recv()
        beside_far.append(net.push(half_rows(above, 1), half_rows(above, 1), down))
        yield at + 2.5 * unit + hold
    beside_down[-1].wait_recv()
    to_sibling(below, 3, 1)
    beside_up[-1].wait_recv()
    to_sibling(above, 1, 1)
    show(3, 1)
    yield at + (3 if light else 2.5) * unit + hold
    for copy in beside_far:
        copy.wait_recv()
    to_sibling(slot({ring: 2, pair: 1}), 2, 1)
    show_sibling(3, 1)
    show(2)
    yield at + (3 if light else 2.5) * unit + hold
    show_sibling(2)
    for copy in passed.values():
        copy.wait_recv()


def gather_rest_flow(net, blocks, slot, ring, pair, local, at, unit):
    up, down = {ring: 1}, {ring: 3}
    mine, below, above, beside = (slot(o) for o in ({}, {ring: 3}, {ring: 1}, {pair: 1}))
    beside_down = [net.push(half_rows(blocks[3], k), half_rows(beside, k), up) for k in (0, 1)]
    beside_up = [net.push(half_rows(blocks[3], k), half_rows(beside, k), down) for k in (1, 0)]
    far = [
        net.push(half_rows(blocks[1], 0), half_rows(below, 0), up),
        net.push(half_rows(blocks[2], 1), half_rows(above, 1), down),
    ]
    here = [
        pltpu.make_async_copy(block, target, local.at[k])
        for k, (block, target) in enumerate(zip(blocks, (mine, below, above, beside)))
    ]
    for copy in here:
        copy.start()
    yield at + 0.7 * unit
    below, above = slot({ring: 3, pair: 1}), slot({ring: 1, pair: 1})
    beside_down[0].wait_recv()
    far.append(net.push(half_rows(below, 0), half_rows(below, 0), up))
    beside_up[0].wait_recv()
    far.append(net.push(half_rows(above, 1), half_rows(above, 1), down))
    yield at + 2.1 * unit
    for copy in far + beside_down[1:] + beside_up[1:]:
        copy.wait_recv()
    for copy in here:
        copy.wait()


def add_into(target, *sources):
    rows = min(32768 // target.shape[1], target.shape[0])

    def step(i, carry):
        at = pl.ds(pl.multiple_of(i * rows, rows), rows)
        total = target[at, :].astype(F32)
        for source in sources:
            total = total + source[at, :].astype(F32)
        target[at, :] = total.astype(target.dtype)
        return carry

    lax.fori_loop(0, target.shape[0] // rows, step, 0)


ROOTS = ((2, 1), (1, 1), (3, 1), (2, 0), (1, 0), (3, 0), (0, 1), (0, 0))


def scatter_flow(
    net, chunk, out, mine, other, landed, local, ring, pair, sibling, light, at, unit, last=True
):
    up, down, across = {ring: 1}, {ring: 3}, {pair: 1}
    loads, shared = [], []
    for k, (i, j) in enumerate(ROOTS):
        if sibling:
            shared.append(net.push(chunk({ring: i, pair: j, "c": 1}), other.at[k], SIBLING))
        if chunk is not None:
            load = pltpu.make_async_copy(chunk({ring: i, pair: j}), mine.at[k], local.at[k])
            load.start()
            loads.append(load)

    def ready(k):
        if chunk is not None:
            loads[k].wait()
        if sibling:
            shared[k].wait_recv()
            add_into(mine.at[k], other.at[k])

    def halves(k, to):
        return (
            net.push(half_rows(mine.at[k], 0), half_rows(landed.at[to], 0), down),
            net.push(half_rows(mine.at[k], 1), half_rows(landed.at[to], 1), up),
        )

    def add_half(k, source, which):
        add_into(half_rows(mine.at[k], which), half_rows(landed.at[source], which))

    def send_half(k, to, which, offset):
        return net.push(half_rows(mine.at[k], which), half_rows(landed.at[to], which), offset)

    if chunk is not None:
        yield at + 0.5
    ready(0)
    if light:
        beside_first, beside_second = halves(0, 0)
        ready(3)
        first, second = halves(3, 3)
        ready(2)
        beside_up = [send_half(2, 2, 1, down)]
        ready(1)
        beside_down = [send_half(1, 1, 0, up)]
        yield at + 0.5 * unit
        beside_first.wait_recv()
        add_half(2, 0, 0)
        beside_up.append(send_half(2, 2, 0, down))
        beside_second.wait_recv()
        add_half(1, 0, 1)
        beside_down.append(send_half(1, 1, 1, up))
    else:
        beside_far = [send_half(0, 0, k, across) for k in range(2)]
        ready(1)
        beside_down = [net.push(mine.at[1], landed.at[1], up)]
        ready(2)
        beside_up = [net.push(mine.at[2], landed.at[2], down)]
        ready(3)
        yield at + 0.6 * unit
        beside_far[0].wait_recv()
        add_half(3, 0, 0)
        first = send_half(3, 3, 0, down)
        yield at + unit
        beside_far[1].wait_recv()
        add_half(3, 0, 1)
        second = send_half(3, 3, 1, up)
    ready(5)
    ready(4)
    if last:
        from_up = [send_half(5, 5, 1, down)]
        from_down = [send_half(4, 6, 0, up)]
    if not light:
        ready(6)
        yield at + 1.1 * unit
        for copy in beside_down + beside_up:
            copy.wait_recv()
        add_into(mine.at[6], landed.at[1], landed.at[2])
        if last:
            from_across = net.push(mine.at[6], landed.at[4], across)
    yield at + (1.1 if light else 1.6) * unit
    first.wait_recv()
    add_half(5, 3, 0)
    if last:
        from_up.append(send_half(5, 5, 0, down))
    yield at + (1.1 if light else 1.8) * unit
    second.wait_recv()
    add_half(4, 3, 1)
    if not last:
        return
    from_down.append(send_half(4, 6, 1, up))
    if light:
        ready(6)
        yield at + 2 * unit
        for copy in beside_down + beside_up:
            copy.wait_recv()
        add_into(mine.at[6], landed.at[1], landed.at[2])
        from_across = net.push(mine.at[6], landed.at[4], across)
    ready(7)
    yield at + (3 if light else 2.5) * unit
    for copy in from_up + from_down + [from_across]:
        copy.wait_recv()
    rows = 32768 // out.shape[1]

    def total(i, carry):
        at = pl.ds(pl.multiple_of(i * rows, rows), rows)
        value = mine[7, at, :].astype(F32) + landed[4, at, :].astype(F32)
        out[at, :] = value + (landed[5, at, :].astype(F32) + landed[6, at, :].astype(F32))
        return carry

    lax.fori_loop(0, out.shape[0] // rows, total, 0)


def gather_slot(net, out, rows, ring, pair):
    order = ("z", "c", "f") if ring == "z" else ("x", "h")

    def slot(offset):
        at = net.place(offset, *order)
        return out.at[pl.ds(pl.multiple_of(at * rows, rows), rows)]

    return slot


def input_slot(net, out):
    def slot(offset):
        row = pl.multiple_of(net.place(offset, "z", "c") * 128, 128)
        column = pl.multiple_of(net.place(offset, "f") * 1024, 1024)
        return out.at[pl.ds(row, 128), pl.ds(column, 1024)]

    return slot


def scatter_chunk(net, ref, ring):
    order = ("z", "c", "f") if ring == "z" else ("x", "h")
    return lambda offset: ref.at[net.place(offset, *order)]


def comm_call(kernel, name, number, pushes, locals_, out_shape, scratch, in_specs, out_specs, *args):
    ins = [i for i, spec in enumerate(in_specs) if spec is VMEM]
    outs = [i for i, spec in enumerate(out_specs) if spec is VMEM]
    shapes = [args[i] for i in ins] + [out_shape[i] for i in outs]
    first = len(args) + len(out_shape)
    last = first + 3 + len(scratch)

    def staged(*refs):
        given, results = list(refs[: len(args)]), list(refs[len(args) : first])
        sems, buffers = refs[last], refs[last + 1 :]
        for k, i in enumerate(ins):
            copy = pltpu.make_async_copy(given[i], buffers[k], sems.at[k])
            copy.start()
            Net.loads.append(copy)
            given[i] = buffers[k]
        stores = []
        for k, i in enumerate(outs, len(ins)):
            stores.append(pltpu.make_async_copy(buffers[k], results[i], sems.at[k]))
            results[i] = buffers[k]
        kernel(*given, *results, *refs[first:last])
        for copy in stores:
            copy.start()
        for copy in stores:
            copy.wait()

    return pl.pallas_call(
        staged,
        out_shape=out_shape,
        in_specs=[ANY] * len(in_specs),
        out_specs=(ANY,) * len(out_specs),
        scratch_shapes=[DMA((pushes,)), DMA((pushes,)), DMA((locals_,))]
        + scratch
        + [DMA((len(shapes),))]
        + [pltpu.VMEM(v.shape, v.dtype) for v in shapes],
        name=name,
        compiler_params=pltpu.CompilerParams(
            collective_id=number, has_side_effects=True, vmem_limit_bytes=60 << 20
        ),
    )(*args)


def scatter_scratch(rows, width, sibling):
    shapes = [pltpu.VMEM((8, rows, width), BF), pltpu.VMEM((7, rows, width), BF)]
    return shapes + ([pltpu.VMEM((8, rows, width), BF)] if sibling else [])


def turn_halves(values):
    lanes = lax.broadcasted_iota(jnp.int32, values.shape, 1)
    first = lax.rem(lanes, HEAD) < HEAD // 2
    return jnp.where(first, pltpu.roll(values, 96, axis=1), pltpu.roll(values, 32, axis=1))


def front_kernel(
    x_ref,
    d_ref,
    w_ref,
    up_ref,
    down_ref,
    seq_ref,
    place_ref,
    gains,
    shifts,
    bias,
    run_tables,
    token_tables,
    rows_out,
    low_out,
    w_out,
    ffn_out,
    q_out,
    kv_out,
    grad_out,
    cosine,
    sine,
    growth,
    order,
    w_norm,
    send,
    recv,
    local,
    x_all,
    in_low,
    w_all,
    blocks,
    near,
    near_sum,
    far,
    kv_here,
    norm_parts,
    norm_got,
    ranks_here,
):
    net = Net(send, recv)
    net.greet(ALL_G, ALL_T)
    me = net.place({}, "z", "c")
    group = net.place({}, "x", "h")
    f = net.at["f"]
    rows = pl.ds(pl.multiple_of(me * 32, 32), 32)
    stores = []

    def store(src, dst, k):
        copy = pltpu.make_async_copy(src, dst, local.at[k])
        copy.start()
        stores.append(copy)

    def norm_block(offset):
        first = net.place(offset, "z", "c") * 128

        def norm_rows(i, carry):
            at = pl.ds(pl.multiple_of(first + i * 16, 16), 16)
            values = x_all[at, :].astype(F32)
            centered = values - jnp.mean(values, axis=1, keepdims=True)
            scale = lax.rsqrt(jnp.mean(centered * centered, axis=1, keepdims=True) + EPS)
            in_low[at, :] = (centered * scale * gains[0:1, :] + shifts[0:1, :]).astype(BF)
            return carry

        lax.fori_loop(0, 8, norm_rows, 0, unroll=4)

    def activations():
        yield from gather_flow(
            net, x_ref, input_slot(net, x_all), "z", "f", local.at[0], True, True, 0, 5.5, 0, norm_block
        )
        ffn_sent = []
        for offset in ALL_ZC:
            to = net.place(offset, "z", "c")
            at = pl.ds(pl.multiple_of(to * 512, 512), 512)
            ffn_sent.append(net.push(up_ref.at[:, at], ffn_out.at[rows, pl.ds(0, 512)], offset))
            ffn_sent.append(net.push(down_ref.at[:, at], ffn_out.at[rows, pl.ds(512, 512)], offset))
        at = pl.ds(pl.multiple_of(me * 512, 512), 512)
        store(up_ref.at[:, at], ffn_out.at[rows, pl.ds(0, 512)], 4)
        store(down_ref.at[:, at], ffn_out.at[rows, pl.ds(512, 512)], 5)
        store(in_low, low_out, 6)
        store(x_all.at[pl.ds(pl.multiple_of((me * 2 + f) * 64, 64), 64)], rows_out, 7)
        yield from gather_flow(
            net, d_ref, input_slot(net, grad_out), "z", "f", local.at[1], True, True, 24, 8
        )
        for copy in ffn_sent:
            copy.wait_recv()

    def run_rank(index):
        lanes = lax.broadcasted_iota(jnp.int32, (1, 128), 1)
        return jnp.sum(jnp.where(lanes == index, near_sum[0:1, :], 0.0), axis=1, keepdims=True)

    def tables(i, carry):
        at = tile(i, RUN)
        block = run_rank(group * 16 + i)
        block = block - jnp.floor(block / 64) * 64
        mask = lax.broadcasted_iota(jnp.int32, (64, 128), 0).astype(F32) == block
        cos_a, sin_a, grow_a = (
            jnp.sum(jnp.where(mask, run_tables[k], 0.0), axis=0, keepdims=True) for k in range(3)
        )
        cos_b, sin_b, grow_b = token_tables[0], token_tables[1], token_tables[2]
        lanes = lax.broadcasted_iota(jnp.int32, (RUN, 128), 1)
        sin = sin_a * cos_b + cos_a * sin_b
        cosine[at, :] = cos_a * cos_b - sin_a * sin_b
        sine[at, :] = jnp.where(lax.rem(lanes, HEAD) < HEAD // 2, -sin, sin)
        growth[at, :] = grow_a * grow_b
        return carry

    def put_order():
        lanes = lax.broadcasted_iota(jnp.int32, (16, 128), 1)
        places = lax.broadcasted_iota(jnp.int32, (16, 128), 0)
        ranks = jnp.zeros((16, 128), F32)
        by_lane = jnp.full((16, 128), 1e9, F32)
        for k in range(16):
            rank = run_rank(group * 16 + k)
            ranks = jnp.where(places == k, rank, ranks)
            by_lane = jnp.where(lanes == k, rank, by_lane)
        slot = jnp.sum((by_lane < ranks).astype(F32), axis=1, keepdims=True)
        hit = lanes.astype(F32) == slot
        runs = jnp.sum(jnp.where(hit, places.astype(F32), 0.0), axis=0, keepdims=True)
        ranks = jnp.sum(jnp.where(hit, ranks, 0.0), axis=0, keepdims=True)
        total = jnp.sum(far[...], axis=0)[0:1]
        order[0:1, :] = total.astype(jnp.int32)
        order[1:2, :] = runs.astype(jnp.int32)
        order[2:3, :] = ranks.astype(jnp.int32)
        order[3:8, :] = jnp.zeros((5, 128), jnp.int32)

    head_at = pl.ds(pl.multiple_of(f * 1024 + me * 128, 128), 128)

    def project(i, carry):
        at = tile(i, 256)
        values = jnp.dot(in_low[at, :], w_all[:, 0:384], preferred_element_type=F32)
        queries = values[:, 0:128] + bias[0:1, head_at]
        keys = values[:, 128:256] + bias[1:2, head_at]
        cos, sin, grow = cosine[at, :], sine[at, :], growth[at, :]
        queries = ((queries * cos + turn_halves(queries) * sin) * grow).astype(BF)
        q_out[at, :] = queries * jnp.bfloat16(0.125)
        keys = (keys * cos + turn_halves(keys) * sin) * (1.0 / grow)
        kv_here[at, 0:128] = keys.astype(BF)
        kv_here[at, 128:256] = (values[:, 256:384] + bias[2:3, head_at]).astype(BF)
        return carry

    def put_ranks():
        lanes = lax.broadcasted_iota(jnp.int32, (1, 128), 1)
        ranks = (seq_ref[...] * 64 + place_ref[...] // RUN).astype(F32)
        first, second = (
            jnp.sum(jnp.where(lanes == k * RUN, ranks, 0.0), axis=1, keepdims=True) for k in range(2)
        )
        at = net.place({}, "x", "h", "z", "c") * 2
        row = jnp.where(lanes == at, first, jnp.where(lanes == at + 1, second, 0.0))
        ranks_here[...] = jnp.broadcast_to(row, (8, 128))

    def attention():
        attn_sent, near_sent = [], []
        put_ranks()
        for offset in ALL_ZC:
            to = net.place(offset, "z", "c")
            attn_sent.append(net.push(w_ref.at[to], blocks.at[rows], offset))
        for offset in ALL_ZC:
            near_sent.append(net.push(ranks_here, near.at[me], offset))
        own = pltpu.make_async_copy(w_ref.at[me], blocks.at[rows], local.at[2])
        own.start()
        near[me] = ranks_here[...]
        own.wait()
        yield 5
        for copy in attn_sent:
            copy.wait_recv()
        weights = gather_flow(
            net, blocks, gather_slot(net, w_all, 256, "x", "h"), "x", "h", local.at[3], False, False, 6, 5.5
        )
        yield next(weights)
        for copy in near_sent:
            copy.wait_recv()
        near_sum[...] = jnp.sum(near[...], axis=0)
        far_sent = [net.push(near_sum, far.at[group], offset) for offset in ALL_T]
        far[group] = near_sum[...]
        lax.fori_loop(0, 16, tables, 0)
        yield from weights
        store(w_all, w_out, 8)
        yield 26
        lax.fori_loop(0, 4, project, 0)
        sending = gather_flow(
            net, kv_here, gather_slot(net, kv_out, 1024, "x", "h"), "x", "h", local.at[9], False, False, 29, 11
        )
        yield next(sending)
        for copy in far_sent:
            copy.wait_recv()
        put_order()
        yield from sending

    def norm_sums():
        yield 25
        gain, shift = gains[1:2, head_at], shifts[1:2, head_at]
        high = [gain.astype(BF), shift.astype(BF)]
        low = [(v - h.astype(F32)).astype(BF) for v, h in zip((gain, shift), high)]
        vectors = jnp.concatenate(high + low + [jnp.zeros((12, 128), BF)], axis=0)

        def norm_vectors(i, carry):
            parts = lax.dot_general(
                vectors, w_all[tile(i, 128), 384:512], NT, preferred_element_type=F32
            )
            norm_parts[i] = parts[0:8] + jnp.concatenate([parts[2:8], parts[8:10]], axis=0)
            return carry

        lax.fori_loop(0, 16, norm_vectors, 0)
        mine = net.place({}, "z", "c", "f")
        sent = []
        for k, offset in enumerate(ALL_G):
            to = net.place(offset, "z", "c", "f")
            sent.append(net.push(norm_parts.at[to], norm_got.at[k], offset))
        yield 41
        for copy in sent:
            copy.wait_recv()
        w_norm[mine] = norm_parts[mine] + jnp.sum(norm_got[...], axis=0)
        sent = [net.push(w_norm.at[mine], w_norm.at[mine], offset) for offset in ALL_G]
        yield 58
        for copy in sent:
            copy.wait_recv()

    run_flows(Flow(attention()), Flow(activations()), Flow(norm_sums()))
    for copy in stores:
        copy.wait()
    net.finish()


def front(number, *args):
    table = sds((1024, 128), F32)
    return comm_call(
        front_kernel,
        "front",
        number,
        23 * 2 + 14 + 7 * 3 + 12 * 2 + 30,
        10,
        (
            sds((64, 2048), BF),
            sds((1024, 2048), BF),
            sds((2048, 512), BF),
            sds((256, 1024), BF),
            sds((1024, 128), BF),
            sds((8192, 256), BF),
            sds((1024, 2048), BF),
            table,
            table,
            table,
            sds((8, 128), jnp.int32),
            sds((16, 8, 128), F32),
        ),
        [
            pltpu.VMEM((1024, 2048), BF),
            pltpu.VMEM((1024, 2048), BF),
            pltpu.VMEM((2048, 512), BF),
            pltpu.VMEM((256, 512), BF),
            pltpu.VMEM((8, 8, 128), F32),
            pltpu.VMEM((8, 128), F32),
            pltpu.VMEM((8, 8, 128), F32),
            pltpu.VMEM((1024, 256), BF),
            pltpu.VMEM((16, 8, 128), F32),
            pltpu.VMEM((15, 8, 128), F32),
            pltpu.VMEM((8, 128), F32),
        ],
        [ANY] * 5 + [VMEM] * 7,
        (ANY,) * 4 + (VMEM, ANY, ANY) + (VMEM,) * 5,
        *args,
    )


def row_sums(values):
    ones = jnp.ones((8, values.shape[1]), F32)
    return lax.dot_general(
        ones, values, NT, preferred_element_type=F32, precision=lax.Precision.HIGHEST
    )[0:1]


def put_sums(target, i, *values):
    sums = row_sums(jnp.concatenate(values, axis=0))
    for k in range(len(values)):
        target[pl.ds(8 * k + i, 1), :] = sums[:, k * 128 : k * 128 + 128]


def tile(i, rows=128):
    return pl.ds(pl.multiple_of(i * rows, rows), rows)


def columns_of(rows_ref, i):
    return rows_ref[i].T


def put_rows(rows_ref, *values):
    for k, value in enumerate(values):
        for i in range(8):
            rows_ref[i, k : k + 1, :] = value[i : i + 1]


def fold_groups(values):
    values = values[:, 0:1024] + values[:, 1024:2048]
    return fold_lanes(values[:, 0:512] + values[:, 512:1024])


def fold_lanes(values):
    return (values[:, 0:128] + values[:, 128:256]) + (values[:, 256:384] + values[:, 384:512])


def middle_kernel(
    att,
    w_attn,
    ffn_block,
    ffn_below,
    ffn_above,
    ffn_beside,
    grad_all_in,
    input_rows,
    b_out,
    b_up,
    gains,
    shifts,
    hid_gain,
    hid_shift,
    w_norm,
    mid,
    grad_mid,
    ffn_part,
    grad_att,
    ffn_up,
    ffn_down,
    ffn_across,
    ffn_own,
    branch_out,
    turned_out,
    hid_vec,
    head_vec,
    row_vec,
    send,
    recv,
    local,
    grad_all,
    out_w,
    w_ffn,
    mid_low,
    branch_all,
    hidden_low,
    pre_low,
    hidden_turned,
    pre_turned,
    attn_low,
    low_rows,
    partial_rows,
    mine,
    landed,
    other,
    t_mine,
    t_landed,
    grad_hidden,
    activated,
    slope,
    normal_attn,
    normal_mid,
    scale_mid,
    sent_a,
    stats_a,
    rows_a,
    sent_b,
    stats_b,
    rows_b,
    sent_c,
    stats_c,
    rows_c,
    branch_rows,
    w_rows,
    folded,
):
    net = Net(send, recv)
    me = net.place({}, "z", "c", "f")
    load_w = pltpu.make_async_copy(w_attn.at[:, pl.ds(384, 128)], out_w, local.at[10])
    load_w.start()
    load_grad = pltpu.make_async_copy(grad_all_in, grad_all, local.at[11])
    load_grad.start()
    net.greet(ALL_G, NEAR_T)
    weights = Flow(
        gather_rest_flow(
            net,
            (ffn_block, ffn_below, ffn_above, ffn_beside),
            gather_slot(net, w_ffn, 256, "x", "h"),
            "x",
            "h",
            local.at[pl.ds(12, 4)],
            0,
            11,
        )
    )
    head_at = pl.ds(
        pl.multiple_of(net.at["f"] * 1024 + net.place({}, "z", "c") * 128, 128), 128
    )
    hidden_at = pl.ds(
        pl.multiple_of(net.at["f"] * 4096 + net.place({}, "z", "c") * 512, 512), 512
    )
    head_gain, head_shift = gains[1:2, head_at], shifts[1:2, head_at]
    gain_here, shift_here, bias_here = hid_gain[:, hidden_at], hid_shift[:, hidden_at], b_up[:, hidden_at]

    def exchange(sent, stats):
        copies = [net.push(sent, stats.at[me], offset) for offset in ALL_G]
        stats[me] = sent[...]
        for copy in copies:
            copy.wait_recv()

    def chunk(offset):
        at = net.place(offset, "z", "c", "f")
        return partial_rows.at[pl.ds(pl.multiple_of(at * 64, 64), 64)]

    def measure(i, carry):
        here = att[tile(i), :]
        centered = here - jnp.mean(here, axis=1, keepdims=True)
        put_sums(sent_a, i, here, centered * centered)
        return carry

    lax.fori_loop(0, 8, measure, 0, unroll=2)
    exchange(sent_a, stats_a)
    center = jnp.sum(stats_a[:, 0:8], axis=0) / 2048
    spread = jnp.sum(
        stats_a[:, 8:16] + 128 * jnp.square(stats_a[:, 0:8] / 128 - center[None]), axis=0
    )
    put_rows(rows_a, center, lax.rsqrt(spread / 2048 + EPS))

    def norm_heads(i, carry):
        columns = columns_of(rows_a, i)
        normal_rows = (att[tile(i), :] - columns[:, 0:1]) * columns[:, 1:2]
        normal_attn[tile(i), :] = normal_rows
        attn_low[tile(i), :] = (normal_rows * head_gain + head_shift).astype(BF)
        return carry

    lax.fori_loop(0, 8, norm_heads, 0, unroll=2)
    load_w.wait()

    def project(i, carry):
        partial_rows[:, tile(i, 256)] = lax.dot_general(
            attn_low[...], out_w[tile(i, 256), :], NT, preferred_element_type=F32
        ).astype(BF)
        return carry

    lax.fori_loop(0, 8, project, 0)
    run_until(
        Flow(scatter_flow(net, chunk, mid, mine, other, landed, local, "z", "f", True, False, 13, 5.5)),
        weights,
    )
    net.finish()

    def mid_norm(i, carry):
        at = tile(i, 16)
        branch_rows[at, :] = mid[at, :]
        rows = input_rows[at, :].astype(F32) + (mid[at, :] + b_out[...])
        mid[at, :] = rows
        centered = rows - jnp.mean(rows, axis=1, keepdims=True)
        scale = lax.rsqrt(jnp.mean(centered * centered, axis=1, keepdims=True) + EPS)
        rows = centered * scale
        normal_mid[at, :] = rows
        scale_mid[at, :] = jnp.broadcast_to(scale, (16, 128))
        low_rows[at, :] = (rows * gains[2:3, :] + shifts[2:3, :]).astype(BF)
        return carry

    lax.fori_loop(0, 4, mid_norm, 0)
    def hidden_grads():
        yield 43
        run_until(weights)
        load_grad.wait()
        for i in range(4):
            grad_hidden[tile(i, 256), :] = jnp.dot(
                grad_all[tile(i, 256), :], w_ffn[:, 512:1024], preferred_element_type=F32
            )
            yield 44

    run_flows(
        Flow(
            gather_flow(
                net, low_rows, gather_slot(net, mid_low, 64, "z", "f"), "z", "f", local.at[0], True, False, 31, 5.5
            )
        ),
        Flow(hidden_grads()),
        weights,
    )
    net.finish()

    def up(i, carry):
        at = tile(i)
        pre = jnp.dot(mid_low[at, :], w_ffn[:, 0:512], preferred_element_type=F32) + bias_here
        below = 0.5 + 0.5 * lax.erf(pre * math.sqrt(0.5))
        act = pre * below
        activated[at, :] = act
        slope[at, :] = below + pre * jnp.exp(-0.5 * pre * pre) * (1.0 / math.sqrt(2.0 * math.pi))
        centered = act - jnp.mean(act, axis=1, keepdims=True)
        scaled = grad_hidden[at, :] * gain_here
        put_sums(
            sent_b,
            i,
            fold_lanes(act),
            fold_lanes(centered * centered),
            fold_lanes(scaled),
            fold_lanes(scaled * centered),
        )
        return carry

    lax.fori_loop(0, 8, up, 0, unroll=2)
    exchange(sent_b, stats_b)
    center = jnp.sum(stats_b[:, 0:8], axis=0) / 8192
    apart = stats_b[:, 0:8] / 512 - center[None]
    spread = jnp.sum(stats_b[:, 8:16] + 512 * jnp.square(apart), axis=0)
    scale = lax.rsqrt(spread / 8192 + EPS)
    mean_back = jnp.sum(stats_b[:, 16:24], axis=0) / 8192
    cross_back = scale * jnp.sum(stats_b[:, 24:32] + apart * stats_b[:, 16:24], axis=0) / 8192
    put_rows(rows_b, center, scale, mean_back, cross_back)

    def hidden(i, carry):
        at = tile(i)
        columns = columns_of(rows_b, i)
        scale = columns[:, 1:2]
        normal_rows = (activated[at, :] - columns[:, 0:1]) * scale
        hidden_low[at, :] = (normal_rows * gain_here + shift_here).astype(BF)
        upstream = grad_hidden[at, :]
        back = scale * (upstream * gain_here - columns[:, 2:3] - normal_rows * columns[:, 3:4])
        low = (back * slope[at, :]).astype(BF)
        pre_low[at, :] = low
        return (
            carry[0] + jnp.sum(low.astype(F32), axis=0, keepdims=True),
            carry[1] + jnp.sum(upstream * normal_rows, axis=0, keepdims=True),
            carry[2] + jnp.sum(upstream, axis=0, keepdims=True),
        )

    sums = lax.fori_loop(0, 8, hidden, (jnp.zeros((1, 512), F32),) * 3)
    for k in range(3):
        hid_vec[k : k + 1, :] = sums[k]

    def project_back(i, carry):
        partial_rows[:, tile(i, 256)] = lax.dot_general(
            pre_low[...], w_ffn[tile(i, 256), 0:512], NT, preferred_element_type=F32
        ).astype(BF)
        return carry

    lax.fori_loop(0, 8, project_back, 0)

    def weight_terms():
        def turn(i, carry):
            pre_turned[:, tile(i)] = pre_low[tile(i), :].T
            hidden_turned[:, tile(i)] = hidden_low[tile(i), :].T
            return carry

        yield 69
        lax.fori_loop(0, 8, turn, 0)
        for k, (i, j) in enumerate(ROOTS):
            yield 70 + k
            columns = tile(net.place({"x": i, "h": j}, "x", "h"), 256)
            t_mine[k, 0:512, :] = jnp.dot(
                pre_turned[...], mid_low[:, columns], preferred_element_type=F32
            ).astype(BF)
            t_mine[k, 512:1024, :] = jnp.dot(
                hidden_turned[...], grad_all[:, columns], preferred_element_type=F32
            ).astype(BF)

    stores = []

    def weight_scatter():
        yield from weight_terms()
        yield from scatter_flow(
            net, None, None, t_mine, None, t_landed, local, "x", "h", False, False, 82, 11, False
        )
        for k in range(4):
            target = (ffn_up, ffn_down, ffn_across, ffn_own)[k]
            sums_store = pltpu.make_async_copy(t_mine.at[4 + k], target, local.at[16 + k])
            sums_store.start()
            stores.append(sums_store)

    weights = Flow(weight_scatter())
    run_until(
        Flow(scatter_flow(net, chunk, grad_mid, mine, other, landed, local, "z", "f", True, False, 68, 5.5)),
        weights,
    )
    net.finish()

    def mid_back(i, carry):
        at = tile(i, 16)
        upstream = grad_mid[at, :]
        normal_rows = normal_mid[at, :]
        scaled = upstream * gains[2:3, :]
        mean = jnp.mean(scaled, axis=1, keepdims=True)
        cross = jnp.mean(scaled * normal_rows, axis=1, keepdims=True)
        out_rows = grad_all[pl.ds(pl.multiple_of(me * 64 + i * 16, 16), 16), :].astype(F32)
        rows = out_rows + scale_mid[at, 0:1] * (scaled - mean - normal_rows * cross)
        grad_mid[at, :] = rows
        low = rows.astype(BF)
        low_rows[at, :] = low
        low = low.astype(F32)
        folded[0, at, :] = fold_groups(low * w_rows[0:1, :])
        folded[1, at, :] = fold_groups(low * (branch_rows[at, :] - w_rows[1:2, :]))
        row_vec[0:1, :] += jnp.sum(upstream * normal_rows, axis=0, keepdims=True)
        row_vec[1:2, :] += jnp.sum(upstream, axis=0, keepdims=True)
        row_vec[2:3, :] += jnp.sum(low, axis=0, keepdims=True)
        row_vec[3:4, :] += jnp.sum(out_rows, axis=0, keepdims=True)
        return carry

    row_vec[...] = jnp.zeros_like(row_vec)
    for g in range(16):
        w_rows[:, g * 128 : g * 128 + 128] = w_norm[g]
    lax.fori_loop(0, 4, mid_back, 0)
    def down():
        for i in range(8):
            yield 87 + i
            partial_rows[:, tile(i, 256)] = lax.dot_general(
                hidden_low[...], w_ffn[tile(i, 256), 512:1024], NT, preferred_element_type=F32
            ).astype(BF)

    def norm_sums():
        yield 86.5
        sums = [row_sums(folded[k]) * (1.0 / 2048) for k in range(2)]
        sent_c[...] = jnp.broadcast_to(jnp.concatenate(sums, axis=1), (8, 128))
        copies = [net.push(sent_c, stats_c.at[me], offset) for offset in ALL_G]
        stats_c[me] = sent_c[...]
        yield 99
        for copy in copies:
            copy.wait_recv()

    run_flows_but(
        weights,
        Flow(
            gather_flow(
                net, low_rows, gather_slot(net, branch_all, 64, "z", "f"), "z", "f", local.at[0], True, True, 86, 5.5
            )
        ),
        Flow(norm_sums()),
        Flow(down()),
    )
    store = pltpu.make_async_copy(partial_rows, ffn_part, local.at[8])
    store.start()

    lanes = lax.broadcasted_iota(jnp.int32, (1, 128), 1)
    for i in range(8):
        a, b = stats_c[2 * i, 0:1, :], stats_c[2 * i + 1, 0:1, :]
        rows_c[i, 0:1, :] = jnp.where(lanes < 64, a, pltpu.roll(b, 64, axis=1))
        rows_c[i, 1:2, :] = jnp.where(lanes < 64, pltpu.roll(a, 64, axis=1), b)
    keep = [
        pltpu.make_async_copy(branch_all, branch_out, local.at[20]),
        pltpu.make_async_copy(pre_turned.at[pl.ds(0, 128)], turned_out, local.at[21]),
    ]
    keep[0].start()

    def attn_back(i, carry):
        at = tile(i)
        upstream = jnp.dot(branch_all[at, :], out_w[...], preferred_element_type=F32)
        normal_rows = normal_attn[at, :]
        columns = columns_of(rows_c, i)
        scale = columns_of(rows_a, i)[:, 1:2]
        grad_att[at, :] = (
            scale * (upstream * head_gain - columns[:, 0:1] - normal_rows * columns[:, 1:2])
        ).astype(BF)
        pre_turned[0:128, at] = attn_low[at, :].T
        return (
            carry[0] + jnp.sum(upstream * normal_rows, axis=0, keepdims=True),
            carry[1] + jnp.sum(upstream, axis=0, keepdims=True),
        )

    sums = lax.fori_loop(0, 8, attn_back, (jnp.zeros((1, 128), F32),) * 2, unroll=2)
    for k in range(2):
        head_vec[k : k + 1, :] = sums[k]
    keep[1].start()
    for copy in keep:
        copy.wait()
    run_until(weights)
    for copy in stores:
        copy.wait()
    store.wait()
    net.finish()


def middle(number, *args):
    wide = pltpu.VMEM((1024, 512), F32)
    low = pltpu.VMEM((1024, 512), BF)
    tall = pltpu.VMEM((512, 1024), BF)
    whole = pltpu.VMEM((1024, 2048), BF)
    return comm_call(
        middle_kernel,
        "middle",
        number,
        15 * 3 + 20 * 4 + 14 * 2,
        22,
        (
            sds((64, 2048), F32),
            sds((64, 2048), F32),
            sds((1024, 2048), BF),
            sds((1024, 128), BF),
            *(sds((1024, 256), BF),) * 4,
            sds((1024, 2048), BF),
            sds((128, 1024), BF),
            sds((8, 512), F32),
            sds((8, 128), F32),
            sds((8, 2048), F32),
        ),
        [
            whole,
            pltpu.VMEM((2048, 128), BF),
            pltpu.VMEM((2048, 1024), BF),
            whole,
            whole,
            low,
            low,
            tall,
            tall,
            pltpu.VMEM((1024, 128), BF),
            pltpu.VMEM((64, 2048), BF),
            whole,
            pltpu.VMEM((8, 64, 2048), BF),
            pltpu.VMEM((7, 64, 2048), BF),
            pltpu.VMEM((8, 64, 2048), BF),
            pltpu.VMEM((8, 1024, 256), BF),
            pltpu.VMEM((7, 1024, 256), BF),
            wide,
            wide,
            wide,
            pltpu.VMEM((1024, 128), F32),
            pltpu.VMEM((64, 2048), F32),
            pltpu.VMEM((64, 128), F32),
            pltpu.VMEM((16, 128), F32),
            pltpu.VMEM((16, 16, 128), F32),
            pltpu.VMEM((8, 8, 128), F32),
            pltpu.VMEM((32, 128), F32),
            pltpu.VMEM((16, 32, 128), F32),
            pltpu.VMEM((8, 8, 128), F32),
            pltpu.VMEM((8, 128), F32),
            pltpu.VMEM((16, 8, 128), F32),
            pltpu.VMEM((8, 8, 128), F32),
            pltpu.VMEM((64, 2048), F32),
            pltpu.VMEM((8, 2048), F32),
            pltpu.VMEM((2, 64, 128), F32),
        ],
        [VMEM] + [ANY] * 6 + [VMEM] * 8,
        (VMEM, VMEM, ANY, VMEM) + (ANY,) * 6 + (VMEM,) * 3,
        *args,
    )


def tail_kernel(
    kv_part,
    ffn_part,
    ffn_own,
    ffn_up,
    ffn_down,
    ffn_across,
    query_grad,
    cosine,
    sine,
    growth,
    w_attn_in,
    in_low_in,
    branch_in,
    attn_turned,
    mid,
    grad_mid,
    input_rows,
    b_down,
    gains,
    hid_vec,
    head_vec,
    row_vec,
    out_half,
    in_half,
    attn_got,
    ffn_got,
    vectors,
    send,
    recv,
    local,
    kv_mine,
    kv_landed,
    kv_grad,
    f_mine,
    f_landed,
    f_other,
    i_mine,
    i_landed,
    i_other,
    w_mine,
    w_landed,
    w_grad,
    w_rows,
    attn_rows,
    ffn_rows,
    out_rows,
    in_rows,
    grad_qkv,
    turned,
    partial_rows,
    w_attn,
    in_low,
    branch_all,
    row_parts,
    row_got,
    packed,
    packed_got,
):
    net = Net(send, recv)
    me = net.place({}, "z", "c", "f")
    here = net.place({}, "z", "c")
    f = net.at["f"]
    load_w = pltpu.make_async_copy(w_attn_in, w_attn, local.at[16])
    load_w.start()
    load_in = pltpu.make_async_copy(in_low_in, in_low, local.at[21])
    load_in.start()
    load_branch = pltpu.make_async_copy(branch_in, branch_all, local.at[22])
    load_branch.start()
    net.greet(ALL_G, ALL_T)

    def to_halves(source, target, k):
        rows = target.at[pl.ds(pl.multiple_of(f * 64, 64), 64)]
        theirs = source.at[:, pl.ds(pl.multiple_of((1 - f) * 1024, 1024), 1024)]
        own = source.at[:, pl.ds(pl.multiple_of(f * 1024, 1024), 1024)]
        copy = net.push(theirs, rows, {"f": 1})
        keep = pltpu.make_async_copy(own, rows, local.at[k])
        keep.start()
        return copy, keep

    def to_rows(source, got, k):
        copies = []
        for offset in ALL_ZC:
            at = net.place(offset, "z", "c")
            copies.append(
                net.push(source.at[pl.ds(pl.multiple_of(at * 32, 32), 32)], got.at[here], offset)
            )
        keep = pltpu.make_async_copy(
            source.at[pl.ds(pl.multiple_of(here * 32, 32), 32)], got.at[here], local.at[k]
        )
        keep.start()
        return copies, keep

    def ffn_weights():
        def turn(i, carry):
            for j in range(2):
                at = slice(j * 128, j * 128 + 128)
                block = ffn_own[tile(i), at].astype(F32) + ffn_up[tile(i), at].astype(F32)
                block = block + (ffn_down[tile(i), at].astype(F32) + ffn_across[tile(i), at].astype(F32))
                block = block.T
                w_rows[j * 128 : j * 128 + 128, tile(i)] = block.astype(BF)
            return carry

        lax.fori_loop(0, 8, turn, 0)
        yield to_rows(w_rows, ffn_got, 17)

    kv_flow = Flow(
        scatter_flow(
            net,
            scatter_chunk(net, kv_part, "x"),
            kv_grad,
            kv_mine,
            None,
            kv_landed,
            local.at[pl.ds(0, 8)],
            "x",
            "h",
            False,
            False,
            0,
            11,
        )
    )
    ffn_flow = Flow(
        scatter_flow(
            net,
            scatter_chunk(net, ffn_part, "z"),
            ffn_rows,
            f_mine,
            f_other,
            f_landed,
            local.at[pl.ds(8, 8)],
            "z",
            "f",
            True,
            True,
            4,
            7,
        )
    )
    kv_flow.step()
    ffn_flow.step()
    ffn_copies, ffn_keep = next(ffn_weights())

    def out_terms():
        yield 6
        load_branch.wait()
        for k, (i, j) in enumerate(ROOTS):
            yield 7 + k
            columns = tile(net.place({"x": i, "h": j}, "x", "h"), 256)
            w_mine[k, 384:512, :] = jnp.dot(
                attn_turned[...], branch_all[:, columns], preferred_element_type=F32
            ).astype(BF)

    run_flows(kv_flow, ffn_flow, Flow(out_terms()))

    def finish_rows(i, carry):
        at = tile(i, 16)
        out_rows[at, :] = mid[at, :] + (ffn_rows[at, :] + b_down[...])
        return carry

    lax.fori_loop(0, 4, finish_rows, 0)
    out_copy, out_keep = to_halves(out_rows, out_half, 18)

    def unrotate(i, carry):
        at = tile(i)
        cos, sin, grow = cosine[at, :], sine[at, :], growth[at, :]
        queries = query_grad[at, :] * grow
        queries = (queries * cos - turn_halves(queries) * sin).astype(BF)
        keys = kv_grad[at, 0:128] / grow
        keys = (keys * cos - turn_halves(keys) * sin).astype(BF)
        values = kv_grad[at, 128:256].astype(BF)
        grad_qkv[at, 0:128] = queries
        grad_qkv[at, 128:256] = keys
        grad_qkv[at, 256:384] = values
        return tuple(
            total + jnp.sum(part.astype(F32), axis=0, keepdims=True)
            for total, part in zip(carry, (queries, keys, values))
        )

    bias = lax.fori_loop(0, 8, unrotate, (jnp.zeros((1, 128), F32),) * 3)
    for k in range(3):
        packed[8 + k : 9 + k, :] = bias[k]
    load_w.wait()

    def project(i, carry):
        partial_rows[:, tile(i, 256)] = lax.dot_general(
            grad_qkv[...], w_attn[tile(i, 256), 0:384], NT, preferred_element_type=F32
        ).astype(BF)
        return carry

    lax.fori_loop(0, 8, project, 0)

    def chunk(offset):
        at = net.place(offset, "z", "c", "f")
        return partial_rows.at[pl.ds(pl.multiple_of(at * 64, 64), 64)]

    def weight_scatter():
        def turn_grads(i, carry):
            turned[:, tile(i)] = grad_qkv[tile(i), :].T
            return carry

        yield 0.6
        lax.fori_loop(0, 8, turn_grads, 0)
        load_in.wait()
        for k, (i, j) in enumerate(ROOTS):
            yield 1 + k
            columns = tile(net.place({"x": i, "h": j}, "x", "h"), 256)
            w_mine[k, 0:384, :] = jnp.dot(
                turned[...], in_low[:, columns], preferred_element_type=F32
            ).astype(BF)
        yield from scatter_flow(
            net, None, w_grad, w_mine, None, w_landed, None, "x", "h", False, True, 0, 5.5
        )

    w_flow = Flow(weight_scatter())
    for _ in range(9):
        w_flow.step()
    in_flow = Flow(
        scatter_flow(net, chunk, in_rows, i_mine, i_other, i_landed, local, "z", "f", True, False, 0, 5.5)
    )
    run_until(in_flow, w_flow)

    def in_back(i, carry):
        at = tile(i, 16)
        rows = input_rows[at, :].astype(F32)
        centered = rows - jnp.mean(rows, axis=1, keepdims=True)
        scale = lax.rsqrt(jnp.mean(centered * centered, axis=1, keepdims=True) + EPS)
        normal_rows = centered * scale
        upstream = in_rows[at, :]
        scaled = upstream * gains[0:1, :]
        mean = jnp.mean(scaled, axis=1, keepdims=True)
        cross = jnp.mean(scaled * normal_rows, axis=1, keepdims=True)
        in_rows[at, :] = grad_mid[at, :] + scale * (scaled - mean - normal_rows * cross)
        return (
            carry[0] + jnp.sum(upstream * normal_rows, axis=0, keepdims=True),
            carry[1] + jnp.sum(upstream, axis=0, keepdims=True),
        )

    sums = lax.fori_loop(0, 4, in_back, (jnp.zeros((1, 2048), F32),) * 2)
    in_copy, in_keep = to_halves(in_rows, in_half, 19)
    run_until(w_flow)

    def turn_weights(i, carry):
        for j in range(2):
            w_grad_rows = w_grad[tile(i), j * 128 : j * 128 + 128].T
            attn_rows[j * 128 : j * 128 + 128, tile(i)] = w_grad_rows
        return carry

    for g in range(16):
        at = slice(g * 128, g * 128 + 128)
        for k in range(2):
            row_parts[g, k : k + 1, :] = sums[k][:, at]
        row_parts[g, 2:6, :] = row_vec[0:4, at]
        row_parts[g, 6:8, :] = jnp.zeros((2, 128), F32)
    copies = []
    for k, offset in enumerate(ALL_G):
        to = net.place(offset, "z", "c", "f")
        copies.append(net.push(row_parts.at[to], row_got.at[k], offset))
    lax.fori_loop(0, 4, turn_weights, 0)
    attn_copies, attn_keep = to_rows(attn_rows, attn_got, 20)
    packed[11:13, :] = head_vec[0:2, :]
    for k in range(3):
        for j in range(4):
            at = 13 + 4 * k + j
            packed[at : at + 1, :] = hid_vec[k : k + 1, j * 128 : j * 128 + 128]
    packed[25:32, :] = jnp.zeros((7, 128), F32)
    for copy in copies:
        copy.wait_recv()
    total = row_parts[me]
    for k in range(15):
        total = total + row_got[k]
    packed[0:8, :] = total
    copies = [net.push(packed, packed_got.at[k], offset) for k, offset in enumerate(ALL_T)]
    for copy in copies:
        copy.wait_recv()
    total = packed[...]
    for k in range(7):
        total = total + packed_got[k]
    vectors[me] = total
    copies = [net.push(vectors.at[me], vectors.at[me], offset) for offset in ALL_G]
    for copy in ffn_copies + attn_copies + copies + [out_copy, in_copy]:
        copy.wait_recv()
    for keep in (ffn_keep, attn_keep, out_keep, in_keep):
        keep.wait()
    net.finish()


def tail(number, *args):
    half = sds((128, 1024), F32)
    rows = pltpu.VMEM((64, 2048), F32)
    return comm_call(
        tail_kernel,
        "tail",
        number,
        12 + 22 + 7 + 20 + 12 + 2 + 7 + 37,
        23,
        (
            half,
            half,
            sds((8, 32, 512), F32),
            sds((8, 32, 1024), BF),
            sds((16, 32, 128), F32),
        ),
        scatter_scratch(1024, 256, False)
        + [pltpu.VMEM((1024, 256), F32)]
        + scatter_scratch(64, 2048, True)
        + scatter_scratch(64, 2048, True)
        + scatter_scratch(512, 256, False)
        + [
            pltpu.VMEM((512, 256), F32),
            pltpu.VMEM((256, 1024), BF),
            pltpu.VMEM((256, 512), F32),
            rows,
            rows,
            rows,
            pltpu.VMEM((1024, 384), BF),
            pltpu.VMEM((384, 1024), BF),
            pltpu.VMEM((1024, 2048), BF),
            pltpu.VMEM((2048, 512), BF),
            pltpu.VMEM((1024, 2048), BF),
            pltpu.VMEM((1024, 2048), BF),
            pltpu.VMEM((16, 8, 128), F32),
            pltpu.VMEM((15, 8, 128), F32),
            pltpu.VMEM((32, 128), F32),
            pltpu.VMEM((7, 32, 128), F32),
        ],
        [ANY, ANY] + [VMEM] * 8 + [ANY] * 3 + [VMEM] * 9,
        (VMEM,) * 5,
        *args,
    )


def assemble_kernel(
    out_in,
    in_in,
    attn_in,
    ffn_in,
    sums_in,
    out_half,
    in_half,
    qkv_out,
    out_out,
    up_out,
    down_out,
    qkv_bias,
    gains_out,
    shifts_out,
    out_bias,
    down_bias,
    up_bias,
    hid_gain_out,
    hid_shift_out,
    attn_got,
    ffn_got,
    sums,
    sems,
):
    pairs = ((out_in, out_half), (in_in, in_half), (sums_in, sums), (attn_in, attn_got), (ffn_in, ffn_got))
    copies = [pltpu.make_async_copy(a, b, sems.at[k]) for k, (a, b) in enumerate(pairs)]
    for copy in copies:
        copy.start()
    for copy in copies:
        copy.wait()

    def weights(i, carry):
        small, large = tile(i, 128), tile(i, 512)
        for j in range(3):
            qkv_out[j, :, small] = attn_got[i, :, j * 128 : j * 128 + 128]
        out_out[:, small] = attn_got[i, :, 384:512]
        up_out[:, large] = ffn_got[i, :, 0:512].astype(F32)
        down_out[:, large] = ffn_got[i, :, 512:1024].astype(F32)
        return carry

    lax.fori_loop(0, 8, weights, 0)

    def place(g, carry):
        by_rows, row_lanes = pl.ds(g, 1), tile(g)
        head = lax.rem(g, 2) * 8 + g // 2
        head_lanes = tile(head)
        for k, (target, j) in enumerate(
            ((gains_out, 0), (shifts_out, 0), (gains_out, 2), (shifts_out, 2))
        ):
            target[j : j + 1, row_lanes] = sums[g, k : k + 1, :]
        out_bias[by_rows, :] = sums[g, 4:5, :]
        down_bias[by_rows, :] = sums[g, 5:6, :]
        qkv_bias[:, head_lanes] = sums[g, 8:11, :]
        gains_out[1:2, head_lanes] = sums[g, 11:12, :]
        shifts_out[1:2, head_lanes] = sums[g, 12:13, :]
        for k, target in enumerate((up_bias, hid_gain_out, hid_shift_out)):
            for j in range(4):
                at = 13 + 4 * k + j
                target[pl.ds(head * 4 + j, 1), :] = sums[g, at : at + 1, :]
        return carry

    lax.fori_loop(0, 16, place, 0)


def assemble(*args):
    vector, hidden = sds((16, 128), F32), sds((64, 128), F32)
    triple = sds((3, 2048), F32)
    half = sds((128, 1024), F32)
    return pl.pallas_call(
        assemble_kernel,
        out_shape=(
            half,
            half,
            sds((3, 32, 1024), F32),
            sds((32, 1024), F32),
            sds((32, 4096), F32),
            sds((32, 4096), F32),
            triple,
            triple,
            triple,
            vector,
            vector,
            hidden,
            hidden,
            hidden,
        ),
        in_specs=[ANY] * 5,
        out_specs=(VMEM,) * 14,
        scratch_shapes=[
            pltpu.VMEM((8, 32, 512), F32),
            pltpu.VMEM((8, 32, 1024), BF),
            pltpu.VMEM((16, 32, 128), F32),
            DMA((5,)),
        ],
        name="assemble",
        compiler_params=pltpu.CompilerParams(vmem_limit_bytes=60 << 20),
    )(*args)


def both_heads(rows, zero):
    lanes = lax.broadcasted_iota(jnp.int32, rows.shape, 1)
    return jnp.where(lanes < HEAD, rows, zero), jnp.where(lanes >= HEAD, rows, zero)


def run_rows(ref, run):
    return ref[pl.ds(pl.multiple_of(run * RUN, RUN), RUN), :]


def pair_rows(ref, run_a, run_b, dtype):
    zero = jnp.zeros((), dtype)
    a = both_heads(run_rows(ref, run_a).astype(dtype), zero)
    b = both_heads(run_rows(ref, run_b).astype(dtype), zero)
    return jnp.concatenate(a + b, axis=0)


def pair_bounds(rank_a, rank_b):
    lanes = lax.broadcasted_iota(jnp.int32, (1, 256), 1)
    rank = jnp.where(lanes < 128, rank_a, rank_b)
    last = rank * RUN + lax.rem(lanes, RUN)
    return (rank // 64) * 4096, last


def seen(chunk, low, last):
    keys = chunk * CHUNK + lax.broadcasted_iota(jnp.int32, (CHUNK, 256), 0)
    return (keys >= low) & (keys <= last)


def sort_keys(order, kv_ref, kv):
    def move(r, carry):
        target = pl.ds(pl.multiple_of(order[0, r] * RUN, RUN), RUN)
        kv[target, :] = run_rows(kv_ref, r)
        return carry

    lax.fori_loop(0, 128, move, 0, unroll=4)


def flip(kv, columns, target):
    def one(i, carry):
        target[i] = kv[tile(i, CHUNK), columns].T
        return carry

    lax.fori_loop(0, 8192 // CHUNK, one, 0, unroll=2)


def over_chunks(rank_a, rank_b, step, start):
    low = (rank_a // 64) * (4096 // CHUNK)
    whole = jnp.where(rank_a // 64 == rank_b // 64, (rank_a // (CHUNK // RUN) - low), 0)

    def two(i, state):
        return step(low + i, state, False)

    state = lax.fori_loop(0, whole, two, start)
    return lax.fori_loop(
        low + whole, rank_b // (CHUNK // RUN) + 1, lambda i, state: step(i, state, True), state
    )


def lane_heads(total):
    turned = total.T
    lanes = lax.broadcasted_iota(jnp.int32, (RUN, 128), 1)
    a = jnp.where(lanes < HEAD, turned[0:64], turned[64:128])
    b = jnp.where(lanes < HEAD, turned[128:192], turned[192:256])
    return a, b


def attend_kernel(order, q_ref, kv_ref, o_ref, lse_ref, kv, flipped):
    sort_keys(order, kv_ref, kv)
    flip(kv, slice(128, 256), flipped)

    def pair(p, carry):
        run_a, run_b = order[1, 2 * p], order[1, 2 * p + 1]
        rank_a, rank_b = order[2, 2 * p], order[2, 2 * p + 1]
        queries = pair_rows(q_ref, run_a, run_b, BF)
        low, last = pair_bounds(rank_a, rank_b)

        def step(i, state, masked):
            peak, total, mixed = state
            scores = lax.dot_general(
                kv[tile(i, CHUNK), 0:128], queries, NT, preferred_element_type=F32
            )
            if masked:
                scores = jnp.where(seen(i, low, last), scores, -1e30)
            new_peak = jnp.maximum(peak, jnp.max(scores, axis=0, keepdims=True))
            weights = jnp.exp(scores - new_peak)
            shrink = jnp.exp(peak - new_peak)
            total = total * shrink + jnp.sum(weights, axis=0, keepdims=True)
            mixed = mixed * shrink + lax.dot_general(
                flipped[i], weights.astype(BF), NN, preferred_element_type=F32
            )
            return new_peak, total, mixed

        start = (
            jnp.full((1, 256), -1e20, F32),
            jnp.zeros((1, 256), F32),
            jnp.zeros((128, 256), F32),
        )
        peak, total, mixed = over_chunks(rank_a, rank_b, step, start)
        a, b = lane_heads(mixed / total)
        o_ref[pl.ds(pl.multiple_of(run_a * RUN, RUN), RUN), :] = a
        o_ref[pl.ds(pl.multiple_of(run_b * RUN, RUN), RUN), :] = b
        lse_ref[p] = peak + jnp.log(total)
        return carry

    lax.fori_loop(0, 8, pair, 0)


def attend(order, queries, kv):
    return pl.pallas_call(
        attend_kernel,
        out_shape=(sds((1024, 128), F32), sds((8, 1, 256), F32)),
        grid_spec=pltpu.PrefetchScalarGridSpec(
            num_scalar_prefetch=1,
            grid=(1,),
            in_specs=[VMEM, VMEM],
            out_specs=(VMEM, VMEM),
            scratch_shapes=[
                pltpu.VMEM((8192, 256), BF),
                pltpu.VMEM((8192 // CHUNK, 128, CHUNK), BF),
            ],
        ),
        name="attend",
        cost_estimate=pl.CostEstimate(flops=30_000_000_000, bytes_accessed=20_000_000, transcendentals=0),
        compiler_params=pltpu.CompilerParams(vmem_limit_bytes=60 << 20),
    )(order, queries, kv)


def attend_back_kernel(
    order, q_ref, kv_ref, g_ref, a_ref, lse_ref, dq_ref, dkv_ref, kv, flipped, dkeys, dvalues
):
    sort_keys(order, kv_ref, kv)
    flip(kv, slice(0, 128), flipped)

    def clear(i, carry):
        dkeys[tile(i, CHUNK), :] = jnp.zeros((CHUNK, 128), F32)
        dvalues[tile(i, CHUNK), :] = jnp.zeros((CHUNK, 128), F32)
        return carry

    lax.fori_loop(0, 8192 // CHUNK, clear, 0)

    def pair(p, carry):
        run_a, run_b = order[1, 2 * p], order[1, 2 * p + 1]
        rank_a, rank_b = order[2, 2 * p], order[2, 2 * p + 1]
        queries = pair_rows(q_ref, run_a, run_b, BF)
        grads = pair_rows(g_ref, run_a, run_b, BF)
        low, last = pair_bounds(rank_a, rank_b)
        product = pair_rows(g_ref, run_a, run_b, F32) * pair_rows(a_ref, run_a, run_b, F32)
        delta = row_sums(product)
        log_total = lse_ref[p]

        def step(i, dq, masked):
            rows = tile(i, CHUNK)
            scores = lax.dot_general(kv[rows, 0:128], queries, NT, preferred_element_type=F32)
            dprobs = lax.dot_general(kv[rows, 128:256], grads, NT, preferred_element_type=F32)
            probs = jnp.exp(scores - log_total)
            if masked:
                probs = jnp.where(seen(i, low, last), probs, 0.0)
            dscores = (probs * (dprobs - delta)).astype(BF)
            dvalues[rows, :] += lax.dot_general(
                probs.astype(BF), grads, NN, preferred_element_type=F32
            )
            dkeys[rows, :] += lax.dot_general(dscores, queries, NN, preferred_element_type=F32)
            return dq + lax.dot_general(flipped[i], dscores, NN, preferred_element_type=F32)

        dq = over_chunks(rank_a, rank_b, step, jnp.zeros((128, 256), F32))
        a, b = lane_heads(dq)
        dq_ref[pl.ds(pl.multiple_of(run_a * RUN, RUN), RUN), :] = a * 0.125
        dq_ref[pl.ds(pl.multiple_of(run_b * RUN, RUN), RUN), :] = b * 0.125
        return carry

    lax.fori_loop(0, 8, pair, 0)

    def back(r, carry):
        source = pl.ds(pl.multiple_of(order[0, r] * RUN, RUN), RUN)
        to = pl.ds(pl.multiple_of(r * RUN, RUN), RUN)
        dkv_ref[to, 0:128] = dkeys[source, :].astype(BF)
        dkv_ref[to, 128:256] = dvalues[source, :].astype(BF)
        return carry

    lax.fori_loop(0, 128, back, 0, unroll=4)


def attend_back(order, queries, kv, grads, attended, log_total):
    return pl.pallas_call(
        attend_back_kernel,
        out_shape=(sds((1024, 128), F32), sds((8192, 256), BF)),
        grid_spec=pltpu.PrefetchScalarGridSpec(
            num_scalar_prefetch=1,
            grid=(1,),
            in_specs=[VMEM] * 5,
            out_specs=(VMEM, VMEM),
            scratch_shapes=[
                pltpu.VMEM((8192, 256), BF),
                pltpu.VMEM((8192 // CHUNK, 128, CHUNK), BF),
                pltpu.VMEM((8192, 128), F32),
                pltpu.VMEM((8192, 128), F32),
            ],
        ),
        name="attend_back",
        cost_estimate=pl.CostEstimate(flops=30_000_000_000, bytes_accessed=20_000_000, transcendentals=0),
        compiler_params=pltpu.CompilerParams(vmem_limit_bytes=60 << 20),
    )(order, queries, kv, grads, attended, log_total)


def lane_tables(seq_length):
    half = HEAD // 2
    indices = (np.arange(128) % half).astype(np.float32)
    inverse_freq = np.exp(-np.log(np.float32(10000.0)) * indices / np.float32(half)).astype(np.float64)
    ratios = np.log((2.0 * indices + 0.4 * HEAD) / (1.4 * HEAD)).astype(np.float64)

    def tables(places, powers):
        angles = places[:, None] * inverse_freq[None, :]
        growth = np.exp(powers[:, None] * ratios[None, :])
        return np.stack([np.cos(angles), np.sin(angles), growth]).astype(np.float32)

    runs = np.arange(64) * float(RUN)
    tokens = np.arange(RUN).astype(np.float64)
    return (
        jnp.asarray(tables(runs, (runs - seq_length // 2) / 512.0)),
        jnp.asarray(tables(tokens, tokens / 512.0)),
    )


def shards(
    layer_input,
    w_qkv,
    w_out,
    w_up,
    w_down,
    b_qkv,
    b_out,
    b_up,
    b_down,
    norm_gains,
    norm_shifts,
    hidden_gain,
    hidden_shift,
    seq_ids,
    positions,
    d_out,
):
    packed = jnp.concatenate(
        [
            w_qkv.reshape(32, 3, 8, 128).transpose(2, 0, 1, 3).reshape(8, 32, 384),
            w_out.reshape(32, 8, 128).transpose(1, 0, 2),
        ],
        axis=2,
    )
    run_tables, token_tables = lane_tables(4096)
    (
        input_rows,
        in_low,
        w_attn,
        ffn_block,
        query_low,
        kv,
        grad_all,
        cosine,
        sine,
        growth,
        order,
        w_norm,
    ) = front(
        1,
        layer_input,
        d_out,
        packed,
        w_up,
        w_down,
        seq_ids.reshape(1, 128),
        positions.reshape(1, 128),
        norm_gains,
        norm_shifts,
        b_qkv,
        run_tables,
        token_tables,
    )
    ffn_near = (
        lax.ppermute(ffn_block, "x", UP),
        lax.ppermute(ffn_block, "x", DOWN),
        lax.ppermute(ffn_block, "h", ACROSS),
    )
    attended, log_total = attend(order, query_low, kv)
    (
        mid,
        grad_mid,
        ffn_part,
        grad_attended,
        ffn_up,
        ffn_down,
        ffn_across,
        ffn_own,
        branch_all,
        attn_turned,
        hid_vec,
        head_vec,
        row_vec,
    ) = middle(
        3,
        attended,
        w_attn,
        ffn_block,
        *ffn_near,
        grad_all,
        input_rows,
        b_out.reshape(1, 2048),
        b_up.reshape(1, 8192),
        norm_gains,
        norm_shifts,
        hidden_gain.reshape(1, 8192),
        hidden_shift.reshape(1, 8192),
        w_norm,
    )
    ffn_got = (
        lax.ppermute(ffn_up, "x", UP),
        lax.ppermute(ffn_down, "x", DOWN),
        lax.ppermute(ffn_across, "h", ACROSS),
    )
    query_grad, kv_part = attend_back(order, query_low, kv, grad_attended, attended, log_total)
    parts = tail(
        4,
        kv_part.reshape(8, 1024, 256),
        ffn_part.reshape(16, 64, 2048),
        ffn_own,
        *ffn_got,
        query_grad,
        cosine,
        sine,
        growth,
        w_attn,
        in_low,
        branch_all,
        attn_turned,
        mid,
        grad_mid,
        input_rows,
        b_down.reshape(1, 2048),
        norm_gains,
        hid_vec,
        head_vec,
        row_vec,
    )
    (
        layer_output,
        input_grad,
        qkv_grad,
        out_grad,
        up_grad,
        down_grad,
        qkv_bias,
        gains_grad,
        shifts_grad,
        out_bias,
        down_bias,
        up_bias,
        hid_gain_grad,
        hid_shift_grad,
    ) = assemble(*parts)
    return (
        layer_output,
        input_grad,
        qkv_grad.transpose(1, 0, 2),
        out_grad,
        up_grad,
        down_grad,
        qkv_bias,
        out_bias.reshape(2048),
        up_bias.reshape(8192),
        down_bias.reshape(2048),
        gains_grad,
        shifts_grad,
        hid_gain_grad.reshape(8192),
        hid_shift_grad.reshape(8192),
    )


def solution(mesh):
    fine = Mesh(mesh.devices.reshape(4, 2, 4, 2, 2), SEQ + ("f",))
    both = P(SEQ, "f")
    return jax.shard_map(
        shards,
        mesh=fine,
        in_specs=(both, P(SEQ, None, "f"), both, both, both)
        + (P(),) * 8
        + (P(SEQ), P(SEQ), both),
        out_specs=(both, both, P(SEQ, None, "f"), both, both, both) + (P(),) * 8,
        check_vma=False,
    )
```

```python
import math

import jax
import jax.numpy as jnp
import numpy as np
from jax import lax
from jax.experimental import pallas as pl
from jax.experimental.pallas import tpu as pltpu
from jax.sharding import Mesh
from jax.sharding import PartitionSpec as P

SEQ = ("x", "h", "z", "c")
TOK = ("x", "h")
HEAD = 64
RUN = 64
CHUNK = 1024
EPS = 1e-05
MESH = pl.DeviceIdType.MESH
BF = jnp.bfloat16
F32 = jnp.float32
DMA = pltpu.SemaphoreType.DMA
ANY = pl.BlockSpec(memory_space=pl.ANY)
VMEM = pl.BlockSpec(memory_space=pltpu.VMEM)
NT = (((1,), (1,)), ((), ()))
TN = (((0,), (0,)), ((), ()))
NN = (((1,), (0,)), ((), ()))


def sds(shape, dtype):
    return jax.ShapeDtypeStruct(shape, dtype)


AXES = {"x": 4, "h": 2, "z": 4, "c": 2, "f": 2}
RING_G, PAIR_G = "z", "f"
RING_T, PAIR_T = "x", "h"


class Net:
    loads = []

    def __init__(self, send, recv):
        self.send, self.recv, self.copies, self.drained = send, recv, [], 0
        self.at = {axis: lax.axis_index(axis) for axis in AXES}

    def device(self, offset):
        return {a: lax.rem(self.at[a] + d + AXES[a], AXES[a]) for a, d in offset.items()}

    def place(self, offset, *axes):
        index = 0
        for a in axes:
            d = offset.get(a, 0)
            at = lax.rem(self.at[a] + d + AXES[a], AXES[a]) if d else self.at[a]
            index = index * AXES[a] + at
        return index

    def greet(self, *groups):
        offsets = {
            tuple((a, o[a]) for a in AXES if o.get(a, 0)) for group in groups for o in group
        }
        barrier = pltpu.get_barrier_semaphore()
        for offset in sorted(offsets):
            pl.semaphore_signal(
                barrier, inc=1, device_id=self.device(dict(offset)), device_id_type=MESH
            )
        pl.semaphore_wait(barrier, len(offsets))
        while self.loads:
            self.loads.pop().wait()

    def push(self, src, dst, offset):
        k = len(self.copies)
        copy = pltpu.make_async_remote_copy(
            src_ref=src,
            dst_ref=dst,
            send_sem=self.send.at[k],
            recv_sem=self.recv.at[k],
            device_id=self.device(offset),
            device_id_type=MESH,
        )
        copy.start()
        self.copies.append(copy)
        return copy

    def finish(self):
        for copy in self.copies[self.drained :]:
            copy.wait_send()
        self.drained = len(self.copies)


UP = [(i, (i + 1) % 4) for i in range(4)]
DOWN = [(i, (i + 3) % 4) for i in range(4)]
ACROSS = [(0, 1), (1, 0)]
SIBLING = {"c": 1}
NEAR_G = [{"z": 1}, {"z": 3}, {"f": 1}, SIBLING]
NEAR_T = [{"x": 1}, {"x": 3}, {"h": 1}]
ALL_T = [{"x": i, "h": j} for i in range(4) for j in range(2)][1:]
ALL_ZC = [{"z": i, "c": j} for i in range(4) for j in range(2)][1:]
ALL_G = [{"z": i, "c": j, "f": k} for i in range(4) for j in range(2) for k in range(2)][1:]


class Flow:
    def __init__(self, steps):
        self.steps = steps
        self.step()

    def step(self):
        self.time = next(self.steps, None)


def run_until(main, *others):
    while main.time is not None:
        ready = [flow for flow in (main,) + others if flow.time is not None]
        min(ready, key=lambda flow: flow.time).step()


def run_flows(*flows):
    for flow in flows:
        run_until(flow, *flows)


def run_flows_but(kept, *flows):
    for flow in flows:
        run_until(flow, kept, *flows)


def half_rows(ref, which):
    rows = ref.shape[0] // 2
    return ref.at[pl.ds(which * rows, rows)]


def gather_flow(
    net, src, slot, ring, pair, local, sibling, light, at, unit, hold=0, arrived=None
):
    up, down, across = {ring: 1}, {ring: 3}, {pair: 1}
    passed = {}

    def to_sibling(ref, i, j):
        if sibling:
            passed[i, j] = net.push(ref, ref, SIBLING)

    def both_ways(ref, target):
        return [
            [net.push(half_rows(ref, k), half_rows(target, k), to) for k in order]
            for to, order in ((up, (0, 1)), (down, (1, 0)))
        ]

    def show(*places):
        if arrived is not None:
            for i in places:
                arrived({ring: i})

    def show_sibling(*places):
        if arrived is not None:
            for i in places:
                for j in range(2):
                    passed.pop((i, j)).wait_recv()
                arrived({ring: i, "c": 1})

    mine = slot({})
    from_down, from_up = both_ways(src, mine)
    if hold:
        yield at + hold
    from_across = net.push(src, mine, across)
    if sibling:
        passed[0, 0] = net.push(src, mine, SIBLING)
    here = pltpu.make_async_copy(src, mine, local)
    here.start()
    below, above, beside, far = (slot({ring: 3}), slot({ring: 1}), slot({pair: 1}), slot({ring: 2}))
    yield at + 0.5 * unit
    from_down[0].wait_recv()
    first = net.push(half_rows(below, 0), half_rows(below, 0), up)
    from_up[0].wait_recv()
    second = net.push(half_rows(above, 1), half_rows(above, 1), down)
    yield at + unit + hold
    from_across.wait_recv()
    if light:
        beside_down, beside_up = both_ways(beside, beside)
    else:
        beside_down = [net.push(beside, beside, up)]
        beside_up = [net.push(beside, beside, down)]
    to_sibling(beside, 0, 1)
    yield at + unit + hold
    from_down[1].wait_recv()
    to_sibling(below, 3, 0)
    from_up[1].wait_recv()
    to_sibling(above, 1, 0)
    here.wait()
    show(0)
    yield at + 1.5 * unit + hold
    first.wait_recv()
    if not light:
        beside_far = [net.push(half_rows(far, 0), half_rows(far, 0), across)]
    second.wait_recv()
    if not light:
        beside_far.append(net.push(half_rows(far, 1), half_rows(far, 1), across))
    to_sibling(far, 2, 0)
    show_sibling(0)
    yield at + (1.7 if light and hold else 2 if light else 2.5) * unit + hold
    below, above = slot({ring: 3, pair: 1}), slot({ring: 1, pair: 1})
    if light:
        beside_down[0].wait_recv()
        beside_far = [net.push(half_rows(below, 0), half_rows(below, 0), up)]
        beside_up[0].wait_recv()
        beside_far.append(net.push(half_rows(above, 1), half_rows(above, 1), down))
        yield at + 2.5 * unit + hold
    beside_down[-1].wait_recv()
    to_sibling(below, 3, 1)
    beside_up[-1].wait_recv()
    to_sibling(above, 1, 1)
    show(3, 1)
    yield at + (3 if light else 2.5) * unit + hold
    for copy in beside_far:
        copy.wait_recv()
    to_sibling(slot({ring: 2, pair: 1}), 2, 1)
    show_sibling(3, 1)
    show(2)
    yield at + (3 if light else 2.5) * unit + hold
    show_sibling(2)
    for copy in passed.values():
        copy.wait_recv()


def gather_rest_flow(net, blocks, slot, ring, pair, local, at, unit):
    up, down = {ring: 1}, {ring: 3}
    mine, below, above, beside = (slot(o) for o in ({}, {ring: 3}, {ring: 1}, {pair: 1}))
    beside_down = [net.push(half_rows(blocks[3], k), half_rows(beside, k), up) for k in (0, 1)]
    beside_up = [net.push(half_rows(blocks[3], k), half_rows(beside, k), down) for k in (1, 0)]
    far = [
        net.push(half_rows(blocks[1], 0), half_rows(below, 0), up),
        net.push(half_rows(blocks[2], 1), half_rows(above, 1), down),
    ]
    here = [
        pltpu.make_async_copy(block, target, local.at[k])
        for k, (block, target) in enumerate(zip(blocks, (mine, below, above, beside)))
    ]
    for copy in here:
        copy.start()
    yield at + 0.7 * unit
    below, above = slot({ring: 3, pair: 1}), slot({ring: 1, pair: 1})
    beside_down[0].wait_recv()
    far.append(net.push(half_rows(below, 0), half_rows(below, 0), up))
    beside_up[0].wait_recv()
    far.append(net.push(half_rows(above, 1), half_rows(above, 1), down))
    yield at + 2.1 * unit
    for copy in far + beside_down[1:] + beside_up[1:]:
        copy.wait_recv()
    for copy in here:
        copy.wait()


def add_into(target, *sources):
    rows = min(32768 // target.shape[1], target.shape[0])

    def step(i, carry):
        at = pl.ds(pl.multiple_of(i * rows, rows), rows)
        total = target[at, :].astype(F32)
        for source in sources:
            total = total + source[at, :].astype(F32)
        target[at, :] = total.astype(target.dtype)
        return carry

    lax.fori_loop(0, target.shape[0] // rows, step, 0)


ROOTS = ((2, 1), (1, 1), (3, 1), (2, 0), (1, 0), (3, 0), (0, 1), (0, 0))


def scatter_flow(
    net, chunk, out, mine, other, landed, local, ring, pair, sibling, light, at, unit, last=True
):
    up, down, across = {ring: 1}, {ring: 3}, {pair: 1}
    loads, shared = [], []
    for k, (i, j) in enumerate(ROOTS):
        if sibling:
            shared.append(net.push(chunk({ring: i, pair: j, "c": 1}), other.at[k], SIBLING))
        if chunk is not None:
            load = pltpu.make_async_copy(chunk({ring: i, pair: j}), mine.at[k], local.at[k])
            load.start()
            loads.append(load)

    def ready(k):
        if chunk is not None:
            loads[k].wait()
        if sibling:
            shared[k].wait_recv()
            add_into(mine.at[k], other.at[k])

    def halves(k, to):
        return (
            net.push(half_rows(mine.at[k], 0), half_rows(landed.at[to], 0), down),
            net.push(half_rows(mine.at[k], 1), half_rows(landed.at[to], 1), up),
        )

    def add_half(k, source, which):
        add_into(half_rows(mine.at[k], which), half_rows(landed.at[source], which))

    def send_half(k, to, which, offset):
        return net.push(half_rows(mine.at[k], which), half_rows(landed.at[to], which), offset)

    if chunk is not None:
        yield at + 0.5
    ready(0)
    if light:
        beside_first, beside_second = halves(0, 0)
        ready(3)
        first, second = halves(3, 3)
        ready(2)
        beside_up = [send_half(2, 2, 1, down)]
        ready(1)
        beside_down = [send_half(1, 1, 0, up)]
        yield at + 0.5 * unit
        beside_first.wait_recv()
        add_half(2, 0, 0)
        beside_up.append(send_half(2, 2, 0, down))
        beside_second.wait_recv()
        add_half(1, 0, 1)
        beside_down.append(send_half(1, 1, 1, up))
    else:
        beside_far = [send_half(0, 0, k, across) for k in range(2)]
        ready(1)
        beside_down = [net.push(mine.at[1], landed.at[1], up)]
        ready(2)
        beside_up = [net.push(mine.at[2], landed.at[2], down)]
        ready(3)
        yield at + 0.6 * unit
        beside_far[0].wait_recv()
        add_half(3, 0, 0)
        first = send_half(3, 3, 0, down)
        yield at + unit
        beside_far[1].wait_recv()
        add_half(3, 0, 1)
        second = send_half(3, 3, 1, up)
    ready(5)
    ready(4)
    if last:
        from_up = [send_half(5, 5, 1, down)]
        from_down = [send_half(4, 6, 0, up)]
    if not light:
        ready(6)
        yield at + 1.1 * unit
        for copy in beside_down + beside_up:
            copy.wait_recv()
        add_into(mine.at[6], landed.at[1], landed.at[2])
        if last:
            from_across = net.push(mine.at[6], landed.at[4], across)
    yield at + (1.1 if light else 1.6) * unit
    first.wait_recv()
    add_half(5, 3, 0)
    if last:
        from_up.append(send_half(5, 5, 0, down))
    yield at + (1.1 if light else 1.8) * unit
    second.wait_recv()
    add_half(4, 3, 1)
    if not last:
        return
    from_down.append(send_half(4, 6, 1, up))
    if light:
        ready(6)
        yield at + 2 * unit
        for copy in beside_down + beside_up:
            copy.wait_recv()
        add_into(mine.at[6], landed.at[1], landed.at[2])
        from_across = net.push(mine.at[6], landed.at[4], across)
    ready(7)
    yield at + (3 if light else 2.5) * unit
    for copy in from_up + from_down + [from_across]:
        copy.wait_recv()
    rows = 32768 // out.shape[1]

    def total(i, carry):
        at = pl.ds(pl.multiple_of(i * rows, rows), rows)
        value = mine[7, at, :].astype(F32) + landed[4, at, :].astype(F32)
        out[at, :] = value + (landed[5, at, :].astype(F32) + landed[6, at, :].astype(F32))
        return carry

    lax.fori_loop(0, out.shape[0] // rows, total, 0)


def gather_slot(net, out, rows, ring, pair):
    order = ("z", "c", "f") if ring == "z" else ("x", "h")

    def slot(offset):
        at = net.place(offset, *order)
        return out.at[pl.ds(pl.multiple_of(at * rows, rows), rows)]

    return slot


def input_slot(net, out):
    def slot(offset):
        row = pl.multiple_of(net.place(offset, "z", "c") * 128, 128)
        column = pl.multiple_of(net.place(offset, "f") * 1024, 1024)
        return out.at[pl.ds(row, 128), pl.ds(column, 1024)]

    return slot


def scatter_chunk(net, ref, ring):
    order = ("z", "c", "f") if ring == "z" else ("x", "h")
    return lambda offset: ref.at[net.place(offset, *order)]


def comm_call(kernel, name, number, pushes, locals_, out_shape, scratch, in_specs, out_specs, *args):
    ins = [i for i, spec in enumerate(in_specs) if spec is VMEM]
    outs = [i for i, spec in enumerate(out_specs) if spec is VMEM]
    shapes = [args[i] for i in ins] + [out_shape[i] for i in outs]
    first = len(args) + len(out_shape)
    last = first + 3 + len(scratch)

    def staged(*refs):
        given, results = list(refs[: len(args)]), list(refs[len(args) : first])
        sems, buffers = refs[last], refs[last + 1 :]
        for k, i in enumerate(ins):
            copy = pltpu.make_async_copy(given[i], buffers[k], sems.at[k])
            copy.start()
            Net.loads.append(copy)
            given[i] = buffers[k]
        stores = []
        for k, i in enumerate(outs, len(ins)):
            stores.append(pltpu.make_async_copy(buffers[k], results[i], sems.at[k]))
            results[i] = buffers[k]
        kernel(*given, *results, *refs[first:last])
        for copy in stores:
            copy.start()
        for copy in stores:
            copy.wait()

    return pl.pallas_call(
        staged,
        out_shape=out_shape,
        in_specs=[ANY] * len(in_specs),
        out_specs=(ANY,) * len(out_specs),
        scratch_shapes=[DMA((pushes,)), DMA((pushes,)), DMA((locals_,))]
        + scratch
        + [DMA((len(shapes),))]
        + [pltpu.VMEM(v.shape, v.dtype) for v in shapes],
        name=name,
        compiler_params=pltpu.CompilerParams(
            collective_id=number, has_side_effects=True, vmem_limit_bytes=60 << 20
        ),
    )(*args)


def scatter_scratch(rows, width, sibling):
    shapes = [pltpu.VMEM((8, rows, width), BF), pltpu.VMEM((7, rows, width), BF)]
    return shapes + ([pltpu.VMEM((8, rows, width), BF)] if sibling else [])


def turn_halves(values):
    lanes = lax.broadcasted_iota(jnp.int32, values.shape, 1)
    first = lax.rem(lanes, HEAD) < HEAD // 2
    return jnp.where(first, pltpu.roll(values, 96, axis=1), pltpu.roll(values, 32, axis=1))


def front_kernel(
    x_ref,
    d_ref,
    w_ref,
    up_ref,
    down_ref,
    seq_ref,
    place_ref,
    gains,
    shifts,
    bias,
    run_tables,
    token_tables,
    rows_out,
    low_out,
    w_out,
    ffn_out,
    q_out,
    kv_out,
    grad_out,
    cosine,
    sine,
    growth,
    order,
    w_norm,
    send,
    recv,
    local,
    x_all,
    in_low,
    w_all,
    blocks,
    near,
    near_sum,
    far,
    kv_here,
    norm_parts,
    norm_got,
    ranks_here,
):
    net = Net(send, recv)
    net.greet(ALL_G, ALL_T)
    me = net.place({}, "z", "c")
    group = net.place({}, "x", "h")
    f = net.at["f"]
    rows = pl.ds(pl.multiple_of(me * 32, 32), 32)
    stores = []

    def store(src, dst, k):
        copy = pltpu.make_async_copy(src, dst, local.at[k])
        copy.start()
        stores.append(copy)

    def norm_block(offset):
        first = net.place(offset, "z", "c") * 128

        def norm_rows(i, carry):
            at = pl.ds(pl.multiple_of(first + i * 16, 16), 16)
            values = x_all[at, :].astype(F32)
            centered = values - jnp.mean(values, axis=1, keepdims=True)
            scale = lax.rsqrt(jnp.mean(centered * centered, axis=1, keepdims=True) + EPS)
            in_low[at, :] = (centered * scale * gains[0:1, :] + shifts[0:1, :]).astype(BF)
            return carry

        lax.fori_loop(0, 8, norm_rows, 0, unroll=4)

    def activations():
        yield from gather_flow(
            net, x_ref, input_slot(net, x_all), "z", "f", local.at[0], True, True, 0, 5.5, 0, norm_block
        )
        ffn_sent = []
        for offset in ALL_ZC:
            to = net.place(offset, "z", "c")
            at = pl.ds(pl.multiple_of(to * 512, 512), 512)
            ffn_sent.append(net.push(up_ref.at[:, at], ffn_out.at[rows, pl.ds(0, 512)], offset))
            ffn_sent.append(net.push(down_ref.at[:, at], ffn_out.at[rows, pl.ds(512, 512)], offset))
        at = pl.ds(pl.multiple_of(me * 512, 512), 512)
        store(up_ref.at[:, at], ffn_out.at[rows, pl.ds(0, 512)], 4)
        store(down_ref.at[:, at], ffn_out.at[rows, pl.ds(512, 512)], 5)
        store(in_low, low_out, 6)
        store(x_all.at[pl.ds(pl.multiple_of((me * 2 + f) * 64, 64), 64)], rows_out, 7)
        yield from gather_flow(
            net, d_ref, input_slot(net, grad_out), "z", "f", local.at[1], True, True, 24, 8
        )
        for copy in ffn_sent:
            copy.wait_recv()

    def run_rank(index):
        lanes = lax.broadcasted_iota(jnp.int32, (1, 128), 1)
        return jnp.sum(jnp.where(lanes == index, near_sum[0:1, :], 0.0), axis=1, keepdims=True)

    def tables(i, carry):
        at = tile(i, RUN)
        block = run_rank(group * 16 + i)
        block = block - jnp.floor(block / 64) * 64
        mask = lax.broadcasted_iota(jnp.int32, (64, 128), 0).astype(F32) == block
        cos_a, sin_a, grow_a = (
            jnp.sum(jnp.where(mask, run_tables[k], 0.0), axis=0, keepdims=True) for k in range(3)
        )
        cos_b, sin_b, grow_b = token_tables[0], token_tables[1], token_tables[2]
        lanes = lax.broadcasted_iota(jnp.int32, (RUN, 128), 1)
        sin = sin_a * cos_b + cos_a * sin_b
        cosine[at, :] = cos_a * cos_b - sin_a * sin_b
        sine[at, :] = jnp.where(lax.rem(lanes, HEAD) < HEAD // 2, -sin, sin)
        growth[at, :] = grow_a * grow_b
        return carry

    def put_order():
        lanes = lax.broadcasted_iota(jnp.int32, (16, 128), 1)
        places = lax.broadcasted_iota(jnp.int32, (16, 128), 0)
        ranks = jnp.zeros((16, 128), F32)
        by_lane = jnp.full((16, 128), 1e9, F32)
        for k in range(16):
            rank = run_rank(group * 16 + k)
            ranks = jnp.where(places == k, rank, ranks)
            by_lane = jnp.where(lanes == k, rank, by_lane)
        slot = jnp.sum((by_lane < ranks).astype(F32), axis=1, keepdims=True)
        hit = lanes.astype(F32) == slot
        runs = jnp.sum(jnp.where(hit, places.astype(F32), 0.0), axis=0, keepdims=True)
        ranks = jnp.sum(jnp.where(hit, ranks, 0.0), axis=0, keepdims=True)
        total = jnp.sum(far[...], axis=0)[0:1]
        order[0:1, :] = total.astype(jnp.int32)
        order[1:2, :] = runs.astype(jnp.int32)
        order[2:3, :] = ranks.astype(jnp.int32)
        order[3:8, :] = jnp.zeros((5, 128), jnp.int32)

    head_at = pl.ds(pl.multiple_of(f * 1024 + me * 128, 128), 128)

    def project(i, carry):
        at = tile(i, 256)
        values = jnp.dot(in_low[at, :], w_all[:, 0:384], preferred_element_type=F32)
        queries = values[:, 0:128] + bias[0:1, head_at]
        keys = values[:, 128:256] + bias[1:2, head_at]
        cos, sin, grow = cosine[at, :], sine[at, :], growth[at, :]
        queries = ((queries * cos + turn_halves(queries) * sin) * grow).astype(BF)
        q_out[at, :] = queries * jnp.bfloat16(0.125)
        keys = (keys * cos + turn_halves(keys) * sin) * (1.0 / grow)
        kv_here[at, 0:128] = keys.astype(BF)
        kv_here[at, 128:256] = (values[:, 256:384] + bias[2:3, head_at]).astype(BF)
        return carry

    def put_ranks():
        lanes = lax.broadcasted_iota(jnp.int32, (1, 128), 1)
        ranks = (seq_ref[...] * 64 + place_ref[...] // RUN).astype(F32)
        first, second = (
            jnp.sum(jnp.where(lanes == k * RUN, ranks, 0.0), axis=1, keepdims=True) for k in range(2)
        )
        at = net.place({}, "x", "h", "z", "c") * 2
        row = jnp.where(lanes == at, first, jnp.where(lanes == at + 1, second, 0.0))
        ranks_here[...] = jnp.broadcast_to(row, (8, 128))

    def attention():
        attn_sent, near_sent = [], []
        put_ranks()
        for offset in ALL_ZC:
            to = net.place(offset, "z", "c")
            attn_sent.append(net.push(w_ref.at[to], blocks.at[rows], offset))
        for offset in ALL_ZC:
            near_sent.append(net.push(ranks_here, near.at[me], offset))
        own = pltpu.make_async_copy(w_ref.at[me], blocks.at[rows], local.at[2])
        own.start()
        near[me] = ranks_here[...]
        own.wait()
        yield 5
        for copy in attn_sent:
            copy.wait_recv()
        weights = gather_flow(
            net, blocks, gather_slot(net, w_all, 256, "x", "h"), "x", "h", local.at[3], False, False, 6, 5.5
        )
        yield next(weights)
        for copy in near_sent:
            copy.wait_recv()
        near_sum[...] = jnp.sum(near[...], axis=0)
        far_sent = [net.push(near_sum, far.at[group], offset) for offset in ALL_T]
        far[group] = near_sum[...]
        lax.fori_loop(0, 16, tables, 0)
        yield from weights
        store(w_all, w_out, 8)
        yield 26
        lax.fori_loop(0, 4, project, 0, unroll=2)
        sending = gather_flow(
            net, kv_here, gather_slot(net, kv_out, 1024, "x", "h"), "x", "h", local.at[9], False, False, 29, 11
        )
        yield next(sending)
        for copy in far_sent:
            copy.wait_recv()
        put_order()
        yield from sending

    def norm_sums():
        yield 25
        gain, shift = gains[1:2, head_at], shifts[1:2, head_at]
        high = [gain.astype(BF), shift.astype(BF)]
        low = [(v - h.astype(F32)).astype(BF) for v, h in zip((gain, shift), high)]
        vectors = jnp.concatenate(high + low + [jnp.zeros((12, 128), BF)], axis=0)

        def norm_vectors(i, carry):
            parts = lax.dot_general(
                vectors, w_all[tile(i, 128), 384:512], NT, preferred_element_type=F32
            )
            norm_parts[i] = parts[0:8] + jnp.concatenate([parts[2:8], parts[8:10]], axis=0)
            return carry

        lax.fori_loop(0, 16, norm_vectors, 0)
        mine = net.place({}, "z", "c", "f")
        sent = []
        for k, offset in enumerate(ALL_G):
            to = net.place(offset, "z", "c", "f")
            sent.append(net.push(norm_parts.at[to], norm_got.at[k], offset))
        yield 41
        for copy in sent:
            copy.wait_recv()
        w_norm[mine] = norm_parts[mine] + jnp.sum(norm_got[...], axis=0)
        sent = [net.push(w_norm.at[mine], w_norm.at[mine], offset) for offset in ALL_G]
        yield 58
        for copy in sent:
            copy.wait_recv()

    run_flows(Flow(attention()), Flow(activations()), Flow(norm_sums()))
    for copy in stores:
        copy.wait()
    net.finish()


def front(number, *args):
    table = sds((1024, 128), F32)
    return comm_call(
        front_kernel,
        "front",
        number,
        23 * 2 + 14 + 7 * 3 + 12 * 2 + 30,
        10,
        (
            sds((64, 2048), BF),
            sds((1024, 2048), BF),
            sds((2048, 512), BF),
            sds((256, 1024), BF),
            sds((1024, 128), BF),
            sds((8192, 256), BF),
            sds((1024, 2048), BF),
            table,
            table,
            table,
            sds((8, 128), jnp.int32),
            sds((16, 8, 128), F32),
        ),
        [
            pltpu.VMEM((1024, 2048), BF),
            pltpu.VMEM((1024, 2048), BF),
            pltpu.VMEM((2048, 512), BF),
            pltpu.VMEM((256, 512), BF),
            pltpu.VMEM((8, 8, 128), F32),
            pltpu.VMEM((8, 128), F32),
            pltpu.VMEM((8, 8, 128), F32),
            pltpu.VMEM((1024, 256), BF),
            pltpu.VMEM((16, 8, 128), F32),
            pltpu.VMEM((15, 8, 128), F32),
            pltpu.VMEM((8, 128), F32),
        ],
        [ANY] * 5 + [VMEM] * 7,
        (ANY,) * 4 + (VMEM, ANY, ANY) + (VMEM,) * 5,
        *args,
    )


def row_sums(values):
    ones = jnp.ones((8, values.shape[1]), F32)
    return lax.dot_general(
        ones, values, NT, preferred_element_type=F32, precision=lax.Precision.HIGHEST
    )[0:1]


def put_sums(target, i, *values):
    sums = row_sums(jnp.concatenate(values, axis=0))
    for k in range(len(values)):
        target[pl.ds(8 * k + i, 1), :] = sums[:, k * 128 : k * 128 + 128]


def tile(i, rows=128):
    return pl.ds(pl.multiple_of(i * rows, rows), rows)


def columns_of(rows_ref, i):
    return rows_ref[i].T


def put_rows(rows_ref, *values):
    for k, value in enumerate(values):
        for i in range(8):
            rows_ref[i, k : k + 1, :] = value[i : i + 1]


def fold_groups(values):
    values = values[:, 0:1024] + values[:, 1024:2048]
    return fold_lanes(values[:, 0:512] + values[:, 512:1024])


def fold_lanes(values):
    return (values[:, 0:128] + values[:, 128:256]) + (values[:, 256:384] + values[:, 384:512])


def middle_kernel(
    att,
    w_attn,
    ffn_block,
    ffn_below,
    ffn_above,
    ffn_beside,
    grad_all_in,
    input_rows,
    b_out,
    b_up,
    gains,
    shifts,
    hid_gain,
    hid_shift,
    w_norm,
    mid,
    grad_mid,
    ffn_part,
    grad_att,
    ffn_up,
    ffn_down,
    ffn_across,
    ffn_own,
    branch_out,
    turned_out,
    hid_vec,
    head_vec,
    row_vec,
    send,
    recv,
    local,
    grad_all,
    out_w,
    w_ffn,
    mid_low,
    branch_all,
    hidden_low,
    pre_low,
    hidden_turned,
    pre_turned,
    attn_low,
    low_rows,
    partial_rows,
    mine,
    landed,
    other,
    t_mine,
    t_landed,
    grad_hidden,
    activated,
    slope,
    normal_attn,
    normal_mid,
    scale_mid,
    sent_a,
    stats_a,
    rows_a,
    sent_b,
    stats_b,
    rows_b,
    sent_c,
    stats_c,
    rows_c,
    branch_rows,
    w_rows,
    folded,
):
    net = Net(send, recv)
    me = net.place({}, "z", "c", "f")
    load_w = pltpu.make_async_copy(w_attn.at[:, pl.ds(384, 128)], out_w, local.at[10])
    load_w.start()
    load_grad = pltpu.make_async_copy(grad_all_in, grad_all, local.at[11])
    load_grad.start()
    net.greet(ALL_G, NEAR_T)
    weights = Flow(
        gather_rest_flow(
            net,
            (ffn_block, ffn_below, ffn_above, ffn_beside),
            gather_slot(net, w_ffn, 256, "x", "h"),
            "x",
            "h",
            local.at[pl.ds(12, 4)],
            0,
            11,
        )
    )
    head_at = pl.ds(
        pl.multiple_of(net.at["f"] * 1024 + net.place({}, "z", "c") * 128, 128), 128
    )
    hidden_at = pl.ds(
        pl.multiple_of(net.at["f"] * 4096 + net.place({}, "z", "c") * 512, 512), 512
    )
    head_gain, head_shift = gains[1:2, head_at], shifts[1:2, head_at]
    gain_here, shift_here, bias_here = hid_gain[:, hidden_at], hid_shift[:, hidden_at], b_up[:, hidden_at]

    def exchange(sent, stats):
        copies = [net.push(sent, stats.at[me], offset) for offset in ALL_G]
        stats[me] = sent[...]
        for copy in copies:
            copy.wait_recv()

    def chunk(offset):
        at = net.place(offset, "z", "c", "f")
        return partial_rows.at[pl.ds(pl.multiple_of(at * 64, 64), 64)]

    def measure(i, carry):
        here = att[tile(i), :]
        centered = here - jnp.mean(here, axis=1, keepdims=True)
        put_sums(sent_a, i, here, centered * centered)
        return carry

    lax.fori_loop(0, 8, measure, 0, unroll=2)
    exchange(sent_a, stats_a)
    center = jnp.sum(stats_a[:, 0:8], axis=0) / 2048
    spread = jnp.sum(
        stats_a[:, 8:16] + 128 * jnp.square(stats_a[:, 0:8] / 128 - center[None]), axis=0
    )
    put_rows(rows_a, center, lax.rsqrt(spread / 2048 + EPS))

    def norm_heads(i, carry):
        columns = columns_of(rows_a, i)
        normal_rows = (att[tile(i), :] - columns[:, 0:1]) * columns[:, 1:2]
        normal_attn[tile(i), :] = normal_rows
        attn_low[tile(i), :] = (normal_rows * head_gain + head_shift).astype(BF)
        return carry

    lax.fori_loop(0, 8, norm_heads, 0, unroll=2)
    load_w.wait()

    def project(i, carry):
        partial_rows[:, tile(i, 256)] = lax.dot_general(
            attn_low[...], out_w[tile(i, 256), :], NT, preferred_element_type=F32
        ).astype(BF)
        return carry

    lax.fori_loop(0, 8, project, 0, unroll=2)
    run_until(
        Flow(scatter_flow(net, chunk, mid, mine, other, landed, local, "z", "f", True, False, 13, 5.5)),
        weights,
    )
    net.finish()

    def mid_norm(i, carry):
        at = tile(i, 16)
        branch_rows[at, :] = mid[at, :]
        rows = input_rows[at, :].astype(F32) + (mid[at, :] + b_out[...])
        mid[at, :] = rows
        centered = rows - jnp.mean(rows, axis=1, keepdims=True)
        scale = lax.rsqrt(jnp.mean(centered * centered, axis=1, keepdims=True) + EPS)
        rows = centered * scale
        normal_mid[at, :] = rows
        scale_mid[at, :] = jnp.broadcast_to(scale, (16, 128))
        low_rows[at, :] = (rows * gains[2:3, :] + shifts[2:3, :]).astype(BF)
        return carry

    lax.fori_loop(0, 4, mid_norm, 0)
    def hidden_grads():
        yield 43
        run_until(weights)
        load_grad.wait()
        for i in range(4):
            grad_hidden[tile(i, 256), :] = jnp.dot(
                grad_all[tile(i, 256), :], w_ffn[:, 512:1024], preferred_element_type=F32
            )
            yield 44

    run_flows(
        Flow(
            gather_flow(
                net, low_rows, gather_slot(net, mid_low, 64, "z", "f"), "z", "f", local.at[0], True, False, 31, 5.5
            )
        ),
        Flow(hidden_grads()),
        weights,
    )
    net.finish()

    def up(i, carry):
        at = tile(i)
        pre = jnp.dot(mid_low[at, :], w_ffn[:, 0:512], preferred_element_type=F32) + bias_here
        below = 0.5 + 0.5 * lax.erf(pre * math.sqrt(0.5))
        act = pre * below
        activated[at, :] = act
        slope[at, :] = below + pre * jnp.exp(-0.5 * pre * pre) * (1.0 / math.sqrt(2.0 * math.pi))
        centered = act - jnp.mean(act, axis=1, keepdims=True)
        scaled = grad_hidden[at, :] * gain_here
        put_sums(
            sent_b,
            i,
            fold_lanes(act),
            fold_lanes(centered * centered),
            fold_lanes(scaled),
            fold_lanes(scaled * centered),
        )
        return carry

    lax.fori_loop(0, 8, up, 0, unroll=2)
    exchange(sent_b, stats_b)
    center = jnp.sum(stats_b[:, 0:8], axis=0) / 8192
    apart = stats_b[:, 0:8] / 512 - center[None]
    spread = jnp.sum(stats_b[:, 8:16] + 512 * jnp.square(apart), axis=0)
    scale = lax.rsqrt(spread / 8192 + EPS)
    mean_back = jnp.sum(stats_b[:, 16:24], axis=0) / 8192
    cross_back = scale * jnp.sum(stats_b[:, 24:32] + apart * stats_b[:, 16:24], axis=0) / 8192
    put_rows(rows_b, center, scale, mean_back, cross_back)

    def hidden(i, carry):
        at = tile(i)
        columns = columns_of(rows_b, i)
        scale = columns[:, 1:2]
        normal_rows = (activated[at, :] - columns[:, 0:1]) * scale
        hidden_low[at, :] = (normal_rows * gain_here + shift_here).astype(BF)
        upstream = grad_hidden[at, :]
        back = scale * (upstream * gain_here - columns[:, 2:3] - normal_rows * columns[:, 3:4])
        low = (back * slope[at, :]).astype(BF)
        pre_low[at, :] = low
        return (
            carry[0] + jnp.sum(low.astype(F32), axis=0, keepdims=True),
            carry[1] + jnp.sum(upstream * normal_rows, axis=0, keepdims=True),
            carry[2] + jnp.sum(upstream, axis=0, keepdims=True),
        )

    sums = lax.fori_loop(0, 8, hidden, (jnp.zeros((1, 512), F32),) * 3, unroll=2)
    for k in range(3):
        hid_vec[k : k + 1, :] = sums[k]

    def project_back(i, carry):
        partial_rows[:, tile(i, 256)] = lax.dot_general(
            pre_low[...], w_ffn[tile(i, 256), 0:512], NT, preferred_element_type=F32
        ).astype(BF)
        return carry

    lax.fori_loop(0, 8, project_back, 0, unroll=2)

    def weight_terms():
        def turn(i, carry):
            pre_turned[:, tile(i)] = pre_low[tile(i), :].T
            hidden_turned[:, tile(i)] = hidden_low[tile(i), :].T
            return carry

        yield 69
        lax.fori_loop(0, 8, turn, 0)
        for k, (i, j) in enumerate(ROOTS):
            yield 70 + k
            columns = tile(net.place({"x": i, "h": j}, "x", "h"), 256)
            t_mine[k, 0:512, :] = jnp.dot(
                pre_turned[...], mid_low[:, columns], preferred_element_type=F32
            ).astype(BF)
            t_mine[k, 512:1024, :] = jnp.dot(
                hidden_turned[...], grad_all[:, columns], preferred_element_type=F32
            ).astype(BF)

    stores = []

    def weight_scatter():
        yield from weight_terms()
        yield from scatter_flow(
            net, None, None, t_mine, None, t_landed, local, "x", "h", False, False, 82, 11, False
        )
        for k in range(4):
            target = (ffn_up, ffn_down, ffn_across, ffn_own)[k]
            sums_store = pltpu.make_async_copy(t_mine.at[4 + k], target, local.at[16 + k])
            sums_store.start()
            stores.append(sums_store)

    weights = Flow(weight_scatter())
    run_until(
        Flow(scatter_flow(net, chunk, grad_mid, mine, other, landed, local, "z", "f", True, False, 68, 5.5)),
        weights,
    )
    net.finish()

    def mid_back(i, carry):
        at = tile(i, 16)
        upstream = grad_mid[at, :]
        normal_rows = normal_mid[at, :]
        scaled = upstream * gains[2:3, :]
        mean = jnp.mean(scaled, axis=1, keepdims=True)
        cross = jnp.mean(scaled * normal_rows, axis=1, keepdims=True)
        out_rows = grad_all[pl.ds(pl.multiple_of(me * 64 + i * 16, 16), 16), :].astype(F32)
        rows = out_rows + scale_mid[at, 0:1] * (scaled - mean - normal_rows * cross)
        grad_mid[at, :] = rows
        low = rows.astype(BF)
        low_rows[at, :] = low
        low = low.astype(F32)
        folded[0, at, :] = fold_groups(low * w_rows[0:1, :])
        folded[1, at, :] = fold_groups(low * (branch_rows[at, :] - w_rows[1:2, :]))
        row_vec[0:1, :] += jnp.sum(upstream * normal_rows, axis=0, keepdims=True)
        row_vec[1:2, :] += jnp.sum(upstream, axis=0, keepdims=True)
        row_vec[2:3, :] += jnp.sum(low, axis=0, keepdims=True)
        row_vec[3:4, :] += jnp.sum(out_rows, axis=0, keepdims=True)
        return carry

    row_vec[...] = jnp.zeros_like(row_vec)
    for g in range(16):
        w_rows[:, g * 128 : g * 128 + 128] = w_norm[g]
    lax.fori_loop(0, 4, mid_back, 0)
    def down():
        for i in range(8):
            yield 87 + i
            partial_rows[:, tile(i, 256)] = lax.dot_general(
                hidden_low[...], w_ffn[tile(i, 256), 512:1024], NT, preferred_element_type=F32
            ).astype(BF)

    def norm_sums():
        yield 86.5
        sums = [row_sums(folded[k]) * (1.0 / 2048) for k in range(2)]
        sent_c[...] = jnp.broadcast_to(jnp.concatenate(sums, axis=1), (8, 128))
        copies = [net.push(sent_c, stats_c.at[me], offset) for offset in ALL_G]
        stats_c[me] = sent_c[...]
        yield 99
        for copy in copies:
            copy.wait_recv()

    run_flows_but(
        weights,
        Flow(
            gather_flow(
                net, low_rows, gather_slot(net, branch_all, 64, "z", "f"), "z", "f", local.at[0], True, True, 86, 5.5
            )
        ),
        Flow(norm_sums()),
        Flow(down()),
    )
    store = pltpu.make_async_copy(partial_rows, ffn_part, local.at[8])
    store.start()

    lanes = lax.broadcasted_iota(jnp.int32, (1, 128), 1)
    for i in range(8):
        a, b = stats_c[2 * i, 0:1, :], stats_c[2 * i + 1, 0:1, :]
        rows_c[i, 0:1, :] = jnp.where(lanes < 64, a, pltpu.roll(b, 64, axis=1))
        rows_c[i, 1:2, :] = jnp.where(lanes < 64, pltpu.roll(a, 64, axis=1), b)
    keep = [
        pltpu.make_async_copy(branch_all, branch_out, local.at[20]),
        pltpu.make_async_copy(pre_turned.at[pl.ds(0, 128)], turned_out, local.at[21]),
    ]
    keep[0].start()

    def attn_back(i, carry):
        at = tile(i)
        upstream = jnp.dot(branch_all[at, :], out_w[...], preferred_element_type=F32)
        normal_rows = normal_attn[at, :]
        columns = columns_of(rows_c, i)
        scale = columns_of(rows_a, i)[:, 1:2]
        grad_att[at, :] = (
            scale * (upstream * head_gain - columns[:, 0:1] - normal_rows * columns[:, 1:2])
        ).astype(BF)
        pre_turned[0:128, at] = attn_low[at, :].T
        return (
            carry[0] + jnp.sum(upstream * normal_rows, axis=0, keepdims=True),
            carry[1] + jnp.sum(upstream, axis=0, keepdims=True),
        )

    sums = lax.fori_loop(0, 8, attn_back, (jnp.zeros((1, 128), F32),) * 2, unroll=2)
    for k in range(2):
        head_vec[k : k + 1, :] = sums[k]
    keep[1].start()
    for copy in keep:
        copy.wait()
    run_until(weights)
    for copy in stores:
        copy.wait()
    store.wait()
    net.finish()


def middle(number, *args):
    wide = pltpu.VMEM((1024, 512), F32)
    low = pltpu.VMEM((1024, 512), BF)
    tall = pltpu.VMEM((512, 1024), BF)
    whole = pltpu.VMEM((1024, 2048), BF)
    return comm_call(
        middle_kernel,
        "middle",
        number,
        15 * 3 + 20 * 4 + 14 * 2,
        22,
        (
            sds((64, 2048), F32),
            sds((64, 2048), F32),
            sds((1024, 2048), BF),
            sds((1024, 128), BF),
            *(sds((1024, 256), BF),) * 4,
            sds((1024, 2048), BF),
            sds((128, 1024), BF),
            sds((8, 512), F32),
            sds((8, 128), F32),
            sds((8, 2048), F32),
        ),
        [
            whole,
            pltpu.VMEM((2048, 128), BF),
            pltpu.VMEM((2048, 1024), BF),
            whole,
            whole,
            low,
            low,
            tall,
            tall,
            pltpu.VMEM((1024, 128), BF),
            pltpu.VMEM((64, 2048), BF),
            whole,
            pltpu.VMEM((8, 64, 2048), BF),
            pltpu.VMEM((7, 64, 2048), BF),
            pltpu.VMEM((8, 64, 2048), BF),
            pltpu.VMEM((8, 1024, 256), BF),
            pltpu.VMEM((7, 1024, 256), BF),
            wide,
            wide,
            wide,
            pltpu.VMEM((1024, 128), F32),
            pltpu.VMEM((64, 2048), F32),
            pltpu.VMEM((64, 128), F32),
            pltpu.VMEM((16, 128), F32),
            pltpu.VMEM((16, 16, 128), F32),
            pltpu.VMEM((8, 8, 128), F32),
            pltpu.VMEM((32, 128), F32),
            pltpu.VMEM((16, 32, 128), F32),
            pltpu.VMEM((8, 8, 128), F32),
            pltpu.VMEM((8, 128), F32),
            pltpu.VMEM((16, 8, 128), F32),
            pltpu.VMEM((8, 8, 128), F32),
            pltpu.VMEM((64, 2048), F32),
            pltpu.VMEM((8, 2048), F32),
            pltpu.VMEM((2, 64, 128), F32),
        ],
        [VMEM] + [ANY] * 6 + [VMEM] * 8,
        (VMEM, VMEM, ANY, VMEM) + (ANY,) * 6 + (VMEM,) * 3,
        *args,
    )


def tail_kernel(
    kv_part,
    ffn_part,
    ffn_own,
    ffn_up,
    ffn_down,
    ffn_across,
    query_grad,
    cosine,
    sine,
    growth,
    w_attn_in,
    in_low_in,
    branch_in,
    attn_turned,
    mid,
    grad_mid,
    input_rows,
    b_down,
    gains,
    hid_vec,
    head_vec,
    row_vec,
    out_half,
    in_half,
    attn_got,
    ffn_got,
    vectors,
    send,
    recv,
    local,
    kv_mine,
    kv_landed,
    kv_grad,
    f_mine,
    f_landed,
    f_other,
    i_mine,
    i_landed,
    i_other,
    w_mine,
    w_landed,
    w_grad,
    w_rows,
    attn_rows,
    ffn_rows,
    out_rows,
    in_rows,
    grad_qkv,
    turned,
    partial_rows,
    w_attn,
    in_low,
    branch_all,
    row_parts,
    row_got,
    packed,
    packed_got,
):
    net = Net(send, recv)
    me = net.place({}, "z", "c", "f")
    here = net.place({}, "z", "c")
    f = net.at["f"]
    load_w = pltpu.make_async_copy(w_attn_in, w_attn, local.at[16])
    load_w.start()
    load_in = pltpu.make_async_copy(in_low_in, in_low, local.at[21])
    load_in.start()
    load_branch = pltpu.make_async_copy(branch_in, branch_all, local.at[22])
    load_branch.start()
    net.greet(ALL_G, ALL_T)

    def to_halves(source, target, k):
        rows = target.at[pl.ds(pl.multiple_of(f * 64, 64), 64)]
        theirs = source.at[:, pl.ds(pl.multiple_of((1 - f) * 1024, 1024), 1024)]
        own = source.at[:, pl.ds(pl.multiple_of(f * 1024, 1024), 1024)]
        copy = net.push(theirs, rows, {"f": 1})
        keep = pltpu.make_async_copy(own, rows, local.at[k])
        keep.start()
        return copy, keep

    def to_rows(source, got, k):
        copies = []
        for offset in ALL_ZC:
            at = net.place(offset, "z", "c")
            copies.append(
                net.push(source.at[pl.ds(pl.multiple_of(at * 32, 32), 32)], got.at[here], offset)
            )
        keep = pltpu.make_async_copy(
            source.at[pl.ds(pl.multiple_of(here * 32, 32), 32)], got.at[here], local.at[k]
        )
        keep.start()
        return copies, keep

    def ffn_weights():
        def turn(i, carry):
            for j in range(2):
                at = slice(j * 128, j * 128 + 128)
                block = ffn_own[tile(i), at].astype(F32) + ffn_up[tile(i), at].astype(F32)
                block = block + (ffn_down[tile(i), at].astype(F32) + ffn_across[tile(i), at].astype(F32))
                block = block.T
                w_rows[j * 128 : j * 128 + 128, tile(i)] = block.astype(BF)
            return carry

        lax.fori_loop(0, 8, turn, 0)
        yield to_rows(w_rows, ffn_got, 17)

    kv_flow = Flow(
        scatter_flow(
            net,
            scatter_chunk(net, kv_part, "x"),
            kv_grad,
            kv_mine,
            None,
            kv_landed,
            local.at[pl.ds(0, 8)],
            "x",
            "h",
            False,
            False,
            0,
            11,
        )
    )
    ffn_flow = Flow(
        scatter_flow(
            net,
            scatter_chunk(net, ffn_part, "z"),
            ffn_rows,
            f_mine,
            f_other,
            f_landed,
            local.at[pl.ds(8, 8)],
            "z",
            "f",
            True,
            True,
            4,
            7,
        )
    )
    kv_flow.step()
    ffn_flow.step()
    ffn_copies, ffn_keep = next(ffn_weights())

    def out_terms():
        yield 6
        load_branch.wait()
        for k, (i, j) in enumerate(ROOTS):
            yield 7 + k
            columns = tile(net.place({"x": i, "h": j}, "x", "h"), 256)
            w_mine[k, 384:512, :] = jnp.dot(
                attn_turned[...], branch_all[:, columns], preferred_element_type=F32
            ).astype(BF)

    run_flows(kv_flow, ffn_flow, Flow(out_terms()))

    def finish_rows(i, carry):
        at = tile(i, 16)
        out_rows[at, :] = mid[at, :] + (ffn_rows[at, :] + b_down[...])
        return carry

    lax.fori_loop(0, 4, finish_rows, 0)
    out_copy, out_keep = to_halves(out_rows, out_half, 18)

    def unrotate(i, carry):
        at = tile(i)
        cos, sin, grow = cosine[at, :], sine[at, :], growth[at, :]
        queries = query_grad[at, :] * grow
        queries = (queries * cos - turn_halves(queries) * sin).astype(BF)
        keys = kv_grad[at, 0:128] / grow
        keys = (keys * cos - turn_halves(keys) * sin).astype(BF)
        values = kv_grad[at, 128:256].astype(BF)
        grad_qkv[at, 0:128] = queries
        grad_qkv[at, 128:256] = keys
        grad_qkv[at, 256:384] = values
        return tuple(
            total + jnp.sum(part.astype(F32), axis=0, keepdims=True)
            for total, part in zip(carry, (queries, keys, values))
        )

    bias = lax.fori_loop(0, 8, unrotate, (jnp.zeros((1, 128), F32),) * 3, unroll=2)
    for k in range(3):
        packed[8 + k : 9 + k, :] = bias[k]
    load_w.wait()

    def project(i, carry):
        partial_rows[:, tile(i, 256)] = lax.dot_general(
            grad_qkv[...], w_attn[tile(i, 256), 0:384], NT, preferred_element_type=F32
        ).astype(BF)
        return carry

    lax.fori_loop(0, 8, project, 0, unroll=2)

    def chunk(offset):
        at = net.place(offset, "z", "c", "f")
        return partial_rows.at[pl.ds(pl.multiple_of(at * 64, 64), 64)]

    def weight_scatter():
        def turn_grads(i, carry):
            turned[:, tile(i)] = grad_qkv[tile(i), :].T
            return carry

        yield 0.6
        lax.fori_loop(0, 8, turn_grads, 0)
        load_in.wait()
        for k, (i, j) in enumerate(ROOTS):
            yield 1 + k
            columns = tile(net.place({"x": i, "h": j}, "x", "h"), 256)
            w_mine[k, 0:384, :] = jnp.dot(
                turned[...], in_low[:, columns], preferred_element_type=F32
            ).astype(BF)
        yield from scatter_flow(
            net, None, w_grad, w_mine, None, w_landed, None, "x", "h", False, True, 0, 5.5
        )

    w_flow = Flow(weight_scatter())
    for _ in range(9):
        w_flow.step()
    in_flow = Flow(
        scatter_flow(net, chunk, in_rows, i_mine, i_other, i_landed, local, "z", "f", True, False, 0, 5.5)
    )
    run_until(in_flow, w_flow)

    def in_back(i, carry):
        at = tile(i, 16)
        rows = input_rows[at, :].astype(F32)
        centered = rows - jnp.mean(rows, axis=1, keepdims=True)
        scale = lax.rsqrt(jnp.mean(centered * centered, axis=1, keepdims=True) + EPS)
        normal_rows = centered * scale
        upstream = in_rows[at, :]
        scaled = upstream * gains[0:1, :]
        mean = jnp.mean(scaled, axis=1, keepdims=True)
        cross = jnp.mean(scaled * normal_rows, axis=1, keepdims=True)
        in_rows[at, :] = grad_mid[at, :] + scale * (scaled - mean - normal_rows * cross)
        return (
            carry[0] + jnp.sum(upstream * normal_rows, axis=0, keepdims=True),
            carry[1] + jnp.sum(upstream, axis=0, keepdims=True),
        )

    sums = lax.fori_loop(0, 4, in_back, (jnp.zeros((1, 2048), F32),) * 2)
    in_copy, in_keep = to_halves(in_rows, in_half, 19)
    run_until(w_flow)

    def turn_weights(i, carry):
        for j in range(2):
            w_grad_rows = w_grad[tile(i), j * 128 : j * 128 + 128].T
            attn_rows[j * 128 : j * 128 + 128, tile(i)] = w_grad_rows
        return carry

    for g in range(16):
        at = slice(g * 128, g * 128 + 128)
        for k in range(2):
            row_parts[g, k : k + 1, :] = sums[k][:, at]
        row_parts[g, 2:6, :] = row_vec[0:4, at]
        row_parts[g, 6:8, :] = jnp.zeros((2, 128), F32)
    copies = []
    for k, offset in enumerate(ALL_G):
        to = net.place(offset, "z", "c", "f")
        copies.append(net.push(row_parts.at[to], row_got.at[k], offset))
    lax.fori_loop(0, 4, turn_weights, 0)
    attn_copies, attn_keep = to_rows(attn_rows, attn_got, 20)
    packed[11:13, :] = head_vec[0:2, :]
    for k in range(3):
        for j in range(4):
            at = 13 + 4 * k + j
            packed[at : at + 1, :] = hid_vec[k : k + 1, j * 128 : j * 128 + 128]
    packed[25:32, :] = jnp.zeros((7, 128), F32)
    for copy in copies:
        copy.wait_recv()
    total = row_parts[me]
    for k in range(15):
        total = total + row_got[k]
    packed[0:8, :] = total
    copies = [net.push(packed, packed_got.at[k], offset) for k, offset in enumerate(ALL_T)]
    for copy in copies:
        copy.wait_recv()
    total = packed[...]
    for k in range(7):
        total = total + packed_got[k]
    vectors[me] = total
    copies = [net.push(vectors.at[me], vectors.at[me], offset) for offset in ALL_G]
    for copy in ffn_copies + attn_copies + copies + [out_copy, in_copy]:
        copy.wait_recv()
    for keep in (ffn_keep, attn_keep, out_keep, in_keep):
        keep.wait()
    net.finish()


def tail(number, *args):
    half = sds((128, 1024), F32)
    rows = pltpu.VMEM((64, 2048), F32)
    return comm_call(
        tail_kernel,
        "tail",
        number,
        12 + 22 + 7 + 20 + 12 + 2 + 7 + 37,
        23,
        (
            half,
            half,
            sds((8, 32, 512), F32),
            sds((8, 32, 1024), BF),
            sds((16, 32, 128), F32),
        ),
        scatter_scratch(1024, 256, False)
        + [pltpu.VMEM((1024, 256), F32)]
        + scatter_scratch(64, 2048, True)
        + scatter_scratch(64, 2048, True)
        + scatter_scratch(512, 256, False)
        + [
            pltpu.VMEM((512, 256), F32),
            pltpu.VMEM((256, 1024), BF),
            pltpu.VMEM((256, 512), F32),
            rows,
            rows,
            rows,
            pltpu.VMEM((1024, 384), BF),
            pltpu.VMEM((384, 1024), BF),
            pltpu.VMEM((1024, 2048), BF),
            pltpu.VMEM((2048, 512), BF),
            pltpu.VMEM((1024, 2048), BF),
            pltpu.VMEM((1024, 2048), BF),
            pltpu.VMEM((16, 8, 128), F32),
            pltpu.VMEM((15, 8, 128), F32),
            pltpu.VMEM((32, 128), F32),
            pltpu.VMEM((7, 32, 128), F32),
        ],
        [ANY, ANY] + [VMEM] * 8 + [ANY] * 3 + [VMEM] * 9,
        (VMEM,) * 5,
        *args,
    )


def assemble_kernel(
    out_in,
    in_in,
    attn_in,
    ffn_in,
    sums_in,
    out_half,
    in_half,
    qkv_out,
    out_out,
    up_out,
    down_out,
    qkv_bias,
    gains_out,
    shifts_out,
    out_bias,
    down_bias,
    up_bias,
    hid_gain_out,
    hid_shift_out,
    attn_got,
    ffn_got,
    sums,
    sems,
):
    pairs = ((out_in, out_half), (in_in, in_half), (sums_in, sums), (attn_in, attn_got), (ffn_in, ffn_got))
    copies = [pltpu.make_async_copy(a, b, sems.at[k]) for k, (a, b) in enumerate(pairs)]
    for copy in copies:
        copy.start()
    for copy in copies:
        copy.wait()

    def weights(i, carry):
        small, large = tile(i, 128), tile(i, 512)
        for j in range(3):
            qkv_out[j, :, small] = attn_got[i, :, j * 128 : j * 128 + 128]
        out_out[:, small] = attn_got[i, :, 384:512]
        up_out[:, large] = ffn_got[i, :, 0:512].astype(F32)
        down_out[:, large] = ffn_got[i, :, 512:1024].astype(F32)
        return carry

    lax.fori_loop(0, 8, weights, 0)

    def place(g, carry):
        by_rows, row_lanes = pl.ds(g, 1), tile(g)
        head = lax.rem(g, 2) * 8 + g // 2
        head_lanes = tile(head)
        for k, (target, j) in enumerate(
            ((gains_out, 0), (shifts_out, 0), (gains_out, 2), (shifts_out, 2))
        ):
            target[j : j + 1, row_lanes] = sums[g, k : k + 1, :]
        out_bias[by_rows, :] = sums[g, 4:5, :]
        down_bias[by_rows, :] = sums[g, 5:6, :]
        qkv_bias[:, head_lanes] = sums[g, 8:11, :]
        gains_out[1:2, head_lanes] = sums[g, 11:12, :]
        shifts_out[1:2, head_lanes] = sums[g, 12:13, :]
        for k, target in enumerate((up_bias, hid_gain_out, hid_shift_out)):
            for j in range(4):
                at = 13 + 4 * k + j
                target[pl.ds(head * 4 + j, 1), :] = sums[g, at : at + 1, :]
        return carry

    lax.fori_loop(0, 16, place, 0)


def assemble(*args):
    vector, hidden = sds((16, 128), F32), sds((64, 128), F32)
    triple = sds((3, 2048), F32)
    half = sds((128, 1024), F32)
    return pl.pallas_call(
        assemble_kernel,
        out_shape=(
            half,
            half,
            sds((3, 32, 1024), F32),
            sds((32, 1024), F32),
            sds((32, 4096), F32),
            sds((32, 4096), F32),
            triple,
            triple,
            triple,
            vector,
            vector,
            hidden,
            hidden,
            hidden,
        ),
        in_specs=[ANY] * 5,
        out_specs=(VMEM,) * 14,
        scratch_shapes=[
            pltpu.VMEM((8, 32, 512), F32),
            pltpu.VMEM((8, 32, 1024), BF),
            pltpu.VMEM((16, 32, 128), F32),
            DMA((5,)),
        ],
        name="assemble",
        compiler_params=pltpu.CompilerParams(vmem_limit_bytes=60 << 20),
    )(*args)


def both_heads(rows, zero):
    lanes = lax.broadcasted_iota(jnp.int32, rows.shape, 1)
    return jnp.where(lanes < HEAD, rows, zero), jnp.where(lanes >= HEAD, rows, zero)


def run_rows(ref, run):
    return ref[pl.ds(pl.multiple_of(run * RUN, RUN), RUN), :]


def pair_rows(ref, run_a, run_b, dtype):
    zero = jnp.zeros((), dtype)
    a = both_heads(run_rows(ref, run_a).astype(dtype), zero)
    b = both_heads(run_rows(ref, run_b).astype(dtype), zero)
    return jnp.concatenate(a + b, axis=0)


def pair_bounds(rank_a, rank_b):
    lanes = lax.broadcasted_iota(jnp.int32, (1, 256), 1)
    rank = jnp.where(lanes < 128, rank_a, rank_b)
    last = rank * RUN + lax.rem(lanes, RUN)
    return (rank // 64) * 4096, last


def seen(chunk, low, last):
    keys = chunk * CHUNK + lax.broadcasted_iota(jnp.int32, (CHUNK, 256), 0)
    return (keys >= low) & (keys <= last)


def sort_keys(order, kv_ref, kv):
    def move(r, carry):
        target = pl.ds(pl.multiple_of(order[0, r] * RUN, RUN), RUN)
        kv[target, :] = run_rows(kv_ref, r)
        return carry

    lax.fori_loop(0, 128, move, 0, unroll=4)


def flip(kv, columns, target):
    def one(i, carry):
        target[i] = kv[tile(i, CHUNK), columns].T
        return carry

    lax.fori_loop(0, 8192 // CHUNK, one, 0, unroll=2)


def over_chunks(rank_a, rank_b, step, start):
    low = (rank_a // 64) * (4096 // CHUNK)
    whole = jnp.where(rank_a // 64 == rank_b // 64, (rank_a // (CHUNK // RUN) - low), 0)

    def two(i, state):
        return step(low + i, state, False)

    state = lax.fori_loop(0, whole, two, start)
    return lax.fori_loop(
        low + whole, rank_b // (CHUNK // RUN) + 1, lambda i, state: step(i, state, True), state
    )


def lane_heads(total):
    turned = total.T
    lanes = lax.broadcasted_iota(jnp.int32, (RUN, 128), 1)
    a = jnp.where(lanes < HEAD, turned[0:64], turned[64:128])
    b = jnp.where(lanes < HEAD, turned[128:192], turned[192:256])
    return a, b


def attend_kernel(order, q_ref, kv_ref, o_ref, lse_ref, kv, flipped):
    sort_keys(order, kv_ref, kv)
    flip(kv, slice(128, 256), flipped)

    def pair(p, carry):
        run_a, run_b = order[1, 2 * p], order[1, 2 * p + 1]
        rank_a, rank_b = order[2, 2 * p], order[2, 2 * p + 1]
        queries = pair_rows(q_ref, run_a, run_b, BF)
        low, last = pair_bounds(rank_a, rank_b)

        def step(i, state, masked):
            peak, total, mixed = state
            scores = lax.dot_general(
                kv[tile(i, CHUNK), 0:128], queries, NT, preferred_element_type=F32
            )
            if masked:
                scores = jnp.where(seen(i, low, last), scores, -1e30)
            new_peak = jnp.maximum(peak, jnp.max(scores, axis=0, keepdims=True))
            weights = jnp.exp(scores - new_peak)
            shrink = jnp.exp(peak - new_peak)
            total = total * shrink + jnp.sum(weights, axis=0, keepdims=True)
            mixed = mixed * shrink + lax.dot_general(
                flipped[i], weights.astype(BF), NN, preferred_element_type=F32
            )
            return new_peak, total, mixed

        start = (
            jnp.full((1, 256), -1e20, F32),
            jnp.zeros((1, 256), F32),
            jnp.zeros((128, 256), F32),
        )
        peak, total, mixed = over_chunks(rank_a, rank_b, step, start)
        a, b = lane_heads(mixed / total)
        o_ref[pl.ds(pl.multiple_of(run_a * RUN, RUN), RUN), :] = a
        o_ref[pl.ds(pl.multiple_of(run_b * RUN, RUN), RUN), :] = b
        lse_ref[p] = peak + jnp.log(total)
        return carry

    lax.fori_loop(0, 8, pair, 0)


def attend(order, queries, kv):
    return pl.pallas_call(
        attend_kernel,
        out_shape=(sds((1024, 128), F32), sds((8, 1, 256), F32)),
        grid_spec=pltpu.PrefetchScalarGridSpec(
            num_scalar_prefetch=1,
            grid=(1,),
            in_specs=[VMEM, VMEM],
            out_specs=(VMEM, VMEM),
            scratch_shapes=[
                pltpu.VMEM((8192, 256), BF),
                pltpu.VMEM((8192 // CHUNK, 128, CHUNK), BF),
            ],
        ),
        name="attend",
        cost_estimate=pl.CostEstimate(flops=30_000_000_000, bytes_accessed=20_000_000, transcendentals=0),
        compiler_params=pltpu.CompilerParams(vmem_limit_bytes=60 << 20),
    )(order, queries, kv)


def attend_back_kernel(
    order, q_ref, kv_ref, g_ref, a_ref, lse_ref, dq_ref, dkv_ref, kv, flipped, dkeys, dvalues
):
    sort_keys(order, kv_ref, kv)
    flip(kv, slice(0, 128), flipped)

    def clear(i, carry):
        dkeys[tile(i, CHUNK), :] = jnp.zeros((CHUNK, 128), F32)
        dvalues[tile(i, CHUNK), :] = jnp.zeros((CHUNK, 128), F32)
        return carry

    lax.fori_loop(0, 8192 // CHUNK, clear, 0)

    def pair(p, carry):
        run_a, run_b = order[1, 2 * p], order[1, 2 * p + 1]
        rank_a, rank_b = order[2, 2 * p], order[2, 2 * p + 1]
        queries = pair_rows(q_ref, run_a, run_b, BF)
        grads = pair_rows(g_ref, run_a, run_b, BF)
        low, last = pair_bounds(rank_a, rank_b)
        product = pair_rows(g_ref, run_a, run_b, F32) * pair_rows(a_ref, run_a, run_b, F32)
        delta = row_sums(product)
        log_total = lse_ref[p]

        def step(i, dq, masked):
            rows = tile(i, CHUNK)
            scores = lax.dot_general(kv[rows, 0:128], queries, NT, preferred_element_type=F32)
            dprobs = lax.dot_general(kv[rows, 128:256], grads, NT, preferred_element_type=F32)
            probs = jnp.exp(scores - log_total)
            if masked:
                probs = jnp.where(seen(i, low, last), probs, 0.0)
            dscores = (probs * (dprobs - delta)).astype(BF)
            dvalues[rows, :] += lax.dot_general(
                probs.astype(BF), grads, NN, preferred_element_type=F32
            )
            dkeys[rows, :] += lax.dot_general(dscores, queries, NN, preferred_element_type=F32)
            return dq + lax.dot_general(flipped[i], dscores, NN, preferred_element_type=F32)

        dq = over_chunks(rank_a, rank_b, step, jnp.zeros((128, 256), F32))
        a, b = lane_heads(dq)
        dq_ref[pl.ds(pl.multiple_of(run_a * RUN, RUN), RUN), :] = a * 0.125
        dq_ref[pl.ds(pl.multiple_of(run_b * RUN, RUN), RUN), :] = b * 0.125
        return carry

    lax.fori_loop(0, 8, pair, 0)

    def back(r, carry):
        source = pl.ds(pl.multiple_of(order[0, r] * RUN, RUN), RUN)
        to = pl.ds(pl.multiple_of(r * RUN, RUN), RUN)
        dkv_ref[to, 0:128] = dkeys[source, :].astype(BF)
        dkv_ref[to, 128:256] = dvalues[source, :].astype(BF)
        return carry

    lax.fori_loop(0, 128, back, 0, unroll=4)


def attend_back(order, queries, kv, grads, attended, log_total):
    return pl.pallas_call(
        attend_back_kernel,
        out_shape=(sds((1024, 128), F32), sds((8192, 256), BF)),
        grid_spec=pltpu.PrefetchScalarGridSpec(
            num_scalar_prefetch=1,
            grid=(1,),
            in_specs=[VMEM] * 5,
            out_specs=(VMEM, VMEM),
            scratch_shapes=[
                pltpu.VMEM((8192, 256), BF),
                pltpu.VMEM((8192 // CHUNK, 128, CHUNK), BF),
                pltpu.VMEM((8192, 128), F32),
                pltpu.VMEM((8192, 128), F32),
            ],
        ),
        name="attend_back",
        cost_estimate=pl.CostEstimate(flops=30_000_000_000, bytes_accessed=20_000_000, transcendentals=0),
        compiler_params=pltpu.CompilerParams(vmem_limit_bytes=60 << 20),
    )(order, queries, kv, grads, attended, log_total)


def lane_tables(seq_length):
    half = HEAD // 2
    indices = (np.arange(128) % half).astype(np.float32)
    inverse_freq = np.exp(-np.log(np.float32(10000.0)) * indices / np.float32(half)).astype(np.float64)
    ratios = np.log((2.0 * indices + 0.4 * HEAD) / (1.4 * HEAD)).astype(np.float64)

    def tables(places, powers):
        angles = places[:, None] * inverse_freq[None, :]
        growth = np.exp(powers[:, None] * ratios[None, :])
        return np.stack([np.cos(angles), np.sin(angles), growth]).astype(np.float32)

    runs = np.arange(64) * float(RUN)
    tokens = np.arange(RUN).astype(np.float64)
    return (
        jnp.asarray(tables(runs, (runs - seq_length // 2) / 512.0)),
        jnp.asarray(tables(tokens, tokens / 512.0)),
    )


def shards(
    layer_input,
    w_qkv,
    w_out,
    w_up,
    w_down,
    b_qkv,
    b_out,
    b_up,
    b_down,
    norm_gains,
    norm_shifts,
    hidden_gain,
    hidden_shift,
    seq_ids,
    positions,
    d_out,
):
    packed = jnp.concatenate(
        [
            w_qkv.reshape(32, 3, 8, 128).transpose(2, 0, 1, 3).reshape(8, 32, 384),
            w_out.reshape(32, 8, 128).transpose(1, 0, 2),
        ],
        axis=2,
    )
    run_tables, token_tables = lane_tables(4096)
    (
        input_rows,
        in_low,
        w_attn,
        ffn_block,
        query_low,
        kv,
        grad_all,
        cosine,
        sine,
        growth,
        order,
        w_norm,
    ) = front(
        1,
        layer_input,
        d_out,
        packed,
        w_up,
        w_down,
        seq_ids.reshape(1, 128),
        positions.reshape(1, 128),
        norm_gains,
        norm_shifts,
        b_qkv,
        run_tables,
        token_tables,
    )
    ffn_near = (
        lax.ppermute(ffn_block, "x", UP),
        lax.ppermute(ffn_block, "x", DOWN),
        lax.ppermute(ffn_block, "h", ACROSS),
    )
    attended, log_total = attend(order, query_low, kv)
    (
        mid,
        grad_mid,
        ffn_part,
        grad_attended,
        ffn_up,
        ffn_down,
        ffn_across,
        ffn_own,
        branch_all,
        attn_turned,
        hid_vec,
        head_vec,
        row_vec,
    ) = middle(
        3,
        attended,
        w_attn,
        ffn_block,
        *ffn_near,
        grad_all,
        input_rows,
        b_out.reshape(1, 2048),
        b_up.reshape(1, 8192),
        norm_gains,
        norm_shifts,
        hidden_gain.reshape(1, 8192),
        hidden_shift.reshape(1, 8192),
        w_norm,
    )
    ffn_got = (
        lax.ppermute(ffn_up, "x", UP),
        lax.ppermute(ffn_down, "x", DOWN),
        lax.ppermute(ffn_across, "h", ACROSS),
    )
    query_grad, kv_part = attend_back(order, query_low, kv, grad_attended, attended, log_total)
    parts = tail(
        4,
        kv_part.reshape(8, 1024, 256),
        ffn_part.reshape(16, 64, 2048),
        ffn_own,
        *ffn_got,
        query_grad,
        cosine,
        sine,
        growth,
        w_attn,
        in_low,
        branch_all,
        attn_turned,
        mid,
        grad_mid,
        input_rows,
        b_down.reshape(1, 2048),
        norm_gains,
        hid_vec,
        head_vec,
        row_vec,
    )
    (
        layer_output,
        input_grad,
        qkv_grad,
        out_grad,
        up_grad,
        down_grad,
        qkv_bias,
        gains_grad,
        shifts_grad,
        out_bias,
        down_bias,
        up_bias,
        hid_gain_grad,
        hid_shift_grad,
    ) = assemble(*parts)
    return (
        layer_output,
        input_grad,
        qkv_grad.transpose(1, 0, 2),
        out_grad,
        up_grad,
        down_grad,
        qkv_bias,
        out_bias.reshape(2048),
        up_bias.reshape(8192),
        down_bias.reshape(2048),
        gains_grad,
        shifts_grad,
        hid_gain_grad.reshape(8192),
        hid_shift_grad.reshape(8192),
    )


def solution(mesh):
    fine = Mesh(mesh.devices.reshape(4, 2, 4, 2, 2), SEQ + ("f",))
    both = P(SEQ, "f")
    return jax.shard_map(
        shards,
        mesh=fine,
        in_specs=(both, P(SEQ, None, "f"), both, both, both)
        + (P(),) * 8
        + (P(SEQ), P(SEQ), both),
        out_specs=(both, both, P(SEQ, None, "f"), both, both, both) + (P(),) * 8,
        check_vma=False,
    )
```

```python
import math

import jax
import jax.numpy as jnp
import numpy as np
from jax import lax
from jax.experimental import pallas as pl
from jax.experimental.pallas import tpu as pltpu
from jax.sharding import Mesh
from jax.sharding import PartitionSpec as P

SEQ = ("x", "h", "z", "c")
TOK = ("x", "h")
HEAD = 64
RUN = 64
CHUNK = 1024
EPS = 1e-05
MESH = pl.DeviceIdType.MESH
BF = jnp.bfloat16
F32 = jnp.float32
DMA = pltpu.SemaphoreType.DMA
ANY = pl.BlockSpec(memory_space=pl.ANY)
VMEM = pl.BlockSpec(memory_space=pltpu.VMEM)
NT = (((1,), (1,)), ((), ()))
TN = (((0,), (0,)), ((), ()))
NN = (((1,), (0,)), ((), ()))


def sds(shape, dtype):
    return jax.ShapeDtypeStruct(shape, dtype)


AXES = {"x": 4, "h": 2, "z": 4, "c": 2, "f": 2}
RING_G, PAIR_G = "z", "f"
RING_T, PAIR_T = "x", "h"


class Net:
    loads = []

    def __init__(self, send, recv):
        self.send, self.recv, self.copies, self.drained = send, recv, [], 0
        self.at = {axis: lax.axis_index(axis) for axis in AXES}

    def device(self, offset):
        return {a: lax.rem(self.at[a] + d + AXES[a], AXES[a]) for a, d in offset.items()}

    def place(self, offset, *axes):
        index = 0
        for a in axes:
            d = offset.get(a, 0)
            at = lax.rem(self.at[a] + d + AXES[a], AXES[a]) if d else self.at[a]
            index = index * AXES[a] + at
        return index

    def greet(self, *groups):
        offsets = {
            tuple((a, o[a]) for a in AXES if o.get(a, 0)) for group in groups for o in group
        }
        barrier = pltpu.get_barrier_semaphore()
        for offset in sorted(offsets):
            pl.semaphore_signal(
                barrier, inc=1, device_id=self.device(dict(offset)), device_id_type=MESH
            )
        pl.semaphore_wait(barrier, len(offsets))
        while self.loads:
            self.loads.pop().wait()

    def push(self, src, dst, offset):
        k = len(self.copies)
        copy = pltpu.make_async_remote_copy(
            src_ref=src,
            dst_ref=dst,
            send_sem=self.send.at[k],
            recv_sem=self.recv.at[k],
            device_id=self.device(offset),
            device_id_type=MESH,
        )
        copy.start()
        self.copies.append(copy)
        return copy

    def finish(self):
        for copy in self.copies[self.drained :]:
            copy.wait_send()
        self.drained = len(self.copies)


UP = [(i, (i + 1) % 4) for i in range(4)]
DOWN = [(i, (i + 3) % 4) for i in range(4)]
ACROSS = [(0, 1), (1, 0)]
SIBLING = {"c": 1}
NEAR_G = [{"z": 1}, {"z": 3}, {"f": 1}, SIBLING]
NEAR_T = [{"x": 1}, {"x": 3}, {"h": 1}]
ALL_T = [{"x": i, "h": j} for i in range(4) for j in range(2)][1:]
ALL_ZC = [{"z": i, "c": j} for i in range(4) for j in range(2)][1:]
ALL_G = [{"z": i, "c": j, "f": k} for i in range(4) for j in range(2) for k in range(2)][1:]


def far_first(offsets):
    hops = lambda o: sum(min(d, AXES[a] - d) * (a != "c") * (2 if a == "h" else 1) for a, d in o.items())
    return sorted(offsets, key=hops, reverse=True)


ALL_T, ALL_ZC, ALL_G = far_first(ALL_T), far_first(ALL_ZC), far_first(ALL_G)


class Flow:
    def __init__(self, steps):
        self.steps = steps
        self.step()

    def step(self):
        self.time = next(self.steps, None)


def run_until(main, *others):
    while main.time is not None:
        ready = [flow for flow in (main,) + others if flow.time is not None]
        min(ready, key=lambda flow: flow.time).step()


def run_flows(*flows):
    for flow in flows:
        run_until(flow, *flows)


def run_flows_but(kept, *flows):
    for flow in flows:
        run_until(flow, kept, *flows)


def half_rows(ref, which):
    rows = ref.shape[0] // 2
    return ref.at[pl.ds(which * rows, rows)]


def gather_flow(
    net, src, slot, ring, pair, local, sibling, light, at, unit, hold=0, arrived=None
):
    up, down, across = {ring: 1}, {ring: 3}, {pair: 1}
    passed = {}

    def to_sibling(ref, i, j):
        if sibling:
            passed[i, j] = net.push(ref, ref, SIBLING)

    def both_ways(ref, target):
        return [
            [net.push(half_rows(ref, k), half_rows(target, k), to) for k in order]
            for to, order in ((up, (0, 1)), (down, (1, 0)))
        ]

    def show(*places):
        if arrived is not None:
            for i in places:
                arrived({ring: i})

    def show_sibling(*places):
        if arrived is not None:
            for i in places:
                for j in range(2):
                    passed.pop((i, j)).wait_recv()
                arrived({ring: i, "c": 1})

    mine = slot({})
    from_down, from_up = both_ways(src, mine)
    if hold:
        yield at + hold
    from_across = net.push(src, mine, across)
    if sibling:
        passed[0, 0] = net.push(src, mine, SIBLING)
    here = pltpu.make_async_copy(src, mine, local)
    here.start()
    below, above, beside, far = (slot({ring: 3}), slot({ring: 1}), slot({pair: 1}), slot({ring: 2}))
    yield at + 0.5 * unit
    from_down[0].wait_recv()
    first = net.push(half_rows(below, 0), half_rows(below, 0), up)
    from_up[0].wait_recv()
    second = net.push(half_rows(above, 1), half_rows(above, 1), down)
    yield at + unit + hold
    from_across.wait_recv()
    if light:
        beside_down, beside_up = both_ways(beside, beside)
    else:
        beside_down = [net.push(beside, beside, up)]
        beside_up = [net.push(beside, beside, down)]
    to_sibling(beside, 0, 1)
    yield at + unit + hold
    from_down[1].wait_recv()
    to_sibling(below, 3, 0)
    from_up[1].wait_recv()
    to_sibling(above, 1, 0)
    here.wait()
    show(0)
    yield at + 1.5 * unit + hold
    first.wait_recv()
    if not light:
        beside_far = [net.push(half_rows(far, 0), half_rows(far, 0), across)]
    second.wait_recv()
    if not light:
        beside_far.append(net.push(half_rows(far, 1), half_rows(far, 1), across))
    to_sibling(far, 2, 0)
    show_sibling(0)
    yield at + (1.7 if light and hold else 2 if light else 2.5) * unit + hold
    below, above = slot({ring: 3, pair: 1}), slot({ring: 1, pair: 1})
    if light:
        beside_down[0].wait_recv()
        beside_far = [net.push(half_rows(below, 0), half_rows(below, 0), up)]
        beside_up[0].wait_recv()
        beside_far.append(net.push(half_rows(above, 1), half_rows(above, 1), down))
        yield at + 2.5 * unit + hold
    beside_down[-1].wait_recv()
    to_sibling(below, 3, 1)
    beside_up[-1].wait_recv()
    to_sibling(above, 1, 1)
    show(3, 1)
    yield at + (3 if light else 2.5) * unit + hold
    for copy in beside_far:
        copy.wait_recv()
    to_sibling(slot({ring: 2, pair: 1}), 2, 1)
    show_sibling(3, 1)
    show(2)
    yield at + (3 if light else 2.5) * unit + hold
    show_sibling(2)
    for copy in passed.values():
        copy.wait_recv()


def gather_rest_flow(net, blocks, slot, ring, pair, local, at, unit):
    up, down = {ring: 1}, {ring: 3}
    mine, below, above, beside = (slot(o) for o in ({}, {ring: 3}, {ring: 1}, {pair: 1}))
    beside_down = [net.push(half_rows(blocks[3], k), half_rows(beside, k), up) for k in (0, 1)]
    beside_up = [net.push(half_rows(blocks[3], k), half_rows(beside, k), down) for k in (1, 0)]
    far = [
        net.push(half_rows(blocks[1], 0), half_rows(below, 0), up),
        net.push(half_rows(blocks[2], 1), half_rows(above, 1), down),
    ]
    here = [
        pltpu.make_async_copy(block, target, local.at[k])
        for k, (block, target) in enumerate(zip(blocks, (mine, below, above, beside)))
    ]
    for copy in here:
        copy.start()
    yield at + 0.7 * unit
    below, above = slot({ring: 3, pair: 1}), slot({ring: 1, pair: 1})
    beside_down[0].wait_recv()
    far.append(net.push(half_rows(below, 0), half_rows(below, 0), up))
    beside_up[0].wait_recv()
    far.append(net.push(half_rows(above, 1), half_rows(above, 1), down))
    yield at + 2.1 * unit
    for copy in far + beside_down[1:] + beside_up[1:]:
        copy.wait_recv()
    for copy in here:
        copy.wait()


def add_into(target, *sources):
    rows = min(32768 // target.shape[1], target.shape[0])

    def step(i, carry):
        at = pl.ds(pl.multiple_of(i * rows, rows), rows)
        total = target[at, :].astype(F32)
        for source in sources:
            total = total + source[at, :].astype(F32)
        target[at, :] = total.astype(target.dtype)
        return carry

    lax.fori_loop(0, target.shape[0] // rows, step, 0)


ROOTS = ((2, 1), (1, 1), (3, 1), (2, 0), (1, 0), (3, 0), (0, 1), (0, 0))


def scatter_flow(
    net, chunk, out, mine, other, landed, local, ring, pair, sibling, light, at, unit, last=True
):
    up, down, across = {ring: 1}, {ring: 3}, {pair: 1}
    loads, shared = [], []
    for k, (i, j) in enumerate(ROOTS):
        if sibling:
            shared.append(net.push(chunk({ring: i, pair: j, "c": 1}), other.at[k], SIBLING))
        if chunk is not None:
            load = pltpu.make_async_copy(chunk({ring: i, pair: j}), mine.at[k], local.at[k])
            load.start()
            loads.append(load)

    def ready(k):
        if chunk is not None:
            loads[k].wait()
        if sibling:
            shared[k].wait_recv()
            add_into(mine.at[k], other.at[k])

    def halves(k, to):
        return (
            net.push(half_rows(mine.at[k], 0), half_rows(landed.at[to], 0), down),
            net.push(half_rows(mine.at[k], 1), half_rows(landed.at[to], 1), up),
        )

    def add_half(k, source, which):
        add_into(half_rows(mine.at[k], which), half_rows(landed.at[source], which))

    def send_half(k, to, which, offset):
        return net.push(half_rows(mine.at[k], which), half_rows(landed.at[to], which), offset)

    if chunk is not None:
        yield at + 0.5
    ready(0)
    if light:
        beside_first, beside_second = halves(0, 0)
        ready(3)
        first, second = halves(3, 3)
        ready(2)
        beside_up = [send_half(2, 2, 1, down)]
        ready(1)
        beside_down = [send_half(1, 1, 0, up)]
        yield at + 0.5 * unit
        beside_first.wait_recv()
        add_half(2, 0, 0)
        beside_up.append(send_half(2, 2, 0, down))
        beside_second.wait_recv()
        add_half(1, 0, 1)
        beside_down.append(send_half(1, 1, 1, up))
    else:
        beside_far = [send_half(0, 0, k, across) for k in range(2)]
        ready(1)
        beside_down = [net.push(mine.at[1], landed.at[1], up)]
        ready(2)
        beside_up = [net.push(mine.at[2], landed.at[2], down)]
        ready(3)
        yield at + 0.6 * unit
        beside_far[0].wait_recv()
        add_half(3, 0, 0)
        first = send_half(3, 3, 0, down)
        yield at + unit
        beside_far[1].wait_recv()
        add_half(3, 0, 1)
        second = send_half(3, 3, 1, up)
    ready(5)
    ready(4)
    if last:
        from_up = [send_half(5, 5, 1, down)]
        from_down = [send_half(4, 6, 0, up)]
    if not light:
        ready(6)
        yield at + 1.1 * unit
        for copy in beside_down + beside_up:
            copy.wait_recv()
        add_into(mine.at[6], landed.at[1], landed.at[2])
        if last:
            from_across = net.push(mine.at[6], landed.at[4], across)
    yield at + (1.1 if light else 1.6) * unit
    first.wait_recv()
    add_half(5, 3, 0)
    if last:
        from_up.append(send_half(5, 5, 0, down))
    yield at + (1.1 if light else 1.8) * unit
    second.wait_recv()
    add_half(4, 3, 1)
    if not last:
        return
    from_down.append(send_half(4, 6, 1, up))
    if light:
        ready(6)
        yield at + 2 * unit
        for copy in beside_down + beside_up:
            copy.wait_recv()
        add_into(mine.at[6], landed.at[1], landed.at[2])
        from_across = net.push(mine.at[6], landed.at[4], across)
    ready(7)
    yield at + (3 if light else 2.5) * unit
    for copy in from_up + from_down + [from_across]:
        copy.wait_recv()
    rows = 32768 // out.shape[1]

    def total(i, carry):
        at = pl.ds(pl.multiple_of(i * rows, rows), rows)
        value = mine[7, at, :].astype(F32) + landed[4, at, :].astype(F32)
        out[at, :] = value + (landed[5, at, :].astype(F32) + landed[6, at, :].astype(F32))
        return carry

    lax.fori_loop(0, out.shape[0] // rows, total, 0)


def gather_slot(net, out, rows, ring, pair):
    order = ("z", "c", "f") if ring == "z" else ("x", "h")

    def slot(offset):
        at = net.place(offset, *order)
        return out.at[pl.ds(pl.multiple_of(at * rows, rows), rows)]

    return slot


def input_slot(net, out):
    def slot(offset):
        row = pl.multiple_of(net.place(offset, "z", "c") * 128, 128)
        column = pl.multiple_of(net.place(offset, "f") * 1024, 1024)
        return out.at[pl.ds(row, 128), pl.ds(column, 1024)]

    return slot


def scatter_chunk(net, ref, ring):
    order = ("z", "c", "f") if ring == "z" else ("x", "h")
    return lambda offset: ref.at[net.place(offset, *order)]


def comm_call(kernel, name, number, pushes, locals_, out_shape, scratch, in_specs, out_specs, *args):
    ins = [i for i, spec in enumerate(in_specs) if spec is VMEM]
    outs = [i for i, spec in enumerate(out_specs) if spec is VMEM]
    shapes = [args[i] for i in ins] + [out_shape[i] for i in outs]
    first = len(args) + len(out_shape)
    last = first + 3 + len(scratch)

    def staged(*refs):
        given, results = list(refs[: len(args)]), list(refs[len(args) : first])
        sems, buffers = refs[last], refs[last + 1 :]
        for k, i in enumerate(ins):
            copy = pltpu.make_async_copy(given[i], buffers[k], sems.at[k])
            copy.start()
            Net.loads.append(copy)
            given[i] = buffers[k]
        stores = []
        for k, i in enumerate(outs, len(ins)):
            stores.append(pltpu.make_async_copy(buffers[k], results[i], sems.at[k]))
            results[i] = buffers[k]
        kernel(*given, *results, *refs[first:last])
        for copy in stores:
            copy.start()
        for copy in stores:
            copy.wait()

    return pl.pallas_call(
        staged,
        out_shape=out_shape,
        in_specs=[ANY] * len(in_specs),
        out_specs=(ANY,) * len(out_specs),
        scratch_shapes=[DMA((pushes,)), DMA((pushes,)), DMA((locals_,))]
        + scratch
        + [DMA((len(shapes),))]
        + [pltpu.VMEM(v.shape, v.dtype) for v in shapes],
        name=name,
        compiler_params=pltpu.CompilerParams(
            collective_id=number, has_side_effects=True, vmem_limit_bytes=60 << 20
        ),
    )(*args)


def scatter_scratch(rows, width, sibling):
    shapes = [pltpu.VMEM((8, rows, width), BF), pltpu.VMEM((7, rows, width), BF)]
    return shapes + ([pltpu.VMEM((8, rows, width), BF)] if sibling else [])


def turn_halves(values):
    lanes = lax.broadcasted_iota(jnp.int32, values.shape, 1)
    first = lax.rem(lanes, HEAD) < HEAD // 2
    return jnp.where(first, pltpu.roll(values, 96, axis=1), pltpu.roll(values, 32, axis=1))


def front_kernel(
    x_ref,
    d_ref,
    w_ref,
    up_ref,
    down_ref,
    seq_ref,
    place_ref,
    gains,
    shifts,
    bias,
    run_tables,
    token_tables,
    rows_out,
    low_out,
    w_out,
    ffn_out,
    q_out,
    kv_out,
    grad_out,
    cosine,
    sine,
    growth,
    order,
    w_norm,
    send,
    recv,
    local,
    x_all,
    in_low,
    w_all,
    blocks,
    near,
    near_sum,
    far,
    kv_here,
    norm_parts,
    norm_got,
    ranks_here,
):
    net = Net(send, recv)
    net.greet(ALL_G, ALL_T)
    me = net.place({}, "z", "c")
    group = net.place({}, "x", "h")
    f = net.at["f"]
    rows = pl.ds(pl.multiple_of(me * 32, 32), 32)
    stores = []

    def store(src, dst, k):
        copy = pltpu.make_async_copy(src, dst, local.at[k])
        copy.start()
        stores.append(copy)

    def norm_block(offset):
        first = net.place(offset, "z", "c") * 128

        def norm_rows(i, carry):
            at = pl.ds(pl.multiple_of(first + i * 16, 16), 16)
            values = x_all[at, :].astype(F32)
            centered = values - jnp.mean(values, axis=1, keepdims=True)
            scale = lax.rsqrt(jnp.mean(centered * centered, axis=1, keepdims=True) + EPS)
            in_low[at, :] = (centered * scale * gains[0:1, :] + shifts[0:1, :]).astype(BF)
            return carry

        lax.fori_loop(0, 8, norm_rows, 0, unroll=4)

    def activations():
        yield from gather_flow(
            net, x_ref, input_slot(net, x_all), "z", "f", local.at[0], True, True, 0, 5.5, 0, norm_block
        )
        ffn_sent = []
        for offset in ALL_ZC:
            to = net.place(offset, "z", "c")
            at = pl.ds(pl.multiple_of(to * 512, 512), 512)
            ffn_sent.append(net.push(up_ref.at[:, at], ffn_out.at[rows, pl.ds(0, 512)], offset))
            ffn_sent.append(net.push(down_ref.at[:, at], ffn_out.at[rows, pl.ds(512, 512)], offset))
        at = pl.ds(pl.multiple_of(me * 512, 512), 512)
        store(up_ref.at[:, at], ffn_out.at[rows, pl.ds(0, 512)], 4)
        store(down_ref.at[:, at], ffn_out.at[rows, pl.ds(512, 512)], 5)
        store(in_low, low_out, 6)
        store(x_all.at[pl.ds(pl.multiple_of((me * 2 + f) * 64, 64), 64)], rows_out, 7)
        yield from gather_flow(
            net, d_ref, input_slot(net, grad_out), "z", "f", local.at[1], True, True, 24, 8
        )
        for copy in ffn_sent:
            copy.wait_recv()

    def run_rank(index):
        lanes = lax.broadcasted_iota(jnp.int32, (1, 128), 1)
        return jnp.sum(jnp.where(lanes == index, near_sum[0:1, :], 0.0), axis=1, keepdims=True)

    def tables(i, carry):
        at = tile(i, RUN)
        block = run_rank(group * 16 + i)
        block = block - jnp.floor(block / 64) * 64
        mask = lax.broadcasted_iota(jnp.int32, (64, 128), 0).astype(F32) == block
        cos_a, sin_a, grow_a = (
            jnp.sum(jnp.where(mask, run_tables[k], 0.0), axis=0, keepdims=True) for k in range(3)
        )
        cos_b, sin_b, grow_b = token_tables[0], token_tables[1], token_tables[2]
        lanes = lax.broadcasted_iota(jnp.int32, (RUN, 128), 1)
        sin = sin_a * cos_b + cos_a * sin_b
        cosine[at, :] = cos_a * cos_b - sin_a * sin_b
        sine[at, :] = jnp.where(lax.rem(lanes, HEAD) < HEAD // 2, -sin, sin)
        growth[at, :] = grow_a * grow_b
        return carry

    def put_order():
        lanes = lax.broadcasted_iota(jnp.int32, (16, 128), 1)
        places = lax.broadcasted_iota(jnp.int32, (16, 128), 0)
        ranks = jnp.zeros((16, 128), F32)
        by_lane = jnp.full((16, 128), 1e9, F32)
        for k in range(16):
            rank = run_rank(group * 16 + k)
            ranks = jnp.where(places == k, rank, ranks)
            by_lane = jnp.where(lanes == k, rank, by_lane)
        slot = jnp.sum((by_lane < ranks).astype(F32), axis=1, keepdims=True)
        hit = lanes.astype(F32) == slot
        runs = jnp.sum(jnp.where(hit, places.astype(F32), 0.0), axis=0, keepdims=True)
        ranks = jnp.sum(jnp.where(hit, ranks, 0.0), axis=0, keepdims=True)
        total = jnp.sum(far[...], axis=0)[0:1]
        order[0:1, :] = total.astype(jnp.int32)
        order[1:2, :] = runs.astype(jnp.int32)
        order[2:3, :] = ranks.astype(jnp.int32)
        order[3:8, :] = jnp.zeros((5, 128), jnp.int32)

    head_at = pl.ds(pl.multiple_of(f * 1024 + me * 128, 128), 128)

    def project(i, carry):
        at = tile(i, 256)
        values = jnp.dot(in_low[at, :], w_all[:, 0:384], preferred_element_type=F32)
        queries = values[:, 0:128] + bias[0:1, head_at]
        keys = values[:, 128:256] + bias[1:2, head_at]
        cos, sin, grow = cosine[at, :], sine[at, :], growth[at, :]
        queries = ((queries * cos + turn_halves(queries) * sin) * grow).astype(BF)
        q_out[at, :] = queries * jnp.bfloat16(0.125)
        keys = (keys * cos + turn_halves(keys) * sin) * (1.0 / grow)
        kv_here[at, 0:128] = keys.astype(BF)
        kv_here[at, 128:256] = (values[:, 256:384] + bias[2:3, head_at]).astype(BF)
        return carry

    def put_ranks():
        lanes = lax.broadcasted_iota(jnp.int32, (1, 128), 1)
        ranks = (seq_ref[...] * 64 + place_ref[...] // RUN).astype(F32)
        first, second = (
            jnp.sum(jnp.where(lanes == k * RUN, ranks, 0.0), axis=1, keepdims=True) for k in range(2)
        )
        at = net.place({}, "x", "h", "z", "c") * 2
        row = jnp.where(lanes == at, first, jnp.where(lanes == at + 1, second, 0.0))
        ranks_here[...] = jnp.broadcast_to(row, (8, 128))

    def attention():
        attn_sent, near_sent = [], []
        put_ranks()
        for offset in ALL_ZC:
            to = net.place(offset, "z", "c")
            attn_sent.append(net.push(w_ref.at[to], blocks.at[rows], offset))
        for offset in ALL_ZC:
            near_sent.append(net.push(ranks_here, near.at[me], offset))
        own = pltpu.make_async_copy(w_ref.at[me], blocks.at[rows], local.at[2])
        own.start()
        near[me] = ranks_here[...]
        own.wait()
        yield 5
        for copy in attn_sent:
            copy.wait_recv()
        weights = gather_flow(
            net, blocks, gather_slot(net, w_all, 256, "x", "h"), "x", "h", local.at[3], False, False, 6, 5.5
        )
        yield next(weights)
        for copy in near_sent:
            copy.wait_recv()
        near_sum[...] = jnp.sum(near[...], axis=0)
        far_sent = [net.push(near_sum, far.at[group], offset) for offset in ALL_T]
        far[group] = near_sum[...]
        lax.fori_loop(0, 16, tables, 0)
        yield from weights
        store(w_all, w_out, 8)
        yield 26
        lax.fori_loop(0, 4, project, 0, unroll=2)
        sending = gather_flow(
            net, kv_here, gather_slot(net, kv_out, 1024, "x", "h"), "x", "h", local.at[9], False, False, 29, 11
        )
        yield next(sending)
        for copy in far_sent:
            copy.wait_recv()
        put_order()
        yield from sending

    def norm_sums():
        yield 25
        gain, shift = gains[1:2, head_at], shifts[1:2, head_at]
        high = [gain.astype(BF), shift.astype(BF)]
        low = [(v - h.astype(F32)).astype(BF) for v, h in zip((gain, shift), high)]
        vectors = jnp.concatenate(high + low + [jnp.zeros((12, 128), BF)], axis=0)

        def norm_vectors(i, carry):
            parts = lax.dot_general(
                vectors, w_all[tile(i, 128), 384:512], NT, preferred_element_type=F32
            )
            norm_parts[i] = parts[0:8] + jnp.concatenate([parts[2:8], parts[8:10]], axis=0)
            return carry

        lax.fori_loop(0, 16, norm_vectors, 0)
        mine = net.place({}, "z", "c", "f")
        sent = []
        for k, offset in enumerate(ALL_G):
            to = net.place(offset, "z", "c", "f")
            sent.append(net.push(norm_parts.at[to], norm_got.at[k], offset))
        yield 41
        for copy in sent:
            copy.wait_recv()
        w_norm[mine] = norm_parts[mine] + jnp.sum(norm_got[...], axis=0)
        sent = [net.push(w_norm.at[mine], w_norm.at[mine], offset) for offset in ALL_G]
        yield 58
        for copy in sent:
            copy.wait_recv()

    run_flows(Flow(attention()), Flow(activations()), Flow(norm_sums()))
    for copy in stores:
        copy.wait()
    net.finish()


def front(number, *args):
    table = sds((1024, 128), F32)
    return comm_call(
        front_kernel,
        "front",
        number,
        23 * 2 + 14 + 7 * 3 + 12 * 2 + 30,
        10,
        (
            sds((64, 2048), BF),
            sds((1024, 2048), BF),
            sds((2048, 512), BF),
            sds((256, 1024), BF),
            sds((1024, 128), BF),
            sds((8192, 256), BF),
            sds((1024, 2048), BF),
            table,
            table,
            table,
            sds((8, 128), jnp.int32),
            sds((16, 8, 128), F32),
        ),
        [
            pltpu.VMEM((1024, 2048), BF),
            pltpu.VMEM((1024, 2048), BF),
            pltpu.VMEM((2048, 512), BF),
            pltpu.VMEM((256, 512), BF),
            pltpu.VMEM((8, 8, 128), F32),
            pltpu.VMEM((8, 128), F32),
            pltpu.VMEM((8, 8, 128), F32),
            pltpu.VMEM((1024, 256), BF),
            pltpu.VMEM((16, 8, 128), F32),
            pltpu.VMEM((15, 8, 128), F32),
            pltpu.VMEM((8, 128), F32),
        ],
        [ANY] * 5 + [VMEM] * 7,
        (ANY,) * 4 + (VMEM, ANY, ANY) + (VMEM,) * 5,
        *args,
    )


def row_sums(values):
    ones = jnp.ones((8, values.shape[1]), F32)
    return lax.dot_general(
        ones, values, NT, preferred_element_type=F32, precision=lax.Precision.HIGHEST
    )[0:1]


def put_sums(target, i, *values):
    sums = row_sums(jnp.concatenate(values, axis=0))
    for k in range(len(values)):
        target[pl.ds(8 * k + i, 1), :] = sums[:, k * 128 : k * 128 + 128]


def tile(i, rows=128):
    return pl.ds(pl.multiple_of(i * rows, rows), rows)


def columns_of(rows_ref, i):
    return rows_ref[i].T


def put_rows(rows_ref, *values):
    for k, value in enumerate(values):
        for i in range(8):
            rows_ref[i, k : k + 1, :] = value[i : i + 1]


def fold_groups(values):
    values = values[:, 0:1024] + values[:, 1024:2048]
    return fold_lanes(values[:, 0:512] + values[:, 512:1024])


def fold_lanes(values):
    return (values[:, 0:128] + values[:, 128:256]) + (values[:, 256:384] + values[:, 384:512])


def middle_kernel(
    att,
    w_attn,
    ffn_block,
    ffn_below,
    ffn_above,
    ffn_beside,
    grad_all_in,
    input_rows,
    b_out,
    b_up,
    gains,
    shifts,
    hid_gain,
    hid_shift,
    w_norm,
    mid,
    grad_mid,
    ffn_part,
    grad_att,
    ffn_up,
    ffn_down,
    ffn_across,
    ffn_own,
    branch_out,
    turned_out,
    hid_vec,
    head_vec,
    row_vec,
    send,
    recv,
    local,
    grad_all,
    out_w,
    w_ffn,
    mid_low,
    branch_all,
    hidden_low,
    pre_low,
    hidden_turned,
    pre_turned,
    attn_low,
    low_rows,
    partial_rows,
    mine,
    landed,
    other,
    t_mine,
    t_landed,
    grad_hidden,
    activated,
    slope,
    normal_attn,
    normal_mid,
    scale_mid,
    sent_a,
    stats_a,
    rows_a,
    sent_b,
    stats_b,
    rows_b,
    sent_c,
    stats_c,
    rows_c,
    branch_rows,
    w_rows,
    folded,
):
    net = Net(send, recv)
    me = net.place({}, "z", "c", "f")
    load_w = pltpu.make_async_copy(w_attn.at[:, pl.ds(384, 128)], out_w, local.at[10])
    load_w.start()
    load_grad = pltpu.make_async_copy(grad_all_in, grad_all, local.at[11])
    load_grad.start()
    net.greet(ALL_G, NEAR_T)
    weights = Flow(
        gather_rest_flow(
            net,
            (ffn_block, ffn_below, ffn_above, ffn_beside),
            gather_slot(net, w_ffn, 256, "x", "h"),
            "x",
            "h",
            local.at[pl.ds(12, 4)],
            0,
            11,
        )
    )
    head_at = pl.ds(
        pl.multiple_of(net.at["f"] * 1024 + net.place({}, "z", "c") * 128, 128), 128
    )
    hidden_at = pl.ds(
        pl.multiple_of(net.at["f"] * 4096 + net.place({}, "z", "c") * 512, 512), 512
    )
    head_gain, head_shift = gains[1:2, head_at], shifts[1:2, head_at]
    gain_here, shift_here, bias_here = hid_gain[:, hidden_at], hid_shift[:, hidden_at], b_up[:, hidden_at]

    def exchange(sent, stats):
        copies = [net.push(sent, stats.at[me], offset) for offset in ALL_G]
        stats[me] = sent[...]
        for copy in copies:
            copy.wait_recv()

    def chunk(offset):
        at = net.place(offset, "z", "c", "f")
        return partial_rows.at[pl.ds(pl.multiple_of(at * 64, 64), 64)]

    def measure(i, carry):
        here = att[tile(i), :]
        centered = here - jnp.mean(here, axis=1, keepdims=True)
        put_sums(sent_a, i, here, centered * centered)
        return carry

    lax.fori_loop(0, 8, measure, 0, unroll=2)
    exchange(sent_a, stats_a)
    center = jnp.sum(stats_a[:, 0:8], axis=0) / 2048
    spread = jnp.sum(
        stats_a[:, 8:16] + 128 * jnp.square(stats_a[:, 0:8] / 128 - center[None]), axis=0
    )
    put_rows(rows_a, center, lax.rsqrt(spread / 2048 + EPS))

    def norm_heads(i, carry):
        columns = columns_of(rows_a, i)
        normal_rows = (att[tile(i), :] - columns[:, 0:1]) * columns[:, 1:2]
        normal_attn[tile(i), :] = normal_rows
        attn_low[tile(i), :] = (normal_rows * head_gain + head_shift).astype(BF)
        return carry

    lax.fori_loop(0, 8, norm_heads, 0, unroll=2)
    load_w.wait()

    def project(i, carry):
        partial_rows[:, tile(i, 256)] = lax.dot_general(
            attn_low[...], out_w[tile(i, 256), :], NT, preferred_element_type=F32
        ).astype(BF)
        return carry

    lax.fori_loop(0, 8, project, 0, unroll=2)
    run_until(
        Flow(scatter_flow(net, chunk, mid, mine, other, landed, local, "z", "f", True, False, 13, 5.5)),
        weights,
    )
    net.finish()

    def mid_norm(i, carry):
        at = tile(i, 16)
        branch_rows[at, :] = mid[at, :]
        rows = input_rows[at, :].astype(F32) + (mid[at, :] + b_out[...])
        mid[at, :] = rows
        centered = rows - jnp.mean(rows, axis=1, keepdims=True)
        scale = lax.rsqrt(jnp.mean(centered * centered, axis=1, keepdims=True) + EPS)
        rows = centered * scale
        normal_mid[at, :] = rows
        scale_mid[at, :] = jnp.broadcast_to(scale, (16, 128))
        low_rows[at, :] = (rows * gains[2:3, :] + shifts[2:3, :]).astype(BF)
        return carry

    lax.fori_loop(0, 4, mid_norm, 0)
    def hidden_grads():
        yield 43
        run_until(weights)
        load_grad.wait()
        for i in range(4):
            grad_hidden[tile(i, 256), :] = jnp.dot(
                grad_all[tile(i, 256), :], w_ffn[:, 512:1024], preferred_element_type=F32
            )
            yield 44

    run_flows(
        Flow(
            gather_flow(
                net, low_rows, gather_slot(net, mid_low, 64, "z", "f"), "z", "f", local.at[0], True, False, 31, 5.5
            )
        ),
        Flow(hidden_grads()),
        weights,
    )
    net.finish()

    def up(i, carry):
        at = tile(i)
        pre = jnp.dot(mid_low[at, :], w_ffn[:, 0:512], preferred_element_type=F32) + bias_here
        below = 0.5 + 0.5 * lax.erf(pre * math.sqrt(0.5))
        act = pre * below
        activated[at, :] = act
        slope[at, :] = below + pre * jnp.exp(-0.5 * pre * pre) * (1.0 / math.sqrt(2.0 * math.pi))
        centered = act - jnp.mean(act, axis=1, keepdims=True)
        scaled = grad_hidden[at, :] * gain_here
        put_sums(
            sent_b,
            i,
            fold_lanes(act),
            fold_lanes(centered * centered),
            fold_lanes(scaled),
            fold_lanes(scaled * centered),
        )
        return carry

    lax.fori_loop(0, 8, up, 0, unroll=2)
    exchange(sent_b, stats_b)
    center = jnp.sum(stats_b[:, 0:8], axis=0) / 8192
    apart = stats_b[:, 0:8] / 512 - center[None]
    spread = jnp.sum(stats_b[:, 8:16] + 512 * jnp.square(apart), axis=0)
    scale = lax.rsqrt(spread / 8192 + EPS)
    mean_back = jnp.sum(stats_b[:, 16:24], axis=0) / 8192
    cross_back = scale * jnp.sum(stats_b[:, 24:32] + apart * stats_b[:, 16:24], axis=0) / 8192
    put_rows(rows_b, center, scale, mean_back, cross_back)

    def hidden(i, carry):
        at = tile(i)
        columns = columns_of(rows_b, i)
        scale = columns[:, 1:2]
        normal_rows = (activated[at, :] - columns[:, 0:1]) * scale
        hidden_low[at, :] = (normal_rows * gain_here + shift_here).astype(BF)
        upstream = grad_hidden[at, :]
        back = scale * (upstream * gain_here - columns[:, 2:3] - normal_rows * columns[:, 3:4])
        low = (back * slope[at, :]).astype(BF)
        pre_low[at, :] = low
        return (
            carry[0] + jnp.sum(low.astype(F32), axis=0, keepdims=True),
            carry[1] + jnp.sum(upstream * normal_rows, axis=0, keepdims=True),
            carry[2] + jnp.sum(upstream, axis=0, keepdims=True),
        )

    sums = lax.fori_loop(0, 8, hidden, (jnp.zeros((1, 512), F32),) * 3, unroll=2)
    for k in range(3):
        hid_vec[k : k + 1, :] = sums[k]

    def project_back(i, carry):
        partial_rows[:, tile(i, 256)] = lax.dot_general(
            pre_low[...], w_ffn[tile(i, 256), 0:512], NT, preferred_element_type=F32
        ).astype(BF)
        return carry

    lax.fori_loop(0, 8, project_back, 0, unroll=2)

    def weight_terms():
        def turn(i, carry):
            pre_turned[:, tile(i)] = pre_low[tile(i), :].T
            hidden_turned[:, tile(i)] = hidden_low[tile(i), :].T
            return carry

        yield 69
        lax.fori_loop(0, 8, turn, 0)
        for k, (i, j) in enumerate(ROOTS):
            yield 70 + k
            columns = tile(net.place({"x": i, "h": j}, "x", "h"), 256)
            t_mine[k, 0:512, :] = jnp.dot(
                pre_turned[...], mid_low[:, columns], preferred_element_type=F32
            ).astype(BF)
            t_mine[k, 512:1024, :] = jnp.dot(
                hidden_turned[...], grad_all[:, columns], preferred_element_type=F32
            ).astype(BF)

    stores = []

    def weight_scatter():
        yield from weight_terms()
        yield from scatter_flow(
            net, None, None, t_mine, None, t_landed, local, "x", "h", False, False, 82, 11, False
        )
        for k in range(4):
            target = (ffn_up, ffn_down, ffn_across, ffn_own)[k]
            sums_store = pltpu.make_async_copy(t_mine.at[4 + k], target, local.at[16 + k])
            sums_store.start()
            stores.append(sums_store)

    weights = Flow(weight_scatter())
    run_until(
        Flow(scatter_flow(net, chunk, grad_mid, mine, other, landed, local, "z", "f", True, False, 68, 5.5)),
        weights,
    )
    net.finish()

    def mid_back(i, carry):
        at = tile(i, 16)
        upstream = grad_mid[at, :]
        normal_rows = normal_mid[at, :]
        scaled = upstream * gains[2:3, :]
        mean = jnp.mean(scaled, axis=1, keepdims=True)
        cross = jnp.mean(scaled * normal_rows, axis=1, keepdims=True)
        out_rows = grad_all[pl.ds(pl.multiple_of(me * 64 + i * 16, 16), 16), :].astype(F32)
        rows = out_rows + scale_mid[at, 0:1] * (scaled - mean - normal_rows * cross)
        grad_mid[at, :] = rows
        low = rows.astype(BF)
        low_rows[at, :] = low
        low = low.astype(F32)
        folded[0, at, :] = fold_groups(low * w_rows[0:1, :])
        folded[1, at, :] = fold_groups(low * (branch_rows[at, :] - w_rows[1:2, :]))
        row_vec[0:1, :] += jnp.sum(upstream * normal_rows, axis=0, keepdims=True)
        row_vec[1:2, :] += jnp.sum(upstream, axis=0, keepdims=True)
        row_vec[2:3, :] += jnp.sum(low, axis=0, keepdims=True)
        row_vec[3:4, :] += jnp.sum(out_rows, axis=0, keepdims=True)
        return carry

    row_vec[...] = jnp.zeros_like(row_vec)
    for g in range(16):
        w_rows[:, g * 128 : g * 128 + 128] = w_norm[g]
    lax.fori_loop(0, 4, mid_back, 0)
    def down():
        for i in range(8):
            yield 87 + i
            partial_rows[:, tile(i, 256)] = lax.dot_general(
                hidden_low[...], w_ffn[tile(i, 256), 512:1024], NT, preferred_element_type=F32
            ).astype(BF)

    def norm_sums():
        yield 86.5
        sums = [row_sums(folded[k]) * (1.0 / 2048) for k in range(2)]
        sent_c[...] = jnp.broadcast_to(jnp.concatenate(sums, axis=1), (8, 128))
        copies = [net.push(sent_c, stats_c.at[me], offset) for offset in ALL_G]
        stats_c[me] = sent_c[...]
        yield 99
        for copy in copies:
            copy.wait_recv()

    run_flows_but(
        weights,
        Flow(
            gather_flow(
                net, low_rows, gather_slot(net, branch_all, 64, "z", "f"), "z", "f", local.at[0], True, True, 86, 5.5
            )
        ),
        Flow(norm_sums()),
        Flow(down()),
    )
    store = pltpu.make_async_copy(partial_rows, ffn_part, local.at[8])
    store.start()

    lanes = lax.broadcasted_iota(jnp.int32, (1, 128), 1)
    for i in range(8):
        a, b = stats_c[2 * i, 0:1, :], stats_c[2 * i + 1, 0:1, :]
        rows_c[i, 0:1, :] = jnp.where(lanes < 64, a, pltpu.roll(b, 64, axis=1))
        rows_c[i, 1:2, :] = jnp.where(lanes < 64, pltpu.roll(a, 64, axis=1), b)
    keep = [
        pltpu.make_async_copy(branch_all, branch_out, local.at[20]),
        pltpu.make_async_copy(pre_turned.at[pl.ds(0, 128)], turned_out, local.at[21]),
    ]
    keep[0].start()

    def attn_back(i, carry):
        at = tile(i)
        upstream = jnp.dot(branch_all[at, :], out_w[...], preferred_element_type=F32)
        normal_rows = normal_attn[at, :]
        columns = columns_of(rows_c, i)
        scale = columns_of(rows_a, i)[:, 1:2]
        grad_att[at, :] = (
            scale * (upstream * head_gain - columns[:, 0:1] - normal_rows * columns[:, 1:2])
        ).astype(BF)
        pre_turned[0:128, at] = attn_low[at, :].T
        return (
            carry[0] + jnp.sum(upstream * normal_rows, axis=0, keepdims=True),
            carry[1] + jnp.sum(upstream, axis=0, keepdims=True),
        )

    sums = lax.fori_loop(0, 8, attn_back, (jnp.zeros((1, 128), F32),) * 2, unroll=2)
    for k in range(2):
        head_vec[k : k + 1, :] = sums[k]
    keep[1].start()
    for copy in keep:
        copy.wait()
    run_until(weights)
    for copy in stores:
        copy.wait()
    store.wait()
    net.finish()


def middle(number, *args):
    wide = pltpu.VMEM((1024, 512), F32)
    low = pltpu.VMEM((1024, 512), BF)
    tall = pltpu.VMEM((512, 1024), BF)
    whole = pltpu.VMEM((1024, 2048), BF)
    return comm_call(
        middle_kernel,
        "middle",
        number,
        15 * 3 + 20 * 4 + 14 * 2,
        22,
        (
            sds((64, 2048), F32),
            sds((64, 2048), F32),
            sds((1024, 2048), BF),
            sds((1024, 128), BF),
            *(sds((1024, 256), BF),) * 4,
            sds((1024, 2048), BF),
            sds((128, 1024), BF),
            sds((8, 512), F32),
            sds((8, 128), F32),
            sds((8, 2048), F32),
        ),
        [
            whole,
            pltpu.VMEM((2048, 128), BF),
            pltpu.VMEM((2048, 1024), BF),
            whole,
            whole,
            low,
            low,
            tall,
            tall,
            pltpu.VMEM((1024, 128), BF),
            pltpu.VMEM((64, 2048), BF),
            whole,
            pltpu.VMEM((8, 64, 2048), BF),
            pltpu.VMEM((7, 64, 2048), BF),
            pltpu.VMEM((8, 64, 2048), BF),
            pltpu.VMEM((8, 1024, 256), BF),
            pltpu.VMEM((7, 1024, 256), BF),
            wide,
            wide,
            wide,
            pltpu.VMEM((1024, 128), F32),
            pltpu.VMEM((64, 2048), F32),
            pltpu.VMEM((64, 128), F32),
            pltpu.VMEM((16, 128), F32),
            pltpu.VMEM((16, 16, 128), F32),
            pltpu.VMEM((8, 8, 128), F32),
            pltpu.VMEM((32, 128), F32),
            pltpu.VMEM((16, 32, 128), F32),
            pltpu.VMEM((8, 8, 128), F32),
            pltpu.VMEM((8, 128), F32),
            pltpu.VMEM((16, 8, 128), F32),
            pltpu.VMEM((8, 8, 128), F32),
            pltpu.VMEM((64, 2048), F32),
            pltpu.VMEM((8, 2048), F32),
            pltpu.VMEM((2, 64, 128), F32),
        ],
        [VMEM] + [ANY] * 6 + [VMEM] * 8,
        (VMEM, VMEM, ANY, VMEM) + (ANY,) * 6 + (VMEM,) * 3,
        *args,
    )


def tail_kernel(
    kv_part,
    ffn_part,
    ffn_own,
    ffn_up,
    ffn_down,
    ffn_across,
    query_grad,
    cosine,
    sine,
    growth,
    w_attn_in,
    in_low_in,
    branch_in,
    attn_turned,
    mid,
    grad_mid,
    input_rows,
    b_down,
    gains,
    hid_vec,
    head_vec,
    row_vec,
    out_half,
    in_half,
    attn_got,
    ffn_got,
    vectors,
    send,
    recv,
    local,
    kv_mine,
    kv_landed,
    kv_grad,
    f_mine,
    f_landed,
    f_other,
    i_mine,
    i_landed,
    i_other,
    w_mine,
    w_landed,
    w_grad,
    w_rows,
    attn_rows,
    ffn_rows,
    out_rows,
    in_rows,
    grad_qkv,
    turned,
    partial_rows,
    w_attn,
    in_low,
    branch_all,
    row_parts,
    row_got,
    packed,
    packed_got,
):
    net = Net(send, recv)
    me = net.place({}, "z", "c", "f")
    here = net.place({}, "z", "c")
    f = net.at["f"]
    load_w = pltpu.make_async_copy(w_attn_in, w_attn, local.at[16])
    load_w.start()
    load_in = pltpu.make_async_copy(in_low_in, in_low, local.at[21])
    load_in.start()
    load_branch = pltpu.make_async_copy(branch_in, branch_all, local.at[22])
    load_branch.start()
    net.greet(ALL_G, ALL_T)

    def to_halves(source, target, k):
        rows = target.at[pl.ds(pl.multiple_of(f * 64, 64), 64)]
        theirs = source.at[:, pl.ds(pl.multiple_of((1 - f) * 1024, 1024), 1024)]
        own = source.at[:, pl.ds(pl.multiple_of(f * 1024, 1024), 1024)]
        copy = net.push(theirs, rows, {"f": 1})
        keep = pltpu.make_async_copy(own, rows, local.at[k])
        keep.start()
        return copy, keep

    def to_rows(source, got, k):
        copies = []
        for offset in ALL_ZC:
            at = net.place(offset, "z", "c")
            copies.append(
                net.push(source.at[pl.ds(pl.multiple_of(at * 32, 32), 32)], got.at[here], offset)
            )
        keep = pltpu.make_async_copy(
            source.at[pl.ds(pl.multiple_of(here * 32, 32), 32)], got.at[here], local.at[k]
        )
        keep.start()
        return copies, keep

    def ffn_weights():
        def turn(i, carry):
            for j in range(2):
                at = slice(j * 128, j * 128 + 128)
                block = ffn_own[tile(i), at].astype(F32) + ffn_up[tile(i), at].astype(F32)
                block = block + (ffn_down[tile(i), at].astype(F32) + ffn_across[tile(i), at].astype(F32))
                block = block.T
                w_rows[j * 128 : j * 128 + 128, tile(i)] = block.astype(BF)
            return carry

        lax.fori_loop(0, 8, turn, 0)
        yield to_rows(w_rows, ffn_got, 17)

    kv_flow = Flow(
        scatter_flow(
            net,
            scatter_chunk(net, kv_part, "x"),
            kv_grad,
            kv_mine,
            None,
            kv_landed,
            local.at[pl.ds(0, 8)],
            "x",
            "h",
            False,
            False,
            0,
            11,
        )
    )
    ffn_flow = Flow(
        scatter_flow(
            net,
            scatter_chunk(net, ffn_part, "z"),
            ffn_rows,
            f_mine,
            f_other,
            f_landed,
            local.at[pl.ds(8, 8)],
            "z",
            "f",
            True,
            True,
            4,
            7,
        )
    )
    kv_flow.step()
    ffn_flow.step()
    ffn_copies, ffn_keep = next(ffn_weights())

    def out_terms():
        yield 6
        load_branch.wait()
        for k, (i, j) in enumerate(ROOTS):
            yield 7 + k
            columns = tile(net.place({"x": i, "h": j}, "x", "h"), 256)
            w_mine[k, 384:512, :] = jnp.dot(
                attn_turned[...], branch_all[:, columns], preferred_element_type=F32
            ).astype(BF)

    run_flows(kv_flow, ffn_flow, Flow(out_terms()))

    def finish_rows(i, carry):
        at = tile(i, 16)
        out_rows[at, :] = mid[at, :] + (ffn_rows[at, :] + b_down[...])
        return carry

    lax.fori_loop(0, 4, finish_rows, 0)
    out_copy, out_keep = to_halves(out_rows, out_half, 18)

    def unrotate(i, carry):
        at = tile(i)
        cos, sin, grow = cosine[at, :], sine[at, :], growth[at, :]
        queries = query_grad[at, :] * grow
        queries = (queries * cos - turn_halves(queries) * sin).astype(BF)
        keys = kv_grad[at, 0:128] / grow
        keys = (keys * cos - turn_halves(keys) * sin).astype(BF)
        values = kv_grad[at, 128:256].astype(BF)
        grad_qkv[at, 0:128] = queries
        grad_qkv[at, 128:256] = keys
        grad_qkv[at, 256:384] = values
        return tuple(
            total + jnp.sum(part.astype(F32), axis=0, keepdims=True)
            for total, part in zip(carry, (queries, keys, values))
        )

    bias = lax.fori_loop(0, 8, unrotate, (jnp.zeros((1, 128), F32),) * 3, unroll=2)
    for k in range(3):
        packed[8 + k : 9 + k, :] = bias[k]
    load_w.wait()

    def project(i, carry):
        partial_rows[:, tile(i, 256)] = lax.dot_general(
            grad_qkv[...], w_attn[tile(i, 256), 0:384], NT, preferred_element_type=F32
        ).astype(BF)
        return carry

    lax.fori_loop(0, 8, project, 0, unroll=2)

    def chunk(offset):
        at = net.place(offset, "z", "c", "f")
        return partial_rows.at[pl.ds(pl.multiple_of(at * 64, 64), 64)]

    def weight_scatter():
        def turn_grads(i, carry):
            turned[:, tile(i)] = grad_qkv[tile(i), :].T
            return carry

        yield 0.6
        lax.fori_loop(0, 8, turn_grads, 0)
        load_in.wait()
        for k, (i, j) in enumerate(ROOTS):
            yield 1 + k
            columns = tile(net.place({"x": i, "h": j}, "x", "h"), 256)
            w_mine[k, 0:384, :] = jnp.dot(
                turned[...], in_low[:, columns], preferred_element_type=F32
            ).astype(BF)
        yield from scatter_flow(
            net, None, w_grad, w_mine, None, w_landed, None, "x", "h", False, True, 0, 5.5
        )

    w_flow = Flow(weight_scatter())
    for _ in range(9):
        w_flow.step()
    in_flow = Flow(
        scatter_flow(net, chunk, in_rows, i_mine, i_other, i_landed, local, "z", "f", True, False, 0, 5.5)
    )
    run_until(in_flow, w_flow)

    def in_back(i, carry):
        at = tile(i, 16)
        rows = input_rows[at, :].astype(F32)
        centered = rows - jnp.mean(rows, axis=1, keepdims=True)
        scale = lax.rsqrt(jnp.mean(centered * centered, axis=1, keepdims=True) + EPS)
        normal_rows = centered * scale
        upstream = in_rows[at, :]
        scaled = upstream * gains[0:1, :]
        mean = jnp.mean(scaled, axis=1, keepdims=True)
        cross = jnp.mean(scaled * normal_rows, axis=1, keepdims=True)
        in_rows[at, :] = grad_mid[at, :] + scale * (scaled - mean - normal_rows * cross)
        return (
            carry[0] + jnp.sum(upstream * normal_rows, axis=0, keepdims=True),
            carry[1] + jnp.sum(upstream, axis=0, keepdims=True),
        )

    sums = lax.fori_loop(0, 4, in_back, (jnp.zeros((1, 2048), F32),) * 2)
    in_copy, in_keep = to_halves(in_rows, in_half, 19)
    run_until(w_flow)

    def turn_weights(i, carry):
        for j in range(2):
            w_grad_rows = w_grad[tile(i), j * 128 : j * 128 + 128].T
            attn_rows[j * 128 : j * 128 + 128, tile(i)] = w_grad_rows
        return carry

    for g in range(16):
        at = slice(g * 128, g * 128 + 128)
        for k in range(2):
            row_parts[g, k : k + 1, :] = sums[k][:, at]
        row_parts[g, 2:6, :] = row_vec[0:4, at]
        row_parts[g, 6:8, :] = jnp.zeros((2, 128), F32)
    copies = []
    for k, offset in enumerate(ALL_G):
        to = net.place(offset, "z", "c", "f")
        copies.append(net.push(row_parts.at[to], row_got.at[k], offset))
    lax.fori_loop(0, 4, turn_weights, 0)
    attn_copies, attn_keep = to_rows(attn_rows, attn_got, 20)
    packed[11:13, :] = head_vec[0:2, :]
    for k in range(3):
        for j in range(4):
            at = 13 + 4 * k + j
            packed[at : at + 1, :] = hid_vec[k : k + 1, j * 128 : j * 128 + 128]
    packed[25:32, :] = jnp.zeros((7, 128), F32)
    for copy in copies:
        copy.wait_recv()
    total = row_parts[me]
    for k in range(15):
        total = total + row_got[k]
    packed[0:8, :] = total
    copies = [net.push(packed, packed_got.at[k], offset) for k, offset in enumerate(ALL_T)]
    for copy in copies:
        copy.wait_recv()
    total = packed[...]
    for k in range(7):
        total = total + packed_got[k]
    vectors[me] = total
    copies = [net.push(vectors.at[me], vectors.at[me], offset) for offset in ALL_G]
    for copy in ffn_copies + attn_copies + copies + [out_copy, in_copy]:
        copy.wait_recv()
    for keep in (ffn_keep, attn_keep, out_keep, in_keep):
        keep.wait()
    net.finish()


def tail(number, *args):
    half = sds((128, 1024), F32)
    rows = pltpu.VMEM((64, 2048), F32)
    return comm_call(
        tail_kernel,
        "tail",
        number,
        12 + 22 + 7 + 20 + 12 + 2 + 7 + 37,
        23,
        (
            half,
            half,
            sds((8, 32, 512), F32),
            sds((8, 32, 1024), BF),
            sds((16, 32, 128), F32),
        ),
        scatter_scratch(1024, 256, False)
        + [pltpu.VMEM((1024, 256), F32)]
        + scatter_scratch(64, 2048, True)
        + scatter_scratch(64, 2048, True)
        + scatter_scratch(512, 256, False)
        + [
            pltpu.VMEM((512, 256), F32),
            pltpu.VMEM((256, 1024), BF),
            pltpu.VMEM((256, 512), F32),
            rows,
            rows,
            rows,
            pltpu.VMEM((1024, 384), BF),
            pltpu.VMEM((384, 1024), BF),
            pltpu.VMEM((1024, 2048), BF),
            pltpu.VMEM((2048, 512), BF),
            pltpu.VMEM((1024, 2048), BF),
            pltpu.VMEM((1024, 2048), BF),
            pltpu.VMEM((16, 8, 128), F32),
            pltpu.VMEM((15, 8, 128), F32),
            pltpu.VMEM((32, 128), F32),
            pltpu.VMEM((7, 32, 128), F32),
        ],
        [ANY, ANY] + [VMEM] * 8 + [ANY] * 3 + [VMEM] * 9,
        (VMEM,) * 5,
        *args,
    )


def assemble_kernel(
    out_in,
    in_in,
    attn_in,
    ffn_in,
    sums_in,
    out_half,
    in_half,
    qkv_out,
    out_out,
    up_out,
    down_out,
    qkv_bias,
    gains_out,
    shifts_out,
    out_bias,
    down_bias,
    up_bias,
    hid_gain_out,
    hid_shift_out,
    attn_got,
    ffn_got,
    sums,
    sems,
):
    pairs = ((out_in, out_half), (in_in, in_half), (sums_in, sums), (attn_in, attn_got), (ffn_in, ffn_got))
    copies = [pltpu.make_async_copy(a, b, sems.at[k]) for k, (a, b) in enumerate(pairs)]
    for copy in copies:
        copy.start()
    for copy in copies:
        copy.wait()

    def weights(i, carry):
        small, large = tile(i, 128), tile(i, 512)
        for j in range(3):
            qkv_out[j, :, small] = attn_got[i, :, j * 128 : j * 128 + 128]
        out_out[:, small] = attn_got[i, :, 384:512]
        up_out[:, large] = ffn_got[i, :, 0:512].astype(F32)
        down_out[:, large] = ffn_got[i, :, 512:1024].astype(F32)
        return carry

    lax.fori_loop(0, 8, weights, 0)

    def place(g, carry):
        by_rows, row_lanes = pl.ds(g, 1), tile(g)
        head = lax.rem(g, 2) * 8 + g // 2
        head_lanes = tile(head)
        for k, (target, j) in enumerate(
            ((gains_out, 0), (shifts_out, 0), (gains_out, 2), (shifts_out, 2))
        ):
            target[j : j + 1, row_lanes] = sums[g, k : k + 1, :]
        out_bias[by_rows, :] = sums[g, 4:5, :]
        down_bias[by_rows, :] = sums[g, 5:6, :]
        qkv_bias[:, head_lanes] = sums[g, 8:11, :]
        gains_out[1:2, head_lanes] = sums[g, 11:12, :]
        shifts_out[1:2, head_lanes] = sums[g, 12:13, :]
        for k, target in enumerate((up_bias, hid_gain_out, hid_shift_out)):
            for j in range(4):
                at = 13 + 4 * k + j
                target[pl.ds(head * 4 + j, 1), :] = sums[g, at : at + 1, :]
        return carry

    lax.fori_loop(0, 16, place, 0)


def assemble(*args):
    vector, hidden = sds((16, 128), F32), sds((64, 128), F32)
    triple = sds((3, 2048), F32)
    half = sds((128, 1024), F32)
    return pl.pallas_call(
        assemble_kernel,
        out_shape=(
            half,
            half,
            sds((3, 32, 1024), F32),
            sds((32, 1024), F32),
            sds((32, 4096), F32),
            sds((32, 4096), F32),
            triple,
            triple,
            triple,
            vector,
            vector,
            hidden,
            hidden,
            hidden,
        ),
        in_specs=[ANY] * 5,
        out_specs=(VMEM,) * 14,
        scratch_shapes=[
            pltpu.VMEM((8, 32, 512), F32),
            pltpu.VMEM((8, 32, 1024), BF),
            pltpu.VMEM((16, 32, 128), F32),
            DMA((5,)),
        ],
        name="assemble",
        compiler_params=pltpu.CompilerParams(vmem_limit_bytes=60 << 20),
    )(*args)


def both_heads(rows, zero):
    lanes = lax.broadcasted_iota(jnp.int32, rows.shape, 1)
    return jnp.where(lanes < HEAD, rows, zero), jnp.where(lanes >= HEAD, rows, zero)


def run_rows(ref, run):
    return ref[pl.ds(pl.multiple_of(run * RUN, RUN), RUN), :]


def pair_rows(ref, run_a, run_b, dtype):
    zero = jnp.zeros((), dtype)
    a = both_heads(run_rows(ref, run_a).astype(dtype), zero)
    b = both_heads(run_rows(ref, run_b).astype(dtype), zero)
    return jnp.concatenate(a + b, axis=0)


def pair_bounds(rank_a, rank_b):
    lanes = lax.broadcasted_iota(jnp.int32, (1, 256), 1)
    rank = jnp.where(lanes < 128, rank_a, rank_b)
    last = rank * RUN + lax.rem(lanes, RUN)
    return (rank // 64) * 4096, last


def seen(chunk, low, last):
    keys = chunk * CHUNK + lax.broadcasted_iota(jnp.int32, (CHUNK, 256), 0)
    return (keys >= low) & (keys <= last)


def sort_keys(order, kv_ref, kv):
    def move(r, carry):
        target = pl.ds(pl.multiple_of(order[0, r] * RUN, RUN), RUN)
        kv[target, :] = run_rows(kv_ref, r)
        return carry

    lax.fori_loop(0, 128, move, 0, unroll=4)


def flip(kv, columns, target):
    def one(i, carry):
        target[i] = kv[tile(i, CHUNK), columns].T
        return carry

    lax.fori_loop(0, 8192 // CHUNK, one, 0, unroll=2)


def over_chunks(rank_a, rank_b, step, start):
    low = (rank_a // 64) * (4096 // CHUNK)
    whole = jnp.where(rank_a // 64 == rank_b // 64, (rank_a // (CHUNK // RUN) - low), 0)

    def two(i, state):
        return step(low + i, state, False)

    state = lax.fori_loop(0, whole, two, start)
    return lax.fori_loop(
        low + whole, rank_b // (CHUNK // RUN) + 1, lambda i, state: step(i, state, True), state
    )


def lane_heads(total):
    turned = total.T
    lanes = lax.broadcasted_iota(jnp.int32, (RUN, 128), 1)
    a = jnp.where(lanes < HEAD, turned[0:64], turned[64:128])
    b = jnp.where(lanes < HEAD, turned[128:192], turned[192:256])
    return a, b


def attend_kernel(order, q_ref, kv_ref, o_ref, lse_ref, kv, flipped):
    sort_keys(order, kv_ref, kv)
    flip(kv, slice(128, 256), flipped)

    def pair(p, carry):
        run_a, run_b = order[1, 2 * p], order[1, 2 * p + 1]
        rank_a, rank_b = order[2, 2 * p], order[2, 2 * p + 1]
        queries = pair_rows(q_ref, run_a, run_b, BF)
        low, last = pair_bounds(rank_a, rank_b)

        def step(i, state, masked):
            peak, total, mixed = state
            scores = lax.dot_general(
                kv[tile(i, CHUNK), 0:128], queries, NT, preferred_element_type=F32
            )
            if masked:
                scores = jnp.where(seen(i, low, last), scores, -1e30)
            new_peak = jnp.maximum(peak, jnp.max(scores, axis=0, keepdims=True))
            weights = jnp.exp(scores - new_peak)
            shrink = jnp.exp(peak - new_peak)
            total = total * shrink + jnp.sum(weights, axis=0, keepdims=True)
            mixed = mixed * shrink + lax.dot_general(
                flipped[i], weights.astype(BF), NN, preferred_element_type=F32
            )
            return new_peak, total, mixed

        start = (
            jnp.full((1, 256), -1e20, F32),
            jnp.zeros((1, 256), F32),
            jnp.zeros((128, 256), F32),
        )
        peak, total, mixed = over_chunks(rank_a, rank_b, step, start)
        a, b = lane_heads(mixed / total)
        o_ref[pl.ds(pl.multiple_of(run_a * RUN, RUN), RUN), :] = a
        o_ref[pl.ds(pl.multiple_of(run_b * RUN, RUN), RUN), :] = b
        lse_ref[p] = peak + jnp.log(total)
        return carry

    lax.fori_loop(0, 8, pair, 0)


def attend(order, queries, kv):
    return pl.pallas_call(
        attend_kernel,
        out_shape=(sds((1024, 128), F32), sds((8, 1, 256), F32)),
        grid_spec=pltpu.PrefetchScalarGridSpec(
            num_scalar_prefetch=1,
            grid=(1,),
            in_specs=[VMEM, VMEM],
            out_specs=(VMEM, VMEM),
            scratch_shapes=[
                pltpu.VMEM((8192, 256), BF),
                pltpu.VMEM((8192 // CHUNK, 128, CHUNK), BF),
            ],
        ),
        name="attend",
        cost_estimate=pl.CostEstimate(flops=30_000_000_000, bytes_accessed=20_000_000, transcendentals=0),
        compiler_params=pltpu.CompilerParams(vmem_limit_bytes=60 << 20),
    )(order, queries, kv)


def attend_back_kernel(
    order, q_ref, kv_ref, g_ref, a_ref, lse_ref, dq_ref, dkv_ref, kv, flipped, dkeys, dvalues
):
    sort_keys(order, kv_ref, kv)
    flip(kv, slice(0, 128), flipped)

    def clear(i, carry):
        dkeys[tile(i, CHUNK), :] = jnp.zeros((CHUNK, 128), F32)
        dvalues[tile(i, CHUNK), :] = jnp.zeros((CHUNK, 128), F32)
        return carry

    lax.fori_loop(0, 8192 // CHUNK, clear, 0)

    def pair(p, carry):
        run_a, run_b = order[1, 2 * p], order[1, 2 * p + 1]
        rank_a, rank_b = order[2, 2 * p], order[2, 2 * p + 1]
        queries = pair_rows(q_ref, run_a, run_b, BF)
        grads = pair_rows(g_ref, run_a, run_b, BF)
        low, last = pair_bounds(rank_a, rank_b)
        product = pair_rows(g_ref, run_a, run_b, F32) * pair_rows(a_ref, run_a, run_b, F32)
        delta = row_sums(product)
        log_total = lse_ref[p]

        def step(i, dq, masked):
            rows = tile(i, CHUNK)
            scores = lax.dot_general(kv[rows, 0:128], queries, NT, preferred_element_type=F32)
            dprobs = lax.dot_general(kv[rows, 128:256], grads, NT, preferred_element_type=F32)
            probs = jnp.exp(scores - log_total)
            if masked:
                probs = jnp.where(seen(i, low, last), probs, 0.0)
            dscores = (probs * (dprobs - delta)).astype(BF)
            dvalues[rows, :] += lax.dot_general(
                probs.astype(BF), grads, NN, preferred_element_type=F32
            )
            dkeys[rows, :] += lax.dot_general(dscores, queries, NN, preferred_element_type=F32)
            return dq + lax.dot_general(flipped[i], dscores, NN, preferred_element_type=F32)

        dq = over_chunks(rank_a, rank_b, step, jnp.zeros((128, 256), F32))
        a, b = lane_heads(dq)
        dq_ref[pl.ds(pl.multiple_of(run_a * RUN, RUN), RUN), :] = a * 0.125
        dq_ref[pl.ds(pl.multiple_of(run_b * RUN, RUN), RUN), :] = b * 0.125
        return carry

    lax.fori_loop(0, 8, pair, 0)

    def back(r, carry):
        source = pl.ds(pl.multiple_of(order[0, r] * RUN, RUN), RUN)
        to = pl.ds(pl.multiple_of(r * RUN, RUN), RUN)
        dkv_ref[to, 0:128] = dkeys[source, :].astype(BF)
        dkv_ref[to, 128:256] = dvalues[source, :].astype(BF)
        return carry

    lax.fori_loop(0, 128, back, 0, unroll=4)


def attend_back(order, queries, kv, grads, attended, log_total):
    return pl.pallas_call(
        attend_back_kernel,
        out_shape=(sds((1024, 128), F32), sds((8192, 256), BF)),
        grid_spec=pltpu.PrefetchScalarGridSpec(
            num_scalar_prefetch=1,
            grid=(1,),
            in_specs=[VMEM] * 5,
            out_specs=(VMEM, VMEM),
            scratch_shapes=[
                pltpu.VMEM((8192, 256), BF),
                pltpu.VMEM((8192 // CHUNK, 128, CHUNK), BF),
                pltpu.VMEM((8192, 128), F32),
                pltpu.VMEM((8192, 128), F32),
            ],
        ),
        name="attend_back",
        cost_estimate=pl.CostEstimate(flops=30_000_000_000, bytes_accessed=20_000_000, transcendentals=0),
        compiler_params=pltpu.CompilerParams(vmem_limit_bytes=60 << 20),
    )(order, queries, kv, grads, attended, log_total)


def lane_tables(seq_length):
    half = HEAD // 2
    indices = (np.arange(128) % half).astype(np.float32)
    inverse_freq = np.exp(-np.log(np.float32(10000.0)) * indices / np.float32(half)).astype(np.float64)
    ratios = np.log((2.0 * indices + 0.4 * HEAD) / (1.4 * HEAD)).astype(np.float64)

    def tables(places, powers):
        angles = places[:, None] * inverse_freq[None, :]
        growth = np.exp(powers[:, None] * ratios[None, :])
        return np.stack([np.cos(angles), np.sin(angles), growth]).astype(np.float32)

    runs = np.arange(64) * float(RUN)
    tokens = np.arange(RUN).astype(np.float64)
    return (
        jnp.asarray(tables(runs, (runs - seq_length // 2) / 512.0)),
        jnp.asarray(tables(tokens, tokens / 512.0)),
    )


def shards(
    layer_input,
    w_qkv,
    w_out,
    w_up,
    w_down,
    b_qkv,
    b_out,
    b_up,
    b_down,
    norm_gains,
    norm_shifts,
    hidden_gain,
    hidden_shift,
    seq_ids,
    positions,
    d_out,
):
    packed = jnp.concatenate(
        [
            w_qkv.reshape(32, 3, 8, 128).transpose(2, 0, 1, 3).reshape(8, 32, 384),
            w_out.reshape(32, 8, 128).transpose(1, 0, 2),
        ],
        axis=2,
    )
    run_tables, token_tables = lane_tables(4096)
    (
        input_rows,
        in_low,
        w_attn,
        ffn_block,
        query_low,
        kv,
        grad_all,
        cosine,
        sine,
        growth,
        order,
        w_norm,
    ) = front(
        1,
        layer_input,
        d_out,
        packed,
        w_up,
        w_down,
        seq_ids.reshape(1, 128),
        positions.reshape(1, 128),
        norm_gains,
        norm_shifts,
        b_qkv,
        run_tables,
        token_tables,
    )
    ffn_near = (
        lax.ppermute(ffn_block, "x", UP),
        lax.ppermute(ffn_block, "x", DOWN),
        lax.ppermute(ffn_block, "h", ACROSS),
    )
    attended, log_total = attend(order, query_low, kv)
    (
        mid,
        grad_mid,
        ffn_part,
        grad_attended,
        ffn_up,
        ffn_down,
        ffn_across,
        ffn_own,
        branch_all,
        attn_turned,
        hid_vec,
        head_vec,
        row_vec,
    ) = middle(
        3,
        attended,
        w_attn,
        ffn_block,
        *ffn_near,
        grad_all,
        input_rows,
        b_out.reshape(1, 2048),
        b_up.reshape(1, 8192),
        norm_gains,
        norm_shifts,
        hidden_gain.reshape(1, 8192),
        hidden_shift.reshape(1, 8192),
        w_norm,
    )
    ffn_got = (
        lax.ppermute(ffn_up, "x", UP),
        lax.ppermute(ffn_down, "x", DOWN),
        lax.ppermute(ffn_across, "h", ACROSS),
    )
    query_grad, kv_part = attend_back(order, query_low, kv, grad_attended, attended, log_total)
    parts = tail(
        4,
        kv_part.reshape(8, 1024, 256),
        ffn_part.reshape(16, 64, 2048),
        ffn_own,
        *ffn_got,
        query_grad,
        cosine,
        sine,
        growth,
        w_attn,
        in_low,
        branch_all,
        attn_turned,
        mid,
        grad_mid,
        input_rows,
        b_down.reshape(1, 2048),
        norm_gains,
        hid_vec,
        head_vec,
        row_vec,
    )
    (
        layer_output,
        input_grad,
        qkv_grad,
        out_grad,
        up_grad,
        down_grad,
        qkv_bias,
        gains_grad,
        shifts_grad,
        out_bias,
        down_bias,
        up_bias,
        hid_gain_grad,
        hid_shift_grad,
    ) = assemble(*parts)
    return (
        layer_output,
        input_grad,
        qkv_grad.transpose(1, 0, 2),
        out_grad,
        up_grad,
        down_grad,
        qkv_bias,
        out_bias.reshape(2048),
        up_bias.reshape(8192),
        down_bias.reshape(2048),
        gains_grad,
        shifts_grad,
        hid_gain_grad.reshape(8192),
        hid_shift_grad.reshape(8192),
    )


def solution(mesh):
    fine = Mesh(mesh.devices.reshape(4, 2, 4, 2, 2), SEQ + ("f",))
    both = P(SEQ, "f")
    return jax.shard_map(
        shards,
        mesh=fine,
        in_specs=(both, P(SEQ, None, "f"), both, both, both)
        + (P(),) * 8
        + (P(SEQ), P(SEQ), both),
        out_specs=(both, both, P(SEQ, None, "f"), both, both, both) + (P(),) * 8,
        check_vma=False,
    )
```
